32 devices in a mesh: cam: 4 (over y, x), batch: 8 (over z, core).
Axes of the slice: x: 2, y: 2, z: 4, core: 2. Of those that a mesh axis runs over, the one named last changes fastest.
Arguments:
- images: bfloat16 [4, 4, 256, 2, 9, 512], P('cam', None, 'batch'), may hold values from -6 to 6
- trajectory: bfloat16 [1024, 16, 512], P(('cam', 'batch')), may hold values from -6 to 6
- view_mask: int32 [1024, 4], P(('cam', 'batch')), may hold values from 0 to 1, as said below
- timesteps: int32 [1024], P(('cam', 'batch')), may hold values from 0 to 999
- out_grad: bfloat16 [1024, 8, 512], P(('cam', 'batch')), may hold values from -6 to 6
- encoder_weight: float32 [4, 512, 2, 4608], P('cam', 'batch'), may hold values from -0.09375 to 0.09375
- encoder_affine: float32 [4, 512, 4], P('cam', 'batch'), may hold values from -0.9 to 1.75
- block_convs: float32 [512, 2, 2560], P('batch'), may hold values from -0.125 to 0.125
- film_weight: float32 [512, 2, 1152], P('batch'), may hold values from -0.1875 to 0.1875
- skip_weight: float32 [512, 512], P('batch'), may hold values from -0.25 to 0.25
- down_weight: float32 [512, 1536], P('batch'), may hold values from -0.15625 to 0.15625
- block_affine: float32 [512, 10], P('batch'), may hold values from -0.9 to 1.75
- first_encoder: float32 [4, 512, 2, 4608], P('cam', 'batch'), may hold values from -40 to 40
- first_affine: float32 [4, 512, 4], P('cam', 'batch'), may hold values from -40 to 40
- first_convs: float32 [512, 2, 2560], P('batch'), may hold values from -384 to 384
- first_film: float32 [512, 2, 1152], P('batch'), may hold values from -384 to 384
- first_skip: float32 [512, 512], P('batch'), may hold values from -384 to 384
- first_down: float32 [512, 1536], P('batch'), may hold values from -384 to 384
- first_block: float32 [512, 10], P('batch'), may hold values from -384 to 384
- second_encoder: float32 [4, 512, 2, 4608], P('cam', 'batch'), may hold values from 46.08 to 184.32
- second_affine: float32 [4, 512, 4], P('cam', 'batch'), may hold values from 46.08 to 184.32
- second_convs: float32 [512, 2, 2560], P('batch'), may hold values from 4096 to 16384
- second_film: float32 [512, 2, 1152], P('batch'), may hold values from 4096 to 16384
- second_skip: float32 [512, 512], P('batch'), may hold values from 4096 to 16384
- second_down: float32 [512, 1536], P('batch'), may hold values from 4096 to 16384
- second_block: float32 [512, 10], P('batch'), may hold values from 4096 to 16384
Outputs:
- block_output: bfloat16 [1024, 8, 512], P(('cam', 'batch'))
- trajectory_grad: float32 [1024, 16, 512], P(('cam', 'batch'))
- images_grad: float32 [4, 4, 256, 2, 9, 512], P('cam', None, 'batch')
- next_encoder: float32 [4, 512, 2, 4608], P('cam', 'batch')
- next_affine: float32 [4, 512, 4], P('cam', 'batch')
- next_convs: float32 [512, 2, 2560], P('batch')
- next_film: float32 [512, 2, 1152], P('batch')
- next_skip: float32 [512, 512], P('batch')
- next_down: float32 [512, 1536], P('batch')
- next_block: float32 [512, 10], P('batch')
- mean_encoder: float32 [4, 512, 2, 4608], P('cam', 'batch')
- mean_affine: float32 [4, 512, 4], P('cam', 'batch')
- mean_convs: float32 [512, 2, 2560], P('batch')
- mean_film: float32 [512, 2, 1152], P('batch')
- mean_skip: float32 [512, 512], P('batch')
- mean_down: float32 [512, 1536], P('batch')
- mean_block: float32 [512, 10], P('batch')
- square_encoder: float32 [4, 512, 2, 4608], P('cam', 'batch')
- square_affine: float32 [4, 512, 4], P('cam', 'batch')
- square_convs: float32 [512, 2, 2560], P('batch')
- square_film: float32 [512, 2, 1152], P('batch')
- square_skip: float32 [512, 512], P('batch')
- square_down: float32 [512, 1536], P('batch')
- square_block: float32 [512, 10], P('batch')
The draws below stay inside these ranges and needn't reach their ends.
Inputs may be any that keep to these rules, and one draw needn't show every extreme that they name: `view_mask`: every sample has at least one present view.
All inputs are finite; a program needn't handle non-finite values.
Results may differ from the reference program's by a relative error of at most 0.012.
Values may be sent and summed in bfloat16 or wider, within the bound.
A program may use at most 384 MiB of HBM per device.

```python
import math
import jax
import jax.numpy as jnp
from jax import lax

C = 512
TEMB = 128
CAMS = 4
OBS = 2
SPATIAL = 9
FR = 16
K = 5
GROUPS = 8
STEP = 5
SAMPLES = 1024
COND = 1152


def affine_table(key, table_shape, gain_columns):
    noise = jax.random.truncated_normal(key, -3.0, 3.0, table_shape, jnp.float32)
    return jnp.where(gain_columns, 1.0 + 0.25 * noise, 0.3 * noise)


def draw_view_mask(key, part):
    key = jax.random.fold_in(key, 7)
    pattern = jax.random.randint(key, (SAMPLES, 1), 1, 2 ** CAMS, dtype=jnp.int32)
    powers = 2 ** jnp.arange(CAMS, dtype=jnp.int32)
    return pattern // powers[None, :] % 2


def draw_encoder_affine(key, part):
    key = jax.random.fold_in(key, 11)
    column_index = jnp.arange(4)
    return affine_table(key, (CAMS, C, 4), column_index % 2 == 0)


def draw_block_affine(key, part):
    key = jax.random.fold_in(key, 13)
    column_index = jnp.arange(10)
    gain_columns = (column_index == 0) | (column_index == 2) | (column_index == 6)
    return affine_table(key, (C, 10), gain_columns)


def touch_ends(entries, stream_key, low, largest):
    extent = entries.shape
    index_at = [jax.random.randint(jax.random.fold_in(stream_key, axis), (), 0, extent[axis]) for axis in range(len(extent))]
    entries = entries.at[tuple(index_at)].set(low)
    longest = extent.index(max(extent))
    index_at[longest] = (index_at[longest] + 1) % extent[longest]
    return entries.at[tuple(index_at)].set(largest)


def block_scale(rng, shape, cuts, low, largest):
    loudness = 1.0
    for position, parts in cuts:
        heights = jax.random.uniform(jax.random.fold_in(jax.random.fold_in(rng, 6), position), (parts,), jnp.float32, low / len(cuts), largest / len(cuts))
        loudness = loudness * jnp.repeat(jnp.exp(heights), shape[position] // parts).reshape((-1,) + (1,) * (len(shape) - 1 - position))
    return loudness


def bell_draw(rng, shape, deviation, limit, cuts=(), kind=jnp.bfloat16):
    entries = jax.random.normal(rng, shape, jnp.float32) * deviation
    if len(cuts) > 0:
        entries = block_scale(rng, shape, cuts, -0.22, 0.18) * entries
    return jnp.clip(entries, min=-limit, max=limit).astype(kind)


def setup_inputs(seed: int = 0) -> dict:
    key_of = jax.random.split(jax.random.key(seed), 27)
    images = bell_draw(key_of[0], (CAMS, CAMS, SAMPLES // CAMS, OBS, SPATIAL, C), 1.0, 6.0, ((0, 4), (2, 8)))
    trajectory = bell_draw(key_of[1], (SAMPLES, FR, C), 1.0, 6.0, ((0, 32),))
    view_mask = draw_view_mask(jax.random.fold_in(key_of[26], 71), 0)
    timesteps = touch_ends(jax.random.randint(key_of[3], (SAMPLES,), 0, 1000), jax.random.fold_in(key_of[3], 1), 0, 999).astype(jnp.int32)
    out_grad = bell_draw(key_of[4], (SAMPLES, FR // 2, C), 1.0, 6.0, ((0, 32),))
    encoder_weight = bell_draw(key_of[5], (CAMS, C, 2, 9 * C), (9 * C) ** -0.5, 0.09375, ((0, 4), (1, 8)), jnp.float32)
    encoder_affine = draw_encoder_affine(jax.random.fold_in(key_of[26], 71), 0)
    block_convs = bell_draw(key_of[7], (C, 2, K * C), (K * C) ** -0.5, 0.125, ((0, 8),), jnp.float32)
    film_weight = bell_draw(key_of[8], (C, 2, COND), COND ** -0.5, 0.1875, ((0, 8),), jnp.float32)
    skip_weight = bell_draw(key_of[9], (C, C), C ** -0.5, 0.25, ((0, 8),), jnp.float32)
    down_weight = bell_draw(key_of[10], (C, 3 * C), (3 * C) ** -0.5, 0.15625, ((0, 8),), jnp.float32)
    block_affine = draw_block_affine(jax.random.fold_in(key_of[26], 71), 0)
    first_encoder = bell_draw(key_of[12], (CAMS, C, 2, 9 * C), (0.05 * (SAMPLES * OBS * SPATIAL) ** 0.5), 40.0, ((0, 4), (1, 8)), jnp.float32)
    first_affine = bell_draw(key_of[13], (CAMS, C, 4), (0.05 * (SAMPLES * OBS * SPATIAL) ** 0.5), 40.0, ((0, 4), (1, 8)), jnp.float32)
    first_convs = bell_draw(key_of[14], (C, 2, K * C), (0.5 * (SAMPLES * FR) ** 0.5), 384.0, ((0, 8),), jnp.float32)
    first_film = bell_draw(key_of[15], (C, 2, COND), (0.5 * (SAMPLES * FR) ** 0.5), 384.0, ((0, 8),), jnp.float32)
    first_skip = bell_draw(key_of[16], (C, C), (0.5 * (SAMPLES * FR) ** 0.5), 384.0, ((0, 8),), jnp.float32)
    first_down = bell_draw(key_of[17], (C, 3 * C), (0.5 * (SAMPLES * FR) ** 0.5), 384.0, ((0, 8),), jnp.float32)
    first_block = bell_draw(key_of[18], (C, 10), (0.5 * (SAMPLES * FR) ** 0.5), 384.0, ((0, 8),), jnp.float32)
    second_encoder = jnp.clip(jnp.exp(math.log(184.32) - 1.3862944 * jax.random.uniform(key_of[19], (CAMS, C, 2, 9 * C), jnp.float32) ** block_scale(key_of[19], (CAMS, C, 2, 9 * C), ((0, 4), (1, 8)), -0.2, 0.2)), 46.08, 184.32)
    second_affine = jnp.clip(jnp.exp(math.log(184.32) - 1.3862944 * jax.random.uniform(key_of[20], (CAMS, C, 4), jnp.float32) ** block_scale(key_of[20], (CAMS, C, 4), ((0, 4), (1, 8)), -0.2, 0.2)), 46.08, 184.32)
    second_convs = jnp.clip(jnp.exp(math.log(16384.0) - 1.3862944 * jax.random.uniform(key_of[21], (C, 2, K * C), jnp.float32) ** block_scale(key_of[21], (C, 2, K * C), ((0, 8),), -0.2, 0.2)), 4096.0, 16384.0)
    second_film = jnp.clip(jnp.exp(math.log(16384.0) - 1.3862944 * jax.random.uniform(key_of[22], (C, 2, COND), jnp.float32) ** block_scale(key_of[22], (C, 2, COND), ((0, 8),), -0.2, 0.2)), 4096.0, 16384.0)
    second_skip = jnp.clip(jnp.exp(math.log(16384.0) - 1.3862944 * jax.random.uniform(key_of[23], (C, C), jnp.float32) ** block_scale(key_of[23], (C, C), ((0, 8),), -0.2, 0.2)), 4096.0, 16384.0)
    second_down = jnp.clip(jnp.exp(math.log(16384.0) - 1.3862944 * jax.random.uniform(key_of[24], (C, 3 * C), jnp.float32) ** block_scale(key_of[24], (C, 3 * C), ((0, 8),), -0.2, 0.2)), 4096.0, 16384.0)
    second_block = jnp.clip(jnp.exp(math.log(16384.0) - 1.3862944 * jax.random.uniform(key_of[25], (C, 10), jnp.float32) ** block_scale(key_of[25], (C, 10), ((0, 8),), -0.2, 0.2)), 4096.0, 16384.0)
    return {"images": images, "trajectory": trajectory, "view_mask": view_mask, "timesteps": timesteps, "out_grad": out_grad, "encoder_weight": encoder_weight, "encoder_affine": encoder_affine, "block_convs": block_convs, "film_weight": film_weight, "skip_weight": skip_weight, "down_weight": down_weight, "block_affine": block_affine, "first_encoder": first_encoder, "first_affine": first_affine, "first_convs": first_convs, "first_film": first_film, "first_skip": first_skip, "first_down": first_down, "first_block": first_block, "second_encoder": second_encoder, "second_affine": second_affine, "second_convs": second_convs, "second_film": second_film, "second_skip": second_skip, "second_down": second_down, "second_block": second_block}


@jax.custom_vjp
def low(v):
    return lax.optimization_barrier(v.astype(jnp.bfloat16)).astype(jnp.float32)

@jax.custom_vjp
def low_back(v):
    return v

def low_keep(v):
    return (low(v), None)

def low_pass(kept, grad):
    return (grad,)

def back_keep(v):
    return (v, None)

def back_low(kept, grad):
    return (low(grad),)
low.defvjp(low_keep, low_pass)
low_back.defvjp(back_keep, back_low)
norm_eps = 1e-05
beta_first = 0.5
beta_second = 0.5
adam_eps = 1e-08
rate_matrix = 0.02
rate_vector = 0.2
decay_matrix = 0.01

def mish(tensor):
    return tensor * jnp.tanh(jax.nn.softplus(tensor))

def group_norm(tensor, groups):
    tensor_shape = tensor.shape
    grouped = tensor.reshape(tensor_shape[0], -1, groups, tensor_shape[-1] // groups)
    centred = grouped - lax.optimization_barrier(jnp.mean(grouped, axis=(1, 3), keepdims=True))
    variance = lax.optimization_barrier(jnp.mean(centred * centred, axis=(1, 3), keepdims=True))
    return (centred * lax.rsqrt(variance + norm_eps)).reshape(tensor_shape)

def time_embed(steps_given, embed_width):
    half_width = embed_width // 2
    frequency = jnp.exp(jnp.arange(half_width, dtype=jnp.float32) * (-math.log(10000.0) / (half_width - 1)))
    argument = steps_given.astype(jnp.float32)[:, None] * frequency[None, :]
    return jnp.concatenate([jnp.sin(argument), jnp.cos(argument)], axis=1)

def grid_conv(tensor, weight):
    padded = jnp.pad(tensor, ((0, 0), (1, 1), (1, 1), (0, 0)))
    columns = jnp.concatenate([padded[:, step_row:step_row + 3, step_column:step_column + 3] for step_row in range(3) for step_column in range(3)], axis=-1)
    return jnp.einsum('nhwk,ok->nhwo', columns, weight, precision=lax.Precision.HIGHEST)

def line_conv(tensor, weight):
    length_all = tensor.shape[1]
    padded = jnp.pad(tensor, ((0, 0), (2, 2), (0, 0)))
    columns = jnp.concatenate([padded[:, offset:offset + length_all] for offset in range(5)], axis=-1)
    return jnp.einsum('sfk,ok->sfo', columns, weight, precision=lax.Precision.HIGHEST)

def down_columns(tensor):
    pairs = tensor.reshape(tensor.shape[0], tensor.shape[1] // 2, 2, tensor.shape[2])
    even_part = pairs[:, :, 0]
    odd_part = pairs[:, :, 1]
    odd_before = jnp.pad(odd_part, ((0, 0), (1, 0), (0, 0)))[:, :-1]
    return jnp.concatenate([odd_before, even_part, odd_part], axis=-1)

def adamw(weight, gradient, moment_one, moment_two, step_rate, weight_decay):
    mean_new = beta_first * moment_one + (1.0 - beta_first) * gradient
    square_new = beta_second * moment_two + (1.0 - beta_second) * gradient * gradient
    mean_hat = mean_new / (1.0 - beta_first ** STEP)
    square_hat = square_new / (1.0 - beta_second ** STEP)
    weight_new = weight - step_rate * (mean_hat / (jnp.sqrt(square_hat) + adam_eps) + weight_decay * weight)
    return (weight_new, mean_new, square_new)

def reference(images, trajectory, view_mask, timesteps, out_grad, encoder_weight, encoder_affine, block_convs, film_weight, skip_weight, down_weight, block_affine, first_encoder, first_affine, first_convs, first_film, first_skip, first_down, first_block, second_encoder, second_affine, second_convs, second_film, second_skip, second_down, second_block):
    present = view_mask.astype(jnp.float32)
    embedded = time_embed(timesteps, TEMB)

    def encode(packed):
        pictures, weights, affine = packed
        flat = pictures.reshape(-1, 3, 3, C)
        section_one = low_back(grid_conv(low(flat), weights[:, 0]))
        active_one = low(jax.nn.silu(group_norm(section_one, C // 16) * affine[:, 0] + affine[:, 1]))
        section_two = low_back(grid_conv(active_one, weights[:, 1]))
        result = jax.nn.silu(group_norm(section_two, C // 16) * affine[:, 2] + affine[:, 3] + flat)
        return low_back(low(lax.optimization_barrier(jnp.mean(result, axis=(1, 2))).reshape(SAMPLES, OBS, C)))

    def forward(image_values, traj_values, weights):
        encoder_low, affine_low, convs_low, film_low, skip_low, down_low, block_low = tuple((low(item) for item in weights))
        pictures = image_values.reshape(CAMS, SAMPLES, OBS, 3, 3, C)
        feats = lax.map(jax.checkpoint(encode), (pictures, encoder_low, affine_low))
        count = lax.optimization_barrier(jnp.sum(present, axis=1))
        pooled = lax.optimization_barrier(jnp.sum(jnp.transpose(present)[:, :, None, None] * feats, axis=0)) / count[:, None, None]
        condition = low(mish(jnp.concatenate([pooled.reshape(SAMPLES, OBS * C), embedded], axis=1)))
        film_out = low_back(jnp.einsum('sk,ojk->sjo', condition, film_low, precision=lax.Precision.HIGHEST)) + jnp.transpose(block_low[:, 6:8])[None]
        traj_low = low(traj_values)
        hidden_a = low_back(line_conv(traj_low, convs_low[:, 0])) + block_low[:, 4]
        middle = low(mish(group_norm(hidden_a, GROUPS) * block_low[:, 0] + block_low[:, 1]) * film_out[:, 0][:, None, :] + film_out[:, 1][:, None, :])
        hidden_b = low_back(line_conv(middle, convs_low[:, 1])) + block_low[:, 5]
        skip_term = low_back(jnp.einsum('sfi,oi->sfo', traj_low, skip_low, precision=lax.Precision.HIGHEST)) + block_low[:, 8]
        summed = low(mish(group_norm(hidden_b, GROUPS) * block_low[:, 2] + block_low[:, 3]) + skip_term)
        return low_back(jnp.einsum('stk,ok->sto', down_columns(summed), down_low, precision=lax.Precision.HIGHEST)) + block_low[:, 9]
    params = (encoder_weight, encoder_affine, block_convs, film_weight, skip_weight, down_weight, block_affine)
    output_value, backward = jax.vjp(forward, images.astype(jnp.float32), trajectory.astype(jnp.float32), params)
    images_grad, trajectory_grad, grads = backward(out_grad.astype(jnp.float32))
    upd_encoder = adamw(encoder_weight, grads[0], first_encoder, second_encoder, rate_matrix, decay_matrix)
    upd_affine = adamw(encoder_affine, grads[1], first_affine, second_affine, rate_vector, 0.0)
    upd_convs = adamw(block_convs, grads[2], first_convs, second_convs, rate_matrix, decay_matrix)
    upd_film = adamw(film_weight, grads[3], first_film, second_film, rate_matrix, decay_matrix)
    upd_skip = adamw(skip_weight, grads[4], first_skip, second_skip, rate_matrix, decay_matrix)
    upd_down = adamw(down_weight, grads[5], first_down, second_down, rate_matrix, decay_matrix)
    upd_block = adamw(block_affine, grads[6], first_block, second_block, rate_vector, 0.0)
    return (output_value.astype(jnp.bfloat16), trajectory_grad, images_grad, upd_encoder[0], upd_affine[0], upd_convs[0], upd_film[0], upd_skip[0], upd_down[0], upd_block[0], upd_encoder[1], upd_affine[1], upd_convs[1], upd_film[1], upd_skip[1], upd_down[1], upd_block[1], upd_encoder[2], upd_affine[2], upd_convs[2], upd_film[2], upd_skip[2], upd_down[2], upd_block[2])
```

```python
import functools
import math

import jax
import jax.numpy as jnp
from jax import lax
from jax.experimental import pallas as pl
from jax.experimental.pallas import tpu as pltpu
from jax.sharding import PartitionSpec as P

TEMB = 128
GROUPS = 8
STEP = 5

norm_eps = 1e-05
beta_first = 0.5
beta_second = 0.5
adam_eps = 1e-08
rate_matrix = 0.02
rate_vector = 0.2
decay_matrix = 0.01

CH = 512
BLK = 128
ENC_GROUP = 16
f32 = jnp.float32
bf16 = jnp.bfloat16
VMEM_BYTES = 60 * 1024 * 1024

NT = (((1,), (1,)), ((), ()))
NN = (((1,), (0,)), ((), ()))
TN = (((0,), (0,)), ((), ()))


def dot(a, b, dims=NN):
    return lax.dot_general(a, b, dims, preferred_element_type=f32)


def group_ones(width, group):
    rows = lax.broadcasted_iota(jnp.int32, (width, width), 0) // group
    cols = lax.broadcasted_iota(jnp.int32, (width, width), 1) // group
    return jnp.where(rows == cols, 1.0, 0.0).astype(bf16)


def group_sum(v, ones):
    high = v.astype(bf16)
    rest = v - high.astype(f32)
    middle = rest.astype(bf16)
    low = (rest - middle.astype(f32)).astype(bf16)
    return dot(high, ones) + dot(middle, ones) + dot(low, ones)


def sigmoid(v):
    return 1.0 / (1.0 + jnp.exp(-v))


def mish_pair(v):
    e = jnp.exp(jnp.minimum(v, 20.0))
    n = e * (e + 2.0)
    inv = 1.0 / (n + 2.0)
    t = n * inv
    return v * t, t + v * (4.0 * e * (1.0 + e)) * inv * inv


def mish_value(v):
    e = jnp.exp(jnp.minimum(v, 20.0))
    n = e * (e + 2.0)
    return v * (n / (n + 2.0))


def span(i):
    return range(max(0, 1 - i), min(2, 3 - i) + 1)


def enc_fwd_kernel(x_ref, w1_ref, w2_ref, aff_ref, z1_ref, r1_ref, a_ref, z2_ref, r2_ref, feat_ref):
    ones = group_ones(BLK, ENC_GROUP)
    inv_n = 1.0 / (9 * ENC_GROUP)

    def conv_norm(src_ref, w_ref, z_ref, r_ref, j):
        wrows = pl.ds(pl.multiple_of(j * BLK, BLK), BLK)
        total = None
        lanes = [pl.ds(pl.multiple_of(p * CH + j * BLK, BLK), BLK) for p in range(9)]
        for p in range(9):
            r, c = divmod(p, 3)
            bs = span(c)
            acc = None
            for a in span(r):
                start = (3 * (r + a - 1) + c + bs[0] - 1) * CH
                wstart = (3 * a + bs[0]) * CH
                wide = len(bs) * CH
                part = dot(src_ref[:, start : start + wide], w_ref[wrows, wstart : wstart + wide], NT)
                acc = part if acc is None else acc + part
            z_ref[:, lanes[p]] = acc
            total = acc if total is None else total + acc
        mean = group_sum(total, ones) * inv_n
        var = None
        for p in range(9):
            centred = z_ref[:, lanes[p]] - mean
            sq = centred * centred
            var = sq if var is None else var + sq
        rstd = lax.rsqrt(group_sum(var, ones) * inv_n + norm_eps)
        r_ref[:, wrows] = rstd
        return wrows, lanes, mean, rstd

    def first(j, carry):
        wrows, lanes, mean, rstd = conv_norm(x_ref, w1_ref, z1_ref, r1_ref, j)
        gain, offset = aff_ref[0:1, wrows], aff_ref[1:2, wrows]
        for p in range(9):
            z = (z1_ref[:, lanes[p]] - mean) * rstd
            z1_ref[:, lanes[p]] = z
            u = z * gain + offset
            a_ref[:, lanes[p]] = (u * sigmoid(u)).astype(bf16)
        return carry

    def second(j, carry):
        wrows, lanes, mean, rstd = conv_norm(a_ref, w2_ref, z2_ref, r2_ref, j)
        gain, offset = aff_ref[2:3, wrows], aff_ref[3:4, wrows]
        total = None
        for p in range(9):
            z = (z2_ref[:, lanes[p]] - mean) * rstd
            z2_ref[:, lanes[p]] = z
            u = z * gain + offset + x_ref[:, lanes[p]].astype(f32)
            act = u * sigmoid(u)
            total = act if total is None else total + act
        feat_ref[:, wrows] = (total * (1.0 / 9.0)).astype(bf16)
        return carry

    lax.fori_loop(0, CH // BLK, first, 0)
    lax.fori_loop(0, CH // BLK, second, 0)


def enc_bwd_kernel(
    x_ref, a_ref, w1_ref, w2_ref, z1_ref, r1_ref, z2_ref, r2_ref, aff_ref, gp_ref,
    dw1_ref, dw2_ref, ig_ref, ag_ref, g_ref, gt_ref, da_ref, pos_ref,
):
    rows = x_ref.shape[0]
    ones = group_ones(BLK, ENC_GROUP)
    inv_n = 1.0 / (9 * ENC_GROUP)

    def norm_back(du_ref, z_ref, r_ref, j, gain, row):
        wrows = pl.ds(pl.multiple_of(j * BLK, BLK), BLK)
        lanes = [pl.ds(pl.multiple_of(p * CH + j * BLK, BLK), BLK) for p in range(9)]
        s0 = jnp.zeros((rows, BLK), f32)
        s1 = jnp.zeros((rows, BLK), f32)
        for p in range(9):
            du = du_ref[:, lanes[p]]
            s0 = s0 + du
            s1 = s1 + du * z_ref[:, lanes[p]]
        ag_ref[row : row + 1, wrows] = jnp.sum(s1, axis=0, keepdims=True)
        ag_ref[row + 1 : row + 2, wrows] = jnp.sum(s0, axis=0, keepdims=True)
        m0 = group_sum(s0 * gain, ones) * inv_n
        m1 = group_sum(s1 * gain, ones) * inv_n
        rstd = r_ref[:, wrows]
        for p in range(9):
            dv = (du_ref[:, lanes[p]] * gain - m0 - z_ref[:, lanes[p]] * m1) * rstd
            g_ref[:, lanes[p]] = dv.astype(bf16)
            gt_ref[wrows, p * rows : (p + 1) * rows] = jnp.transpose(dv).astype(bf16)

    def weight_back(src_ref, dw_ref):
        for p in range(9):
            pos_ref[p * rows : (p + 1) * rows, :] = src_ref[:, p * CH : (p + 1) * CH]
        for a in range(3):
            for b in range(3):
                r_lo, r_hi = max(0, 1 - a), min(2, 3 - a)
                c_lo, c_hi = max(0, 1 - b), min(2, 3 - b)
                if b == 1:
                    runs = [(3 * r_lo, 3 * (r_hi - r_lo + 1))]
                else:
                    runs = [(3 * r + c_lo, c_hi - c_lo + 1) for r in range(r_lo, r_hi + 1)]
                shift = 3 * (a - 1) + b - 1
                for half in range(2):
                    hrows = slice(half * 256, half * 256 + 256)
                    acc = None
                    for p, n in runs:
                        part = dot(
                            gt_ref[hrows, p * rows : (p + n) * rows],
                            pos_ref[(p + shift) * rows : (p + shift + n) * rows, :],
                        )
                        acc = part if acc is None else acc + part
                    t = 3 * a + b
                    dw_ref[hrows, t * CH : (t + 1) * CH] = acc.astype(bf16)

    def input_back(w_ref, q):
        r, c = divmod(q, 3)
        acc = None
        for a in range(3):
            for b in range(3):
                pr, pc = r - a + 1, c - b + 1
                if 0 <= pr < 3 and 0 <= pc < 3:
                    p, t = 3 * pr + pc, 3 * a + b
                    part = dot(g_ref[:, p * CH : (p + 1) * CH], w_ref[:, t * CH : (t + 1) * CH])
                    acc = part if acc is None else acc + part
        return acc

    def second(j, carry):
        wrows = pl.ds(pl.multiple_of(j * BLK, BLK), BLK)
        gain, offset = aff_ref[2:3, wrows], aff_ref[3:4, wrows]
        pooled = gp_ref[:, wrows].astype(f32) * (1.0 / 9.0)
        for p in range(9):
            lanes = pl.ds(pl.multiple_of(p * CH + j * BLK, BLK), BLK)
            u = z2_ref[:, lanes] * gain + offset + x_ref[:, lanes].astype(f32)
            s = sigmoid(u)
            ig_ref[:, lanes] = pooled * (s * (1.0 + u * (1.0 - s)))
        norm_back(ig_ref, z2_ref, r2_ref, j, gain, 2)
        return carry

    lax.fori_loop(0, CH // BLK, second, 0)
    weight_back(a_ref, dw2_ref)
    for q in range(9):
        da_ref[:, q * CH : (q + 1) * CH] = input_back(w2_ref, q)

    def first(j, carry):
        wrows = pl.ds(pl.multiple_of(j * BLK, BLK), BLK)
        gain, offset = aff_ref[0:1, wrows], aff_ref[1:2, wrows]
        for p in range(9):
            lanes = pl.ds(pl.multiple_of(p * CH + j * BLK, BLK), BLK)
            u = z1_ref[:, lanes] * gain + offset
            s = sigmoid(u)
            da_ref[:, lanes] = da_ref[:, lanes] * (s * (1.0 + u * (1.0 - s)))
        norm_back(da_ref, z1_ref, r1_ref, j, gain, 0)
        return carry

    lax.fori_loop(0, CH // BLK, first, 0)
    weight_back(x_ref, dw1_ref)
    for q in range(9):
        ig_ref[:, q * CH : (q + 1) * CH] = ig_ref[:, q * CH : (q + 1) * CH] + input_back(w1_ref, q)


def temporal_kernel(
    traj_ref, og_ref, arr_ref, mask_ref, emb_ref, wa_ref, wb_ref, f0_ref, f1_ref, ws_ref, wd_ref, aff_ref,
    out_ref, tg_ref, dviews_ref, dwa_ref, dwb_ref, df0_ref, df1_ref, dws_ref, dwd_ref, ag_ref,
    pad_t, pad_m, pad_h, za_ref, zb_ref, sum_ref,
):
    ns = mask_ref.shape[0]
    rows = traj_ref.shape[0]
    nf = rows // ns
    edge = 2 * ns
    ones = group_ones(CH, CH // GROUPS)
    inv_n = 1.0 / (nf * (CH // GROUPS))
    aff = lambda i: aff_ref[i : i + 1, :]

    def frames(v):
        return v.reshape(nf, ns, CH)

    def fill(pad_ref, v):
        pad_ref[0:edge, :] = jnp.zeros((edge, CH), bf16)
        pad_ref[edge : edge + rows, :] = v
        pad_ref[edge + rows : edge + rows + edge, :] = jnp.zeros((edge, CH), bf16)

    def conv5(pad_ref, w_ref):
        acc = None
        for t in range(5):
            part = dot(pad_ref[t * ns : t * ns + rows, :], w_ref[:, t * CH : (t + 1) * CH], NT)
            acc = part if acc is None else acc + part
        return acc

    def conv5_back(pad_ref, w_ref):
        acc = None
        for t in range(5):
            part = dot(pad_ref[(4 - t) * ns : (4 - t) * ns + rows, :], w_ref[:, t * CH : (t + 1) * CH])
            acc = part if acc is None else acc + part
        return acc

    def norm(v):
        v = frames(v)
        mean = group_sum(jnp.sum(v, axis=0), ones) * inv_n
        centred = v - mean[None]
        rstd = lax.rsqrt(group_sum(jnp.sum(centred * centred, axis=0), ones) * inv_n + norm_eps)
        return centred * rstd[None], rstd

    def norm_back(du, z, rstd, gain):
        s0 = jnp.sum(du, axis=0)
        s1 = jnp.sum(du * z, axis=0)
        m0 = group_sum(s0 * gain, ones) * inv_n
        m1 = group_sum(s1 * gain, ones) * inv_n
        dv = (du * gain[None] - m0[None] - z * m1[None]) * rstd[None]
        return dv, jnp.sum(s1, axis=0, keepdims=True), jnp.sum(s0, axis=0, keepdims=True)

    mask = mask_ref[...]
    count = jnp.sum(mask, axis=1, keepdims=True)
    cams = arr_ref.shape[0]
    pooled = None
    for cam in range(cams):
        part = mask[:, cam : cam + 1] * arr_ref[cam].astype(f32)
        pooled = part if pooled is None else pooled + part
    pooled = pooled / count
    pm, pd = mish_pair(pooled)
    cond_v = pm.astype(bf16)
    cond_e = mish_value(emb_ref[...]).astype(bf16)
    width = cond_v.shape[1]
    film = []
    for i, w_ref in ((6, f0_ref), (7, f1_ref)):
        film.append(dot(cond_v, w_ref[:, :width], NT) + dot(cond_e, w_ref[:, width:], NT) + aff(i))
    scale, shift = film

    fill(pad_t, traj_ref[...])
    za, rstd_a = norm(conv5(pad_t, wa_ref) + aff(4))
    za_ref[...] = za.reshape(rows, CH)
    act_a = mish_value(za * aff(0)[None] + aff(1)[None])
    fill(pad_m, (act_a * scale[None] + shift[None]).astype(bf16).reshape(rows, CH))
    zb, rstd_b = norm(conv5(pad_m, wb_ref) + aff(5))
    zb_ref[...] = zb.reshape(rows, CH)
    skip = frames(dot(traj_ref[...], ws_ref[...], NT)) + aff(8)[None]
    summed = (mish_value(zb * aff(2)[None] + aff(3)[None]) + skip).astype(bf16)
    pairs = summed.reshape(nf // 2, 2, ns, CH)
    half = rows // 2
    sum_ref[0:ns, :] = jnp.zeros((ns, CH), bf16)
    sum_ref[ns : ns + half, :] = pairs[:, 1].reshape(half, CH)
    sum_ref[ns + half : ns + 2 * half, :] = pairs[:, 0].reshape(half, CH)
    taps = (0, ns + half, ns)
    out = None
    og = og_ref[...]
    dcols = []
    for t in range(3):
        cols = sum_ref[taps[t] : taps[t] + half, :]
        w = wd_ref[:, t * CH : (t + 1) * CH]
        part = dot(cols, w, NT)
        out = part if out is None else out + part
        dcols.append(dot(og, w).reshape(nf // 2, ns, CH))
        dwd_ref[:, t * CH : (t + 1) * CH] = dot(og, cols, TN).astype(bf16)
    out_ref[...] = (out + aff(9)).astype(bf16)
    ag_ref[9:10, :] = jnp.sum(og.astype(f32), axis=0, keepdims=True)

    before = jnp.concatenate([dcols[0][1:], jnp.zeros((1, ns, CH), f32)], axis=0)
    dsum = jnp.stack([dcols[1], dcols[2] + before], axis=1).reshape(nf, ns, CH)
    ag_ref[8:9, :] = jnp.sum(dsum, axis=(0, 1)).reshape(1, CH)
    dskip = dsum.astype(bf16).reshape(rows, CH)
    dws_ref[...] = dot(dskip, traj_ref[...], TN).astype(bf16)
    tg_ref[...] = dot(dskip, ws_ref[...])
    zb = frames(zb_ref[...])
    _, slope = mish_pair(zb * aff(2)[None] + aff(3)[None])
    dhb, ag_ref[2:3, :], ag_ref[3:4, :] = norm_back(dsum * slope, zb, rstd_b, aff(2))
    ag_ref[5:6, :] = jnp.sum(dhb, axis=(0, 1)).reshape(1, CH)
    fill(pad_h, dhb.astype(bf16).reshape(rows, CH))
    hb = pad_h[edge : edge + rows, :]
    for t in range(5):
        dwb_ref[:, t * CH : (t + 1) * CH] = dot(hb, pad_m[t * ns : t * ns + rows, :], TN).astype(bf16)
    dmid = frames(conv5_back(pad_h, wb_ref))
    za = frames(za_ref[...])
    act_a, slope = mish_pair(za * aff(0)[None] + aff(1)[None])
    dscale = jnp.sum(dmid * act_a, axis=0)
    dshift = jnp.sum(dmid, axis=0)
    dha, ag_ref[0:1, :], ag_ref[1:2, :] = norm_back(dmid * scale[None] * slope, za, rstd_a, aff(0))
    ag_ref[4:5, :] = jnp.sum(dha, axis=(0, 1)).reshape(1, CH)
    ag_ref[6:7, :] = jnp.sum(dscale, axis=0, keepdims=True)
    ag_ref[7:8, :] = jnp.sum(dshift, axis=0, keepdims=True)
    ag_ref[10:, :] = jnp.zeros((ag_ref.shape[0] - 10, CH), f32)
    fill(pad_h, dha.astype(bf16).reshape(rows, CH))
    ha = pad_h[edge : edge + rows, :]
    for t in range(5):
        dwa_ref[:, t * CH : (t + 1) * CH] = dot(ha, pad_t[t * ns : t * ns + rows, :], TN).astype(bf16)
    tg_ref[...] = tg_ref[...] + conv5_back(pad_h, wa_ref)

    dcond = None
    for grad, w_ref, dw_ref in ((dscale, f0_ref, df0_ref), (dshift, f1_ref, df1_ref)):
        low = grad.astype(bf16)
        dw_ref[:, :width] = dot(low, cond_v, TN).astype(bf16)
        dw_ref[:, width:] = dot(low, cond_e, TN).astype(bf16)
        part = dot(low, w_ref[:, :width])
        dcond = part if dcond is None else dcond + part
    dviews = dcond * pd / count
    for cam in range(cams):
        dviews_ref[cam] = (mask[:, cam : cam + 1] * dviews).astype(bf16)


def call(kernel, outs, scratch=(), cost=None):
    return pl.pallas_call(
        kernel,
        out_shape=[jax.ShapeDtypeStruct(s, d) for s, d in outs],
        scratch_shapes=list(scratch),
        compiler_params=pltpu.CompilerParams(vmem_limit_bytes=VMEM_BYTES),
        cost_estimate=cost,
    )


def time_embed(steps_given, embed_width):
    half_width = embed_width // 2
    frequency = jnp.exp(
        jnp.arange(half_width, dtype=jnp.float32) * (-math.log(10000.0) / (half_width - 1))
    )
    argument = steps_given.astype(jnp.float32)[:, None] * frequency[None, :]
    return jnp.concatenate([jnp.sin(argument), jnp.cos(argument)], axis=1)


def adamw(weight, gradient, moment_one, moment_two, step_rate, weight_decay):
    mean_new = beta_first * moment_one + (1.0 - beta_first) * gradient
    square_new = beta_second * moment_two + (1.0 - beta_second) * gradient * gradient
    mean_hat = mean_new / (1.0 - beta_first**STEP)
    square_hat = square_new / (1.0 - beta_second**STEP)
    weight_new = weight - step_rate * (
        mean_hat / (jnp.sqrt(square_hat) + adam_eps) + weight_decay * weight
    )
    return (weight_new, mean_new, square_new)


def shards(
    images, trajectory, view_mask, timesteps, out_grad,
    encoder_weight, encoder_affine, block_convs, film_weight, skip_weight, down_weight, block_affine,
    first_encoder, first_affine, first_convs, first_film, first_skip, first_down, first_block,
    second_encoder, second_affine, second_convs, second_film, second_skip, second_down, second_block,
):
    ns, nf, ch = trajectory.shape
    cams = images.shape[1]
    obs = images.shape[3]
    n_img = cams * images.shape[2] * obs
    cond = film_weight.shape[2]

    def gather(v):
        return lax.all_gather(v.astype(bf16), "batch", axis=0, tiled=True)

    w1 = gather(encoder_weight[0, :, 0])
    w2 = gather(encoder_weight[0, :, 1])
    enc_aff = jnp.pad(jnp.transpose(gather(encoder_affine[0])).astype(f32), ((0, 4), (0, 0)))
    wa = gather(block_convs[:, 0])
    wb = gather(block_convs[:, 1])
    f0 = gather(film_weight[:, 0])
    f1 = gather(film_weight[:, 1])
    ws = gather(skip_weight)
    wd = gather(down_weight)
    blk_aff = jnp.pad(jnp.transpose(gather(block_affine)).astype(f32), ((0, 6), (0, 0)))

    x = images.reshape(n_img, 9 * ch)
    wide = 9 * ch
    z1, r1, act, z2, r2, feat = call(
        enc_fwd_kernel,
        [((n_img, wide), f32), ((n_img, ch), f32), ((n_img, wide), bf16),
         ((n_img, wide), f32), ((n_img, ch), f32), ((n_img, ch), bf16)],
    )(x, w1, w2, enc_aff)

    outgoing = feat.reshape(1, cams, ns, obs * ch)
    arrived = lax.all_to_all(outgoing, "cam", split_axis=1, concat_axis=0, tiled=True)[:, 0]
    present = view_mask.astype(f32)
    embedded = time_embed(timesteps, TEMB)
    traj_fm = jnp.transpose(trajectory, (1, 0, 2)).reshape(nf * ns, ch)
    og_fm = jnp.transpose(out_grad, (1, 0, 2)).reshape(nf // 2 * ns, ch)
    rows = nf * ns
    (out_fm, tg_fm, dviews, dwa, dwb, df0, df1, dws, dwd, blk_grad) = call(
        temporal_kernel,
        [((rows // 2, ch), bf16), ((rows, ch), f32), ((cams, ns, obs * ch), bf16),
         ((ch, 5 * ch), bf16), ((ch, 5 * ch), bf16), ((ch, cond), bf16), ((ch, cond), bf16),
         ((ch, ch), bf16), ((ch, 3 * ch), bf16), ((16, ch), f32)],
        [pltpu.VMEM((rows + 4 * ns, ch), bf16)] * 3
        + [pltpu.VMEM((rows, ch), f32)] * 2
        + [pltpu.VMEM((rows + ns, ch), bf16)],
    )(traj_fm, og_fm, arrived, present, embedded, wa, wb, f0, f1, ws, wd, blk_aff)
    block_output = jnp.transpose(out_fm.reshape(nf // 2, ns, ch), (1, 0, 2))
    trajectory_grad = jnp.transpose(tg_fm.reshape(nf, ns, ch), (1, 0, 2))

    returned = lax.all_to_all(dviews[:, None], "cam", split_axis=0, concat_axis=1, tiled=True)
    gp = returned.reshape(n_img, ch)
    dw1, dw2, ig, aff_grad = call(
        enc_bwd_kernel,
        [((ch, wide), bf16), ((ch, wide), bf16), ((n_img, wide), f32), ((8, ch), f32)],
        [pltpu.VMEM((n_img, wide), bf16), pltpu.VMEM((ch, 9 * n_img), bf16),
         pltpu.VMEM((n_img, wide), f32), pltpu.VMEM((9 * n_img, ch), bf16)],
    )(x, act, w1, w2, z1, r1, z2, r2, enc_aff, gp)
    images_grad = ig.reshape(images.shape)

    def scatter(v):
        return lax.psum_scatter(v, "batch", scatter_dimension=0, tiled=True)

    def total(v):
        return scatter(lax.psum(v, "cam")).astype(f32)

    convs_share = jnp.stack([total(dwa), total(dwb)], axis=1)
    film_share = jnp.stack([total(df0), total(df1)], axis=1)
    skip_share = total(dws)
    down_share = total(dwd)
    block_share = scatter(lax.psum(jnp.transpose(blk_grad[:10]), "cam"))
    encoder_share = jnp.stack([scatter(dw1).astype(f32), scatter(dw2).astype(f32)], axis=1)
    affine_share = scatter(jnp.transpose(aff_grad[:4]))

    upd = (
        adamw(encoder_weight, encoder_share[None], first_encoder, second_encoder, rate_matrix, decay_matrix),
        adamw(encoder_affine, affine_share[None], first_affine, second_affine, rate_vector, 0.0),
        adamw(block_convs, convs_share, first_convs, second_convs, rate_matrix, decay_matrix),
        adamw(film_weight, film_share, first_film, second_film, rate_matrix, decay_matrix),
        adamw(skip_weight, skip_share, first_skip, second_skip, rate_matrix, decay_matrix),
        adamw(down_weight, down_share, first_down, second_down, rate_matrix, decay_matrix),
        adamw(block_affine, block_share, first_block, second_block, rate_vector, 0.0),
    )
    return (
        (block_output, trajectory_grad, images_grad)
        + tuple(u[0] for u in upd)
        + tuple(u[1] for u in upd)
        + tuple(u[2] for u in upd)
    )


def solution(mesh):
    sample = P(("cam", "batch"))
    params = (P("cam", "batch"), P("cam", "batch")) + (P("batch"),) * 5
    images_spec = P("cam", None, "batch")
    return jax.shard_map(
        shards,
        mesh=mesh,
        in_specs=(images_spec, sample, sample, sample, sample) + params * 3,
        out_specs=(sample, sample, images_spec) + params * 3,
        check_vma=False,
    )
```

```python
import functools
import math

import jax
import jax.numpy as jnp
from jax import lax
from jax.experimental import pallas as pl
from jax.experimental.pallas import tpu as pltpu
from jax.sharding import PartitionSpec as P

TEMB = 128
GROUPS = 8
STEP = 5

norm_eps = 1e-05
beta_first = 0.5
beta_second = 0.5
adam_eps = 1e-08
rate_matrix = 0.02
rate_vector = 0.2
decay_matrix = 0.01

CH = 512
BLK = 128
ENC_GROUP = 16
f32 = jnp.float32
bf16 = jnp.bfloat16
VMEM_BYTES = 60 * 1024 * 1024

NT = (((1,), (1,)), ((), ()))
NN = (((1,), (0,)), ((), ()))
TN = (((0,), (0,)), ((), ()))


def dot(a, b, dims=NN):
    return lax.dot_general(a, b, dims, preferred_element_type=f32)


def group_ones(width, group):
    rows = lax.broadcasted_iota(jnp.int32, (width, width), 0) // group
    cols = lax.broadcasted_iota(jnp.int32, (width, width), 1) // group
    return jnp.where(rows == cols, 1.0, 0.0).astype(bf16)


def group_sum(v, ones):
    high = v.astype(bf16)
    rest = v - high.astype(f32)
    middle = rest.astype(bf16)
    low = (rest - middle.astype(f32)).astype(bf16)
    return dot(high, ones) + dot(middle, ones) + dot(low, ones)


def sigmoid(v):
    return 1.0 / (1.0 + jnp.exp(-v))


def mish_pair(v):
    e = jnp.exp(jnp.minimum(v, 20.0))
    n = e * (e + 2.0)
    inv = 1.0 / (n + 2.0)
    t = n * inv
    return v * t, t + v * (4.0 * e * (1.0 + e)) * inv * inv


def mish_value(v):
    e = jnp.exp(jnp.minimum(v, 20.0))
    n = e * (e + 2.0)
    return v * (n / (n + 2.0))


def span(i):
    return range(max(0, 1 - i), min(2, 3 - i) + 1)


MESH = pl.DeviceIdType.MESH


def batch_copy(src, dst, send_sem, recv_sem, target):
    return pltpu.make_async_remote_copy(
        src_ref=src, dst_ref=dst, send_sem=send_sem, recv_sem=recv_sem,
        device_id={"batch": target}, device_id_type=MESH,
    )


def cam_copy(src, dst, send_sem, recv_sem, target):
    return pltpu.make_async_remote_copy(
        src_ref=src, dst_ref=dst, send_sem=send_sem, recv_sem=recv_sem,
        device_id={"cam": target}, device_id_type=MESH,
    )


def line_barrier(cams, nz):
    me, cam = lax.axis_index("batch"), lax.axis_index("cam")
    zi, core = me // 2, me % 2
    barrier = pltpu.get_barrier_semaphore()
    pl.semaphore_signal(barrier, inc=1, device_id={"batch": me + 1 - 2 * core}, device_id_type=MESH)
    for step in range(1, cams):
        pl.semaphore_signal(barrier, inc=1, device_id={"cam": (cam + step) % cams}, device_id_type=MESH)

    @pl.when(zi > 0)
    def _():
        pl.semaphore_signal(barrier, inc=1, device_id={"batch": me - 2}, device_id_type=MESH)

    @pl.when(zi < nz - 1)
    def _():
        pl.semaphore_signal(barrier, inc=1, device_id={"batch": me + 2}, device_id_type=MESH)

    ends = (zi == 0).astype(jnp.int32) + (zi == nz - 1).astype(jnp.int32)
    pl.semaphore_wait(barrier, cams + 2 - ends)


def enc_fwd_kernel(
    n, cams, x_ref, own_ref,
    z1_out, r1_ref, a_out, z2_out, r2_ref, arr_ref, w_out, aff_ref,
    w_ref, z1_ref, a_ref, z2_ref, feat_ref, arr_s,
    zsend, zrecv, csend, crecv, wsem, osem, fsend, frecv,
):
    nz = n // 2
    rows = own_ref.shape[1]
    spb = BLK // rows
    n_img = x_ref.shape[0]
    me, cam = lax.axis_index("batch"), lax.axis_index("cam")
    zi, core = me // 2, me % 2
    partner = me + 1 - 2 * core
    ones = group_ones(BLK, ENC_GROUP)
    inv_n = 1.0 / (9 * ENC_GROUP)

    line_barrier(cams, nz)

    def z_copy(conv, k, way):
        ref = w_ref.at[conv, 2 * k + core]
        return batch_copy(ref, ref, zsend.at[conv, way, k], zrecv.at[conv, k], me - 2 + 4 * way)

    def core_copy(conv, k, which):
        ref = w_ref.at[conv, 2 * k + which]
        return batch_copy(ref, ref, csend.at[conv, k], crecv.at[conv, k], partner)

    def moves(s):
        low, high = zi - s, zi + s
        return (
            (high, high < nz, (high < nz) & (zi > 0), 0),
            (low, low >= 0, (low >= 0) & (zi < nz - 1), 1),
        )

    def send(conv, s):
        for k, _, passed, way in moves(s):
            @pl.when(passed)
            def _():
                z_copy(conv, k, way).start()

    def receive(conv, s):
        for k, held, _, way in moves(s):
            @pl.when(held)
            def _():
                z_copy(conv, k, way).wait_recv()
                core_copy(conv, k, core).start()

    for conv in range(2):
        w_ref[conv, me] = own_ref[conv]
    for conv in range(2):
        core_copy(conv, zi, core).start()

    def rows_of(conv, j, start, wide):
        block = w_ref[conv, pl.ds(j * spb, spb), :, start : start + wide]
        return block.reshape(BLK, wide)

    def w_save(conv, j):
        part = pl.ds(j * spb, spb)
        return pltpu.make_async_copy(w_ref.at[conv, part], w_out.at[conv, part], wsem.at[conv, j])

    def conv_norm(src_ref, conv, z_ref, r_ref, j):
        lanes = pl.ds(pl.multiple_of(j * BLK, BLK), BLK)
        total = None
        for p in range(9):
            r, c = divmod(p, 3)
            bs = span(c)
            acc = None
            for a in span(r):
                start = (3 * (r + a - 1) + c + bs[0] - 1) * CH
                wide = len(bs) * CH
                part = dot(src_ref[:, start : start + wide], rows_of(conv, j, (3 * a + bs[0]) * CH, wide), NT)
                acc = part if acc is None else acc + part
            z_ref[p, :, lanes] = acc
            total = acc if total is None else total + acc
        mean = group_sum(total, ones) * inv_n
        var = None
        for p in range(9):
            centred = z_ref[p, :, lanes] - mean
            sq = centred * centred
            var = sq if var is None else var + sq
        rstd = lax.rsqrt(group_sum(var, ones) * inv_n + norm_eps)
        r_ref[:, lanes] = rstd
        return lanes, mean, rstd

    def first(j):
        aff_ref[:, lanes_of(j)] = jnp.transpose(rows_of(0, j, 9 * CH, BLK).astype(f32))[0:8]
        lanes, mean, rstd = conv_norm(x_ref, 0, z1_ref, r1_ref, j)
        gain, offset = aff_ref[0:1, lanes], aff_ref[1:2, lanes]
        for p in range(9):
            z = (z1_ref[p, :, lanes] - mean) * rstd
            z1_ref[p, :, lanes] = z
            u = z * gain + offset
            a_ref[:, pl.ds(pl.multiple_of(p * CH + j * BLK, BLK), BLK)] = (u * sigmoid(u)).astype(bf16)

    def second(j):
        lanes, mean, rstd = conv_norm(a_ref, 1, z2_ref, r2_ref, j)
        gain, offset = aff_ref[2:3, lanes], aff_ref[3:4, lanes]
        total = None
        for p in range(9):
            z = (z2_ref[p, :, lanes] - mean) * rstd
            z2_ref[p, :, lanes] = z
            pic = x_ref[:, pl.ds(pl.multiple_of(p * CH + j * BLK, BLK), BLK)].astype(f32)
            u = z * gain + offset + pic
            act = u * sigmoid(u)
            total = act if total is None else total + act
        out = (total * (1.0 / 9.0)).astype(bf16)
        feat_ref[:, :, :, lanes] = out.reshape(feat_ref.shape[:3] + (BLK,))

    def lanes_of(j):
        return pl.ds(pl.multiple_of(j * BLK, BLK), BLK)

    def arrived(conv, k):
        core_copy(conv, k, 1 - core).wait_recv()

    def phase(conv, block):
        streaming = spb == 2

        def step(s, carry):
            if conv == 0:
                @pl.when(s < nz - 1)
                def _():
                    send(0, s)

                @pl.when(s == nz - 1)
                def _():
                    send(1, 0)
            else:
                @pl.when((s > 0) & (s < nz - 1))
                def _():
                    send(1, s)

            def side(d, carry):
                k = zi + s - 2 * s * d

                @pl.when((k >= 0) & (k < nz) & (s + 1 > d))
                def _():
                    arrived(conv, k)
                    if streaming:
                        w_save(conv, k).start()
                        block(k)
                return carry

            lax.fori_loop(0, 2, side, 0)

            @pl.when(s < nz - 1)
            def _():
                receive(conv, s + 1)
            return carry

        lax.fori_loop(0, nz, step, 0)
        if not streaming:
            def rest(j, carry):
                w_save(conv, j).start()
                block(j)
                return carry

            lax.fori_loop(0, CH // BLK, rest, 0)

    phase(0, first)
    saves = [pltpu.make_async_copy(z1_ref, z1_out, osem.at[0])]
    saves += [
        pltpu.make_async_copy(a_ref.at[:, p * CH : (p + 1) * CH], a_out.at[p], osem.at[2 + p])
        for p in range(9)
    ]
    for save in saves:
        save.start()
    phase(1, second)
    last = pltpu.make_async_copy(z2_ref, z2_out, osem.at[1])
    last.start()

    def feat_copy(to, sender):
        return cam_copy(feat_ref.at[:, to], arr_s.at[sender], fsend.at[to], frecv.at[sender], to)

    for step in range(1, cams):
        feat_copy((cam + step) % cams, cam).start()
    arr_s[cam] = feat_ref[:, cam]
    for step in range(1, cams):
        other = (cam + step) % cams
        feat_copy(other, other).wait_recv()
    arr_ref[...] = arr_s[...]
    for step in range(1, cams):
        feat_copy((cam + step) % cams, cam).wait_send()

    for conv in range(2):
        def drain(k, carry):
            s = k - zi

            @pl.when((s >= 0) & (s < nz - 1) & (zi > 0))
            def _():
                z_copy(conv, k, 0).wait_send()

            @pl.when((s <= 0) & (s > 1 - nz) & (zi < nz - 1))
            def _():
                z_copy(conv, k, 1).wait_send()

            core_copy(conv, k, core).wait_send()
            return carry

        lax.fori_loop(0, nz, drain, 0)

        def saved(j, carry):
            w_save(conv, j).wait()
            return carry

        lax.fori_loop(0, CH // BLK, saved, 0)
    for save in saves:
        save.wait()
    last.wait()


def enc_bwd_kernel(
    n, cams, x_hbm, a_hbm, w_hbm, z1_hbm, r1_ref, z2_hbm, r2_ref, aff_ref, dviews_ref,
    ig_ref, genc_ref, gaff_ref,
    x_ref, a_ref, w_ref, z1_ref, z2_ref, g_ref, gt_ref, ag_ref, gp_ref,
    dwf, core_out, core_in, slots,
    lsem, csend, crecv, zsend, zrecv, fsend, frecv,
):
    nz = n // 2
    rows = CH // n
    n_img = z1_ref.shape[1]
    me, cam = lax.axis_index("batch"), lax.axis_index("cam")
    zi, core = me // 2, me % 2
    partner = me + 1 - 2 * core
    ones = group_ones(BLK, ENC_GROUP)
    inv_n = 1.0 / (9 * ENC_GROUP)
    chunk = 3 * CH

    def load_w(conv):
        return pltpu.make_async_copy(w_hbm.at[conv, :, :, 0 : 9 * CH], w_ref, lsem.at[3])

    loads = {
        "z2": pltpu.make_async_copy(z2_hbm, z2_ref, lsem.at[0]),
        "z1": pltpu.make_async_copy(z1_hbm, z1_ref, lsem.at[1]),
        "a": pltpu.make_async_copy(a_hbm, a_ref, lsem.at[2]),
    }
    x_loads = [
        pltpu.make_async_copy(x_hbm.at[:, p * CH : (p + 1) * CH], x_ref.at[p], lsem.at[4 + p])
        for p in range(9)
    ]
    loads["z2"].start()
    for load in x_loads:
        load.start()
    loads["a"].start()
    load_w(1).start()
    loads["z1"].start()

    line_barrier(cams, nz)

    def view_copy(to, sender):
        return cam_copy(dviews_ref.at[to], gp_ref.at[:, sender], fsend.at[to], frecv.at[sender], to)

    for step in range(1, cams):
        view_copy((cam + step) % cams, cam).start()
    gp_ref[:, cam] = dviews_ref[cam]
    ag_ref[...] = jnp.zeros_like(ag_ref)
    for step in range(1, cams):
        other = (cam + step) % cams
        view_copy(other, other).wait_recv()
    for load in x_loads:
        load.wait()
    loads["z2"].wait()

    def lanes_of(j):
        return pl.ds(pl.multiple_of(j * BLK, BLK), BLK)

    def norm_back(du_ref, z_ref, r_ref, j, gain, row):
        lanes = lanes_of(j)
        s0 = jnp.zeros((n_img, BLK), f32)
        s1 = jnp.zeros((n_img, BLK), f32)
        for p in range(9):
            du = du_ref[p, :, lanes]
            s0 = s0 + du
            s1 = s1 + du * z_ref[p, :, lanes]
        ag_ref[row : row + 1, lanes] = jnp.sum(s1, axis=0, keepdims=True)
        ag_ref[row + 1 : row + 2, lanes] = jnp.sum(s0, axis=0, keepdims=True)
        m0 = group_sum(s0 * gain, ones) * inv_n
        m1 = group_sum(s1 * gain, ones) * inv_n
        rstd = r_ref[:, lanes]
        for p in range(9):
            dv = (du_ref[p, :, lanes] * gain - m0 - z_ref[p, :, lanes] * m1) * rstd
            g_ref[p, :, lanes] = dv.astype(bf16)
            gt_ref[lanes, p * n_img : (p + 1) * n_img] = jnp.transpose(dv).astype(bf16)

    def second(j, carry):
        lanes = lanes_of(j)
        gain, offset = aff_ref[2:3, lanes], aff_ref[3:4, lanes]
        pooled = gp_ref[:, :, :, lanes].reshape(n_img, BLK).astype(f32) * (1.0 / 9.0)
        for p in range(9):
            u = z2_ref[p, :, lanes] * gain + offset + x_ref[p, :, lanes].astype(f32)
            s = sigmoid(u)
            ig_ref[p, :, lanes] = pooled * (s * (1.0 + u * (1.0 - s)))
        norm_back(ig_ref, z2_ref, r2_ref, j, gain, 2)
        return carry

    def first(j, carry):
        lanes = lanes_of(j)
        gain, offset = aff_ref[0:1, lanes], aff_ref[1:2, lanes]
        for p in range(9):
            u = z1_ref[p, :, lanes] * gain + offset
            s = sigmoid(u)
            z2_ref[p, :, lanes] = z2_ref[p, :, lanes] * (s * (1.0 + u * (1.0 - s)))
        norm_back(z2_ref, z1_ref, r1_ref, j, gain, 0)
        return carry

    def width(k):
        return chunk + BLK if k == 5 else chunk

    def core_copy(k):
        cols = pl.ds(0, width(k))
        return batch_copy(
            core_out.at[k % 2, :, :, cols], core_in.at[k, :, :, cols], csend.at[k], crecv.at[k], partner
        )

    def make_chunk(k):
        src_ref = a_ref if k < 3 else x_ref
        a = k % 3
        r_lo, r_hi = max(0, 1 - a), min(2, 3 - a)
        for b in range(3):
            c_lo, c_hi = max(0, 1 - b), min(2, 3 - b)
            if b == 1:
                runs = [(3 * r_lo, 3 * (r_hi - r_lo + 1))]
            else:
                runs = [(3 * r + c_lo, c_hi - c_lo + 1) for r in range(r_lo, r_hi + 1)]
            shift = 3 * (a - 1) + b - 1
            for half in range(2):
                acc = None
                for p, m in runs:
                    part = dot(
                        gt_ref[half * 256 : half * 256 + 256, p * n_img : (p + m) * n_img],
                        src_ref[p + shift : p + shift + m].reshape(m * n_img, CH),
                    )
                    acc = part if acc is None else acc + part
                dwf[k % 2, half * n // 2 : (half + 1) * n // 2, :, b * CH : (b + 1) * CH] = acc.reshape(
                    n // 2, rows, CH
                )
        if k == 5:
            dwf[1, :, :, chunk:] = jnp.transpose(ag_ref[...]).reshape(n, rows, BLK)
        if k >= 2:
            core_copy(k - 2).wait_send()

        def pack(d, carry):
            core_out[k % 2, d, :, 0 : width(k)] = dwf[k % 2, 2 * d + 1 - core, :, 0 : width(k)].astype(bf16)
            return carry

        lax.fori_loop(0, nz, pack, 0)
        core_copy(k).start()

    def term(k, d):
        return dwf[k % 2, 2 * d + core, :, 0 : width(k)] + core_in[k, d, :, 0 : width(k)].astype(f32)

    def line_copy(k, way, s):
        cols = pl.ds(0, width(k))
        return batch_copy(
            slots.at[k, way, s - 1, :, cols], slots.at[k, way, s, :, cols],
            zsend.at[k, way, s], zrecv.at[k, way, s], me - 2 + 4 * way,
        )

    def serve(k, s):
        for way in range(2):
            ahead = zi if way else nz - 1 - zi
            d = nz - s + zi if way else s - nz + zi
            cols = pl.ds(0, width(k))

            @pl.when((ahead < nz - 1) & (s > ahead))
            def _():
                @pl.when(ahead > 0)
                def _():
                    line_copy(k, way, s - 1).wait_recv()
                    slots[k, way, s - 1, :, cols] = (
                        slots[k, way, s - 1, :, cols].astype(f32) + term(k, d)
                    ).astype(bf16)

                @pl.when(ahead == 0)
                def _():
                    slots[k, way, s - 1, :, cols] = term(k, d).astype(bf16)

                line_copy(k, way, s).start()

    def service(g):
        k, part = divmod(g, 3)
        if part == 0:
            core_copy(k).wait_recv()
        lo, hi = 1 + part * (nz - 1) // 3, 1 + (part + 1) * (nz - 1) // 3
        if hi - lo == 1:
            serve(k, lo)
        elif hi > lo:
            def body(s, carry):
                serve(k, s)
                return carry

            lax.fori_loop(lo, hi, body, 0)

    def finish(k):
        conv, a = 1 - k // 3, k % 3
        total = term(k, zi)
        cols = slice(0, width(k))

        def write(v):
            genc_ref[conv, :, a * chunk : (a + 1) * chunk] = v[:, 0:chunk]
            if k == 5:
                gaff_ref[...] = v[:, chunk:]

        last = nz - 1

        @pl.when(zi > 0)
        def _():
            line_copy(k, 1, last).wait_recv()

        @pl.when(zi < nz - 1)
        def _():
            line_copy(k, 0, last).wait_recv()

        @pl.when(zi == 0)
        def _():
            write(total + slots[k, 0, last, :, cols].astype(f32))

        @pl.when(zi == nz - 1)
        def _():
            write(total + slots[k, 1, last, :, cols].astype(f32))

        @pl.when((zi > 0) & (zi < nz - 1))
        def _():
            write(total + slots[k, 0, last, :, cols].astype(f32) + slots[k, 1, last, :, cols].astype(f32))

    def input_back(q):
        r, c = divmod(q, 3)
        acc = None
        for a in range(3):
            for b in range(3):
                pr, pc = r - a + 1, c - b + 1
                if 0 <= pr < 3 and 0 <= pc < 3:
                    t = 3 * a + b
                    w = w_ref[:, :, t * CH : (t + 1) * CH].reshape(CH, CH)
                    part = dot(g_ref[3 * pr + pc], w)
                    acc = part if acc is None else acc + part
        return acc

    def back_second(*qs):
        for q in qs:
            if q == 0:
                load_w(1).wait()
            z2_ref[q] = input_back(q)
            if q == 8:
                load_w(0).start()

    def back_first(*qs):
        for q in qs:
            if q == 0:
                load_w(0).wait()
            ig_ref[q] = ig_ref[q] + input_back(q)

    lax.fori_loop(0, CH // BLK, second, 0)
    loads["a"].wait()
    make_chunk(0)
    service(0)
    make_chunk(1)
    service(1)
    back_second(0, 1, 2)
    service(2)
    back_second(3, 4)
    service(3)
    finish(0)
    make_chunk(2)
    service(4)
    back_second(5, 6)
    service(5)
    back_second(7, 8)
    service(6)
    finish(1)
    loads["z1"].wait()
    lax.fori_loop(0, 2, first, 0)
    service(7)
    lax.fori_loop(2, 4, first, 0)
    service(8)
    make_chunk(3)
    service(9)
    finish(2)
    make_chunk(4)
    service(10)
    back_first(0, 1)
    service(11)
    back_first(2, 3)
    service(12)
    finish(3)
    make_chunk(5)
    service(13)
    back_first(4, 5)
    service(14)
    back_first(6)
    service(15)
    finish(4)
    back_first(7)
    service(16)
    back_first(8)
    service(17)
    finish(5)

    core_copy(4).wait_send()
    core_copy(5).wait_send()
    for k in range(6):
        def drain(s, carry):
            for way in range(2):
                ahead = zi if way else nz - 1 - zi

                @pl.when((ahead < nz - 1) & (s > ahead))
                def _():
                    line_copy(k, way, s).wait_send()
            return carry

        lax.fori_loop(1, nz, drain, 0)
    for step in range(1, cams):
        view_copy((cam + step) % cams, cam).wait_send()


def temporal_kernel(
    traj_ref, og_ref, arr_ref, mask_ref, emb_ref, t_ref,
    out_ref, tg_ref, dviews_ref, dt_ref,
    pad_t, pad_m, pad_h, za_ref, zb_ref, sum_ref, aff_ref, ag_ref,
):
    cond = (t_ref.shape[1] - 14 * CH - BLK) // 2
    cuts = [0]
    for wide in (5 * CH, 5 * CH, cond, cond, CH, 3 * CH, BLK):
        cuts.append(cuts[-1] + wide)
    wa_ref, wb_ref, f0_ref, f1_ref, ws_ref, wd_ref = [
        t_ref.at[:, cuts[i] : cuts[i + 1]] for i in range(6)
    ]
    dwa_ref, dwb_ref, df0_ref, df1_ref, dws_ref, dwd_ref = [
        dt_ref.at[:, cuts[i] : cuts[i + 1]] for i in range(6)
    ]
    aff_ref[...] = jnp.transpose(t_ref[:, cuts[6] :].astype(f32))
    ag_ref[...] = jnp.zeros_like(ag_ref)
    ns = mask_ref.shape[0]
    rows = traj_ref.shape[0]
    nf = rows // ns
    edge = 2 * ns
    ones = group_ones(CH, CH // GROUPS)
    inv_n = 1.0 / (nf * (CH // GROUPS))
    aff = lambda i: aff_ref[i : i + 1, :]

    def frames(v):
        return v.reshape(nf, ns, CH)

    def fill(pad_ref, v):
        pad_ref[0:edge, :] = jnp.zeros((edge, CH), bf16)
        pad_ref[edge : edge + rows, :] = v
        pad_ref[edge + rows : edge + rows + edge, :] = jnp.zeros((edge, CH), bf16)

    def conv5(pad_ref, w_ref):
        acc = None
        for t in range(5):
            part = dot(pad_ref[t * ns : t * ns + rows, :], w_ref[:, t * CH : (t + 1) * CH], NT)
            acc = part if acc is None else acc + part
        return acc

    def conv5_back(pad_ref, w_ref):
        acc = None
        for t in range(5):
            part = dot(pad_ref[(4 - t) * ns : (4 - t) * ns + rows, :], w_ref[:, t * CH : (t + 1) * CH])
            acc = part if acc is None else acc + part
        return acc

    def norm(v):
        v = frames(v)
        mean = group_sum(jnp.sum(v, axis=0), ones) * inv_n
        centred = v - mean[None]
        rstd = lax.rsqrt(group_sum(jnp.sum(centred * centred, axis=0), ones) * inv_n + norm_eps)
        return centred * rstd[None], rstd

    def norm_back(du, z, rstd, gain):
        s0 = jnp.sum(du, axis=0)
        s1 = jnp.sum(du * z, axis=0)
        m0 = group_sum(s0 * gain, ones) * inv_n
        m1 = group_sum(s1 * gain, ones) * inv_n
        dv = (du * gain[None] - m0[None] - z * m1[None]) * rstd[None]
        return dv, jnp.sum(s1, axis=0, keepdims=True), jnp.sum(s0, axis=0, keepdims=True)

    mask = mask_ref[...]
    count = jnp.sum(mask, axis=1, keepdims=True)
    cams = arr_ref.shape[0]
    obs = arr_ref.shape[1]
    conds, slopes = [], []
    for o in range(obs):
        pooled = None
        for cam in range(cams):
            part = mask[:, cam : cam + 1] * arr_ref[cam, o].astype(f32)
            pooled = part if pooled is None else pooled + part
        value, slope = mish_pair(pooled / count)
        conds.append(value.astype(bf16))
        slopes.append(slope)
    conds.append(mish_value(emb_ref[...]).astype(bf16))
    lanes = [slice(o * CH, (o + 1) * CH) for o in range(obs)] + [slice(obs * CH, cond)]
    film = []
    for i, w_ref in ((6, f0_ref), (7, f1_ref)):
        film.append(sum(dot(v, w_ref[:, cols], NT) for v, cols in zip(conds, lanes)) + aff(i))
    scale, shift = film

    fill(pad_t, traj_ref[...])
    za, rstd_a = norm(conv5(pad_t, wa_ref) + aff(4))
    za_ref[...] = za.reshape(rows, CH)
    act_a = mish_value(za * aff(0)[None] + aff(1)[None])
    fill(pad_m, (act_a * scale[None] + shift[None]).astype(bf16).reshape(rows, CH))
    zb, rstd_b = norm(conv5(pad_m, wb_ref) + aff(5))
    zb_ref[...] = zb.reshape(rows, CH)
    skip = frames(dot(traj_ref[...], ws_ref[...], NT)) + aff(8)[None]
    summed = (mish_value(zb * aff(2)[None] + aff(3)[None]) + skip).astype(bf16)
    pairs = summed.reshape(nf // 2, 2, ns, CH)
    half = rows // 2
    sum_ref[0:ns, :] = jnp.zeros((ns, CH), bf16)
    sum_ref[ns : ns + half, :] = pairs[:, 1].reshape(half, CH)
    sum_ref[ns + half : ns + 2 * half, :] = pairs[:, 0].reshape(half, CH)
    taps = (0, ns + half, ns)
    out = None
    og = og_ref[...]
    dcols = []
    for t in range(3):
        cols = sum_ref[taps[t] : taps[t] + half, :]
        w = wd_ref[:, t * CH : (t + 1) * CH]
        part = dot(cols, w, NT)
        out = part if out is None else out + part
        dcols.append(dot(og, w).reshape(nf // 2, ns, CH))
        dwd_ref[:, t * CH : (t + 1) * CH] = dot(og, cols, TN).astype(bf16)
    out_ref[...] = (out + aff(9)).astype(bf16)
    ag_ref[9:10, :] = jnp.sum(og.astype(f32), axis=0, keepdims=True)

    before = jnp.concatenate([dcols[0][1:], jnp.zeros((1, ns, CH), f32)], axis=0)
    dsum = jnp.stack([dcols[1], dcols[2] + before], axis=1).reshape(nf, ns, CH)
    ag_ref[8:9, :] = jnp.sum(dsum, axis=(0, 1)).reshape(1, CH)
    dskip = dsum.astype(bf16).reshape(rows, CH)
    dws_ref[...] = dot(dskip, traj_ref[...], TN).astype(bf16)
    tg_ref[...] = dot(dskip, ws_ref[...])
    zb = frames(zb_ref[...])
    _, slope = mish_pair(zb * aff(2)[None] + aff(3)[None])
    dhb, ag_ref[2:3, :], ag_ref[3:4, :] = norm_back(dsum * slope, zb, rstd_b, aff(2))
    ag_ref[5:6, :] = jnp.sum(dhb, axis=(0, 1)).reshape(1, CH)
    fill(pad_h, dhb.astype(bf16).reshape(rows, CH))
    hb = pad_h[edge : edge + rows, :]
    for t in range(5):
        dwb_ref[:, t * CH : (t + 1) * CH] = dot(hb, pad_m[t * ns : t * ns + rows, :], TN).astype(bf16)
    dmid = frames(conv5_back(pad_h, wb_ref))
    za = frames(za_ref[...])
    act_a, slope = mish_pair(za * aff(0)[None] + aff(1)[None])
    dscale = jnp.sum(dmid * act_a, axis=0)
    dshift = jnp.sum(dmid, axis=0)
    dha, ag_ref[0:1, :], ag_ref[1:2, :] = norm_back(dmid * scale[None] * slope, za, rstd_a, aff(0))
    ag_ref[4:5, :] = jnp.sum(dha, axis=(0, 1)).reshape(1, CH)
    ag_ref[6:7, :] = jnp.sum(dscale, axis=0, keepdims=True)
    ag_ref[7:8, :] = jnp.sum(dshift, axis=0, keepdims=True)
    fill(pad_h, dha.astype(bf16).reshape(rows, CH))
    ha = pad_h[edge : edge + rows, :]
    for t in range(5):
        dwa_ref[:, t * CH : (t + 1) * CH] = dot(ha, pad_t[t * ns : t * ns + rows, :], TN).astype(bf16)
    tg_ref[...] = tg_ref[...] + conv5_back(pad_h, wa_ref)

    lows = (dscale.astype(bf16), dshift.astype(bf16))
    for low, dw_ref in zip(lows, (df0_ref, df1_ref)):
        for v, cols in zip(conds, lanes):
            dw_ref[:, cols] = dot(low, v, TN).astype(bf16)
    for o in range(obs):
        dcond = dot(lows[0], f0_ref[:, lanes[o]]) + dot(lows[1], f1_ref[:, lanes[o]])
        dview = dcond * slopes[o] / count
        for cam in range(cams):
            dviews_ref[cam, o] = (mask[:, cam : cam + 1] * dview).astype(bf16)
    dt_ref[:, cuts[6] :] = jnp.transpose(ag_ref[...]).astype(bf16)


def call(kernel, outs, in_specs, out_specs, scratch=(), collective_id=None, cost=None):
    extra = {} if collective_id is None else dict(collective_id=collective_id, has_side_effects=True)
    return pl.pallas_call(
        kernel,
        out_shape=[jax.ShapeDtypeStruct(s, d) for s, d in outs],
        in_specs=in_specs,
        out_specs=out_specs,
        scratch_shapes=list(scratch),
        compiler_params=pltpu.CompilerParams(vmem_limit_bytes=VMEM_BYTES, **extra),
        cost_estimate=cost,
    )


def work(microseconds):
    return pl.CostEstimate(
        flops=int(microseconds * 1e9), bytes_accessed=int(microseconds * 3e6), transcendentals=0
    )


V = pl.BlockSpec(memory_space=pltpu.VMEM)
H = pl.BlockSpec(memory_space=pl.ANY)
DMA = pltpu.SemaphoreType.DMA


def time_embed(steps_given, embed_width):
    half_width = embed_width // 2
    frequency = jnp.exp(
        jnp.arange(half_width, dtype=jnp.float32) * (-math.log(10000.0) / (half_width - 1))
    )
    argument = steps_given.astype(jnp.float32)[:, None] * frequency[None, :]
    return jnp.concatenate([jnp.sin(argument), jnp.cos(argument)], axis=1)


def adamw(weight, gradient, moment_one, moment_two, step_rate, weight_decay):
    mean_new = beta_first * moment_one + (1.0 - beta_first) * gradient
    square_new = beta_second * moment_two + (1.0 - beta_second) * gradient * gradient
    mean_hat = mean_new / (1.0 - beta_first**STEP)
    square_hat = square_new / (1.0 - beta_second**STEP)
    weight_new = weight - step_rate * (
        mean_hat / (jnp.sqrt(square_hat) + adam_eps) + weight_decay * weight
    )
    return (weight_new, mean_new, square_new)


def shards(
    n, images, trajectory, view_mask, timesteps, out_grad,
    encoder_weight, encoder_affine, block_convs, film_weight, skip_weight, down_weight, block_affine,
    first_encoder, first_affine, first_convs, first_film, first_skip, first_down, first_block,
    second_encoder, second_affine, second_convs, second_film, second_skip, second_down, second_block,
):
    ns, nf, ch = trajectory.shape
    cams, obs = images.shape[1], images.shape[3]
    n_img = cams * images.shape[2] * obs
    nz, per = n // 2, ch // n
    cond = film_weight.shape[2]
    wide = 9 * ch
    rows = nf * ns

    own_t = jnp.concatenate(
        [block_convs[:, 0], block_convs[:, 1], film_weight[:, 0], film_weight[:, 1], skip_weight, down_weight,
         jnp.pad(block_affine, ((0, 0), (0, BLK - block_affine.shape[1])))],
        axis=1,
    ).astype(bf16)
    part = per // cams
    own_part = lax.dynamic_slice_in_dim(own_t, lax.axis_index("cam") * part, part, 0)
    line_t = lax.all_gather(own_part, "batch", axis=0)
    all_t = lax.all_gather(line_t, "cam", axis=1).reshape(ch, own_t.shape[1])

    own_w = jnp.concatenate(
        [jnp.transpose(encoder_weight[0], (1, 0, 2)),
         jnp.broadcast_to(jnp.pad(encoder_affine[0], ((0, 0), (0, BLK - 4)))[None], (2, per, BLK))],
        axis=2,
    ).astype(bf16)
    x = jnp.transpose(images[0], (2, 0, 1, 3, 4)).reshape(n_img, wide)
    pos = (9, n_img, ch)
    z1, r1, act, z2, r2, arrived, w_all, enc_aff = call(
        functools.partial(enc_fwd_kernel, n, cams),
        [(pos, f32), ((n_img, ch), f32), (pos, bf16), (pos, f32), ((n_img, ch), f32),
         ((cams, obs, ns, ch), bf16), ((2, n, per, wide + BLK), bf16), ((8, ch), f32)],
        [V, V],
        [H, V, H, H, V, V, H, V],
        [pltpu.VMEM((2, n, per, wide + BLK), bf16), pltpu.VMEM(pos, f32), pltpu.VMEM((n_img, wide), bf16),
         pltpu.VMEM(pos, f32), pltpu.VMEM((obs, cams, ns, ch), bf16), pltpu.VMEM((cams, obs, ns, ch), bf16),
         DMA((2, 2, nz)), DMA((2, nz)), DMA((2, nz)), DMA((2, nz)), DMA((2, ch // BLK)), DMA((11,)),
         DMA((cams,)), DMA((cams,))],
        collective_id=0,
        cost=work(90),
    )(x, own_w)

    present = view_mask.astype(f32)
    embedded = time_embed(timesteps, TEMB)
    traj_fm = jnp.transpose(trajectory, (1, 0, 2)).reshape(rows, ch)
    og_fm = jnp.transpose(out_grad, (1, 0, 2)).reshape(rows // 2, ch)
    out_fm, tg_fm, dviews, dt = call(
        temporal_kernel,
        [((rows // 2, ch), bf16), ((rows, ch), f32), ((cams, obs, ns, ch), bf16), (all_t.shape, bf16)],
        [V] * 6,
        [V] * 4,
        [pltpu.VMEM((rows + 4 * ns, ch), bf16)] * 3
        + [pltpu.VMEM((rows, ch), f32)] * 2
        + [pltpu.VMEM((rows + ns, ch), bf16)]
        + [pltpu.VMEM((BLK, ch), f32)] * 2,
        cost=work(20),
    )(traj_fm, og_fm, arrived, present, embedded, all_t)
    block_output = jnp.transpose(out_fm.reshape(nf // 2, ns, ch), (1, 0, 2))
    trajectory_grad = jnp.transpose(tg_fm.reshape(nf, ns, ch), (1, 0, 2))

    cut = lax.psum_scatter(dt.reshape(n, cams, part, -1), "cam", scatter_dimension=1, tiled=False)
    cut = lax.psum_scatter(cut, "batch", scatter_dimension=0, tiled=False)
    gt = lax.all_gather(cut, "cam", axis=0, tiled=True).astype(f32)

    chunk = 3 * ch + BLK
    ig, genc, gaff = call(
        functools.partial(enc_bwd_kernel, n, cams),
        [(pos, f32), ((2, per, wide), f32), ((per, BLK), f32)],
        [H, H, H, H, V, H, V, V, V],
        [V, V, V],
        [pltpu.VMEM(pos, bf16), pltpu.VMEM(pos, bf16), pltpu.VMEM((n, per, wide), bf16), pltpu.VMEM(pos, f32),
         pltpu.VMEM(pos, f32), pltpu.VMEM(pos, bf16), pltpu.VMEM((ch, 9 * n_img), bf16),
         pltpu.VMEM((BLK, ch), f32), pltpu.VMEM((obs, cams, ns, ch), bf16),
         pltpu.VMEM((2, n, per, chunk), f32), pltpu.VMEM((2, nz, per, chunk), bf16),
         pltpu.VMEM((6, nz, per, chunk), bf16), pltpu.VMEM((6, 2, nz, per, chunk), bf16),
         DMA((13,)), DMA((6,)), DMA((6,)), DMA((6, 2, nz)), DMA((6, 2, nz)), DMA((cams,)), DMA((cams,))],
        collective_id=1,
        cost=work(100),
    )(x, act, w_all, z1, r1, z2, r2, enc_aff, dviews)
    images_grad = jnp.transpose(ig.reshape((9, obs) + images.shape[1:3] + (ch,)), (2, 3, 1, 0, 4))[None]

    cuts = [0]
    for size in (5 * ch, 5 * ch, cond, cond, ch, 3 * ch):
        cuts.append(cuts[-1] + size)
    pieces = [gt[:, cuts[i] : cuts[i + 1]] for i in range(6)]
    convs_share = jnp.stack(pieces[0:2], axis=1)
    film_share = jnp.stack(pieces[2:4], axis=1)
    encoder_share = jnp.transpose(genc, (1, 0, 2))[None]
    upd = (
        adamw(encoder_weight, encoder_share, first_encoder, second_encoder, rate_matrix, decay_matrix),
        adamw(encoder_affine, gaff[None, :, :4], first_affine, second_affine, rate_vector, 0.0),
        adamw(block_convs, convs_share, first_convs, second_convs, rate_matrix, decay_matrix),
        adamw(film_weight, film_share, first_film, second_film, rate_matrix, decay_matrix),
        adamw(skip_weight, pieces[4], first_skip, second_skip, rate_matrix, decay_matrix),
        adamw(down_weight, pieces[5], first_down, second_down, rate_matrix, decay_matrix),
        adamw(block_affine, gt[:, cuts[6] : cuts[6] + 10], first_block, second_block, rate_vector, 0.0),
    )
    return (
        (block_output, trajectory_grad, images_grad)
        + tuple(u[0] for u in upd)
        + tuple(u[1] for u in upd)
        + tuple(u[2] for u in upd)
    )


def solution(mesh):
    sample = P(("cam", "batch"))
    params = (P("cam", "batch"), P("cam", "batch")) + (P("batch"),) * 5
    images_spec = P("cam", None, "batch")
    return jax.shard_map(
        functools.partial(shards, mesh.shape["batch"]),
        mesh=mesh,
        in_specs=(images_spec, sample, sample, sample, sample) + params * 3,
        out_specs=(sample, sample, images_spec) + params * 3,
        check_vma=False,
    )
```

```python
import functools
import math

import jax
import jax.numpy as jnp
from jax import lax
from jax.experimental import pallas as pl
from jax.experimental.pallas import tpu as pltpu
from jax.sharding import PartitionSpec as P

TEMB = 128
GROUPS = 8
STEP = 5

norm_eps = 1e-05
beta_first = 0.5
beta_second = 0.5
adam_eps = 1e-08
rate_matrix = 0.02
rate_vector = 0.2
decay_matrix = 0.01

CH = 512
BLK = 128
ENC_GROUP = 16
f32 = jnp.float32
bf16 = jnp.bfloat16
VMEM_BYTES = 60 * 1024 * 1024

NT = (((1,), (1,)), ((), ()))
NN = (((1,), (0,)), ((), ()))
TN = (((0,), (0,)), ((), ()))


def dot(a, b, dims=NN):
    return lax.dot_general(a, b, dims, preferred_element_type=f32)


def group_ones(width, group):
    rows = lax.broadcasted_iota(jnp.int32, (width, width), 0) // group
    cols = lax.broadcasted_iota(jnp.int32, (width, width), 1) // group
    return jnp.where(rows == cols, 1.0, 0.0).astype(bf16)


def group_sum(v, ones):
    high = v.astype(bf16)
    rest = v - high.astype(f32)
    middle = rest.astype(bf16)
    low = (rest - middle.astype(f32)).astype(bf16)
    return dot(high, ones) + dot(middle, ones) + dot(low, ones)


def sigmoid(v):
    return 1.0 / (1.0 + jnp.exp(-v))


def mish_pair(v):
    e = jnp.exp(jnp.minimum(v, 20.0))
    n = e * (e + 2.0)
    inv = 1.0 / (n + 2.0)
    t = n * inv
    return v * t, t + v * (4.0 * e * (1.0 + e)) * inv * inv


def mish_value(v):
    e = jnp.exp(jnp.minimum(v, 20.0))
    n = e * (e + 2.0)
    return v * (n / (n + 2.0))


def span(i):
    return range(max(0, 1 - i), min(2, 3 - i) + 1)


MESH = pl.DeviceIdType.MESH


def batch_copy(src, dst, send_sem, recv_sem, target):
    return pltpu.make_async_remote_copy(
        src_ref=src, dst_ref=dst, send_sem=send_sem, recv_sem=recv_sem,
        device_id={"batch": target}, device_id_type=MESH,
    )


def cam_copy(src, dst, send_sem, recv_sem, target):
    return pltpu.make_async_remote_copy(
        src_ref=src, dst_ref=dst, send_sem=send_sem, recv_sem=recv_sem,
        device_id={"cam": target}, device_id_type=MESH,
    )


def line_barrier(cams, nz):
    me, cam = lax.axis_index("batch"), lax.axis_index("cam")
    zi, core = me // 2, me % 2
    barrier = pltpu.get_barrier_semaphore()
    pl.semaphore_signal(barrier, inc=1, device_id={"batch": me + 1 - 2 * core}, device_id_type=MESH)
    for step in range(1, cams):
        pl.semaphore_signal(barrier, inc=1, device_id={"cam": (cam + step) % cams}, device_id_type=MESH)

    @pl.when(zi > 0)
    def _():
        pl.semaphore_signal(barrier, inc=1, device_id={"batch": me - 2}, device_id_type=MESH)

    @pl.when(zi < nz - 1)
    def _():
        pl.semaphore_signal(barrier, inc=1, device_id={"batch": me + 2}, device_id_type=MESH)

    ends = (zi == 0).astype(jnp.int32) + (zi == nz - 1).astype(jnp.int32)
    pl.semaphore_wait(barrier, cams + 2 - ends)


def enc_fwd_kernel(
    n, cams, x_ref, own_ref,
    z1_out, r1_ref, a_out, z2_out, r2_ref, arr_ref, w_out, aff_ref,
    w_ref, z1_ref, a_ref, z2_ref, feat_ref, arr_s,
    zsend, zrecv, csend, crecv, wsem, osem, fsend, frecv,
):
    nz = n // 2
    rows = own_ref.shape[1]
    spb = BLK // rows
    n_img = x_ref.shape[0]
    me, cam = lax.axis_index("batch"), lax.axis_index("cam")
    zi, core = me // 2, me % 2
    partner = me + 1 - 2 * core
    ones = group_ones(BLK, ENC_GROUP)
    inv_n = 1.0 / (9 * ENC_GROUP)

    line_barrier(cams, nz)

    def z_copy(conv, k, way):
        ref = w_ref.at[conv, 2 * k + core]
        return batch_copy(ref, ref, zsend.at[conv, way, k], zrecv.at[conv, k], me - 2 + 4 * way)

    def core_copy(conv, k, which):
        ref = w_ref.at[conv, 2 * k + which]
        return batch_copy(ref, ref, csend.at[conv, k], crecv.at[conv, k], partner)

    def moves(s):
        low, high = zi - s, zi + s
        return (
            (high, high < nz, (high < nz) & (zi > 0), 0),
            (low, low >= 0, (low >= 0) & (zi < nz - 1), 1),
        )

    def send(conv, s):
        for k, _, passed, way in moves(s):
            @pl.when(passed)
            def _():
                z_copy(conv, k, way).start()

    def receive(conv, s):
        for k, held, _, way in moves(s):
            @pl.when(held)
            def _():
                z_copy(conv, k, way).wait_recv()
                core_copy(conv, k, core).start()

    for conv in range(2):
        w_ref[conv, me] = own_ref[conv]
    for conv in range(2):
        core_copy(conv, zi, core).start()

    def rows_of(conv, j, start, wide):
        block = w_ref[conv, pl.ds(j * spb, spb), :, start : start + wide]
        return block.reshape(BLK, wide)

    def w_save(conv, j):
        part = pl.ds(j * spb, spb)
        return pltpu.make_async_copy(w_ref.at[conv, part], w_out.at[conv, part], wsem.at[conv, j])

    def conv_norm(src_ref, conv, z_ref, r_ref, j):
        lanes = pl.ds(pl.multiple_of(j * BLK, BLK), BLK)
        total = None
        for p in range(9):
            r, c = divmod(p, 3)
            bs = span(c)
            acc = None
            for a in span(r):
                start = (3 * (r + a - 1) + c + bs[0] - 1) * CH
                wide = len(bs) * CH
                part = dot(src_ref[:, start : start + wide], rows_of(conv, j, (3 * a + bs[0]) * CH, wide), NT)
                acc = part if acc is None else acc + part
            z_ref[p, :, lanes] = acc
            total = acc if total is None else total + acc
        mean = group_sum(total, ones) * inv_n
        var = None
        for p in range(9):
            centred = z_ref[p, :, lanes] - mean
            sq = centred * centred
            var = sq if var is None else var + sq
        rstd = lax.rsqrt(group_sum(var, ones) * inv_n + norm_eps)
        r_ref[:, lanes] = rstd
        return lanes, mean, rstd

    def first(j):
        aff_ref[:, lanes_of(j)] = jnp.transpose(rows_of(0, j, 9 * CH, BLK).astype(f32))[0:8]
        lanes, mean, rstd = conv_norm(x_ref, 0, z1_ref, r1_ref, j)
        gain, offset = aff_ref[0:1, lanes], aff_ref[1:2, lanes]
        for p in range(9):
            z = (z1_ref[p, :, lanes] - mean) * rstd
            z1_ref[p, :, lanes] = z
            u = z * gain + offset
            a_ref[:, pl.ds(pl.multiple_of(p * CH + j * BLK, BLK), BLK)] = (u * sigmoid(u)).astype(bf16)

    def second(j):
        lanes, mean, rstd = conv_norm(a_ref, 1, z2_ref, r2_ref, j)
        gain, offset = aff_ref[2:3, lanes], aff_ref[3:4, lanes]
        total = None
        for p in range(9):
            z = (z2_ref[p, :, lanes] - mean) * rstd
            z2_ref[p, :, lanes] = z
            pic = x_ref[:, pl.ds(pl.multiple_of(p * CH + j * BLK, BLK), BLK)].astype(f32)
            u = z * gain + offset + pic
            act = u * sigmoid(u)
            total = act if total is None else total + act
        out = (total * (1.0 / 9.0)).astype(bf16)
        feat_ref[:, :, :, lanes] = out.reshape(feat_ref.shape[:3] + (BLK,))

    def lanes_of(j):
        return pl.ds(pl.multiple_of(j * BLK, BLK), BLK)

    def arrived(conv, k):
        core_copy(conv, k, 1 - core).wait_recv()

    def phase(conv, block):
        streaming = spb == 2

        def step(s, carry):
            if conv == 0:
                @pl.when(s < nz - 1)
                def _():
                    send(0, s)

                @pl.when(s == nz - 1)
                def _():
                    send(1, 0)
            else:
                @pl.when((s > 0) & (s < nz - 1))
                def _():
                    send(1, s)

            def side(d, carry):
                k = zi + s - 2 * s * d

                @pl.when((k >= 0) & (k < nz) & (s + 1 > d))
                def _():
                    arrived(conv, k)
                    if streaming:
                        w_save(conv, k).start()
                        block(k)
                return carry

            lax.fori_loop(0, 2, side, 0)

            @pl.when(s < nz - 1)
            def _():
                receive(conv, s + 1)
            return carry

        lax.fori_loop(0, nz, step, 0)
        if not streaming:
            def rest(j, carry):
                w_save(conv, j).start()
                block(j)
                return carry

            lax.fori_loop(0, CH // BLK, rest, 0)

    phase(0, first)
    saves = [pltpu.make_async_copy(z1_ref, z1_out, osem.at[0])]
    saves += [
        pltpu.make_async_copy(a_ref.at[:, p * CH : (p + 1) * CH], a_out.at[p], osem.at[2 + p])
        for p in range(9)
    ]
    for save in saves:
        save.start()
    phase(1, second)
    last = pltpu.make_async_copy(z2_ref, z2_out, osem.at[1])
    last.start()

    def feat_copy(to, sender):
        return cam_copy(feat_ref.at[:, to], arr_s.at[sender], fsend.at[to], frecv.at[sender], to)

    for step in range(1, cams):
        feat_copy((cam + step) % cams, cam).start()
    arr_s[cam] = feat_ref[:, cam]
    for step in range(1, cams):
        other = (cam + step) % cams
        feat_copy(other, other).wait_recv()
    arr_ref[...] = arr_s[...]
    for step in range(1, cams):
        feat_copy((cam + step) % cams, cam).wait_send()

    for conv in range(2):
        def drain(k, carry):
            s = k - zi

            @pl.when((s >= 0) & (s < nz - 1) & (zi > 0))
            def _():
                z_copy(conv, k, 0).wait_send()

            @pl.when((s <= 0) & (s > 1 - nz) & (zi < nz - 1))
            def _():
                z_copy(conv, k, 1).wait_send()

            core_copy(conv, k, core).wait_send()
            return carry

        lax.fori_loop(0, nz, drain, 0)

        def saved(j, carry):
            w_save(conv, j).wait()
            return carry

        lax.fori_loop(0, CH // BLK, saved, 0)
    for save in saves:
        save.wait()
    last.wait()


def enc_bwd_kernel(
    n, cams, cond, x_hbm, a_hbm, w_hbm, z1_hbm, r1_ref, z2_hbm, r2_ref, aff_ref, dviews_ref, dt_hbm,
    ig_ref, genc_ref, gaff_ref, gconvs_ref, gfilm_ref, gskip_ref, gdown_ref, gblk_ref,
    x_ref, a_ref, w_ref, z1_ref, z2_ref, g_ref, gt_ref, ag_ref, gp_ref,
    dwf, core_out, core_in, slots, t_own, t_sum, t_peer, t_slots, t_all,
    lsem, csend, crecv, zsend, zrecv, fsend, frecv,
    tlsem, tcsend, tcrecv, tpsend, tprecv, tzsend, tzrecv, tfsend, tfrecv,
):
    nz = n // 2
    rows = CH // n
    n_img = z1_ref.shape[1]
    me, cam = lax.axis_index("batch"), lax.axis_index("cam")
    zi, core = me // 2, me % 2
    partner = me + 1 - 2 * core
    ones = group_ones(BLK, ENC_GROUP)
    inv_n = 1.0 / (9 * ENC_GROUP)
    chunk = 3 * CH

    def load_w(conv):
        return pltpu.make_async_copy(w_hbm.at[conv, :, :, 0 : 9 * CH], w_ref, lsem.at[3])

    loads = {
        "z2": pltpu.make_async_copy(z2_hbm, z2_ref, lsem.at[0]),
        "z1": pltpu.make_async_copy(z1_hbm, z1_ref, lsem.at[1]),
        "a": pltpu.make_async_copy(a_hbm, a_ref, lsem.at[2]),
    }
    x_loads = [
        pltpu.make_async_copy(x_hbm.at[:, p * CH : (p + 1) * CH], x_ref.at[p], lsem.at[4 + p])
        for p in range(9)
    ]
    loads["z2"].start()
    for load in x_loads:
        load.start()
    loads["a"].start()
    load_w(1).start()
    loads["z1"].start()

    def own_load(i):
        return pltpu.make_async_copy(dt_hbm.at[i // cams, core, i % cams], t_own.at[i % 2], tlsem.at[i])

    own_load(0).start()

    line_barrier(cams, nz)

    def view_copy(to, sender):
        return cam_copy(dviews_ref.at[to], gp_ref.at[:, sender], fsend.at[to], frecv.at[sender], to)

    for step in range(1, cams):
        view_copy((cam + step) % cams, cam).start()

    def t_core(k):
        return batch_copy(dt_hbm.at[k, 1 - core], t_sum.at[k], tcsend.at[k], tcrecv.at[k], partner)

    def t_peers(k, step):
        to = (cam + step) % cams
        return cam_copy(t_sum.at[k, to], t_peer.at[step - 1, k], tpsend.at[step - 1, k], tprecv.at[step - 1, k], to)

    def t_start(k, carry):
        t_core(k).start()
        return carry

    lax.fori_loop(0, nz, t_start, 0)

    def t_spread(lo, hi):
        def body(k, carry):
            t_core(k).wait_recv()

            def quarter(q, carry):
                i = k * cams + q

                @pl.when(i + 1 < nz * cams)
                def _():
                    own_load(i + 1).start()

                own_load(i).wait()
                t_sum[k, q] = (t_sum[k, q].astype(f32) + t_own[i % 2].astype(f32)).astype(bf16)
                return carry

            lax.fori_loop(0, cams, quarter, 0)
            for step in range(1, cams):
                t_peers(k, step).start()
            return carry

        lax.fori_loop(lo, hi, body, 0)

    gp_ref[:, cam] = dviews_ref[cam]
    ag_ref[...] = jnp.zeros_like(ag_ref)
    for step in range(1, cams):
        other = (cam + step) % cams
        view_copy(other, other).wait_recv()
    for load in x_loads:
        load.wait()
    loads["z2"].wait()

    def lanes_of(j):
        return pl.ds(pl.multiple_of(j * BLK, BLK), BLK)

    def norm_back(du_ref, z_ref, r_ref, j, gain, row):
        lanes = lanes_of(j)
        s0 = jnp.zeros((n_img, BLK), f32)
        s1 = jnp.zeros((n_img, BLK), f32)
        for p in range(9):
            du = du_ref[p, :, lanes]
            s0 = s0 + du
            s1 = s1 + du * z_ref[p, :, lanes]
        ag_ref[row : row + 1, lanes] = jnp.sum(s1, axis=0, keepdims=True)
        ag_ref[row + 1 : row + 2, lanes] = jnp.sum(s0, axis=0, keepdims=True)
        m0 = group_sum(s0 * gain, ones) * inv_n
        m1 = group_sum(s1 * gain, ones) * inv_n
        rstd = r_ref[:, lanes]
        for p in range(9):
            dv = (du_ref[p, :, lanes] * gain - m0 - z_ref[p, :, lanes] * m1) * rstd
            g_ref[p, :, lanes] = dv.astype(bf16)
            gt_ref[lanes, p * n_img : (p + 1) * n_img] = jnp.transpose(dv).astype(bf16)

    def second(j, carry):
        lanes = lanes_of(j)
        gain, offset = aff_ref[2:3, lanes], aff_ref[3:4, lanes]
        pooled = gp_ref[:, :, :, lanes].reshape(n_img, BLK).astype(f32) * (1.0 / 9.0)
        for p in range(9):
            u = z2_ref[p, :, lanes] * gain + offset + x_ref[p, :, lanes].astype(f32)
            s = sigmoid(u)
            ig_ref[p, :, lanes] = pooled * (s * (1.0 + u * (1.0 - s)))
        norm_back(ig_ref, z2_ref, r2_ref, j, gain, 2)
        return carry

    def first(j, carry):
        lanes = lanes_of(j)
        gain, offset = aff_ref[0:1, lanes], aff_ref[1:2, lanes]
        for p in range(9):
            u = z1_ref[p, :, lanes] * gain + offset
            s = sigmoid(u)
            z2_ref[p, :, lanes] = z2_ref[p, :, lanes] * (s * (1.0 + u * (1.0 - s)))
        norm_back(z2_ref, z1_ref, r1_ref, j, gain, 0)
        return carry

    def width(k):
        return chunk + BLK if k == 5 else chunk

    def core_copy(k):
        cols = pl.ds(0, width(k))
        return batch_copy(
            core_out.at[k % 2, :, :, cols], core_in.at[k % 3, :, :, cols], csend.at[k], crecv.at[k], partner
        )

    def keep(k, d0, lane, v):
        count, wide = v.shape[0] // (2 * rows), v.shape[1]
        parts = v.reshape(count, 2, rows, wide)
        even, odd = parts[:, 0], parts[:, 1]
        dwf[k % 2, d0 : d0 + count, :, lane : lane + wide] = jnp.where(core == 0, even, odd)
        core_out[k % 2, d0 : d0 + count, :, lane : lane + wide] = jnp.where(core == 0, odd, even).astype(bf16)

    def make_chunk(k):
        if k >= 2:
            core_copy(k - 2).wait_send()
        src_ref = a_ref if k < 3 else x_ref
        a = k % 3
        r_lo, r_hi = max(0, 1 - a), min(2, 3 - a)
        for b in range(3):
            c_lo, c_hi = max(0, 1 - b), min(2, 3 - b)
            if b == 1:
                runs = [(3 * r_lo, 3 * (r_hi - r_lo + 1))]
            else:
                runs = [(3 * r + c_lo, c_hi - c_lo + 1) for r in range(r_lo, r_hi + 1)]
            shift = 3 * (a - 1) + b - 1
            for half in range(2):
                acc = None
                for p, m in runs:
                    part = dot(
                        gt_ref[half * 256 : half * 256 + 256, p * n_img : (p + m) * n_img],
                        src_ref[p + shift : p + shift + m].reshape(m * n_img, CH),
                    )
                    acc = part if acc is None else acc + part
                keep(k, half * nz // 2, b * CH, acc)
        if k == 5:
            keep(k, 0, chunk, jnp.transpose(ag_ref[...]))
        core_copy(k).start()

    def term(k, d):
        return dwf[k % 2, d, :, 0 : width(k)] + core_in[k % 3, d, :, 0 : width(k)].astype(f32)

    def line_copy(k, way, s):
        if k == 6:
            return batch_copy(
                t_slots.at[way, s - 1], t_slots.at[way, s], tzsend.at[way, s], tzrecv.at[way, s], me - 2 + 4 * way
            )
        cols = pl.ds(0, width(k))
        return batch_copy(
            slots.at[k % 3, way, s - 1, :, cols], slots.at[k % 3, way, s, :, cols],
            zsend.at[k, way, s], zrecv.at[k, way, s], me - 2 + 4 * way,
        )

    def slot(k, way, s):
        return t_slots.at[way, s] if k == 6 else slots.at[k % 3, way, s, :, pl.ds(0, width(k))]

    def t_term(d):
        total = t_sum[d, cam].astype(f32)
        for step in range(1, cams):
            total = total + t_peer[step - 1, d].astype(f32)
        return total

    def serve(k, s):
        for way in range(2):
            ahead = zi if way else nz - 1 - zi
            d = nz - s + zi if way else s - nz + zi
            ref = slot(k, way, s - 1)

            @pl.when((ahead < nz - 1) & (s > ahead))
            def _():
                own = t_term(d) if k == 6 else term(k, d)

                @pl.when(ahead > 0)
                def _():
                    line_copy(k, way, s - 1).wait_recv()
                    ref[...] = (ref[...].astype(f32) + own).astype(bf16)

                @pl.when(ahead == 0)
                def _():
                    ref[...] = own.astype(bf16)

                line_copy(k, way, s).start()

    def steps(k, part):
        lo, hi = 1 + part * (nz - 1) // 3, 1 + (part + 1) * (nz - 1) // 3
        if hi - lo == 1:
            serve(k, lo)
        elif hi > lo:
            def body(s, carry):
                serve(k, s)
                return carry

            lax.fori_loop(lo, hi, body, 0)

    def service(g):
        k, part = divmod(g, 3)
        if part == 0:
            core_copy(k).wait_recv()
        steps(k, part)

    def collect(k, total, write):
        last = nz - 1

        @pl.when(zi > 0)
        def _():
            line_copy(k, 1, last).wait_recv()

        @pl.when(zi < nz - 1)
        def _():
            line_copy(k, 0, last).wait_recv()

        @pl.when(zi == 0)
        def _():
            write(total + slot(k, 0, last)[...].astype(f32))

        @pl.when(zi == nz - 1)
        def _():
            write(total + slot(k, 1, last)[...].astype(f32))

        @pl.when((zi > 0) & (zi < nz - 1))
        def _():
            write(total + slot(k, 0, last)[...].astype(f32) + slot(k, 1, last)[...].astype(f32))

        def drain(s, carry):
            for way in range(2):
                ahead = zi if way else nz - 1 - zi

                @pl.when((ahead < nz - 1) & (s > ahead))
                def _():
                    line_copy(k, way, s).wait_send()
            return carry

        lax.fori_loop(1, nz, drain, 0)

    def finish(k):
        def write(v):
            genc_ref[:, 1 - k // 3, (k % 3) * chunk : (k % 3 + 1) * chunk] = v[:, 0:chunk]
            if k == 5:
                gaff_ref[...] = jnp.transpose(v[:, chunk:])[0 : gaff_ref.shape[0]]

        collect(k, term(k, zi), write)

    def t_arrived():
        for step in range(1, cams):
            def body(k, carry):
                t_peers(k, step).wait_recv()
                return carry

            lax.fori_loop(0, nz, body, 0)

    def t_final(to, sender):
        return cam_copy(t_all.at[cam], t_all.at[sender], tfsend.at[to], tfrecv.at[sender], to)

    def t_finish():
        def write(v):
            t_all[cam] = v.astype(bf16)

        collect(6, t_term(zi), write)
        for step in range(1, cams):
            t_final((cam + step) % cams, cam).start()

    def t_write():
        for step in range(1, cams):
            other = (cam + step) % cams
            t_final(other, other).wait_recv()

        def cut(lo, wide):
            return t_all[:, :, lo : lo + wide].reshape(rows, wide).astype(f32)

        at = 0
        for ref, wide in ((gconvs_ref, 5 * CH), (gfilm_ref, cond)):
            for which in range(2):
                ref[:, which, :] = cut(at, wide)
                at += wide
        for ref, wide in ((gskip_ref, CH), (gdown_ref, 3 * CH)):
            ref[...] = cut(at, wide)
            at += wide
        gblk_ref[...] = jnp.transpose(cut(at, BLK))[0 : gblk_ref.shape[0]]

    def input_back(q):
        r, c = divmod(q, 3)
        acc = None
        for a in range(3):
            for b in range(3):
                pr, pc = r - a + 1, c - b + 1
                if 0 <= pr < 3 and 0 <= pc < 3:
                    t = 3 * a + b
                    w = w_ref[:, :, t * CH : (t + 1) * CH].reshape(CH, CH)
                    part = dot(g_ref[3 * pr + pc], w)
                    acc = part if acc is None else acc + part
        return acc

    def back_second(*qs):
        for q in qs:
            if q == 0:
                load_w(1).wait()
            z2_ref[q] = input_back(q)
            if q == 8:
                load_w(0).start()

    def back_first(*qs):
        for q in qs:
            if q == 0:
                load_w(0).wait()
            ig_ref[q] = ig_ref[q] + input_back(q)

    lax.fori_loop(0, CH // BLK, second, 0)
    loads["a"].wait()
    make_chunk(0)
    service(0)
    t_spread(0, nz // 2)
    make_chunk(1)
    service(1)
    t_spread(nz // 2, nz)
    back_second(0, 1, 2)
    service(2)
    back_second(3, 4)
    service(3)
    finish(0)
    make_chunk(2)
    service(4)
    back_second(5, 6)
    service(5)
    back_second(7, 8)
    service(6)
    finish(1)
    loads["z1"].wait()
    lax.fori_loop(0, 2, first, 0)
    service(7)
    lax.fori_loop(2, 4, first, 0)
    service(8)
    make_chunk(3)
    service(9)
    finish(2)
    make_chunk(4)
    service(10)
    back_first(0, 1)
    service(11)
    back_first(2, 3)
    service(12)
    finish(3)
    make_chunk(5)
    service(13)
    back_first(4, 5)
    service(14)
    t_arrived()
    steps(6, 0)
    finish(4)
    back_first(6)
    steps(6, 1)
    back_first(7)
    steps(6, 2)
    back_first(8)
    service(15)
    t_finish()
    service(16)
    service(17)
    t_write()
    finish(5)

    def t_drain(k, carry):
        t_core(k).wait_send()
        for step in range(1, cams):
            t_peers(k, step).wait_send()
        return carry

    lax.fori_loop(0, nz, t_drain, 0)
    for step in range(1, cams):
        t_final((cam + step) % cams, cam).wait_send()
    core_copy(4).wait_send()
    core_copy(5).wait_send()
    for step in range(1, cams):
        view_copy((cam + step) % cams, cam).wait_send()


def temporal_kernel(
    traj_ref, og_ref, arr_ref, mask_ref, emb_ref, t_ref,
    out_ref, tg_ref, dviews_ref, dt_ref,
    pad_t, pad_m, pad_h, za_ref, zb_ref, sum_ref, aff_ref, ag_ref,
):
    cond = (t_ref.shape[1] - 14 * CH - BLK) // 2
    cuts = [0]
    for wide in (5 * CH, 5 * CH, cond, cond, CH, 3 * CH, BLK):
        cuts.append(cuts[-1] + wide)
    wa_ref, wb_ref, f0_ref, f1_ref, ws_ref, wd_ref = [
        t_ref.at[:, cuts[i] : cuts[i + 1]] for i in range(6)
    ]
    dwa_ref, dwb_ref, df0_ref, df1_ref, dws_ref, dwd_ref = [
        dt_ref.at[:, cuts[i] : cuts[i + 1]] for i in range(6)
    ]
    aff_ref[...] = jnp.transpose(t_ref[:, cuts[6] :].astype(f32))
    ag_ref[...] = jnp.zeros_like(ag_ref)
    ns = mask_ref.shape[0]
    rows = traj_ref.shape[0]
    nf = rows // ns
    edge = 2 * ns
    ones = group_ones(CH, CH // GROUPS)
    inv_n = 1.0 / (nf * (CH // GROUPS))
    aff = lambda i: aff_ref[i : i + 1, :]

    def frames(v):
        return v.reshape(nf, ns, CH)

    def fill(pad_ref, v):
        pad_ref[0:edge, :] = jnp.zeros((edge, CH), bf16)
        pad_ref[edge : edge + rows, :] = v
        pad_ref[edge + rows : edge + rows + edge, :] = jnp.zeros((edge, CH), bf16)

    def conv5(pad_ref, w_ref):
        acc = None
        for t in range(5):
            part = dot(pad_ref[t * ns : t * ns + rows, :], w_ref[:, t * CH : (t + 1) * CH], NT)
            acc = part if acc is None else acc + part
        return acc

    def conv5_back(pad_ref, w_ref):
        acc = None
        for t in range(5):
            part = dot(pad_ref[(4 - t) * ns : (4 - t) * ns + rows, :], w_ref[:, t * CH : (t + 1) * CH])
            acc = part if acc is None else acc + part
        return acc

    def norm(v):
        v = frames(v)
        mean = group_sum(jnp.sum(v, axis=0), ones) * inv_n
        centred = v - mean[None]
        rstd = lax.rsqrt(group_sum(jnp.sum(centred * centred, axis=0), ones) * inv_n + norm_eps)
        return centred * rstd[None], rstd

    def norm_back(du, z, rstd, gain):
        s0 = jnp.sum(du, axis=0)
        s1 = jnp.sum(du * z, axis=0)
        m0 = group_sum(s0 * gain, ones) * inv_n
        m1 = group_sum(s1 * gain, ones) * inv_n
        dv = (du * gain[None] - m0[None] - z * m1[None]) * rstd[None]
        return dv, jnp.sum(s1, axis=0, keepdims=True), jnp.sum(s0, axis=0, keepdims=True)

    mask = mask_ref[...]
    count = jnp.sum(mask, axis=1, keepdims=True)
    cams = arr_ref.shape[0]
    obs = arr_ref.shape[1]
    conds, slopes = [], []
    for o in range(obs):
        pooled = None
        for cam in range(cams):
            part = mask[:, cam : cam + 1] * arr_ref[cam, o].astype(f32)
            pooled = part if pooled is None else pooled + part
        value, slope = mish_pair(pooled / count)
        conds.append(value.astype(bf16))
        slopes.append(slope)
    conds.append(mish_value(emb_ref[...]).astype(bf16))
    lanes = [slice(o * CH, (o + 1) * CH) for o in range(obs)] + [slice(obs * CH, cond)]
    film = []
    for i, w_ref in ((6, f0_ref), (7, f1_ref)):
        film.append(sum(dot(v, w_ref[:, cols], NT) for v, cols in zip(conds, lanes)) + aff(i))
    scale, shift = film

    fill(pad_t, traj_ref[...])
    za, rstd_a = norm(conv5(pad_t, wa_ref) + aff(4))
    za_ref[...] = za.reshape(rows, CH)
    act_a = mish_value(za * aff(0)[None] + aff(1)[None])
    fill(pad_m, (act_a * scale[None] + shift[None]).astype(bf16).reshape(rows, CH))
    zb, rstd_b = norm(conv5(pad_m, wb_ref) + aff(5))
    zb_ref[...] = zb.reshape(rows, CH)
    skip = frames(dot(traj_ref[...], ws_ref[...], NT)) + aff(8)[None]
    summed = (mish_value(zb * aff(2)[None] + aff(3)[None]) + skip).astype(bf16)
    pairs = summed.reshape(nf // 2, 2, ns, CH)
    half = rows // 2
    sum_ref[0:ns, :] = jnp.zeros((ns, CH), bf16)
    sum_ref[ns : ns + half, :] = pairs[:, 1].reshape(half, CH)
    sum_ref[ns + half : ns + 2 * half, :] = pairs[:, 0].reshape(half, CH)
    taps = (0, ns + half, ns)
    out = None
    og = og_ref[...]
    dcols = []
    for t in range(3):
        cols = sum_ref[taps[t] : taps[t] + half, :]
        w = wd_ref[:, t * CH : (t + 1) * CH]
        part = dot(cols, w, NT)
        out = part if out is None else out + part
        dcols.append(dot(og, w).reshape(nf // 2, ns, CH))
        dwd_ref[:, t * CH : (t + 1) * CH] = dot(og, cols, TN).astype(bf16)
    out_ref[...] = (out + aff(9)).astype(bf16)
    ag_ref[9:10, :] = jnp.sum(og.astype(f32), axis=0, keepdims=True)

    before = jnp.concatenate([dcols[0][1:], jnp.zeros((1, ns, CH), f32)], axis=0)
    dsum = jnp.stack([dcols[1], dcols[2] + before], axis=1).reshape(nf, ns, CH)
    ag_ref[8:9, :] = jnp.sum(dsum, axis=(0, 1)).reshape(1, CH)
    dskip = dsum.astype(bf16).reshape(rows, CH)
    dws_ref[...] = dot(dskip, traj_ref[...], TN).astype(bf16)
    tg_ref[...] = dot(dskip, ws_ref[...])
    zb = frames(zb_ref[...])
    _, slope = mish_pair(zb * aff(2)[None] + aff(3)[None])
    dhb, ag_ref[2:3, :], ag_ref[3:4, :] = norm_back(dsum * slope, zb, rstd_b, aff(2))
    ag_ref[5:6, :] = jnp.sum(dhb, axis=(0, 1)).reshape(1, CH)
    fill(pad_h, dhb.astype(bf16).reshape(rows, CH))
    hb = pad_h[edge : edge + rows, :]
    for t in range(5):
        dwb_ref[:, t * CH : (t + 1) * CH] = dot(hb, pad_m[t * ns : t * ns + rows, :], TN).astype(bf16)
    dmid = frames(conv5_back(pad_h, wb_ref))
    za = frames(za_ref[...])
    act_a, slope = mish_pair(za * aff(0)[None] + aff(1)[None])
    dscale = jnp.sum(dmid * act_a, axis=0)
    dshift = jnp.sum(dmid, axis=0)
    dha, ag_ref[0:1, :], ag_ref[1:2, :] = norm_back(dmid * scale[None] * slope, za, rstd_a, aff(0))
    ag_ref[4:5, :] = jnp.sum(dha, axis=(0, 1)).reshape(1, CH)
    ag_ref[6:7, :] = jnp.sum(dscale, axis=0, keepdims=True)
    ag_ref[7:8, :] = jnp.sum(dshift, axis=0, keepdims=True)
    fill(pad_h, dha.astype(bf16).reshape(rows, CH))
    ha = pad_h[edge : edge + rows, :]
    for t in range(5):
        dwa_ref[:, t * CH : (t + 1) * CH] = dot(ha, pad_t[t * ns : t * ns + rows, :], TN).astype(bf16)
    tg_ref[...] = tg_ref[...] + conv5_back(pad_h, wa_ref)

    lows = (dscale.astype(bf16), dshift.astype(bf16))
    for low, dw_ref in zip(lows, (df0_ref, df1_ref)):
        for v, cols in zip(conds, lanes):
            dw_ref[:, cols] = dot(low, v, TN).astype(bf16)
    for o in range(obs):
        dcond = dot(lows[0], f0_ref[:, lanes[o]]) + dot(lows[1], f1_ref[:, lanes[o]])
        dview = dcond * slopes[o] / count
        for cam in range(cams):
            dviews_ref[cam, o] = (mask[:, cam : cam + 1] * dview).astype(bf16)
    dt_ref[:, cuts[6] :] = jnp.transpose(ag_ref[...]).astype(bf16)


def call(kernel, outs, in_specs, out_specs, scratch=(), collective_id=None, cost=None):
    extra = {} if collective_id is None else dict(collective_id=collective_id, has_side_effects=True)
    return pl.pallas_call(
        kernel,
        out_shape=[jax.ShapeDtypeStruct(s, d) for s, d in outs],
        in_specs=in_specs,
        out_specs=out_specs,
        scratch_shapes=list(scratch),
        compiler_params=pltpu.CompilerParams(vmem_limit_bytes=VMEM_BYTES, **extra),
        cost_estimate=cost,
    )


def work(microseconds):
    return pl.CostEstimate(
        flops=int(microseconds * 1e9), bytes_accessed=int(microseconds * 3e6), transcendentals=0
    )


V = pl.BlockSpec(memory_space=pltpu.VMEM)
H = pl.BlockSpec(memory_space=pl.ANY)
DMA = pltpu.SemaphoreType.DMA


def time_embed(steps_given, embed_width):
    half_width = embed_width // 2
    frequency = jnp.exp(
        jnp.arange(half_width, dtype=jnp.float32) * (-math.log(10000.0) / (half_width - 1))
    )
    argument = steps_given.astype(jnp.float32)[:, None] * frequency[None, :]
    return jnp.concatenate([jnp.sin(argument), jnp.cos(argument)], axis=1)


def adamw(weight, gradient, moment_one, moment_two, step_rate, weight_decay):
    mean_new = beta_first * moment_one + (1.0 - beta_first) * gradient
    square_new = beta_second * moment_two + (1.0 - beta_second) * gradient * gradient
    mean_hat = mean_new / (1.0 - beta_first**STEP)
    square_hat = square_new / (1.0 - beta_second**STEP)
    weight_new = weight - step_rate * (
        mean_hat / (jnp.sqrt(square_hat) + adam_eps) + weight_decay * weight
    )
    return (weight_new, mean_new, square_new)


def adam_kernel(*refs):
    for i in range(7):
        w_ref, m_ref, v_ref, g_ref = refs[4 * i : 4 * i + 4]
        outs = refs[28 + 3 * i : 31 + 3 * i]

        def update():
            vector = i in (1, 6)
            rate, decay = (rate_vector, 0.0) if vector else (rate_matrix, decay_matrix)
            new = adamw(w_ref[...], g_ref[...], m_ref[...], v_ref[...], rate, decay)
            for ref, value in zip(outs, new):
                ref[...] = value

        if i in (1, 6):
            pl.when(pl.program_id(0) == 0)(update)
        else:
            update()


def adam_call(shown, grads, rows):
    step = min(rows, 8)

    def spec(v):
        if v.shape[0] != rows:
            return pl.BlockSpec(v.shape, lambda r: (0, 0))
        return pl.BlockSpec((step,) + v.shape[1:], lambda r: (r,) + (0,) * (v.ndim - 1))

    ins = []
    for i in range(7):
        ins += [shown[0][i], shown[1][i], shown[2][i], grads[i]]
    outs = [w for w in shown[0] for _ in range(3)]
    return pl.pallas_call(
        adam_kernel,
        grid=(rows // step,),
        out_shape=[jax.ShapeDtypeStruct(v.shape, f32) for v in outs],
        in_specs=[spec(v) for v in ins],
        out_specs=[spec(v) for v in outs],
        compiler_params=pltpu.CompilerParams(vmem_limit_bytes=VMEM_BYTES),
        cost_estimate=work(12),
    )(*ins)


def shards(
    n, images, trajectory, view_mask, timesteps, out_grad,
    encoder_weight, encoder_affine, block_convs, film_weight, skip_weight, down_weight, block_affine,
    first_encoder, first_affine, first_convs, first_film, first_skip, first_down, first_block,
    second_encoder, second_affine, second_convs, second_film, second_skip, second_down, second_block,
):
    ns, nf, ch = trajectory.shape
    cams, obs = images.shape[1], images.shape[3]
    n_img = cams * images.shape[2] * obs
    nz, per = n // 2, ch // n
    cond = film_weight.shape[2]
    wide = 9 * ch
    rows = nf * ns

    own_t = jnp.concatenate(
        [block_convs[:, 0], block_convs[:, 1], film_weight[:, 0], film_weight[:, 1], skip_weight, down_weight,
         jnp.pad(block_affine, ((0, 0), (0, BLK - block_affine.shape[1])))],
        axis=1,
    ).astype(bf16)
    part = per // cams
    own_part = lax.dynamic_slice_in_dim(own_t, lax.axis_index("cam") * part, part, 0)
    line_t = lax.all_gather(own_part, "batch", axis=0)
    all_t = lax.all_gather(line_t, "cam", axis=1).reshape(ch, own_t.shape[1])

    own_w = jnp.concatenate(
        [jnp.transpose(encoder_weight[0], (1, 0, 2)),
         jnp.broadcast_to(jnp.pad(encoder_affine[0], ((0, 0), (0, BLK - 4)))[None], (2, per, BLK))],
        axis=2,
    ).astype(bf16)
    x = jnp.transpose(images[0], (2, 0, 1, 3, 4)).reshape(n_img, wide)
    pos = (9, n_img, ch)
    z1, r1, act, z2, r2, arrived, w_all, enc_aff = call(
        functools.partial(enc_fwd_kernel, n, cams),
        [(pos, f32), ((n_img, ch), f32), (pos, bf16), (pos, f32), ((n_img, ch), f32),
         ((cams, obs, ns, ch), bf16), ((2, n, per, wide + BLK), bf16), ((8, ch), f32)],
        [V, V],
        [H, V, H, H, V, V, H, V],
        [pltpu.VMEM((2, n, per, wide + BLK), bf16), pltpu.VMEM(pos, f32), pltpu.VMEM((n_img, wide), bf16),
         pltpu.VMEM(pos, f32), pltpu.VMEM((obs, cams, ns, ch), bf16), pltpu.VMEM((cams, obs, ns, ch), bf16),
         DMA((2, 2, nz)), DMA((2, nz)), DMA((2, nz)), DMA((2, nz)), DMA((2, ch // BLK)), DMA((11,)),
         DMA((cams,)), DMA((cams,))],
        collective_id=0,
        cost=work(90),
    )(x, own_w)

    present = view_mask.astype(f32)
    embedded = time_embed(timesteps, TEMB)
    traj_fm = jnp.transpose(trajectory, (1, 0, 2)).reshape(rows, ch)
    og_fm = jnp.transpose(out_grad, (1, 0, 2)).reshape(rows // 2, ch)
    out_fm, tg_fm, dviews, dt = call(
        temporal_kernel,
        [((rows // 2, ch), bf16), ((rows, ch), f32), ((cams, obs, ns, ch), bf16), (all_t.shape, bf16)],
        [V] * 6,
        [V] * 4,
        [pltpu.VMEM((rows + 4 * ns, ch), bf16)] * 3
        + [pltpu.VMEM((rows, ch), f32)] * 2
        + [pltpu.VMEM((rows + ns, ch), bf16)]
        + [pltpu.VMEM((BLK, ch), f32)] * 2,
        cost=work(20),
    )(traj_fm, og_fm, arrived, present, embedded, all_t)
    block_output = jnp.transpose(out_fm.reshape(nf // 2, ns, ch), (1, 0, 2))
    trajectory_grad = jnp.transpose(tg_fm.reshape(nf, ns, ch), (1, 0, 2))

    chunk = 3 * ch + BLK
    t_wide = all_t.shape[1]
    ig, genc, gaff, gconvs, gfilm, gskip, gdown, gblk = call(
        functools.partial(enc_bwd_kernel, n, cams, cond),
        [(pos, f32), ((per, 2, wide), f32), ((4, per), f32), ((per, 2, 5 * ch), f32),
         ((per, 2, cond), f32), ((per, ch), f32), ((per, 3 * ch), f32), ((10, per), f32)],
        [H, H, H, H, V, H, V, V, V, H],
        [V] * 8,
        [pltpu.VMEM(pos, bf16), pltpu.VMEM(pos, bf16), pltpu.VMEM((n, per, wide), bf16), pltpu.VMEM(pos, f32),
         pltpu.VMEM(pos, f32), pltpu.VMEM(pos, bf16), pltpu.VMEM((ch, 9 * n_img), bf16),
         pltpu.VMEM((BLK, ch), f32), pltpu.VMEM((obs, cams, ns, ch), bf16),
         pltpu.VMEM((2, nz, per, chunk), f32), pltpu.VMEM((2, nz, per, chunk), bf16),
         pltpu.VMEM((3, nz, per, chunk), bf16), pltpu.VMEM((3, 2, nz, per, chunk), bf16),
         pltpu.VMEM((2, part, t_wide), bf16), pltpu.VMEM((nz, cams, part, t_wide), bf16),
         pltpu.VMEM((cams - 1, nz, part, t_wide), bf16), pltpu.VMEM((2, nz, part, t_wide), bf16),
         pltpu.VMEM((cams, part, t_wide), bf16),
         DMA((13,)), DMA((6,)), DMA((6,)), DMA((6, 2, nz)), DMA((6, 2, nz)), DMA((cams,)), DMA((cams,)),
         DMA((nz * cams,)), DMA((nz,)), DMA((nz,)), DMA((cams - 1, nz)), DMA((cams - 1, nz)),
         DMA((2, nz)), DMA((2, nz)), DMA((cams,)), DMA((cams,))],
        collective_id=1,
        cost=work(100),
    )(x, act, w_all, z1, r1, z2, r2, enc_aff, dviews, dt.reshape(nz, 2, cams, part, t_wide))
    images_grad = jnp.transpose(ig.reshape((9, obs) + images.shape[1:3] + (ch,)), (2, 3, 1, 0, 4))[None]

    def turned(v):
        return jnp.transpose(v.reshape(v.shape[-2:]))

    weights = (encoder_weight, encoder_affine, block_convs, film_weight, skip_weight, down_weight, block_affine)
    firsts = (first_encoder, first_affine, first_convs, first_film, first_skip, first_down, first_block)
    seconds = (second_encoder, second_affine, second_convs, second_film, second_skip, second_down, second_block)
    shown = [
        [turned(v) if i in (1, 6) else v.reshape(v.shape[-3:]) if i == 0 else v for i, v in enumerate(group)]
        for group in (weights, firsts, seconds)
    ]
    news = adam_call(shown, (genc, gaff, gconvs, gfilm, gskip, gdown, gblk), per)
    upd = [
        tuple((turned(v) if i in (1, 6) else v).reshape(w.shape) for v in news[3 * i : 3 * i + 3])
        for i, w in enumerate(weights)
    ]
    return (
        (block_output, trajectory_grad, images_grad)
        + tuple(u[0] for u in upd)
        + tuple(u[1] for u in upd)
        + tuple(u[2] for u in upd)
    )


def solution(mesh):
    sample = P(("cam", "batch"))
    params = (P("cam", "batch"), P("cam", "batch")) + (P("batch"),) * 5
    images_spec = P("cam", None, "batch")
    return jax.shard_map(
        functools.partial(shards, mesh.shape["batch"]),
        mesh=mesh,
        in_specs=(images_spec, sample, sample, sample, sample) + params * 3,
        out_specs=(sample, sample, images_spec) + params * 3,
        check_vma=False,
    )
```

```python
import functools
import math

import jax
import jax.numpy as jnp
from jax import lax
from jax.experimental import pallas as pl
from jax.experimental.pallas import tpu as pltpu
from jax.sharding import PartitionSpec as P

TEMB = 128
GROUPS = 8
STEP = 5

norm_eps = 1e-05
beta_first = 0.5
beta_second = 0.5
adam_eps = 1e-08
rate_matrix = 0.02
rate_vector = 0.2
decay_matrix = 0.01

CH = 512
BLK = 128
ENC_GROUP = 16
f32 = jnp.float32
bf16 = jnp.bfloat16
VMEM_BYTES = 61 * 1024 * 1024

NT = (((1,), (1,)), ((), ()))
NN = (((1,), (0,)), ((), ()))
TN = (((0,), (0,)), ((), ()))


def dot(a, b, dims=NN):
    return lax.dot_general(a, b, dims, preferred_element_type=f32)


def group_ones(width, group):
    rows = lax.broadcasted_iota(jnp.int32, (width, width), 0) // group
    cols = lax.broadcasted_iota(jnp.int32, (width, width), 1) // group
    return jnp.where(rows == cols, 1.0, 0.0).astype(bf16)


def group_sum(v, ones):
    high = v.astype(bf16)
    rest = v - high.astype(f32)
    middle = rest.astype(bf16)
    low = (rest - middle.astype(f32)).astype(bf16)
    return dot(high, ones) + dot(middle, ones) + dot(low, ones)


def sigmoid(v):
    return 1.0 / (1.0 + jnp.exp(-v))


def mish_pair(v):
    e = jnp.exp(jnp.minimum(v, 20.0))
    n = e * (e + 2.0)
    inv = 1.0 / (n + 2.0)
    t = n * inv
    return v * t, t + v * (4.0 * e * (1.0 + e)) * inv * inv


def mish_value(v):
    e = jnp.exp(jnp.minimum(v, 20.0))
    n = e * (e + 2.0)
    return v * (n / (n + 2.0))


def span(i):
    return range(max(0, 1 - i), min(2, 3 - i) + 1)


MESH = pl.DeviceIdType.MESH


def batch_copy(src, dst, send_sem, recv_sem, target):
    return pltpu.make_async_remote_copy(
        src_ref=src, dst_ref=dst, send_sem=send_sem, recv_sem=recv_sem,
        device_id={"batch": target}, device_id_type=MESH,
    )


def cam_copy(src, dst, send_sem, recv_sem, target):
    return pltpu.make_async_remote_copy(
        src_ref=src, dst_ref=dst, send_sem=send_sem, recv_sem=recv_sem,
        device_id={"cam": target}, device_id_type=MESH,
    )


def line_barrier(cams, nz):
    me, cam = lax.axis_index("batch"), lax.axis_index("cam")
    zi, core = me // 2, me % 2
    barrier = pltpu.get_barrier_semaphore()
    pl.semaphore_signal(barrier, inc=1, device_id={"batch": me + 1 - 2 * core}, device_id_type=MESH)
    for step in range(1, cams):
        pl.semaphore_signal(barrier, inc=1, device_id={"cam": (cam + step) % cams}, device_id_type=MESH)

    @pl.when(zi > 0)
    def _():
        pl.semaphore_signal(barrier, inc=1, device_id={"batch": me - 2}, device_id_type=MESH)

    @pl.when(zi < nz - 1)
    def _():
        pl.semaphore_signal(barrier, inc=1, device_id={"batch": me + 2}, device_id_type=MESH)

    ends = (zi == 0).astype(jnp.int32) + (zi == nz - 1).astype(jnp.int32)
    pl.semaphore_wait(barrier, cams + 2 - ends)


PART = 5 * CH


def pack_temporal(ref, convs_ref, film_ref, skip_ref, down_ref, ext_ref):
    rows, cond = film_ref.shape[0], film_ref.shape[2]
    for q in range(2):
        ref[q] = convs_ref[:, q, :].astype(bf16)
        ref[2, :, q * cond : (q + 1) * cond] = film_ref[:, q, :].astype(bf16)
    ref[2, :, 2 * cond : 2 * cond + BLK] = ext_ref[...]
    ref[2, :, 2 * cond + BLK :] = jnp.zeros((rows, PART - 2 * cond - BLK), bf16)
    ref[3, :, 0:CH] = skip_ref[...].astype(bf16)
    ref[3, :, CH : 4 * CH] = down_ref[...].astype(bf16)
    ref[3, :, 4 * CH :] = jnp.zeros((rows, PART - 4 * CH), bf16)


def enc_fwd_kernel(
    n, cams, x_ref, enc_hbm, convs_ref, film_ref, skip_ref, down_ref, ext_ref,
    z1_out, r1_ref, a_out, z2_out, r2_ref, arr_ref, w_out, aff_ref, t_out,
    w_ref, z1_ref, a_ref, z2_ref, feat_ref, arr_s, t_ref, enc_buf,
    zsend, zrecv, csend, crecv, wsem, osem, fsend, frecv,
    tzsend, tzrecv, tcsend, tcrecv, tpsend, tprecv, tsem, esem,
):
    nz = n // 2
    rows = ext_ref.shape[0]
    piece = enc_buf.shape[1]
    spb = BLK // rows
    n_img = x_ref.shape[0]
    me, cam = lax.axis_index("batch"), lax.axis_index("cam")
    zi, core = me // 2, me % 2
    partner = me + 1 - 2 * core
    ones = group_ones(BLK, ENC_GROUP)
    inv_n = 1.0 / (9 * ENC_GROUP)

    def enc_load(i):
        return pltpu.make_async_copy(enc_hbm.at[pl.ds(i * piece, piece)], enc_buf.at[i % 2], esem.at[i])

    enc_load(0).start()
    pack_temporal(t_ref.at[zi, core], convs_ref, film_ref, skip_ref, down_ref, ext_ref)

    line_barrier(cams, nz)

    def tz_copy(k, way):
        ref = t_ref.at[k, core, cam]
        return batch_copy(ref, ref, tzsend.at[way, k], tzrecv.at[k], me - 2 + 4 * way)

    def tc_copy(k, which, q):
        ref = t_ref.at[k, which, q]
        return batch_copy(ref, ref, tcsend.at[k, q], tcrecv.at[k, q], partner)

    def tp_copy(k, step, q):
        ref = t_ref.at[k, core, q]
        return cam_copy(ref, ref, tpsend.at[step - 1, k], tprecv.at[step - 1, k], (cam + step) % cams)

    def t_send(s):
        for k, _, passed, way in moves(s):
            @pl.when(passed)
            def _():
                tz_copy(k, way).start()

    def t_receive(s):
        for k, held, _, way in moves(s):
            @pl.when(held)
            def _():
                tz_copy(k, way).wait_recv()
                for step in range(1, cams):
                    tp_copy(k, step, cam).start()
                tc_copy(k, core, cam).start()

    def t_collect(d):
        for k, held, _, _ in moves(d):
            @pl.when(held & (d > 0))
            def _():
                for step in range(1, cams):
                    q = (cam + cams - step) % cams
                    tp_copy(k, step, q).wait_recv()
                    tc_copy(k, core, q).start()

    def t_save():
        return pltpu.make_async_copy(t_ref, t_out, tsem)

    def t_complete():
        def body(k, carry):
            for q in range(cams):
                tc_copy(k, 1 - core, q).wait_recv()
            return carry

        lax.fori_loop(0, nz, body, 0)
        t_save().start()

    def z_copy(conv, k, way):
        ref = w_ref.at[conv, 2 * k + core]
        return batch_copy(ref, ref, zsend.at[conv, way, k], zrecv.at[conv, k], me - 2 + 4 * way)

    def core_copy(conv, k, which):
        ref = w_ref.at[conv, 2 * k + which]
        return batch_copy(ref, ref, csend.at[conv, k], crecv.at[conv, k], partner)

    def moves(s):
        low, high = zi - s, zi + s
        return (
            (high, high < nz, (high < nz) & (zi > 0), 0),
            (low, low >= 0, (low >= 0) & (zi < nz - 1), 1),
        )

    def send(conv, s):
        for k, _, passed, way in moves(s):
            @pl.when(passed)
            def _():
                z_copy(conv, k, way).start()

    def receive(conv, s):
        for k, held, _, way in moves(s):
            @pl.when(held)
            def _():
                z_copy(conv, k, way).wait_recv()
                core_copy(conv, k, core).start()

    t_send(0)
    for q in range(cams):
        tc_copy(zi, core, q).start()
    for conv in range(2):
        w_ref[conv, me, :, 9 * CH :] = ext_ref[...]
    count = rows // piece

    def pack(i, carry):
        @pl.when(i + 1 < count)
        def _():
            enc_load(i + 1).start()

        enc_load(i).wait()
        for conv in range(2):
            w_ref[conv, me, pl.ds(pl.multiple_of(i * piece, piece), piece), 0 : 9 * CH] = (
                enc_buf[i % 2, :, conv, :].astype(bf16)
            )
        return carry

    lax.fori_loop(0, count, pack, 0)
    for conv in range(2):
        core_copy(conv, zi, core).start()

    def t_step(s, carry):
        @pl.when(s == nz - 1)
        def _():
            send(0, 0)

        t_receive(s)

        @pl.when(s < nz - 1)
        def _():
            t_send(s)
        return carry

    lax.fori_loop(1, nz, t_step, 0)

    def rows_of(conv, j, start, wide):
        block = w_ref[conv, pl.ds(j * spb, spb), :, start : start + wide]
        return block.reshape(BLK, wide)

    def w_save(conv, j):
        part = pl.ds(j * spb, spb)
        return pltpu.make_async_copy(w_ref.at[conv, part], w_out.at[conv, part], wsem.at[conv, j])

    def conv_norm(src_ref, conv, z_ref, r_ref, j):
        lanes = pl.ds(pl.multiple_of(j * BLK, BLK), BLK)
        total = None
        for p in range(9):
            r, c = divmod(p, 3)
            bs = span(c)
            acc = None
            for a in span(r):
                start = (3 * (r + a - 1) + c + bs[0] - 1) * CH
                wide = len(bs) * CH
                part = dot(src_ref[:, start : start + wide], rows_of(conv, j, (3 * a + bs[0]) * CH, wide), NT)
                acc = part if acc is None else acc + part
            z_ref[p, :, lanes] = acc
            total = acc if total is None else total + acc
        mean = group_sum(total, ones) * inv_n
        var = None
        for p in range(9):
            centred = z_ref[p, :, lanes] - mean
            sq = centred * centred
            var = sq if var is None else var + sq
        rstd = lax.rsqrt(group_sum(var, ones) * inv_n + norm_eps)
        r_ref[:, lanes] = rstd
        return lanes, mean, rstd

    def first(j):
        aff_ref[:, lanes_of(j)] = jnp.transpose(rows_of(0, j, 9 * CH, BLK).astype(f32))[0:8]
        lanes, mean, rstd = conv_norm(x_ref, 0, z1_ref, r1_ref, j)
        gain, offset = aff_ref[0:1, lanes], aff_ref[1:2, lanes]
        for p in range(9):
            z = (z1_ref[p, :, lanes] - mean) * rstd
            z1_ref[p, :, lanes] = z
            u = z * gain + offset
            a_ref[:, pl.ds(pl.multiple_of(p * CH + j * BLK, BLK), BLK)] = (u * sigmoid(u)).astype(bf16)

    def second(j):
        lanes, mean, rstd = conv_norm(a_ref, 1, z2_ref, r2_ref, j)
        gain, offset = aff_ref[2:3, lanes], aff_ref[3:4, lanes]
        total = None
        for p in range(9):
            z = (z2_ref[p, :, lanes] - mean) * rstd
            z2_ref[p, :, lanes] = z
            pic = x_ref[:, pl.ds(pl.multiple_of(p * CH + j * BLK, BLK), BLK)].astype(f32)
            u = z * gain + offset + pic
            act = u * sigmoid(u)
            total = act if total is None else total + act
        out = (total * (1.0 / 9.0)).astype(bf16)
        feat_ref[:, :, :, lanes] = out.reshape(feat_ref.shape[:3] + (BLK,))

    def lanes_of(j):
        return pl.ds(pl.multiple_of(j * BLK, BLK), BLK)

    def arrived(conv, k):
        core_copy(conv, k, 1 - core).wait_recv()

    def phase(conv, block):
        streaming = spb == 2

        def step(s, carry):
            if conv == 0:
                @pl.when((s > 0) & (s < nz - 1))
                def _():
                    send(0, s)

                @pl.when(s == nz - 1)
                def _():
                    send(1, 0)
            else:
                @pl.when((s > 0) & (s < nz - 1))
                def _():
                    send(1, s)

            def side(d, carry):
                k = zi + s - 2 * s * d

                @pl.when((k >= 0) & (k < nz) & (s + 1 > d))
                def _():
                    arrived(conv, k)
                    if streaming:
                        w_save(conv, k).start()
                        block(k)
                return carry

            lax.fori_loop(0, 2, side, 0)
            if conv == 1:
                t_collect(2 * s)
                t_collect(2 * s + 1)
                pl.when(s == nz - 2)(t_complete)

            @pl.when(s < nz - 1)
            def _():
                receive(conv, s + 1)
            return carry

        lax.fori_loop(0, nz, step, 0)
        if not streaming:
            def rest(j, carry):
                w_save(conv, j).start()
                block(j)
                return carry

            lax.fori_loop(0, CH // BLK, rest, 0)

    phase(0, first)
    saves = [pltpu.make_async_copy(z1_ref, z1_out, osem.at[0])]
    saves += [
        pltpu.make_async_copy(a_ref.at[:, p * CH : (p + 1) * CH], a_out.at[p], osem.at[2 + p])
        for p in range(9)
    ]
    for save in saves:
        save.start()
    phase(1, second)
    last = pltpu.make_async_copy(z2_ref, z2_out, osem.at[1])
    last.start()

    def feat_copy(to, sender):
        return cam_copy(feat_ref.at[:, to], arr_s.at[sender], fsend.at[to], frecv.at[sender], to)

    for step in range(1, cams):
        feat_copy((cam + step) % cams, cam).start()
    arr_s[cam] = feat_ref[:, cam]
    for step in range(1, cams):
        other = (cam + step) % cams
        feat_copy(other, other).wait_recv()
    arr_ref[...] = arr_s[...]
    for step in range(1, cams):
        feat_copy((cam + step) % cams, cam).wait_send()

    for conv in range(2):
        def drain(k, carry):
            s = k - zi

            @pl.when((s >= 0) & (s < nz - 1) & (zi > 0))
            def _():
                z_copy(conv, k, 0).wait_send()

            @pl.when((s <= 0) & (s > 1 - nz) & (zi < nz - 1))
            def _():
                z_copy(conv, k, 1).wait_send()

            core_copy(conv, k, core).wait_send()
            return carry

        lax.fori_loop(0, nz, drain, 0)

        def saved(j, carry):
            w_save(conv, j).wait()
            return carry

        lax.fori_loop(0, CH // BLK, saved, 0)
    for save in saves:
        save.wait()
    last.wait()

    def t_drain(k, carry):
        s = k - zi

        @pl.when((s >= 0) & (s < nz - 1) & (zi > 0))
        def _():
            tz_copy(k, 0).wait_send()

        @pl.when((s <= 0) & (s > 1 - nz) & (zi < nz - 1))
        def _():
            tz_copy(k, 1).wait_send()

        @pl.when(s != 0)
        def _():
            for step in range(1, cams):
                tp_copy(k, step, cam).wait_send()

        for q in range(cams):
            tc_copy(k, core, q).wait_send()
        return carry

    lax.fori_loop(0, nz, t_drain, 0)
    t_save().wait()


def enc_bwd_kernel(
    n, cams, cond, x_hbm, a_hbm, w_hbm, z1_hbm, r1_ref, z2_hbm, r2_ref, aff_ref, dviews_ref, dt_hbm,
    ig_ref, genc_ref, gaff_ref, gconvs_ref, gfilm_ref, gskip_ref, gdown_ref, gblk_ref,
    x_ref, a_ref, w_ref, z1_ref, z2_ref, g_ref, gt_ref, ag_ref, gp_ref,
    dwf, core_out, core_in, slots, t_own, t_sum, t_peer, t_slots, t_all,
    lsem, csend, crecv, zsend, zrecv, fsend, frecv,
    tlsem, tcsend, tcrecv, tpsend, tprecv, tzsend, tzrecv, tfsend, tfrecv,
):
    nz = n // 2
    rows = CH // n
    n_img = z1_ref.shape[1]
    me, cam = lax.axis_index("batch"), lax.axis_index("cam")
    zi, core = me // 2, me % 2
    partner = me + 1 - 2 * core
    ones = group_ones(BLK, ENC_GROUP)
    inv_n = 1.0 / (9 * ENC_GROUP)
    chunk = 3 * CH

    def load_w(conv):
        return pltpu.make_async_copy(w_hbm.at[conv, :, :, 0 : 9 * CH], w_ref, lsem.at[3])

    loads = {
        "z2": pltpu.make_async_copy(z2_hbm, z2_ref, lsem.at[0]),
        "z1": pltpu.make_async_copy(z1_hbm, z1_ref, lsem.at[1]),
        "a": pltpu.make_async_copy(a_hbm, a_ref, lsem.at[2]),
    }
    x_loads = [
        pltpu.make_async_copy(x_hbm.at[:, p * CH : (p + 1) * CH], x_ref.at[p], lsem.at[4 + p])
        for p in range(9)
    ]
    loads["z2"].start()
    for load in x_loads:
        load.start()
    loads["a"].start()
    load_w(1).start()
    loads["z1"].start()

    def own_load(i):
        return pltpu.make_async_copy(dt_hbm.at[i // cams, core, i % cams], t_own.at[i % 2], tlsem.at[i])

    own_load(0).start()

    line_barrier(cams, nz)

    def view_copy(to, sender):
        return cam_copy(dviews_ref.at[to], gp_ref.at[:, sender], fsend.at[to], frecv.at[sender], to)

    for step in range(1, cams):
        view_copy((cam + step) % cams, cam).start()

    def t_core(k):
        return batch_copy(dt_hbm.at[k, 1 - core], t_sum.at[k], tcsend.at[k], tcrecv.at[k], partner)

    def t_peers(k, step):
        to = (cam + step) % cams
        return cam_copy(t_sum.at[k, to], t_peer.at[step - 1, k], tpsend.at[step - 1, k], tprecv.at[step - 1, k], to)

    def t_start(k, carry):
        t_core(k).start()
        return carry

    lax.fori_loop(0, nz, t_start, 0)

    def t_spread(lo, hi):
        def body(k, carry):
            t_core(k).wait_recv()

            def quarter(q, carry):
                i = k * cams + q

                @pl.when(i + 1 < nz * cams)
                def _():
                    own_load(i + 1).start()

                own_load(i).wait()
                t_sum[k, q] = (t_sum[k, q].astype(f32) + t_own[i % 2].astype(f32)).astype(bf16)
                return carry

            lax.fori_loop(0, cams, quarter, 0)
            for step in range(1, cams):
                t_peers(k, step).start()
            return carry

        lax.fori_loop(lo, hi, body, 0)

    gp_ref[:, cam] = dviews_ref[cam]
    ag_ref[...] = jnp.zeros_like(ag_ref)
    for step in range(1, cams):
        other = (cam + step) % cams
        view_copy(other, other).wait_recv()
    for load in x_loads:
        load.wait()
    loads["z2"].wait()

    def lanes_of(j):
        return pl.ds(pl.multiple_of(j * BLK, BLK), BLK)

    def norm_back(du_ref, z_ref, r_ref, j, gain, row):
        lanes = lanes_of(j)
        s0 = jnp.zeros((n_img, BLK), f32)
        s1 = jnp.zeros((n_img, BLK), f32)
        for p in range(9):
            du = du_ref[p, :, lanes]
            s0 = s0 + du
            s1 = s1 + du * z_ref[p, :, lanes]
        ag_ref[row : row + 1, lanes] = jnp.sum(s1, axis=0, keepdims=True)
        ag_ref[row + 1 : row + 2, lanes] = jnp.sum(s0, axis=0, keepdims=True)
        m0 = group_sum(s0 * gain, ones) * inv_n
        m1 = group_sum(s1 * gain, ones) * inv_n
        rstd = r_ref[:, lanes]
        for p in range(9):
            dv = (du_ref[p, :, lanes] * gain - m0 - z_ref[p, :, lanes] * m1) * rstd
            g_ref[p, :, lanes] = dv.astype(bf16)
            gt_ref[lanes, p * n_img : (p + 1) * n_img] = jnp.transpose(dv).astype(bf16)

    def second(j, carry):
        lanes = lanes_of(j)
        gain, offset = aff_ref[2:3, lanes], aff_ref[3:4, lanes]
        pooled = gp_ref[:, :, :, lanes].reshape(n_img, BLK).astype(f32) * (1.0 / 9.0)
        for p in range(9):
            u = z2_ref[p, :, lanes] * gain + offset + x_ref[p, :, lanes].astype(f32)
            s = sigmoid(u)
            ig_ref[p, :, lanes] = pooled * (s * (1.0 + u * (1.0 - s)))
        norm_back(ig_ref, z2_ref, r2_ref, j, gain, 2)
        return carry

    def first(j, carry):
        lanes = lanes_of(j)
        gain, offset = aff_ref[0:1, lanes], aff_ref[1:2, lanes]
        for p in range(9):
            u = z1_ref[p, :, lanes] * gain + offset
            s = sigmoid(u)
            z2_ref[p, :, lanes] = z2_ref[p, :, lanes] * (s * (1.0 + u * (1.0 - s)))
        norm_back(z2_ref, z1_ref, r1_ref, j, gain, 0)
        return carry

    def width(k):
        return chunk + BLK if k == 5 else chunk

    def core_copy(k):
        cols = pl.ds(0, width(k))
        return batch_copy(
            core_out.at[k % 2, :, :, cols], core_in.at[k % 3, :, :, cols], csend.at[k], crecv.at[k], partner
        )

    def keep(k, d0, lane, v):
        count, wide = v.shape[0] // (2 * rows), v.shape[1]
        parts = v.reshape(count, 2, rows, wide)
        even, odd = parts[:, 0], parts[:, 1]
        dwf[k % 2, d0 : d0 + count, :, lane : lane + wide] = jnp.where(core == 0, even, odd)
        core_out[k % 2, d0 : d0 + count, :, lane : lane + wide] = jnp.where(core == 0, odd, even).astype(bf16)

    def make_chunk(k):
        if k >= 2:
            core_copy(k - 2).wait_send()
        src_ref = a_ref if k < 3 else x_ref
        a = k % 3
        r_lo, r_hi = max(0, 1 - a), min(2, 3 - a)
        for b in range(3):
            c_lo, c_hi = max(0, 1 - b), min(2, 3 - b)
            if b == 1:
                runs = [(3 * r_lo, 3 * (r_hi - r_lo + 1))]
            else:
                runs = [(3 * r + c_lo, c_hi - c_lo + 1) for r in range(r_lo, r_hi + 1)]
            shift = 3 * (a - 1) + b - 1
            for half in range(2):
                acc = None
                for p, m in runs:
                    part = dot(
                        gt_ref[half * 256 : half * 256 + 256, p * n_img : (p + m) * n_img],
                        src_ref[p + shift : p + shift + m].reshape(m * n_img, CH),
                    )
                    acc = part if acc is None else acc + part
                keep(k, half * nz // 2, b * CH, acc)
        if k == 5:
            keep(k, 0, chunk, jnp.transpose(ag_ref[...]))
        core_copy(k).start()

    def term(k, d):
        return dwf[k % 2, d, :, 0 : width(k)] + core_in[k % 3, d, :, 0 : width(k)].astype(f32)

    def line_copy(k, way, s):
        if k == 6:
            return batch_copy(
                t_slots.at[way, s - 1], t_slots.at[way, s], tzsend.at[way, s], tzrecv.at[way, s], me - 2 + 4 * way
            )
        cols = pl.ds(0, width(k))
        return batch_copy(
            slots.at[k % 3, way, s - 1, :, cols], slots.at[k % 3, way, s, :, cols],
            zsend.at[k, way, s], zrecv.at[k, way, s], me - 2 + 4 * way,
        )

    def slot(k, way, s):
        return t_slots.at[way, s] if k == 6 else slots.at[k % 3, way, s, :, pl.ds(0, width(k))]

    def t_term(d):
        total = t_sum[d, cam].astype(f32)
        for step in range(1, cams):
            total = total + t_peer[step - 1, d].astype(f32)
        return total

    def serve(k, s):
        for way in range(2):
            ahead = zi if way else nz - 1 - zi
            d = nz - s + zi if way else s - nz + zi
            ref = slot(k, way, s - 1)

            @pl.when((ahead < nz - 1) & (s > ahead))
            def _():
                own = t_term(d) if k == 6 else term(k, d)

                @pl.when(ahead > 0)
                def _():
                    line_copy(k, way, s - 1).wait_recv()
                    ref[...] = (ref[...].astype(f32) + own).astype(bf16)

                @pl.when(ahead == 0)
                def _():
                    ref[...] = own.astype(bf16)

                line_copy(k, way, s).start()

    def steps(k, part):
        lo, hi = 1 + part * (nz - 1) // 3, 1 + (part + 1) * (nz - 1) // 3
        if hi - lo == 1:
            serve(k, lo)
        elif hi > lo:
            def body(s, carry):
                serve(k, s)
                return carry

            lax.fori_loop(lo, hi, body, 0)

    def service(g):
        k, part = divmod(g, 3)
        if part == 0:
            core_copy(k).wait_recv()
        steps(k, part)

    def collect(k, total, write):
        last = nz - 1

        @pl.when(zi > 0)
        def _():
            line_copy(k, 1, last).wait_recv()

        @pl.when(zi < nz - 1)
        def _():
            line_copy(k, 0, last).wait_recv()

        @pl.when(zi == 0)
        def _():
            write(total + slot(k, 0, last)[...].astype(f32))

        @pl.when(zi == nz - 1)
        def _():
            write(total + slot(k, 1, last)[...].astype(f32))

        @pl.when((zi > 0) & (zi < nz - 1))
        def _():
            write(total + slot(k, 0, last)[...].astype(f32) + slot(k, 1, last)[...].astype(f32))

        def drain(s, carry):
            for way in range(2):
                ahead = zi if way else nz - 1 - zi

                @pl.when((ahead < nz - 1) & (s > ahead))
                def _():
                    line_copy(k, way, s).wait_send()
            return carry

        lax.fori_loop(1, nz, drain, 0)

    def finish(k):
        def write(v):
            genc_ref[:, 1 - k // 3, (k % 3) * chunk : (k % 3 + 1) * chunk] = v[:, 0:chunk]
            if k == 5:
                gaff_ref[...] = jnp.transpose(v[:, chunk:])[0 : gaff_ref.shape[0]]

        collect(k, term(k, zi), write)

    def t_arrived():
        for step in range(1, cams):
            def body(k, carry):
                t_peers(k, step).wait_recv()
                return carry

            lax.fori_loop(0, nz, body, 0)

    def t_final(to, sender):
        return cam_copy(t_all.at[cam], t_all.at[sender], tfsend.at[to], tfrecv.at[sender], to)

    def t_finish():
        def write(v):
            t_all[cam] = v.astype(bf16)

        collect(6, t_term(zi), write)
        for step in range(1, cams):
            t_final((cam + step) % cams, cam).start()

    def t_write():
        for step in range(1, cams):
            other = (cam + step) % cams
            t_final(other, other).wait_recv()

        def cut(q, lo, wide):
            return t_all[q, :, lo : lo + wide].astype(f32)

        for which in range(2):
            gconvs_ref[:, which, :] = cut(which, 0, PART)
            gfilm_ref[:, which, :] = cut(2, which * cond, cond)
        gblk_ref[...] = jnp.transpose(cut(2, 2 * cond, BLK))[0 : gblk_ref.shape[0]]
        gskip_ref[...] = cut(3, 0, CH)
        gdown_ref[...] = cut(3, CH, 3 * CH)

    def input_back(q):
        r, c = divmod(q, 3)
        acc = None
        for a in range(3):
            for b in range(3):
                pr, pc = r - a + 1, c - b + 1
                if 0 <= pr < 3 and 0 <= pc < 3:
                    t = 3 * a + b
                    w = w_ref[:, :, t * CH : (t + 1) * CH].reshape(CH, CH)
                    part = dot(g_ref[3 * pr + pc], w)
                    acc = part if acc is None else acc + part
        return acc

    def back_second(*qs):
        for q in qs:
            if q == 0:
                load_w(1).wait()
            z2_ref[q] = input_back(q)
            if q == 8:
                load_w(0).start()

    def back_first(*qs):
        for q in qs:
            if q == 0:
                load_w(0).wait()
            ig_ref[q] = ig_ref[q] + input_back(q)

    lax.fori_loop(0, CH // BLK, second, 0)
    loads["a"].wait()
    make_chunk(0)
    service(0)
    t_spread(0, nz // 2)
    make_chunk(1)
    service(1)
    t_spread(nz // 2, nz)
    back_second(0, 1, 2)
    service(2)
    back_second(3, 4)
    service(3)
    finish(0)
    make_chunk(2)
    service(4)
    back_second(5, 6)
    service(5)
    back_second(7, 8)
    service(6)
    finish(1)
    loads["z1"].wait()
    lax.fori_loop(0, 2, first, 0)
    service(7)
    lax.fori_loop(2, 4, first, 0)
    service(8)
    make_chunk(3)
    service(9)
    finish(2)
    make_chunk(4)
    service(10)
    back_first(0, 1)
    service(11)
    back_first(2, 3)
    service(12)
    finish(3)
    make_chunk(5)
    service(13)
    back_first(4, 5)
    service(14)
    t_arrived()
    steps(6, 0)
    finish(4)
    back_first(6)
    steps(6, 1)
    back_first(7)
    steps(6, 2)
    back_first(8)
    service(15)
    t_finish()
    service(16)
    service(17)
    t_write()
    finish(5)

    def t_drain(k, carry):
        t_core(k).wait_send()
        for step in range(1, cams):
            t_peers(k, step).wait_send()
        return carry

    lax.fori_loop(0, nz, t_drain, 0)
    for step in range(1, cams):
        t_final((cam + step) % cams, cam).wait_send()
    core_copy(4).wait_send()
    core_copy(5).wait_send()
    for step in range(1, cams):
        view_copy((cam + step) % cams, cam).wait_send()


def temporal_kernel(
    traj_ref, og_ref, arr_ref, mask_ref, emb_ref, t_ref,
    out_ref, tg_ref, dviews_ref, dt_ref,
    pad_t, pad_m, pad_h, za_ref, zb_ref, sum_ref, aff_ref, ag_ref,
):
    nz, rows_t = t_ref.shape[0], t_ref.shape[3]
    cond = arr_ref.shape[1] * CH + emb_ref.shape[1]

    class Part:
        def __init__(self, ref, q, lo, wide):
            self.ref, self.q, self.lo, self.wide = ref, q, lo, wide

        def cols(self, key):
            if not isinstance(key, tuple):
                return slice(self.lo, self.lo + self.wide)
            start, stop, _ = key[1].indices(self.wide)
            return slice(self.lo + start, self.lo + stop)

        def __getitem__(self, key):
            v = self.ref[:, :, self.q, :, self.cols(key)]
            return v.reshape(2 * nz * rows_t, v.shape[-1])

        def __setitem__(self, key, v):
            self.ref[:, :, self.q, :, self.cols(key)] = v.reshape(nz, 2, rows_t, v.shape[-1])

    places = ((0, 0, PART), (1, 0, PART), (2, 0, cond), (2, cond, cond), (3, 0, CH), (3, CH, 3 * CH), (2, 2 * cond, BLK))
    wa_ref, wb_ref, f0_ref, f1_ref, ws_ref, wd_ref, ext_ref = [Part(t_ref, *place) for place in places]
    dwa_ref, dwb_ref, df0_ref, df1_ref, dws_ref, dwd_ref, dext_ref = [Part(dt_ref, *place) for place in places]
    for q, lo in ((2, 2 * cond + BLK), (3, 4 * CH)):
        dt_ref[:, :, q, :, lo:] = jnp.zeros((nz, 2, rows_t, PART - lo), bf16)
    aff_ref[...] = jnp.transpose(ext_ref[...].astype(f32))
    ag_ref[...] = jnp.zeros_like(ag_ref)
    ns = mask_ref.shape[0]
    rows = traj_ref.shape[0]
    nf = rows // ns
    edge = 2 * ns
    ones = group_ones(CH, CH // GROUPS)
    inv_n = 1.0 / (nf * (CH // GROUPS))
    aff = lambda i: aff_ref[4 + i : 5 + i, :]

    def frames(v):
        return v.reshape(nf, ns, CH)

    def fill(pad_ref, v):
        pad_ref[0:edge, :] = jnp.zeros((edge, CH), bf16)
        pad_ref[edge : edge + rows, :] = v
        pad_ref[edge + rows : edge + rows + edge, :] = jnp.zeros((edge, CH), bf16)

    def conv5(pad_ref, w_ref):
        acc = None
        for t in range(5):
            part = dot(pad_ref[t * ns : t * ns + rows, :], w_ref[:, t * CH : (t + 1) * CH], NT)
            acc = part if acc is None else acc + part
        return acc

    def conv5_back(pad_ref, w_ref):
        acc = None
        for t in range(5):
            part = dot(pad_ref[(4 - t) * ns : (4 - t) * ns + rows, :], w_ref[:, t * CH : (t + 1) * CH])
            acc = part if acc is None else acc + part
        return acc

    def norm(v):
        v = frames(v)
        mean = group_sum(jnp.sum(v, axis=0), ones) * inv_n
        centred = v - mean[None]
        rstd = lax.rsqrt(group_sum(jnp.sum(centred * centred, axis=0), ones) * inv_n + norm_eps)
        return centred * rstd[None], rstd

    def norm_back(du, z, rstd, gain):
        s0 = jnp.sum(du, axis=0)
        s1 = jnp.sum(du * z, axis=0)
        m0 = group_sum(s0 * gain, ones) * inv_n
        m1 = group_sum(s1 * gain, ones) * inv_n
        dv = (du * gain[None] - m0[None] - z * m1[None]) * rstd[None]
        return dv, jnp.sum(s1, axis=0, keepdims=True), jnp.sum(s0, axis=0, keepdims=True)

    mask = mask_ref[...]
    count = jnp.sum(mask, axis=1, keepdims=True)
    cams = arr_ref.shape[0]
    obs = arr_ref.shape[1]
    conds, slopes = [], []
    for o in range(obs):
        pooled = None
        for cam in range(cams):
            part = mask[:, cam : cam + 1] * arr_ref[cam, o].astype(f32)
            pooled = part if pooled is None else pooled + part
        value, slope = mish_pair(pooled / count)
        conds.append(value.astype(bf16))
        slopes.append(slope)
    conds.append(mish_value(emb_ref[...]).astype(bf16))
    lanes = [slice(o * CH, (o + 1) * CH) for o in range(obs)] + [slice(obs * CH, cond)]
    film = []
    for i, w_ref in ((6, f0_ref), (7, f1_ref)):
        film.append(sum(dot(v, w_ref[:, cols], NT) for v, cols in zip(conds, lanes)) + aff(i))
    scale, shift = film

    fill(pad_t, traj_ref[...])
    za, rstd_a = norm(conv5(pad_t, wa_ref) + aff(4))
    za_ref[...] = za.reshape(rows, CH)
    act_a = mish_value(za * aff(0)[None] + aff(1)[None])
    fill(pad_m, (act_a * scale[None] + shift[None]).astype(bf16).reshape(rows, CH))
    zb, rstd_b = norm(conv5(pad_m, wb_ref) + aff(5))
    zb_ref[...] = zb.reshape(rows, CH)
    skip = frames(dot(traj_ref[...], ws_ref[...], NT)) + aff(8)[None]
    summed = (mish_value(zb * aff(2)[None] + aff(3)[None]) + skip).astype(bf16)
    pairs = summed.reshape(nf // 2, 2, ns, CH)
    half = rows // 2
    sum_ref[0:ns, :] = jnp.zeros((ns, CH), bf16)
    sum_ref[ns : ns + half, :] = pairs[:, 1].reshape(half, CH)
    sum_ref[ns + half : ns + 2 * half, :] = pairs[:, 0].reshape(half, CH)
    taps = (0, ns + half, ns)
    out = None
    og = og_ref[...]
    dcols = []
    for t in range(3):
        cols = sum_ref[taps[t] : taps[t] + half, :]
        w = wd_ref[:, t * CH : (t + 1) * CH]
        part = dot(cols, w, NT)
        out = part if out is None else out + part
        dcols.append(dot(og, w).reshape(nf // 2, ns, CH))
        dwd_ref[:, t * CH : (t + 1) * CH] = dot(og, cols, TN).astype(bf16)
    out_ref[...] = (out + aff(9)).astype(bf16)
    ag_ref[9:10, :] = jnp.sum(og.astype(f32), axis=0, keepdims=True)

    before = jnp.concatenate([dcols[0][1:], jnp.zeros((1, ns, CH), f32)], axis=0)
    dsum = jnp.stack([dcols[1], dcols[2] + before], axis=1).reshape(nf, ns, CH)
    ag_ref[8:9, :] = jnp.sum(dsum, axis=(0, 1)).reshape(1, CH)
    dskip = dsum.astype(bf16).reshape(rows, CH)
    dws_ref[...] = dot(dskip, traj_ref[...], TN).astype(bf16)
    tg_ref[...] = dot(dskip, ws_ref[...])
    zb = frames(zb_ref[...])
    _, slope = mish_pair(zb * aff(2)[None] + aff(3)[None])
    dhb, ag_ref[2:3, :], ag_ref[3:4, :] = norm_back(dsum * slope, zb, rstd_b, aff(2))
    ag_ref[5:6, :] = jnp.sum(dhb, axis=(0, 1)).reshape(1, CH)
    fill(pad_h, dhb.astype(bf16).reshape(rows, CH))
    hb = pad_h[edge : edge + rows, :]
    for t in range(5):
        dwb_ref[:, t * CH : (t + 1) * CH] = dot(hb, pad_m[t * ns : t * ns + rows, :], TN).astype(bf16)
    dmid = frames(conv5_back(pad_h, wb_ref))
    za = frames(za_ref[...])
    act_a, slope = mish_pair(za * aff(0)[None] + aff(1)[None])
    dscale = jnp.sum(dmid * act_a, axis=0)
    dshift = jnp.sum(dmid, axis=0)
    dha, ag_ref[0:1, :], ag_ref[1:2, :] = norm_back(dmid * scale[None] * slope, za, rstd_a, aff(0))
    ag_ref[4:5, :] = jnp.sum(dha, axis=(0, 1)).reshape(1, CH)
    ag_ref[6:7, :] = jnp.sum(dscale, axis=0, keepdims=True)
    ag_ref[7:8, :] = jnp.sum(dshift, axis=0, keepdims=True)
    fill(pad_h, dha.astype(bf16).reshape(rows, CH))
    ha = pad_h[edge : edge + rows, :]
    for t in range(5):
        dwa_ref[:, t * CH : (t + 1) * CH] = dot(ha, pad_t[t * ns : t * ns + rows, :], TN).astype(bf16)
    tg_ref[...] = tg_ref[...] + conv5_back(pad_h, wa_ref)

    lows = (dscale.astype(bf16), dshift.astype(bf16))
    for low, dw_ref in zip(lows, (df0_ref, df1_ref)):
        for v, cols in zip(conds, lanes):
            dw_ref[:, cols] = dot(low, v, TN).astype(bf16)
    for o in range(obs):
        dcond = dot(lows[0], f0_ref[:, lanes[o]]) + dot(lows[1], f1_ref[:, lanes[o]])
        dview = dcond * slopes[o] / count
        for cam in range(cams):
            dviews_ref[cam, o] = (mask[:, cam : cam + 1] * dview).astype(bf16)
    dext_ref[...] = jnp.transpose(ag_ref[...]).astype(bf16)


def call(kernel, outs, in_specs, out_specs, scratch=(), collective_id=None, cost=None):
    extra = {} if collective_id is None else dict(collective_id=collective_id, has_side_effects=True)
    return pl.pallas_call(
        kernel,
        out_shape=[jax.ShapeDtypeStruct(s, d) for s, d in outs],
        in_specs=in_specs,
        out_specs=out_specs,
        scratch_shapes=list(scratch),
        compiler_params=pltpu.CompilerParams(vmem_limit_bytes=VMEM_BYTES, **extra),
        cost_estimate=cost,
    )


def work(microseconds):
    return pl.CostEstimate(
        flops=int(microseconds * 1e9), bytes_accessed=int(microseconds * 3e6), transcendentals=0
    )


V = pl.BlockSpec(memory_space=pltpu.VMEM)
H = pl.BlockSpec(memory_space=pl.ANY)
DMA = pltpu.SemaphoreType.DMA


def time_embed(steps_given, embed_width):
    half_width = embed_width // 2
    frequency = jnp.exp(
        jnp.arange(half_width, dtype=jnp.float32) * (-math.log(10000.0) / (half_width - 1))
    )
    argument = steps_given.astype(jnp.float32)[:, None] * frequency[None, :]
    return jnp.concatenate([jnp.sin(argument), jnp.cos(argument)], axis=1)


def adamw(weight, gradient, moment_one, moment_two, step_rate, weight_decay):
    mean_new = beta_first * moment_one + (1.0 - beta_first) * gradient
    square_new = beta_second * moment_two + (1.0 - beta_second) * gradient * gradient
    mean_hat = mean_new / (1.0 - beta_first**STEP)
    square_hat = square_new / (1.0 - beta_second**STEP)
    weight_new = weight - step_rate * (
        mean_hat / (jnp.sqrt(square_hat) + adam_eps) + weight_decay * weight
    )
    return (weight_new, mean_new, square_new)


def adam_kernel(*refs):
    for i in range(7):
        w_ref, m_ref, v_ref, g_ref = refs[4 * i : 4 * i + 4]
        outs = refs[28 + 3 * i : 31 + 3 * i]

        def update():
            vector = i in (1, 6)
            rate, decay = (rate_vector, 0.0) if vector else (rate_matrix, decay_matrix)
            new = adamw(w_ref[...], g_ref[...], m_ref[...], v_ref[...], rate, decay)
            for ref, value in zip(outs, new):
                ref[...] = value

        if i in (1, 6):
            pl.when(pl.program_id(0) == 0)(update)
        else:
            update()


def adam_call(shown, grads, rows):
    step = min(rows, 8)

    def spec(v):
        if v.shape[0] != rows:
            return pl.BlockSpec(v.shape, lambda r: (0, 0))
        return pl.BlockSpec((step,) + v.shape[1:], lambda r: (r,) + (0,) * (v.ndim - 1))

    ins = []
    for i in range(7):
        ins += [shown[0][i], shown[1][i], shown[2][i], grads[i]]
    outs = [w for w in shown[0] for _ in range(3)]
    return pl.pallas_call(
        adam_kernel,
        grid=(rows // step,),
        out_shape=[jax.ShapeDtypeStruct(v.shape, f32) for v in outs],
        in_specs=[spec(v) for v in ins],
        out_specs=[spec(v) for v in outs],
        compiler_params=pltpu.CompilerParams(vmem_limit_bytes=VMEM_BYTES),
        cost_estimate=work(12),
    )(*ins)


def shards(
    n, images, trajectory, view_mask, timesteps, out_grad,
    encoder_weight, encoder_affine, block_convs, film_weight, skip_weight, down_weight, block_affine,
    first_encoder, first_affine, first_convs, first_film, first_skip, first_down, first_block,
    second_encoder, second_affine, second_convs, second_film, second_skip, second_down, second_block,
):
    ns, nf, ch = trajectory.shape
    cams, obs = images.shape[1], images.shape[3]
    n_img = cams * images.shape[2] * obs
    nz, per = n // 2, ch // n
    cond = film_weight.shape[2]
    wide = 9 * ch
    rows = nf * ns

    ext = jnp.concatenate([encoder_affine[0], block_affine], axis=1)
    ext = jnp.pad(ext, ((0, 0), (0, BLK - ext.shape[1]))).astype(bf16)
    x = jnp.transpose(images[0], (2, 0, 1, 3, 4)).reshape(n_img, wide)
    pos = (9, n_img, ch)
    t_shape = (nz, 2, cams, per, PART)
    z1, r1, act, z2, r2, arrived, w_all, enc_aff, all_t = call(
        functools.partial(enc_fwd_kernel, n, cams),
        [(pos, f32), ((n_img, ch), f32), (pos, bf16), (pos, f32), ((n_img, ch), f32),
         ((cams, obs, ns, ch), bf16), ((2, n, per, wide + BLK), bf16), ((8, ch), f32), (t_shape, bf16)],
        [V, H, V, V, V, V, V],
        [H, V, H, H, V, V, H, V, H],
        [pltpu.VMEM((2, n, per, wide + BLK), bf16), pltpu.VMEM(pos, f32), pltpu.VMEM((n_img, wide), bf16),
         pltpu.VMEM(pos, f32), pltpu.VMEM((obs, cams, ns, ch), bf16), pltpu.VMEM((cams, obs, ns, ch), bf16),
         pltpu.VMEM(t_shape, bf16), pltpu.VMEM((2, min(per, 16), 2, wide), f32),
         DMA((2, 2, nz)), DMA((2, nz)), DMA((2, nz)), DMA((2, nz)), DMA((2, ch // BLK)), DMA((11,)),
         DMA((cams,)), DMA((cams,)),
         DMA((2, nz)), DMA((nz,)), DMA((nz, cams)), DMA((nz, cams)), DMA((cams - 1, nz)), DMA((cams - 1, nz)),
         DMA(()), DMA((max(per // 16, 1),))],
        collective_id=0,
        cost=work(90),
    )(x, encoder_weight[0], block_convs, film_weight, skip_weight, down_weight, ext)

    present = view_mask.astype(f32)
    embedded = time_embed(timesteps, TEMB)
    traj_fm = jnp.transpose(trajectory, (1, 0, 2)).reshape(rows, ch)
    og_fm = jnp.transpose(out_grad, (1, 0, 2)).reshape(rows // 2, ch)
    out_fm, tg_fm, dviews, dt = call(
        temporal_kernel,
        [((rows // 2, ch), bf16), ((rows, ch), f32), ((cams, obs, ns, ch), bf16), (all_t.shape, bf16)],
        [V] * 6,
        [V] * 4,
        [pltpu.VMEM((rows + 4 * ns, ch), bf16)] * 3
        + [pltpu.VMEM((rows, ch), f32)] * 2
        + [pltpu.VMEM((rows + ns, ch), bf16)]
        + [pltpu.VMEM((BLK, ch), f32)] * 2,
        cost=work(20),
    )(traj_fm, og_fm, arrived, present, embedded, all_t)
    block_output = jnp.transpose(out_fm.reshape(nf // 2, ns, ch), (1, 0, 2))
    trajectory_grad = jnp.transpose(tg_fm.reshape(nf, ns, ch), (1, 0, 2))

    chunk = 3 * ch + BLK
    ig, genc, gaff, gconvs, gfilm, gskip, gdown, gblk = call(
        functools.partial(enc_bwd_kernel, n, cams, cond),
        [(pos, f32), ((per, 2, wide), f32), ((4, per), f32), ((per, 2, 5 * ch), f32),
         ((per, 2, cond), f32), ((per, ch), f32), ((per, 3 * ch), f32), ((10, per), f32)],
        [H, H, H, H, V, H, V, V, V, H],
        [V] * 8,
        [pltpu.VMEM(pos, bf16), pltpu.VMEM(pos, bf16), pltpu.VMEM((n, per, wide), bf16), pltpu.VMEM(pos, f32),
         pltpu.VMEM(pos, f32), pltpu.VMEM(pos, bf16), pltpu.VMEM((ch, 9 * n_img), bf16),
         pltpu.VMEM((BLK, ch), f32), pltpu.VMEM((obs, cams, ns, ch), bf16),
         pltpu.VMEM((2, nz, per, chunk), f32), pltpu.VMEM((2, nz, per, chunk), bf16),
         pltpu.VMEM((3, nz, per, chunk), bf16), pltpu.VMEM((3, 2, nz, per, chunk), bf16),
         pltpu.VMEM((2, per, PART), bf16), pltpu.VMEM((nz, cams, per, PART), bf16),
         pltpu.VMEM((cams - 1, nz, per, PART), bf16), pltpu.VMEM((2, nz, per, PART), bf16),
         pltpu.VMEM((cams, per, PART), bf16),
         DMA((13,)), DMA((6,)), DMA((6,)), DMA((6, 2, nz)), DMA((6, 2, nz)), DMA((cams,)), DMA((cams,)),
         DMA((nz * cams,)), DMA((nz,)), DMA((nz,)), DMA((cams - 1, nz)), DMA((cams - 1, nz)),
         DMA((2, nz)), DMA((2, nz)), DMA((cams,)), DMA((cams,))],
        collective_id=1,
        cost=work(100),
    )(x, act, w_all, z1, r1, z2, r2, enc_aff, dviews, dt)
    images_grad = jnp.transpose(ig.reshape((9, obs) + images.shape[1:3] + (ch,)), (2, 3, 1, 0, 4))[None]

    def turned(v):
        return jnp.transpose(v.reshape(v.shape[-2:]))

    weights = (encoder_weight, encoder_affine, block_convs, film_weight, skip_weight, down_weight, block_affine)
    firsts = (first_encoder, first_affine, first_convs, first_film, first_skip, first_down, first_block)
    seconds = (second_encoder, second_affine, second_convs, second_film, second_skip, second_down, second_block)
    shown = [
        [turned(v) if i in (1, 6) else v.reshape(v.shape[-3:]) if i == 0 else v for i, v in enumerate(group)]
        for group in (weights, firsts, seconds)
    ]
    news = adam_call(shown, (genc, gaff, gconvs, gfilm, gskip, gdown, gblk), per)
    upd = [
        tuple((turned(v) if i in (1, 6) else v).reshape(w.shape) for v in news[3 * i : 3 * i + 3])
        for i, w in enumerate(weights)
    ]
    return (
        (block_output, trajectory_grad, images_grad)
        + tuple(u[0] for u in upd)
        + tuple(u[1] for u in upd)
        + tuple(u[2] for u in upd)
    )


def solution(mesh):
    sample = P(("cam", "batch"))
    params = (P("cam", "batch"), P("cam", "batch")) + (P("batch"),) * 5
    images_spec = P("cam", None, "batch")
    return jax.shard_map(
        functools.partial(shards, mesh.shape["batch"]),
        mesh=mesh,
        in_specs=(images_spec, sample, sample, sample, sample) + params * 3,
        out_specs=(sample, sample, images_spec) + params * 3,
        check_vma=False,
    )
```

```python
import functools
import math

import jax
import jax.numpy as jnp
from jax import lax
from jax.experimental import pallas as pl
from jax.experimental.pallas import tpu as pltpu
from jax.sharding import PartitionSpec as P

TEMB = 128
GROUPS = 8
STEP = 5

norm_eps = 1e-05
beta_first = 0.5
beta_second = 0.5
adam_eps = 1e-08
rate_matrix = 0.02
rate_vector = 0.2
decay_matrix = 0.01

CH = 512
BLK = 128
ENC_GROUP = 16
f32 = jnp.float32
bf16 = jnp.bfloat16
VMEM_BYTES = 61 * 1024 * 1024

NT = (((1,), (1,)), ((), ()))
NN = (((1,), (0,)), ((), ()))
TN = (((0,), (0,)), ((), ()))


def dot(a, b, dims=NN):
    return lax.dot_general(a, b, dims, preferred_element_type=f32)


def group_ones(width, group):
    rows = lax.broadcasted_iota(jnp.int32, (width, width), 0) // group
    cols = lax.broadcasted_iota(jnp.int32, (width, width), 1) // group
    return jnp.where(rows == cols, 1.0, 0.0).astype(bf16)


def group_sum(v, ones):
    high = v.astype(bf16)
    rest = v - high.astype(f32)
    middle = rest.astype(bf16)
    low = (rest - middle.astype(f32)).astype(bf16)
    return dot(high, ones) + dot(middle, ones) + dot(low, ones)


def sigmoid(v):
    return 1.0 / (1.0 + jnp.exp(-v))


def mish_pair(v):
    e = jnp.exp(jnp.minimum(v, 20.0))
    n = e * (e + 2.0)
    inv = 1.0 / (n + 2.0)
    t = n * inv
    return v * t, t + v * (4.0 * e * (1.0 + e)) * inv * inv


def mish_value(v):
    e = jnp.exp(jnp.minimum(v, 20.0))
    n = e * (e + 2.0)
    return v * (n / (n + 2.0))


def span(i):
    return range(max(0, 1 - i), min(2, 3 - i) + 1)


MESH = pl.DeviceIdType.MESH


def batch_copy(src, dst, send_sem, recv_sem, target):
    return pltpu.make_async_remote_copy(
        src_ref=src, dst_ref=dst, send_sem=send_sem, recv_sem=recv_sem,
        device_id={"batch": target}, device_id_type=MESH,
    )


def cam_copy(src, dst, send_sem, recv_sem, target):
    return pltpu.make_async_remote_copy(
        src_ref=src, dst_ref=dst, send_sem=send_sem, recv_sem=recv_sem,
        device_id={"cam": target}, device_id_type=MESH,
    )


def line_barrier(cams, nz):
    me, cam = lax.axis_index("batch"), lax.axis_index("cam")
    zi, core = me // 2, me % 2
    barrier = pltpu.get_barrier_semaphore()
    pl.semaphore_signal(barrier, inc=1, device_id={"batch": me + 1 - 2 * core}, device_id_type=MESH)
    for step in range(1, cams):
        pl.semaphore_signal(barrier, inc=1, device_id={"cam": (cam + step) % cams}, device_id_type=MESH)

    @pl.when(zi > 0)
    def _():
        pl.semaphore_signal(barrier, inc=1, device_id={"batch": me - 2}, device_id_type=MESH)

    @pl.when(zi < nz - 1)
    def _():
        pl.semaphore_signal(barrier, inc=1, device_id={"batch": me + 2}, device_id_type=MESH)

    ends = (zi == 0).astype(jnp.int32) + (zi == nz - 1).astype(jnp.int32)
    pl.semaphore_wait(barrier, cams + 2 - ends)


PART = 5 * CH


def pack_temporal(ref, convs_ref, film_ref, skip_ref, down_ref, ext_ref):
    rows, cond = film_ref.shape[0], film_ref.shape[2]
    for q in range(2):
        ref[q] = convs_ref[:, q, :].astype(bf16)
        ref[2, :, q * cond : (q + 1) * cond] = film_ref[:, q, :].astype(bf16)
    ref[2, :, 2 * cond : 2 * cond + BLK] = ext_ref[...]
    ref[2, :, 2 * cond + BLK :] = jnp.zeros((rows, PART - 2 * cond - BLK), bf16)
    ref[3, :, 0:CH] = skip_ref[...].astype(bf16)
    ref[3, :, CH : 4 * CH] = down_ref[...].astype(bf16)
    ref[3, :, 4 * CH :] = jnp.zeros((rows, PART - 4 * CH), bf16)


def enc_fwd_kernel(
    n, cams, img_ref, enc_hbm, convs_ref, film_ref, skip_ref, down_ref, ext_ref,
    z1_out, r1_ref, a_out, z2_out, r2_ref, arr_ref, w_out, aff_ref, t_out, x_out,
    x_ref, w_ref, z1_ref, a_ref, z2_ref, feat_ref, arr_s, t_ref, enc_buf,
    zsend, zrecv, csend, crecv, wsem, osem, fsend, frecv,
    tzsend, tzrecv, tcsend, tcrecv, tpsend, tprecv, tsem, esem, xsem,
):
    nz = n // 2
    rows = ext_ref.shape[0]
    piece = enc_buf.shape[1]
    spb = BLK // rows
    n_img = x_ref.shape[0]
    me, cam = lax.axis_index("batch"), lax.axis_index("cam")
    zi, core = me // 2, me % 2
    partner = me + 1 - 2 * core
    ones = group_ones(BLK, ENC_GROUP)
    inv_n = 1.0 / (9 * ENC_GROUP)

    def enc_load(i):
        return pltpu.make_async_copy(enc_hbm.at[pl.ds(i * piece, piece)], enc_buf.at[i % 2], esem.at[i])

    enc_load(0).start()
    pack_temporal(t_ref.at[zi, core], convs_ref, film_ref, skip_ref, down_ref, ext_ref)

    line_barrier(cams, nz)

    def tz_copy(k, way):
        ref = t_ref.at[k, core, cam]
        return batch_copy(ref, ref, tzsend.at[way, k], tzrecv.at[k], me - 2 + 4 * way)

    def tc_copy(k, which, q):
        ref = t_ref.at[k, which, q]
        return batch_copy(ref, ref, tcsend.at[k, q], tcrecv.at[k, q], partner)

    def tp_copy(k, step, q):
        ref = t_ref.at[k, core, q]
        return cam_copy(ref, ref, tpsend.at[step - 1, k], tprecv.at[step - 1, k], (cam + step) % cams)

    def t_send(s):
        for k, _, passed, way in moves(s):
            @pl.when(passed)
            def _():
                tz_copy(k, way).start()

    def t_receive(s):
        for k, held, _, way in moves(s):
            @pl.when(held)
            def _():
                tz_copy(k, way).wait_recv()
                for step in range(1, cams):
                    tp_copy(k, step, cam).start()
                tc_copy(k, core, cam).start()

    def t_collect(d):
        for k, held, _, _ in moves(d):
            @pl.when(held & (d > 0))
            def _():
                for step in range(1, cams):
                    q = (cam + cams - step) % cams
                    tp_copy(k, step, q).wait_recv()
                    tc_copy(k, core, q).start()

    def t_save():
        return pltpu.make_async_copy(t_ref, t_out, tsem)

    def t_complete():
        def body(k, carry):
            for q in range(cams):
                tc_copy(k, 1 - core, q).wait_recv()
            return carry

        lax.fori_loop(0, nz, body, 0)
        t_save().start()

    def z_copy(conv, k, way):
        ref = w_ref.at[conv, 2 * k + core]
        return batch_copy(ref, ref, zsend.at[conv, way, k], zrecv.at[conv, k], me - 2 + 4 * way)

    def core_copy(conv, k, which):
        ref = w_ref.at[conv, 2 * k + which]
        return batch_copy(ref, ref, csend.at[conv, k], crecv.at[conv, k], partner)

    def moves(s):
        low, high = zi - s, zi + s
        return (
            (high, high < nz, (high < nz) & (zi > 0), 0),
            (low, low >= 0, (low >= 0) & (zi < nz - 1), 1),
        )

    def send(conv, s):
        for k, _, passed, way in moves(s):
            @pl.when(passed)
            def _():
                z_copy(conv, k, way).start()

    def receive(conv, s):
        for k, held, _, way in moves(s):
            @pl.when(held)
            def _():
                z_copy(conv, k, way).wait_recv()
                core_copy(conv, k, core).start()

    t_send(0)
    for q in range(cams):
        tc_copy(zi, core, q).start()
    for conv in range(2):
        w_ref[conv, me, :, 9 * CH :] = ext_ref[...]
    count = rows // piece

    def pack(i, carry):
        @pl.when(i + 1 < count)
        def _():
            enc_load(i + 1).start()

        enc_load(i).wait()
        for conv in range(2):
            w_ref[conv, me, pl.ds(pl.multiple_of(i * piece, piece), piece), 0 : 9 * CH] = (
                enc_buf[i % 2, :, conv, :].astype(bf16)
            )
        return carry

    lax.fori_loop(0, count, pack, 0)

    def x_save(p):
        return pltpu.make_async_copy(x_ref.at[:, p * CH : (p + 1) * CH], x_out.at[p], xsem.at[p])

    half = n_img // 2
    for p in range(9):
        pair = img_ref[:, p].astype(f32)
        for o in range(2):
            x_ref[o * half : (o + 1) * half, p * CH : (p + 1) * CH] = pair[:, o].astype(bf16)
        x_save(p).start()
    for conv in range(2):
        core_copy(conv, zi, core).start()

    def t_step(s, carry):
        @pl.when(s == nz - 1)
        def _():
            send(0, 0)

        t_receive(s)

        @pl.when(s < nz - 1)
        def _():
            t_send(s)
        return carry

    lax.fori_loop(1, nz, t_step, 0)

    def rows_of(conv, j, start, wide):
        block = w_ref[conv, pl.ds(j * spb, spb), :, start : start + wide]
        return block.reshape(BLK, wide)

    def w_save(conv, j):
        part = pl.ds(j * spb, spb)
        return pltpu.make_async_copy(w_ref.at[conv, part], w_out.at[conv, part], wsem.at[conv, j])

    def conv_norm(src_ref, conv, z_ref, r_ref, j):
        lanes = pl.ds(pl.multiple_of(j * BLK, BLK), BLK)
        total = None
        for p in range(9):
            r, c = divmod(p, 3)
            bs = span(c)
            acc = None
            for a in span(r):
                start = (3 * (r + a - 1) + c + bs[0] - 1) * CH
                wide = len(bs) * CH
                part = dot(src_ref[:, start : start + wide], rows_of(conv, j, (3 * a + bs[0]) * CH, wide), NT)
                acc = part if acc is None else acc + part
            z_ref[p, :, lanes] = acc
            total = acc if total is None else total + acc
        mean = group_sum(total, ones) * inv_n
        var = None
        for p in range(9):
            centred = z_ref[p, :, lanes] - mean
            sq = centred * centred
            var = sq if var is None else var + sq
        rstd = lax.rsqrt(group_sum(var, ones) * inv_n + norm_eps)
        r_ref[:, lanes] = rstd
        return lanes, mean, rstd

    def first(j):
        aff_ref[:, lanes_of(j)] = jnp.transpose(rows_of(0, j, 9 * CH, BLK).astype(f32))[0:8]
        lanes, mean, rstd = conv_norm(x_ref, 0, z1_ref, r1_ref, j)
        gain, offset = aff_ref[0:1, lanes], aff_ref[1:2, lanes]
        for p in range(9):
            z = (z1_ref[p, :, lanes] - mean) * rstd
            z1_ref[p, :, lanes] = z
            u = z * gain + offset
            a_ref[:, pl.ds(pl.multiple_of(p * CH + j * BLK, BLK), BLK)] = (u * sigmoid(u)).astype(bf16)

    def second(j):
        lanes, mean, rstd = conv_norm(a_ref, 1, z2_ref, r2_ref, j)
        gain, offset = aff_ref[2:3, lanes], aff_ref[3:4, lanes]
        total = None
        for p in range(9):
            z = (z2_ref[p, :, lanes] - mean) * rstd
            z2_ref[p, :, lanes] = z
            pic = x_ref[:, pl.ds(pl.multiple_of(p * CH + j * BLK, BLK), BLK)].astype(f32)
            u = z * gain + offset + pic
            act = u * sigmoid(u)
            total = act if total is None else total + act
        out = (total * (1.0 / 9.0)).astype(bf16)
        feat_ref[:, :, :, lanes] = out.reshape(feat_ref.shape[:3] + (BLK,))

    def lanes_of(j):
        return pl.ds(pl.multiple_of(j * BLK, BLK), BLK)

    def arrived(conv, k):
        core_copy(conv, k, 1 - core).wait_recv()

    def phase(conv, block):
        streaming = spb == 2

        def step(s, carry):
            if conv == 0:
                @pl.when((s > 0) & (s < nz - 1))
                def _():
                    send(0, s)

                @pl.when(s == nz - 1)
                def _():
                    send(1, 0)
            else:
                @pl.when((s > 0) & (s < nz - 1))
                def _():
                    send(1, s)

            def side(d, carry):
                k = zi + s - 2 * s * d

                @pl.when((k >= 0) & (k < nz) & (s + 1 > d))
                def _():
                    arrived(conv, k)
                    if streaming:
                        w_save(conv, k).start()
                        block(k)
                return carry

            lax.fori_loop(0, 2, side, 0)
            if conv == 1:
                t_collect(2 * s)
                t_collect(2 * s + 1)
                pl.when(s == nz - 2)(t_complete)

            @pl.when(s < nz - 1)
            def _():
                receive(conv, s + 1)
            return carry

        lax.fori_loop(0, nz, step, 0)
        if not streaming:
            def rest(j, carry):
                w_save(conv, j).start()
                block(j)
                return carry

            lax.fori_loop(0, CH // BLK, rest, 0)

    phase(0, first)
    saves = [pltpu.make_async_copy(z1_ref, z1_out, osem.at[0])]
    saves += [
        pltpu.make_async_copy(a_ref.at[:, p * CH : (p + 1) * CH], a_out.at[p], osem.at[2 + p])
        for p in range(9)
    ]
    for save in saves:
        save.start()
    phase(1, second)
    last = pltpu.make_async_copy(z2_ref, z2_out, osem.at[1])
    last.start()

    def feat_copy(to, sender):
        return cam_copy(feat_ref.at[:, to], arr_s.at[sender], fsend.at[to], frecv.at[sender], to)

    for step in range(1, cams):
        feat_copy((cam + step) % cams, cam).start()
    arr_s[cam] = feat_ref[:, cam]
    for step in range(1, cams):
        other = (cam + step) % cams
        feat_copy(other, other).wait_recv()
    arr_ref[...] = arr_s[...]
    for step in range(1, cams):
        feat_copy((cam + step) % cams, cam).wait_send()

    for conv in range(2):
        def drain(k, carry):
            s = k - zi

            @pl.when((s >= 0) & (s < nz - 1) & (zi > 0))
            def _():
                z_copy(conv, k, 0).wait_send()

            @pl.when((s <= 0) & (s > 1 - nz) & (zi < nz - 1))
            def _():
                z_copy(conv, k, 1).wait_send()

            core_copy(conv, k, core).wait_send()
            return carry

        lax.fori_loop(0, nz, drain, 0)

        def saved(j, carry):
            w_save(conv, j).wait()
            return carry

        lax.fori_loop(0, CH // BLK, saved, 0)
    for save in saves:
        save.wait()
    last.wait()

    def t_drain(k, carry):
        s = k - zi

        @pl.when((s >= 0) & (s < nz - 1) & (zi > 0))
        def _():
            tz_copy(k, 0).wait_send()

        @pl.when((s <= 0) & (s > 1 - nz) & (zi < nz - 1))
        def _():
            tz_copy(k, 1).wait_send()

        @pl.when(s != 0)
        def _():
            for step in range(1, cams):
                tp_copy(k, step, cam).wait_send()

        for q in range(cams):
            tc_copy(k, core, q).wait_send()
        return carry

    lax.fori_loop(0, nz, t_drain, 0)
    t_save().wait()
    for p in range(9):
        x_save(p).wait()


def enc_bwd_kernel(
    n, cams, cond, x_hbm, a_hbm, w_hbm, z1_hbm, r1_ref, z2_hbm, r2_ref, aff_ref, dviews_ref, dt_hbm,
    ig_ref, genc_ref, gaff_ref, gconvs_ref, gfilm_ref, gskip_ref, gdown_ref, gblk_ref,
    x_ref, a_ref, w_ref, z1_ref, z2_ref, g_ref, gt_ref, ag_ref, gp_ref,
    dwf, core_out, core_in, slots, t_own, t_sum, t_peer, t_slots, t_all,
    lsem, csend, crecv, zsend, zrecv, fsend, frecv,
    tlsem, tcsend, tcrecv, tpsend, tprecv, tzsend, tzrecv, tfsend, tfrecv,
):
    nz = n // 2
    rows = CH // n
    n_img = z1_ref.shape[1]
    me, cam = lax.axis_index("batch"), lax.axis_index("cam")
    zi, core = me // 2, me % 2
    partner = me + 1 - 2 * core
    ones = group_ones(BLK, ENC_GROUP)
    inv_n = 1.0 / (9 * ENC_GROUP)
    chunk = 3 * CH

    def load_w(conv):
        return pltpu.make_async_copy(w_hbm.at[conv, :, :, 0 : 9 * CH], w_ref, lsem.at[3])

    loads = {
        "z2": pltpu.make_async_copy(z2_hbm, z2_ref, lsem.at[0]),
        "z1": pltpu.make_async_copy(z1_hbm, z1_ref, lsem.at[1]),
        "a": pltpu.make_async_copy(a_hbm, a_ref, lsem.at[2]),
    }
    x_loads = [pltpu.make_async_copy(x_hbm, x_ref, lsem.at[4])]
    loads["z2"].start()
    for load in x_loads:
        load.start()
    loads["a"].start()
    load_w(1).start()
    loads["z1"].start()

    def own_load(i):
        return pltpu.make_async_copy(dt_hbm.at[i // cams, core, i % cams], t_own.at[i % 2], tlsem.at[i])

    own_load(0).start()

    line_barrier(cams, nz)

    def view_copy(to, sender):
        return cam_copy(dviews_ref.at[to], gp_ref.at[:, sender], fsend.at[to], frecv.at[sender], to)

    for step in range(1, cams):
        view_copy((cam + step) % cams, cam).start()

    def t_core(k):
        return batch_copy(dt_hbm.at[k, 1 - core], t_sum.at[k], tcsend.at[k], tcrecv.at[k], partner)

    def t_peers(k, step):
        to = (cam + step) % cams
        return cam_copy(t_sum.at[k, to], t_peer.at[step - 1, k], tpsend.at[step - 1, k], tprecv.at[step - 1, k], to)

    def t_start(k, carry):
        t_core(k).start()
        return carry

    lax.fori_loop(0, nz, t_start, 0)

    def t_spread(lo, hi):
        def body(k, carry):
            t_core(k).wait_recv()

            def quarter(q, carry):
                i = k * cams + q

                @pl.when(i + 1 < nz * cams)
                def _():
                    own_load(i + 1).start()

                own_load(i).wait()
                t_sum[k, q] = (t_sum[k, q].astype(f32) + t_own[i % 2].astype(f32)).astype(bf16)
                return carry

            lax.fori_loop(0, cams, quarter, 0)
            for step in range(1, cams):
                t_peers(k, step).start()
            return carry

        lax.fori_loop(lo, hi, body, 0)

    gp_ref[:, cam] = dviews_ref[cam]
    ag_ref[...] = jnp.zeros_like(ag_ref)
    for step in range(1, cams):
        other = (cam + step) % cams
        view_copy(other, other).wait_recv()
    for load in x_loads:
        load.wait()
    loads["z2"].wait()

    def lanes_of(j):
        return pl.ds(pl.multiple_of(j * BLK, BLK), BLK)

    def norm_back(du_ref, z_ref, r_ref, j, gain, row):
        lanes = lanes_of(j)
        s0 = jnp.zeros((n_img, BLK), f32)
        s1 = jnp.zeros((n_img, BLK), f32)
        for p in range(9):
            du = du_ref[p, :, lanes]
            s0 = s0 + du
            s1 = s1 + du * z_ref[p, :, lanes]
        ag_ref[row : row + 1, lanes] = jnp.sum(s1, axis=0, keepdims=True)
        ag_ref[row + 1 : row + 2, lanes] = jnp.sum(s0, axis=0, keepdims=True)
        m0 = group_sum(s0 * gain, ones) * inv_n
        m1 = group_sum(s1 * gain, ones) * inv_n
        rstd = r_ref[:, lanes]
        for p in range(9):
            dv = (du_ref[p, :, lanes] * gain - m0 - z_ref[p, :, lanes] * m1) * rstd
            g_ref[p, :, lanes] = dv.astype(bf16)
            gt_ref[lanes, p * n_img : (p + 1) * n_img] = jnp.transpose(dv).astype(bf16)

    def second(j, carry):
        lanes = lanes_of(j)
        gain, offset = aff_ref[2:3, lanes], aff_ref[3:4, lanes]
        pooled = gp_ref[:, :, :, lanes].reshape(n_img, BLK).astype(f32) * (1.0 / 9.0)
        for p in range(9):
            u = z2_ref[p, :, lanes] * gain + offset + x_ref[p, :, lanes].astype(f32)
            s = sigmoid(u)
            ig_ref[p, :, lanes] = pooled * (s * (1.0 + u * (1.0 - s)))
        norm_back(ig_ref, z2_ref, r2_ref, j, gain, 2)
        return carry

    def first(j, carry):
        lanes = lanes_of(j)
        gain, offset = aff_ref[0:1, lanes], aff_ref[1:2, lanes]
        for p in range(9):
            u = z1_ref[p, :, lanes] * gain + offset
            s = sigmoid(u)
            z2_ref[p, :, lanes] = z2_ref[p, :, lanes] * (s * (1.0 + u * (1.0 - s)))
        norm_back(z2_ref, z1_ref, r1_ref, j, gain, 0)
        return carry

    def width(k):
        return chunk + BLK if k == 5 else chunk

    def core_copy(k):
        cols = pl.ds(0, width(k))
        return batch_copy(
            core_out.at[k % 2, :, :, cols], core_in.at[k % 3, :, :, cols], csend.at[k], crecv.at[k], partner
        )

    def keep(k, d0, lane, v):
        count, wide = v.shape[0] // (2 * rows), v.shape[1]
        parts = v.reshape(count, 2, rows, wide)
        even, odd = parts[:, 0], parts[:, 1]
        dwf[k % 2, d0 : d0 + count, :, lane : lane + wide] = jnp.where(core == 0, even, odd)
        core_out[k % 2, d0 : d0 + count, :, lane : lane + wide] = jnp.where(core == 0, odd, even).astype(bf16)

    def make_chunk(k):
        if k >= 2:
            core_copy(k - 2).wait_send()
        src_ref = a_ref if k < 3 else x_ref
        a = k % 3
        r_lo, r_hi = max(0, 1 - a), min(2, 3 - a)
        for b in range(3):
            c_lo, c_hi = max(0, 1 - b), min(2, 3 - b)
            if b == 1:
                runs = [(3 * r_lo, 3 * (r_hi - r_lo + 1))]
            else:
                runs = [(3 * r + c_lo, c_hi - c_lo + 1) for r in range(r_lo, r_hi + 1)]
            shift = 3 * (a - 1) + b - 1
            for half in range(2):
                acc = None
                for p, m in runs:
                    part = dot(
                        gt_ref[half * 256 : half * 256 + 256, p * n_img : (p + m) * n_img],
                        src_ref[p + shift : p + shift + m].reshape(m * n_img, CH),
                    )
                    acc = part if acc is None else acc + part
                keep(k, half * nz // 2, b * CH, acc)
        if k == 5:
            keep(k, 0, chunk, jnp.transpose(ag_ref[...]))
        core_copy(k).start()

    def term(k, d):
        return dwf[k % 2, d, :, 0 : width(k)] + core_in[k % 3, d, :, 0 : width(k)].astype(f32)

    def line_copy(k, way, s):
        if k == 6:
            return batch_copy(
                t_slots.at[way, s - 1], t_slots.at[way, s], tzsend.at[way, s], tzrecv.at[way, s], me - 2 + 4 * way
            )
        cols = pl.ds(0, width(k))
        return batch_copy(
            slots.at[k % 3, way, s - 1, :, cols], slots.at[k % 3, way, s, :, cols],
            zsend.at[k, way, s], zrecv.at[k, way, s], me - 2 + 4 * way,
        )

    def slot(k, way, s):
        return t_slots.at[way, s] if k == 6 else slots.at[k % 3, way, s, :, pl.ds(0, width(k))]

    def t_term(d):
        total = t_sum[d, cam].astype(f32)
        for step in range(1, cams):
            total = total + t_peer[step - 1, d].astype(f32)
        return total

    def serve(k, s):
        for way in range(2):
            ahead = zi if way else nz - 1 - zi
            d = nz - s + zi if way else s - nz + zi
            ref = slot(k, way, s - 1)

            @pl.when((ahead < nz - 1) & (s > ahead))
            def _():
                own = t_term(d) if k == 6 else term(k, d)

                @pl.when(ahead > 0)
                def _():
                    line_copy(k, way, s - 1).wait_recv()
                    ref[...] = (ref[...].astype(f32) + own).astype(bf16)

                @pl.when(ahead == 0)
                def _():
                    ref[...] = own.astype(bf16)

                line_copy(k, way, s).start()

    def steps(k, part):
        lo, hi = 1 + part * (nz - 1) // 3, 1 + (part + 1) * (nz - 1) // 3
        if hi - lo == 1:
            serve(k, lo)
        elif hi > lo:
            def body(s, carry):
                serve(k, s)
                return carry

            lax.fori_loop(lo, hi, body, 0)

    def service(g):
        k, part = divmod(g, 3)
        if part == 0:
            core_copy(k).wait_recv()
        steps(k, part)

    def collect(k, total, write):
        last = nz - 1

        @pl.when(zi > 0)
        def _():
            line_copy(k, 1, last).wait_recv()

        @pl.when(zi < nz - 1)
        def _():
            line_copy(k, 0, last).wait_recv()

        @pl.when(zi == 0)
        def _():
            write(total + slot(k, 0, last)[...].astype(f32))

        @pl.when(zi == nz - 1)
        def _():
            write(total + slot(k, 1, last)[...].astype(f32))

        @pl.when((zi > 0) & (zi < nz - 1))
        def _():
            write(total + slot(k, 0, last)[...].astype(f32) + slot(k, 1, last)[...].astype(f32))

        def drain(s, carry):
            for way in range(2):
                ahead = zi if way else nz - 1 - zi

                @pl.when((ahead < nz - 1) & (s > ahead))
                def _():
                    line_copy(k, way, s).wait_send()
            return carry

        lax.fori_loop(1, nz, drain, 0)

    def finish(k):
        def write(v):
            genc_ref[1 - k // 3, :, (k % 3) * chunk : (k % 3 + 1) * chunk] = v[:, 0:chunk]
            if k == 5:
                gaff_ref[...] = jnp.transpose(v[:, chunk:])[0 : gaff_ref.shape[0]]

        collect(k, term(k, zi), write)

    def t_arrived():
        for step in range(1, cams):
            def body(k, carry):
                t_peers(k, step).wait_recv()
                return carry

            lax.fori_loop(0, nz, body, 0)

    def t_final(to, sender):
        return cam_copy(t_all.at[cam], t_all.at[sender], tfsend.at[to], tfrecv.at[sender], to)

    def t_finish():
        def write(v):
            t_all[cam] = v.astype(bf16)

        collect(6, t_term(zi), write)
        for step in range(1, cams):
            t_final((cam + step) % cams, cam).start()

    def t_write():
        for step in range(1, cams):
            other = (cam + step) % cams
            t_final(other, other).wait_recv()

        def cut(q, lo, wide):
            return t_all[q, :, lo : lo + wide].astype(f32)

        for which in range(2):
            gconvs_ref[which] = cut(which, 0, PART)
            gfilm_ref[which] = cut(2, which * cond, cond)
        gblk_ref[...] = jnp.transpose(cut(2, 2 * cond, BLK))[0 : gblk_ref.shape[0]]
        gskip_ref[...] = cut(3, 0, CH)
        gdown_ref[...] = cut(3, CH, 3 * CH)

    def input_back(q):
        r, c = divmod(q, 3)
        acc = None
        for a in range(3):
            for b in range(3):
                pr, pc = r - a + 1, c - b + 1
                if 0 <= pr < 3 and 0 <= pc < 3:
                    t = 3 * a + b
                    w = w_ref[:, :, t * CH : (t + 1) * CH].reshape(CH, CH)
                    part = dot(g_ref[3 * pr + pc], w)
                    acc = part if acc is None else acc + part
        return acc

    def back_second(*qs):
        for q in qs:
            if q == 0:
                load_w(1).wait()
            z2_ref[q] = input_back(q)
            if q == 8:
                load_w(0).start()

    def back_first(*qs):
        for q in qs:
            if q == 0:
                load_w(0).wait()
            ig_ref[q] = ig_ref[q] + input_back(q)

    lax.fori_loop(0, CH // BLK, second, 0)
    loads["a"].wait()
    make_chunk(0)
    service(0)
    t_spread(0, nz // 2)
    make_chunk(1)
    service(1)
    t_spread(nz // 2, nz)
    back_second(0, 1, 2)
    service(2)
    back_second(3, 4)
    service(3)
    finish(0)
    make_chunk(2)
    service(4)
    back_second(5, 6)
    service(5)
    back_second(7, 8)
    service(6)
    finish(1)
    loads["z1"].wait()
    lax.fori_loop(0, 2, first, 0)
    service(7)
    lax.fori_loop(2, 4, first, 0)
    service(8)
    make_chunk(3)
    service(9)
    finish(2)
    make_chunk(4)
    service(10)
    back_first(0, 1)
    service(11)
    back_first(2, 3)
    service(12)
    finish(3)
    make_chunk(5)
    service(13)
    back_first(4, 5)
    service(14)
    t_arrived()
    steps(6, 0)
    finish(4)
    back_first(6)
    steps(6, 1)
    back_first(7)
    steps(6, 2)
    back_first(8)
    service(15)
    t_finish()
    service(16)
    service(17)
    t_write()
    finish(5)

    def t_drain(k, carry):
        t_core(k).wait_send()
        for step in range(1, cams):
            t_peers(k, step).wait_send()
        return carry

    lax.fori_loop(0, nz, t_drain, 0)
    for step in range(1, cams):
        t_final((cam + step) % cams, cam).wait_send()
    core_copy(4).wait_send()
    core_copy(5).wait_send()
    for step in range(1, cams):
        view_copy((cam + step) % cams, cam).wait_send()


def temporal_kernel(
    traj_ref, og_ref, arr_ref, mask_ref, emb_ref, t_ref,
    out_ref, tg_ref, dviews_ref, dt_ref,
    pad_t, pad_m, pad_h, za_ref, zb_ref, sum_ref, aff_ref, ag_ref,
):
    nz, rows_t = t_ref.shape[0], t_ref.shape[3]
    cond = arr_ref.shape[1] * CH + emb_ref.shape[1]

    class Part:
        def __init__(self, ref, q, lo, wide):
            self.ref, self.q, self.lo, self.wide = ref, q, lo, wide

        def cols(self, key):
            if not isinstance(key, tuple):
                return slice(self.lo, self.lo + self.wide)
            start, stop, _ = key[1].indices(self.wide)
            return slice(self.lo + start, self.lo + stop)

        def __getitem__(self, key):
            v = self.ref[:, :, self.q, :, self.cols(key)]
            return v.reshape(2 * nz * rows_t, v.shape[-1])

        def __setitem__(self, key, v):
            self.ref[:, :, self.q, :, self.cols(key)] = v.reshape(nz, 2, rows_t, v.shape[-1])

    places = ((0, 0, PART), (1, 0, PART), (2, 0, cond), (2, cond, cond), (3, 0, CH), (3, CH, 3 * CH), (2, 2 * cond, BLK))
    wa_ref, wb_ref, f0_ref, f1_ref, ws_ref, wd_ref, ext_ref = [Part(t_ref, *place) for place in places]
    dwa_ref, dwb_ref, df0_ref, df1_ref, dws_ref, dwd_ref, dext_ref = [Part(dt_ref, *place) for place in places]
    for q, lo in ((2, 2 * cond + BLK), (3, 4 * CH)):
        dt_ref[:, :, q, :, lo:] = jnp.zeros((nz, 2, rows_t, PART - lo), bf16)
    aff_ref[...] = jnp.transpose(ext_ref[...].astype(f32))
    ag_ref[...] = jnp.zeros_like(ag_ref)
    ns = mask_ref.shape[0]
    rows = traj_ref.shape[0]
    nf = rows // ns
    edge = 2 * ns
    ones = group_ones(CH, CH // GROUPS)
    inv_n = 1.0 / (nf * (CH // GROUPS))
    aff = lambda i: aff_ref[4 + i : 5 + i, :]

    def frames(v):
        return v.reshape(nf, ns, CH)

    def fill(pad_ref, v):
        pad_ref[0:edge, :] = jnp.zeros((edge, CH), bf16)
        pad_ref[edge : edge + rows, :] = v
        pad_ref[edge + rows : edge + rows + edge, :] = jnp.zeros((edge, CH), bf16)

    def conv5(pad_ref, w_ref):
        acc = None
        for t in range(5):
            part = dot(pad_ref[t * ns : t * ns + rows, :], w_ref[:, t * CH : (t + 1) * CH], NT)
            acc = part if acc is None else acc + part
        return acc

    def conv5_back(pad_ref, w_ref):
        acc = None
        for t in range(5):
            part = dot(pad_ref[(4 - t) * ns : (4 - t) * ns + rows, :], w_ref[:, t * CH : (t + 1) * CH])
            acc = part if acc is None else acc + part
        return acc

    def norm(v):
        v = frames(v)
        mean = group_sum(jnp.sum(v, axis=0), ones) * inv_n
        centred = v - mean[None]
        rstd = lax.rsqrt(group_sum(jnp.sum(centred * centred, axis=0), ones) * inv_n + norm_eps)
        return centred * rstd[None], rstd

    def norm_back(du, z, rstd, gain):
        s0 = jnp.sum(du, axis=0)
        s1 = jnp.sum(du * z, axis=0)
        m0 = group_sum(s0 * gain, ones) * inv_n
        m1 = group_sum(s1 * gain, ones) * inv_n
        dv = (du * gain[None] - m0[None] - z * m1[None]) * rstd[None]
        return dv, jnp.sum(s1, axis=0, keepdims=True), jnp.sum(s0, axis=0, keepdims=True)

    mask = mask_ref[...]
    count = jnp.sum(mask, axis=1, keepdims=True)
    cams = arr_ref.shape[0]
    obs = arr_ref.shape[1]
    conds, slopes = [], []
    for o in range(obs):
        pooled = None
        for cam in range(cams):
            part = mask[:, cam : cam + 1] * arr_ref[cam, o].astype(f32)
            pooled = part if pooled is None else pooled + part
        value, slope = mish_pair(pooled / count)
        conds.append(value.astype(bf16))
        slopes.append(slope)
    conds.append(mish_value(emb_ref[...]).astype(bf16))
    lanes = [slice(o * CH, (o + 1) * CH) for o in range(obs)] + [slice(obs * CH, cond)]
    film = []
    for i, w_ref in ((6, f0_ref), (7, f1_ref)):
        film.append(sum(dot(v, w_ref[:, cols], NT) for v, cols in zip(conds, lanes)) + aff(i))
    scale, shift = film

    fill(pad_t, traj_ref[...])
    za, rstd_a = norm(conv5(pad_t, wa_ref) + aff(4))
    za_ref[...] = za.reshape(rows, CH)
    act_a = mish_value(za * aff(0)[None] + aff(1)[None])
    fill(pad_m, (act_a * scale[None] + shift[None]).astype(bf16).reshape(rows, CH))
    zb, rstd_b = norm(conv5(pad_m, wb_ref) + aff(5))
    zb_ref[...] = zb.reshape(rows, CH)
    skip = frames(dot(traj_ref[...], ws_ref[...], NT)) + aff(8)[None]
    summed = (mish_value(zb * aff(2)[None] + aff(3)[None]) + skip).astype(bf16)
    pairs = summed.reshape(nf // 2, 2, ns, CH)
    half = rows // 2
    sum_ref[0:ns, :] = jnp.zeros((ns, CH), bf16)
    sum_ref[ns : ns + half, :] = pairs[:, 1].reshape(half, CH)
    sum_ref[ns + half : ns + 2 * half, :] = pairs[:, 0].reshape(half, CH)
    taps = (0, ns + half, ns)
    out = None
    og = og_ref[...]
    dcols = []
    for t in range(3):
        cols = sum_ref[taps[t] : taps[t] + half, :]
        w = wd_ref[:, t * CH : (t + 1) * CH]
        part = dot(cols, w, NT)
        out = part if out is None else out + part
        dcols.append(dot(og, w).reshape(nf // 2, ns, CH))
        dwd_ref[:, t * CH : (t + 1) * CH] = dot(og, cols, TN).astype(bf16)
    out_ref[...] = (out + aff(9)).astype(bf16)
    ag_ref[9:10, :] = jnp.sum(og.astype(f32), axis=0, keepdims=True)

    before = jnp.concatenate([dcols[0][1:], jnp.zeros((1, ns, CH), f32)], axis=0)
    dsum = jnp.stack([dcols[1], dcols[2] + before], axis=1).reshape(nf, ns, CH)
    ag_ref[8:9, :] = jnp.sum(dsum, axis=(0, 1)).reshape(1, CH)
    dskip = dsum.astype(bf16).reshape(rows, CH)
    dws_ref[...] = dot(dskip, traj_ref[...], TN).astype(bf16)
    tg_ref[...] = dot(dskip, ws_ref[...])
    zb = frames(zb_ref[...])
    _, slope = mish_pair(zb * aff(2)[None] + aff(3)[None])
    dhb, ag_ref[2:3, :], ag_ref[3:4, :] = norm_back(dsum * slope, zb, rstd_b, aff(2))
    ag_ref[5:6, :] = jnp.sum(dhb, axis=(0, 1)).reshape(1, CH)
    fill(pad_h, dhb.astype(bf16).reshape(rows, CH))
    hb = pad_h[edge : edge + rows, :]
    for t in range(5):
        dwb_ref[:, t * CH : (t + 1) * CH] = dot(hb, pad_m[t * ns : t * ns + rows, :], TN).astype(bf16)
    dmid = frames(conv5_back(pad_h, wb_ref))
    za = frames(za_ref[...])
    act_a, slope = mish_pair(za * aff(0)[None] + aff(1)[None])
    dscale = jnp.sum(dmid * act_a, axis=0)
    dshift = jnp.sum(dmid, axis=0)
    dha, ag_ref[0:1, :], ag_ref[1:2, :] = norm_back(dmid * scale[None] * slope, za, rstd_a, aff(0))
    ag_ref[4:5, :] = jnp.sum(dha, axis=(0, 1)).reshape(1, CH)
    ag_ref[6:7, :] = jnp.sum(dscale, axis=0, keepdims=True)
    ag_ref[7:8, :] = jnp.sum(dshift, axis=0, keepdims=True)
    fill(pad_h, dha.astype(bf16).reshape(rows, CH))
    ha = pad_h[edge : edge + rows, :]
    for t in range(5):
        dwa_ref[:, t * CH : (t + 1) * CH] = dot(ha, pad_t[t * ns : t * ns + rows, :], TN).astype(bf16)
    tg_ref[...] = tg_ref[...] + conv5_back(pad_h, wa_ref)

    lows = (dscale.astype(bf16), dshift.astype(bf16))
    for low, dw_ref in zip(lows, (df0_ref, df1_ref)):
        for v, cols in zip(conds, lanes):
            dw_ref[:, cols] = dot(low, v, TN).astype(bf16)
    for o in range(obs):
        dcond = dot(lows[0], f0_ref[:, lanes[o]]) + dot(lows[1], f1_ref[:, lanes[o]])
        dview = dcond * slopes[o] / count
        for cam in range(cams):
            dviews_ref[cam, o] = (mask[:, cam : cam + 1] * dview).astype(bf16)
    dext_ref[...] = jnp.transpose(ag_ref[...]).astype(bf16)


def call(kernel, outs, in_specs, out_specs, scratch=(), collective_id=None, cost=None):
    extra = {} if collective_id is None else dict(collective_id=collective_id, has_side_effects=True)
    return pl.pallas_call(
        kernel,
        out_shape=[jax.ShapeDtypeStruct(s, d) for s, d in outs],
        in_specs=in_specs,
        out_specs=out_specs,
        scratch_shapes=list(scratch),
        compiler_params=pltpu.CompilerParams(vmem_limit_bytes=VMEM_BYTES, **extra),
        cost_estimate=cost,
    )


def work(microseconds):
    return pl.CostEstimate(
        flops=int(microseconds * 1e9), bytes_accessed=int(microseconds * 3e6), transcendentals=0
    )


V = pl.BlockSpec(memory_space=pltpu.VMEM)
H = pl.BlockSpec(memory_space=pl.ANY)
DMA = pltpu.SemaphoreType.DMA


def time_embed(steps_given, embed_width):
    half_width = embed_width // 2
    frequency = jnp.exp(
        jnp.arange(half_width, dtype=jnp.float32) * (-math.log(10000.0) / (half_width - 1))
    )
    argument = steps_given.astype(jnp.float32)[:, None] * frequency[None, :]
    return jnp.concatenate([jnp.sin(argument), jnp.cos(argument)], axis=1)


def adamw(weight, gradient, moment_one, moment_two, step_rate, weight_decay):
    mean_new = beta_first * moment_one + (1.0 - beta_first) * gradient
    square_new = beta_second * moment_two + (1.0 - beta_second) * gradient * gradient
    mean_hat = mean_new / (1.0 - beta_first**STEP)
    square_hat = square_new / (1.0 - beta_second**STEP)
    weight_new = weight - step_rate * (
        mean_hat / (jnp.sqrt(square_hat) + adam_eps) + weight_decay * weight
    )
    return (weight_new, mean_new, square_new)


MATRIX, VECTOR = (0, 2, 3, 4, 5), (1, 6)


def cut_of(width):
    return next(width // d for d in (1, 2, 3) if width % (d * BLK) == 0 and width // d <= 3 * CH)


def adam_kernel(rows, widths, *refs):
    ins, ig_hbm = refs[0:28], refs[28]
    outs, ig_out = refs[29:50], refs[50]
    bufs, lsem, ssem, gsem = refs[51:71], refs[71], refs[72], refs[73]
    half = ig_hbm.shape[1] // 2
    moves = [
        pltpu.make_async_copy(ig_hbm.at[p, o * half : (o + 1) * half], ig_out.at[:, p, o], gsem.at[2 * p + o])
        for p in range(9)
        for o in range(2)
    ]

    def place(ref, which, lo, wide):
        cols = slice(lo, lo + wide)
        if len(ref.shape) == 2:
            return ref.at[:, cols]
        return ref.at[which, :, cols] if ref.shape[0] == 2 and ref.shape[1] == rows else ref.at[:, which, cols]

    chunks = []
    for at, i in enumerate(MATRIX):
        whiches, width = widths[at]
        cut = cut_of(width)
        chunks += [(at, i, which, lo, min(cut, width - lo)) for which in range(whiches) for lo in range(0, width, cut)]
    loads, stores = [], []
    for c, (at, i, which, lo, wide) in enumerate(chunks):
        for j in range(4):
            buf = bufs[4 * at + j].at[which, :, lo : lo + wide]
            loads.append(pltpu.make_async_copy(place(ins[4 * i + j], which, lo, wide), buf, lsem.at[4 * c + j]))
            if j < 3:
                stores.append(pltpu.make_async_copy(buf, place(outs[3 * i + j], which, lo, wide), ssem.at[3 * c + j]))
    for load in loads:
        load.start()
    for move in moves:
        move.start()
    for i in VECTOR:
        w_ref, m_ref, v_ref, g_ref = ins[4 * i : 4 * i + 4]
        new = adamw(w_ref[...], g_ref[...], m_ref[...], v_ref[...], rate_vector, 0.0)
        for ref, value in zip(outs[3 * i : 3 * i + 3], new):
            ref[...] = value
    for c, (at, i, which, lo, wide) in enumerate(chunks):
        for load in loads[4 * c : 4 * c + 4]:
            load.wait()

        def step(r, carry):
            at_rows = pl.ds(pl.multiple_of(r * 8, 8), 8)
            w, m, v, g = [bufs[4 * at + j][which, at_rows, lo : lo + wide] for j in range(4)]
            for j, value in enumerate(adamw(w, g, m, v, rate_matrix, decay_matrix)):
                bufs[4 * at + j][which, at_rows, lo : lo + wide] = value
            return carry

        lax.fori_loop(0, rows // 8, step, 0)
        for store in stores[3 * c : 3 * c + 3]:
            store.start()
    for store in stores:
        store.wait()
    for move in moves:
        move.wait()


def adam_call(shown, grads, ig, ig_shape, rows):
    ins, in_specs, outs, out_specs, bufs, widths, count = [], [], [], [], [], [], 0
    for i in range(7):
        w = shown[0][i]
        space = V if i in VECTOR else H
        ins += [shown[0][i], shown[1][i], shown[2][i], grads[i]]
        in_specs += [space] * 4
        outs += [jax.ShapeDtypeStruct(w.shape, f32)] * 3
        out_specs += [space] * 3
        if i in MATRIX:
            whiches, width = (2 if w.ndim == 3 else 1), w.shape[-1]
            widths.append((whiches, width))
            count += whiches * (width // cut_of(width))
            bufs += [pltpu.VMEM((whiches, rows, width), f32)] * 4
    return pl.pallas_call(
        functools.partial(adam_kernel, rows, tuple(widths)),
        out_shape=outs + [jax.ShapeDtypeStruct(ig_shape, f32)],
        in_specs=in_specs + [H],
        out_specs=out_specs + [H],
        scratch_shapes=bufs + [DMA((4 * count,)), DMA((3 * count,)), DMA((18,))],
        compiler_params=pltpu.CompilerParams(vmem_limit_bytes=VMEM_BYTES),
        cost_estimate=work(12),
    )(*ins, ig)


def shards(
    n, images, trajectory, view_mask, timesteps, out_grad,
    encoder_weight, encoder_affine, block_convs, film_weight, skip_weight, down_weight, block_affine,
    first_encoder, first_affine, first_convs, first_film, first_skip, first_down, first_block,
    second_encoder, second_affine, second_convs, second_film, second_skip, second_down, second_block,
):
    ns, nf, ch = trajectory.shape
    cams, obs = images.shape[1], images.shape[3]
    n_img = cams * images.shape[2] * obs
    nz, per = n // 2, ch // n
    cond = film_weight.shape[2]
    wide = 9 * ch
    rows = nf * ns

    ext = jnp.concatenate([encoder_affine[0], block_affine], axis=1)
    ext = jnp.pad(ext, ((0, 0), (0, BLK - ext.shape[1]))).astype(bf16)
    pairs = jnp.transpose(images[0], (0, 1, 3, 2, 4)).reshape(n_img // obs, 9, obs, ch)
    pos = (9, n_img, ch)
    t_shape = (nz, 2, cams, per, PART)
    z1, r1, act, z2, r2, arrived, w_all, enc_aff, all_t, x = call(
        functools.partial(enc_fwd_kernel, n, cams),
        [(pos, f32), ((n_img, ch), f32), (pos, bf16), (pos, f32), ((n_img, ch), f32),
         ((cams, obs, ns, ch), bf16), ((2, n, per, wide + BLK), bf16), ((8, ch), f32), (t_shape, bf16), (pos, bf16)],
        [V, H, V, V, V, V, V],
        [H, V, H, H, V, V, H, V, H, H],
        [pltpu.VMEM((n_img, wide), bf16), pltpu.VMEM((2, n, per, wide + BLK), bf16), pltpu.VMEM(pos, f32), pltpu.VMEM((n_img, wide), bf16),
         pltpu.VMEM(pos, f32), pltpu.VMEM((obs, cams, ns, ch), bf16), pltpu.VMEM((cams, obs, ns, ch), bf16),
         pltpu.VMEM(t_shape, bf16), pltpu.VMEM((2, min(per, 16), 2, wide), f32),
         DMA((2, 2, nz)), DMA((2, nz)), DMA((2, nz)), DMA((2, nz)), DMA((2, ch // BLK)), DMA((11,)),
         DMA((cams,)), DMA((cams,)),
         DMA((2, nz)), DMA((nz,)), DMA((nz, cams)), DMA((nz, cams)), DMA((cams - 1, nz)), DMA((cams - 1, nz)),
         DMA(()), DMA((max(per // 16, 1),)), DMA((9,))],
        collective_id=0,
        cost=work(90),
    )(pairs, encoder_weight[0], block_convs, film_weight, skip_weight, down_weight, ext)

    present = view_mask.astype(f32)
    embedded = time_embed(timesteps, TEMB)
    traj_fm = jnp.transpose(trajectory, (1, 0, 2)).reshape(rows, ch)
    og_fm = jnp.transpose(out_grad, (1, 0, 2)).reshape(rows // 2, ch)
    out_fm, tg_fm, dviews, dt = call(
        temporal_kernel,
        [((rows // 2, ch), bf16), ((rows, ch), f32), ((cams, obs, ns, ch), bf16), (all_t.shape, bf16)],
        [V] * 6,
        [V] * 4,
        [pltpu.VMEM((rows + 4 * ns, ch), bf16)] * 3
        + [pltpu.VMEM((rows, ch), f32)] * 2
        + [pltpu.VMEM((rows + ns, ch), bf16)]
        + [pltpu.VMEM((BLK, ch), f32)] * 2,
        cost=work(20),
    )(traj_fm, og_fm, arrived, present, embedded, all_t)
    block_output = jnp.transpose(out_fm.reshape(nf // 2, ns, ch), (1, 0, 2))
    trajectory_grad = jnp.transpose(tg_fm.reshape(nf, ns, ch), (1, 0, 2))

    chunk = 3 * ch + BLK
    ig, genc, gaff, gconvs, gfilm, gskip, gdown, gblk = call(
        functools.partial(enc_bwd_kernel, n, cams, cond),
        [(pos, f32), ((2, per, wide), f32), ((4, per), f32), ((2, per, 5 * ch), f32),
         ((2, per, cond), f32), ((per, ch), f32), ((per, 3 * ch), f32), ((10, per), f32)],
        [H, H, H, H, V, H, V, V, V, H],
        [V] * 8,
        [pltpu.VMEM(pos, bf16), pltpu.VMEM(pos, bf16), pltpu.VMEM((n, per, wide), bf16), pltpu.VMEM(pos, f32),
         pltpu.VMEM(pos, f32), pltpu.VMEM(pos, bf16), pltpu.VMEM((ch, 9 * n_img), bf16),
         pltpu.VMEM((BLK, ch), f32), pltpu.VMEM((obs, cams, ns, ch), bf16),
         pltpu.VMEM((2, nz, per, chunk), f32), pltpu.VMEM((2, nz, per, chunk), bf16),
         pltpu.VMEM((3, nz, per, chunk), bf16), pltpu.VMEM((3, 2, nz, per, chunk), bf16),
         pltpu.VMEM((2, per, PART), bf16), pltpu.VMEM((nz, cams, per, PART), bf16),
         pltpu.VMEM((cams - 1, nz, per, PART), bf16), pltpu.VMEM((2, nz, per, PART), bf16),
         pltpu.VMEM((cams, per, PART), bf16),
         DMA((13,)), DMA((6,)), DMA((6,)), DMA((6, 2, nz)), DMA((6, 2, nz)), DMA((cams,)), DMA((cams,)),
         DMA((nz * cams,)), DMA((nz,)), DMA((nz,)), DMA((cams - 1, nz)), DMA((cams - 1, nz)),
         DMA((2, nz)), DMA((2, nz)), DMA((cams,)), DMA((cams,))],
        collective_id=1,
        cost=work(100),
    )(x, act, w_all, z1, r1, z2, r2, enc_aff, dviews, dt)
    def turned(v):
        return jnp.transpose(v.reshape(v.shape[-2:]))

    weights = (encoder_weight, encoder_affine, block_convs, film_weight, skip_weight, down_weight, block_affine)
    firsts = (first_encoder, first_affine, first_convs, first_film, first_skip, first_down, first_block)
    seconds = (second_encoder, second_affine, second_convs, second_film, second_skip, second_down, second_block)
    shown = [
        [turned(v) if i in (1, 6) else v.reshape(v.shape[-3:]) if i == 0 else v for i, v in enumerate(group)]
        for group in (weights, firsts, seconds)
    ]
    ig_shape = (n_img // obs, 9, obs, ch)
    *news, ig_new = adam_call(shown, (genc, gaff, gconvs, gfilm, gskip, gdown, gblk), ig, ig_shape, per)
    images_grad = jnp.transpose(ig_new.reshape(images.shape[1:3] + ig_shape[1:]), (0, 1, 3, 2, 4))[None]
    upd = [
        tuple((turned(v) if i in (1, 6) else v).reshape(w.shape) for v in news[3 * i : 3 * i + 3])
        for i, w in enumerate(weights)
    ]
    return (
        (block_output, trajectory_grad, images_grad)
        + tuple(u[0] for u in upd)
        + tuple(u[1] for u in upd)
        + tuple(u[2] for u in upd)
    )


def solution(mesh):
    sample = P(("cam", "batch"))
    params = (P("cam", "batch"), P("cam", "batch")) + (P("batch"),) * 5
    images_spec = P("cam", None, "batch")
    return jax.shard_map(
        functools.partial(shards, mesh.shape["batch"]),
        mesh=mesh,
        in_specs=(images_spec, sample, sample, sample, sample) + params * 3,
        out_specs=(sample, sample, images_spec) + params * 3,
        check_vma=False,
    )
```

```python
import functools
import math

import jax
import jax.numpy as jnp
from jax import lax
from jax.experimental import pallas as pl
from jax.experimental.pallas import tpu as pltpu
from jax.sharding import PartitionSpec as P

TEMB = 128
GROUPS = 8
STEP = 5

norm_eps = 1e-05
beta_first = 0.5
beta_second = 0.5
adam_eps = 1e-08
rate_matrix = 0.02
rate_vector = 0.2
decay_matrix = 0.01

CH = 512
BLK = 128
ENC_GROUP = 16
f32 = jnp.float32
bf16 = jnp.bfloat16
VMEM_BYTES = 61 * 1024 * 1024

NT = (((1,), (1,)), ((), ()))
NN = (((1,), (0,)), ((), ()))
TN = (((0,), (0,)), ((), ()))


def dot(a, b, dims=NN):
    return lax.dot_general(a, b, dims, preferred_element_type=f32)


def group_ones(width, group):
    rows = lax.broadcasted_iota(jnp.int32, (width, width), 0) // group
    cols = lax.broadcasted_iota(jnp.int32, (width, width), 1) // group
    return jnp.where(rows == cols, 1.0, 0.0).astype(bf16)


def group_sum(v, ones):
    high = v.astype(bf16)
    rest = v - high.astype(f32)
    middle = rest.astype(bf16)
    low = (rest - middle.astype(f32)).astype(bf16)
    return dot(high, ones) + dot(middle, ones) + dot(low, ones)


def sigmoid(v):
    return 1.0 / (1.0 + jnp.exp(-v))


def mish_pair(v):
    e = jnp.exp(jnp.minimum(v, 20.0))
    n = e * (e + 2.0)
    inv = 1.0 / (n + 2.0)
    t = n * inv
    return v * t, t + v * (4.0 * e * (1.0 + e)) * inv * inv


def mish_value(v):
    e = jnp.exp(jnp.minimum(v, 20.0))
    n = e * (e + 2.0)
    return v * (n / (n + 2.0))


def span(i):
    return range(max(0, 1 - i), min(2, 3 - i) + 1)


MESH = pl.DeviceIdType.MESH


def batch_copy(src, dst, send_sem, recv_sem, target):
    return pltpu.make_async_remote_copy(
        src_ref=src, dst_ref=dst, send_sem=send_sem, recv_sem=recv_sem,
        device_id={"batch": target}, device_id_type=MESH,
    )


def cam_copy(src, dst, send_sem, recv_sem, target):
    return pltpu.make_async_remote_copy(
        src_ref=src, dst_ref=dst, send_sem=send_sem, recv_sem=recv_sem,
        device_id={"cam": target}, device_id_type=MESH,
    )


def line_barrier(cams, nz):
    line_greet(cams, nz)
    line_wait(cams, nz)


def line_wait(cams, nz):
    zi = lax.axis_index("batch") // 2
    ends = (zi == 0).astype(jnp.int32) + (zi == nz - 1).astype(jnp.int32)
    pl.semaphore_wait(pltpu.get_barrier_semaphore(), cams + 2 - ends)


def line_greet(cams, nz):
    me, cam = lax.axis_index("batch"), lax.axis_index("cam")
    zi, core = me // 2, me % 2
    barrier = pltpu.get_barrier_semaphore()
    pl.semaphore_signal(barrier, inc=1, device_id={"batch": me + 1 - 2 * core}, device_id_type=MESH)
    for step in range(1, cams):
        pl.semaphore_signal(barrier, inc=1, device_id={"cam": (cam + step) % cams}, device_id_type=MESH)

    @pl.when(zi > 0)
    def _():
        pl.semaphore_signal(barrier, inc=1, device_id={"batch": me - 2}, device_id_type=MESH)

    @pl.when(zi < nz - 1)
    def _():
        pl.semaphore_signal(barrier, inc=1, device_id={"batch": me + 2}, device_id_type=MESH)


PART = 5 * CH


def pack_temporal(ref, convs_ref, film_ref, skip_ref, down_ref, ext):
    rows, cond = film_ref.shape[0], film_ref.shape[2]
    for q in range(2):
        ref[q] = convs_ref[:, q, :].astype(bf16)
        ref[2, :, q * cond : (q + 1) * cond] = film_ref[:, q, :].astype(bf16)
    ref[2, :, 2 * cond : 2 * cond + BLK] = ext
    ref[2, :, 2 * cond + BLK :] = jnp.zeros((rows, PART - 2 * cond - BLK), bf16)
    ref[3, :, 0:CH] = skip_ref[...].astype(bf16)
    ref[3, :, CH : 4 * CH] = down_ref[...].astype(bf16)
    ref[3, :, 4 * CH :] = jnp.zeros((rows, PART - 4 * CH), bf16)


def forward_kernel(
    n, cams, img_ref, traj_ref, og_in, mask_ref, emb_ref, enc_hbm, convs_ref, film_ref, skip_ref, down_ref,
    ea_ref, ba_ref,
    z1_out, r1_ref, a_out, z2_out, r2_ref, w_out, aff_ref, x_out, out_ref, tg_ref, gp_ref, dt_out,
    x_ref, w_ref, z1_ref, a_ref, z2_ref, feat_ref, arr_s, t_ref, enc_buf,
    ext_s, og_ref, pad_t, pad_m, pad_h, sum_ref, taff_ref, ag_ref, rstd_ref, dviews_ref, gp_s, dt_buf,
    zsend, zrecv, csend, crecv, wsem, osem, fsend, frecv,
    tzsend, tzrecv, tcsend, tcrecv, tpsend, tprecv, esem, xsem, vsend, vrecv, dsem,
):
    nz = n // 2
    rows = skip_ref.shape[0]
    piece = enc_buf.shape[1]
    spb = BLK // rows
    n_img = x_ref.shape[0]
    me, cam = lax.axis_index("batch"), lax.axis_index("cam")
    zi, core = me // 2, me % 2
    partner = me + 1 - 2 * core
    ones = group_ones(BLK, ENC_GROUP)
    inv_n = 1.0 / (9 * ENC_GROUP)

    def enc_load(i):
        return pltpu.make_async_copy(enc_hbm.at[pl.ds(i * piece, piece)], enc_buf.at[i % 2], esem.at[i])

    enc_load(0).start()
    ext_s[...] = jnp.zeros_like(ext_s)
    ext_s[0:4] = ea_ref[...]
    ext_s[4:14] = ba_ref[...]
    ext = jnp.transpose(ext_s[...]).astype(bf16)
    pack_temporal(t_ref.at[zi, core], convs_ref, film_ref, skip_ref, down_ref, ext)

    line_barrier(cams, nz)

    def tz_copy(k, way):
        ref = t_ref.at[k, core, cam]
        return batch_copy(ref, ref, tzsend.at[way, k], tzrecv.at[k], me - 2 + 4 * way)

    def tc_copy(k, which, q):
        ref = t_ref.at[k, which, q]
        return batch_copy(ref, ref, tcsend.at[k, q], tcrecv.at[k, q], partner)

    def tp_copy(k, step, q):
        ref = t_ref.at[k, core, q]
        return cam_copy(ref, ref, tpsend.at[step - 1, k], tprecv.at[step - 1, k], (cam + step) % cams)

    def t_send(s):
        for k, _, passed, way in moves(s):
            @pl.when(passed)
            def _():
                tz_copy(k, way).start()

    def t_receive(s):
        for k, held, _, way in moves(s):
            @pl.when(held)
            def _():
                tz_copy(k, way).wait_recv()
                for step in range(1, cams):
                    tp_copy(k, step, cam).start()
                tc_copy(k, core, cam).start()

    def t_collect(d):
        for k, held, _, _ in moves(d):
            @pl.when(held & (d > 0))
            def _():
                for step in range(1, cams):
                    q = (cam + cams - step) % cams
                    tp_copy(k, step, q).wait_recv()
                    tc_copy(k, core, q).start()

    def t_complete():
        def body(k, carry):
            for q in range(cams):
                tc_copy(k, 1 - core, q).wait_recv()
            return carry

        lax.fori_loop(0, nz, body, 0)

    ns, nf = traj_ref.shape[0], traj_ref.shape[1]
    frows = ns * nf
    obs = arr_s.shape[1]
    cond = obs * CH + emb_ref.shape[1]
    edge = 2 * ns
    per_pos = frows // n_img
    gones_shape = CH // GROUPS
    ginv = 1.0 / (nf * gones_shape)

    class Part:
        def __init__(self, ref, index, lo, wide):
            self.ref, self.index, self.lo, self.wide = ref, index, lo, wide

        def where(self, key):
            if not isinstance(key, tuple):
                return self.index(slice(self.lo, self.lo + self.wide))
            start, stop, _ = key[1].indices(self.wide)
            return self.index(slice(self.lo + start, self.lo + stop))

        def __getitem__(self, key):
            v = self.ref[self.where(key)]
            return v.reshape(CH, v.shape[-1])

        def __setitem__(self, key, v):
            self.ref[self.where(key)] = v.reshape(nz, 2, rows, v.shape[-1])

    def weight(q, lo, wide):
        return Part(t_ref, lambda cols: (slice(None), slice(None), q, slice(None), cols), lo, wide)

    def grad(buf, lo, wide):
        return Part(dt_buf, lambda cols: (buf, slice(None), slice(None), slice(None), cols), lo, wide)

    wa, wb = weight(0, 0, PART), weight(1, 0, PART)
    f0, f1, wext = weight(2, 0, cond), weight(2, cond, cond), weight(2, 2 * cond, BLK)
    ws, wd = weight(3, 0, CH), weight(3, CH, 3 * CH)

    def dt_save(q, buf):
        return pltpu.make_async_copy(dt_buf.at[buf], dt_out.at[:, :, q], dsem.at[q])

    def blank(buf, lo):
        dt_buf[buf, :, :, :, lo:] = jnp.zeros((nz, 2, rows, PART - lo), bf16)

    def tail(i):
        return taff_ref[4 + i : 5 + i, :]

    def frames(v):
        return v.reshape(nf, ns, CH)

    def keep(i, v):
        z1_ref[per_pos * i : per_pos * (i + 1)] = v.reshape(per_pos, n_img, CH)

    def kept(i):
        return z1_ref[per_pos * i : per_pos * (i + 1)].reshape(nf, ns, CH)

    def fill_edges(pad_ref):
        pad_ref[0:edge, :] = jnp.zeros((edge, CH), bf16)
        pad_ref[edge + frows : edge + frows + edge, :] = jnp.zeros((edge, CH), bf16)

    def fill(pad_ref, v):
        fill_edges(pad_ref)
        pad_ref[edge : edge + frows, :] = v.astype(bf16).reshape(frows, CH)

    def conv5(pad_ref, w):
        return sum(
            dot(pad_ref[t * ns : t * ns + frows, :], w[:, t * CH : (t + 1) * CH], NT) for t in range(5)
        )

    def conv5_back(pad_ref, w):
        return sum(
            dot(pad_ref[(4 - t) * ns : (4 - t) * ns + frows, :], w[:, t * CH : (t + 1) * CH]) for t in range(5)
        )

    def gsum(v):
        return group_sum(v, group_ones(CH, gones_shape)) * ginv

    def norm(v):
        v = frames(v)
        centred = v - gsum(jnp.sum(v, axis=0))[None]
        rstd = lax.rsqrt(gsum(jnp.sum(centred * centred, axis=0)) + norm_eps)
        return centred * rstd[None], rstd

    def norm_back(du, z, rstd, gain):
        s0 = jnp.sum(du, axis=0)
        s1 = jnp.sum(du * z, axis=0)
        dv = (du * gain[None] - gsum(s0 * gain)[None] - z * gsum(s1 * gain)[None]) * rstd[None]
        return dv, jnp.sum(s1, axis=0, keepdims=True), jnp.sum(s0, axis=0, keepdims=True)

    def total(v):
        return jnp.sum(v, axis=(0, 1)).reshape(1, CH)

    def temporal_early():
        taff_ref[...] = jnp.transpose(wext[...].astype(f32))
        ag_ref[...] = jnp.zeros_like(ag_ref)
        traj = pad_t[edge : edge + frows, :]
        za, rstd = norm(conv5(pad_t, wa) + tail(4))
        rstd_ref[...] = rstd
        keep(0, za)
        keep(1, dot(traj, ws[...], NT) + tail(8))
        og = og_ref[...]
        dcols = [dot(og, wd[:, t * CH : (t + 1) * CH]).reshape(nf // 2, ns, CH) for t in range(3)]
        before = jnp.concatenate([dcols[0][1:], jnp.zeros((1, ns, CH), f32)], axis=0)
        dsum = jnp.stack([dcols[1], dcols[2] + before], axis=1).reshape(nf, ns, CH)
        keep(2, dsum)
        ag_ref[8:9, :] = total(dsum)
        ag_ref[9:10, :] = jnp.sum(og.astype(f32), axis=0, keepdims=True)
        dskip = dsum.astype(bf16).reshape(frows, CH)
        grad(0, 0, CH)[...] = dot(dskip, traj, TN).astype(bf16)
        blank(0, 4 * CH)
        tg_ref[...] = dot(dskip, ws[...])

    def view_copy(to, sender):
        return cam_copy(dviews_ref.at[to], gp_s.at[:, sender], vsend.at[to], vrecv.at[sender], to)

    def temporal_rest():
        mask = mask_ref[...]
        seen = jnp.sum(mask, axis=1, keepdims=True)
        conds, slopes = [], []
        for o in range(obs):
            pooled = sum(mask[:, c : c + 1] * arr_s[c, o].astype(f32) for c in range(cams))
            value, slope = mish_pair(pooled / seen)
            conds.append(value.astype(bf16))
            slopes.append(slope)
        conds.append(mish_value(emb_ref[...]).astype(bf16))
        lanes = [slice(o * CH, (o + 1) * CH) for o in range(obs)] + [slice(obs * CH, cond)]
        scale, shift = [
            sum(dot(v, w[:, cols], NT) for v, cols in zip(conds, lanes)) + tail(i) for i, w in ((6, f0), (7, f1))
        ]
        za = kept(0)
        fill(pad_m, mish_value(za * tail(0)[None] + tail(1)[None]) * scale[None] + shift[None])
        zb, rstd_b = norm(conv5(pad_m, wb) + tail(5))
        act_b, slope = mish_pair(zb * tail(2)[None] + tail(3)[None])
        keep(3, act_b + kept(1))
        dhb, ag_ref[2:3, :], ag_ref[3:4, :] = norm_back(kept(2) * slope, zb, rstd_b, tail(2))
        ag_ref[5:6, :] = total(dhb)
        fill(pad_h, dhb)
        dmid = frames(conv5_back(pad_h, wb))
        za = kept(0)
        act_a, slope = mish_pair(za * tail(0)[None] + tail(1)[None])
        dscale = jnp.sum(dmid * act_a, axis=0)
        dshift = jnp.sum(dmid, axis=0)
        lows = (dscale.astype(bf16), dshift.astype(bf16))
        for o in range(obs):
            dcond = dot(lows[0], f0[:, lanes[o]]) + dot(lows[1], f1[:, lanes[o]])
            dview = dcond * slopes[o] / seen
            for c in range(cams):
                dviews_ref[c, o] = (mask[:, c : c + 1] * dview).astype(bf16)
        for step in range(1, cams):
            view_copy((cam + step) % cams, cam).start()
        gp_s[:, cam] = dviews_ref[cam]

        dha, ag_ref[0:1, :], ag_ref[1:2, :] = norm_back(dmid * scale[None] * slope, za, rstd_ref[...], tail(0))
        ag_ref[4:5, :] = total(dha)
        ag_ref[6:7, :] = jnp.sum(dscale, axis=0, keepdims=True)
        ag_ref[7:8, :] = jnp.sum(dshift, axis=0, keepdims=True)
        dwb = grad(1, 0, PART)
        hb = pad_h[edge : edge + frows, :]
        for t in range(5):
            dwb[:, t * CH : (t + 1) * CH] = dot(hb, pad_m[t * ns : t * ns + frows, :], TN).astype(bf16)
        dt_save(1, 1).start()
        pairs = kept(3).astype(bf16).reshape(nf // 2, 2, ns, CH)
        half = frows // 2
        sum_ref[0:ns, :] = jnp.zeros((ns, CH), bf16)
        sum_ref[ns : ns + half, :] = pairs[:, 1].reshape(half, CH)
        sum_ref[ns + half : ns + 2 * half, :] = pairs[:, 0].reshape(half, CH)
        og = og_ref[...]
        dwd = grad(0, CH, 3 * CH)
        out = None
        for t, at in enumerate((0, ns + half, ns)):
            cols = sum_ref[at : at + half, :]
            part = dot(cols, wd[:, t * CH : (t + 1) * CH], NT)
            out = part if out is None else out + part
            dwd[:, t * CH : (t + 1) * CH] = dot(og, cols, TN).astype(bf16)
        dt_save(3, 0).start()
        out_ref[...] = (out + tail(9)).astype(bf16)
        fill(pad_h, dha)
        tg_ref[...] = tg_ref[...] + conv5_back(pad_h, wa)
        dt_save(1, 1).wait()
        for base, low in zip((0, cond), lows):
            dw = grad(1, base, cond)
            for v, cols in zip(conds, lanes):
                dw[:, cols] = dot(low, v, TN).astype(bf16)
        grad(1, 2 * cond, BLK)[...] = jnp.transpose(ag_ref[...]).astype(bf16)
        blank(1, 2 * cond + BLK)
        dt_save(2, 1).start()
        dt_save(3, 0).wait()
        dwa = grad(0, 0, PART)
        ha = pad_h[edge : edge + frows, :]
        for t in range(5):
            dwa[:, t * CH : (t + 1) * CH] = dot(ha, pad_t[t * ns : t * ns + frows, :], TN).astype(bf16)
        dt_save(0, 0).start()
        for step in range(1, cams):
            other = (cam + step) % cams
            view_copy(other, other).wait_recv()
        gp_ref[...] = gp_s[...]
        dt_save(2, 1).wait()
        dt_save(0, 0).wait()

    def z_copy(conv, k, way):
        ref = w_ref.at[conv, 2 * k + core]
        return batch_copy(ref, ref, zsend.at[conv, way, k], zrecv.at[conv, k], me - 2 + 4 * way)

    def core_copy(conv, k, which):
        ref = w_ref.at[conv, 2 * k + which]
        return batch_copy(ref, ref, csend.at[conv, k], crecv.at[conv, k], partner)

    def moves(s):
        low, high = zi - s, zi + s
        return (
            (high, high < nz, (high < nz) & (zi > 0), 0),
            (low, low >= 0, (low >= 0) & (zi < nz - 1), 1),
        )

    def send(conv, s):
        for k, _, passed, way in moves(s):
            @pl.when(passed)
            def _():
                z_copy(conv, k, way).start()

    def receive(conv, s):
        for k, held, _, way in moves(s):
            @pl.when(held)
            def _():
                z_copy(conv, k, way).wait_recv()
                core_copy(conv, k, core).start()

    t_send(0)
    for q in range(cams):
        tc_copy(zi, core, q).start()
    for conv in range(2):
        w_ref[conv, me, :, 9 * CH :] = ext
    count = rows // piece

    def pack(i, carry):
        @pl.when(i + 1 < count)
        def _():
            enc_load(i + 1).start()

        enc_load(i).wait()
        for conv in range(2):
            w_ref[conv, me, pl.ds(pl.multiple_of(i * piece, piece), piece), 0 : 9 * CH] = (
                enc_buf[i % 2, :, conv, :].astype(bf16)
            )
        return carry

    lax.fori_loop(0, count, pack, 0)

    def x_save(p):
        return pltpu.make_async_copy(x_ref.at[:, p * CH : (p + 1) * CH], x_out.at[p], xsem.at[p])

    fill_edges(pad_t)
    moved = traj_ref[...].astype(f32)
    for f in range(nf):
        pad_t[edge + f * ns : edge + (f + 1) * ns, :] = moved[:, f].astype(bf16)
    moved = og_in[...].astype(f32)
    for f in range(nf // 2):
        og_ref[f * ns : (f + 1) * ns, :] = moved[:, f].astype(bf16)
    half = n_img // 2
    for p in range(9):
        pair = img_ref[:, p].astype(f32)
        for o in range(2):
            x_ref[o * half : (o + 1) * half, p * CH : (p + 1) * CH] = pair[:, o].astype(bf16)
        x_save(p).start()
    for conv in range(2):
        core_copy(conv, zi, core).start()

    def t_step(s, carry):
        @pl.when(s == nz - 1)
        def _():
            send(0, 0)

        t_receive(s)

        @pl.when(s < nz - 1)
        def _():
            t_send(s)
        return carry

    lax.fori_loop(1, nz, t_step, 0)

    def rows_of(conv, j, start, wide):
        block = w_ref[conv, pl.ds(j * spb, spb), :, start : start + wide]
        return block.reshape(BLK, wide)

    def w_save(conv, j):
        part = pl.ds(j * spb, spb)
        return pltpu.make_async_copy(w_ref.at[conv, part], w_out.at[conv, part], wsem.at[conv, j])

    def conv_norm(src_ref, conv, z_ref, r_ref, j):
        lanes = pl.ds(pl.multiple_of(j * BLK, BLK), BLK)
        total = None
        for p in range(9):
            r, c = divmod(p, 3)
            bs = span(c)
            acc = None
            for a in span(r):
                start = (3 * (r + a - 1) + c + bs[0] - 1) * CH
                wide = len(bs) * CH
                part = dot(src_ref[:, start : start + wide], rows_of(conv, j, (3 * a + bs[0]) * CH, wide), NT)
                acc = part if acc is None else acc + part
            z_ref[p, :, lanes] = acc
            total = acc if total is None else total + acc
        mean = group_sum(total, ones) * inv_n
        var = None
        for p in range(9):
            centred = z_ref[p, :, lanes] - mean
            sq = centred * centred
            var = sq if var is None else var + sq
        rstd = lax.rsqrt(group_sum(var, ones) * inv_n + norm_eps)
        r_ref[:, lanes] = rstd
        return lanes, mean, rstd

    def first(j):
        aff_ref[:, lanes_of(j)] = jnp.transpose(rows_of(0, j, 9 * CH, BLK).astype(f32))[0:8]
        lanes, mean, rstd = conv_norm(x_ref, 0, z1_ref, r1_ref, j)
        gain, offset = aff_ref[0:1, lanes], aff_ref[1:2, lanes]
        for p in range(9):
            z = (z1_ref[p, :, lanes] - mean) * rstd
            z1_ref[p, :, lanes] = z
            u = z * gain + offset
            a_ref[:, pl.ds(pl.multiple_of(p * CH + j * BLK, BLK), BLK)] = (u * sigmoid(u)).astype(bf16)

    def second(j):
        lanes, mean, rstd = conv_norm(a_ref, 1, z2_ref, r2_ref, j)
        gain, offset = aff_ref[2:3, lanes], aff_ref[3:4, lanes]
        total = None
        for p in range(9):
            z = (z2_ref[p, :, lanes] - mean) * rstd
            z2_ref[p, :, lanes] = z
            pic = x_ref[:, pl.ds(pl.multiple_of(p * CH + j * BLK, BLK), BLK)].astype(f32)
            u = z * gain + offset + pic
            act = u * sigmoid(u)
            total = act if total is None else total + act
        out = (total * (1.0 / 9.0)).astype(bf16)
        feat_ref[:, :, :, lanes] = out.reshape(feat_ref.shape[:3] + (BLK,))

    def lanes_of(j):
        return pl.ds(pl.multiple_of(j * BLK, BLK), BLK)

    def arrived(conv, k):
        core_copy(conv, k, 1 - core).wait_recv()

    def phase(conv, block):
        streaming = spb == 2

        def step(s, carry):
            if conv == 0:
                @pl.when((s > 0) & (s < nz - 1))
                def _():
                    send(0, s)

                @pl.when(s == nz - 1)
                def _():
                    send(1, 0)
            else:
                @pl.when((s > 0) & (s < nz - 1))
                def _():
                    send(1, s)

            def side(d, carry):
                k = zi + s - 2 * s * d

                @pl.when((k >= 0) & (k < nz) & (s + 1 > d))
                def _():
                    arrived(conv, k)
                    if streaming:
                        w_save(conv, k).start()
                        block(k)
                return carry

            lax.fori_loop(0, 2, side, 0)
            if conv == 1:
                t_collect(2 * s)
                t_collect(2 * s + 1)

                @pl.when(s == nz - 2)
                def _():
                    t_complete()
                    saves[0].wait()
                    temporal_early()

            @pl.when(s < nz - 1)
            def _():
                receive(conv, s + 1)
            return carry

        lax.fori_loop(0, nz, step, 0)
        if not streaming:
            def rest(j, carry):
                w_save(conv, j).start()
                block(j)
                return carry

            lax.fori_loop(0, CH // BLK, rest, 0)

    phase(0, first)
    saves = [pltpu.make_async_copy(z1_ref, z1_out, osem.at[0])]
    saves += [
        pltpu.make_async_copy(a_ref.at[:, p * CH : (p + 1) * CH], a_out.at[p], osem.at[2 + p])
        for p in range(9)
    ]
    for save in saves:
        save.start()
    phase(1, second)
    last = pltpu.make_async_copy(z2_ref, z2_out, osem.at[1])
    last.start()

    def feat_copy(to, sender):
        return cam_copy(feat_ref.at[:, to], arr_s.at[sender], fsend.at[to], frecv.at[sender], to)

    for step in range(1, cams):
        feat_copy((cam + step) % cams, cam).start()
    arr_s[cam] = feat_ref[:, cam]
    for step in range(1, cams):
        other = (cam + step) % cams
        feat_copy(other, other).wait_recv()
    temporal_rest()
    for step in range(1, cams):
        feat_copy((cam + step) % cams, cam).wait_send()

    for conv in range(2):
        def drain(k, carry):
            s = k - zi

            @pl.when((s >= 0) & (s < nz - 1) & (zi > 0))
            def _():
                z_copy(conv, k, 0).wait_send()

            @pl.when((s <= 0) & (s > 1 - nz) & (zi < nz - 1))
            def _():
                z_copy(conv, k, 1).wait_send()

            core_copy(conv, k, core).wait_send()
            return carry

        lax.fori_loop(0, nz, drain, 0)

        def saved(j, carry):
            w_save(conv, j).wait()
            return carry

        lax.fori_loop(0, CH // BLK, saved, 0)
    for save in saves[1:]:
        save.wait()
    last.wait()

    def t_drain(k, carry):
        s = k - zi

        @pl.when((s >= 0) & (s < nz - 1) & (zi > 0))
        def _():
            tz_copy(k, 0).wait_send()

        @pl.when((s <= 0) & (s > 1 - nz) & (zi < nz - 1))
        def _():
            tz_copy(k, 1).wait_send()

        @pl.when(s != 0)
        def _():
            for step in range(1, cams):
                tp_copy(k, step, cam).wait_send()

        for q in range(cams):
            tc_copy(k, core, q).wait_send()
        return carry

    lax.fori_loop(0, nz, t_drain, 0)
    for p in range(9):
        x_save(p).wait()
    for step in range(1, cams):
        view_copy((cam + step) % cams, cam).wait_send()


def enc_bwd_kernel(
    n, cams, cond, x_hbm, a_hbm, w_hbm, z1_hbm, r1_ref, z2_hbm, r2_ref, aff_ref, gp_ref, dt_hbm,
    ig_ref, genc_ref, gaff_ref, gconvs_ref, gfilm_ref, gskip_ref, gdown_ref, gblk_ref,
    x_ref, a_ref, w_ref, z1_ref, z2_ref, g_ref, gt_ref, ag_ref,
    dwf, core_out, core_in, slots, t_own, t_sum, t_peer, t_slots, t_all,
    lsem, csend, crecv, zsend, zrecv,
    tlsem, tcsend, tcrecv, tpsend, tprecv, tzsend, tzrecv, tfsend, tfrecv,
):
    nz = n // 2
    rows = CH // n
    n_img = z1_ref.shape[1]
    me, cam = lax.axis_index("batch"), lax.axis_index("cam")
    zi, core = me // 2, me % 2
    partner = me + 1 - 2 * core
    ones = group_ones(BLK, ENC_GROUP)
    inv_n = 1.0 / (9 * ENC_GROUP)
    chunk = 3 * CH

    def load_w(conv):
        return pltpu.make_async_copy(w_hbm.at[conv, :, :, 0 : 9 * CH], w_ref, lsem.at[3])

    loads = {
        "z2": pltpu.make_async_copy(z2_hbm, z2_ref, lsem.at[0]),
        "z1": pltpu.make_async_copy(z1_hbm, z1_ref, lsem.at[1]),
        "a": pltpu.make_async_copy(a_hbm, a_ref, lsem.at[2]),
    }
    x_loads = [pltpu.make_async_copy(x_hbm, x_ref, lsem.at[4])]
    loads["z2"].start()
    for load in x_loads:
        load.start()
    loads["a"].start()
    load_w(1).start()
    loads["z1"].start()

    def own_load(i):
        return pltpu.make_async_copy(dt_hbm.at[i // cams, core, i % cams], t_own.at[i % 2], tlsem.at[i])

    own_load(0).start()

    line_greet(cams, nz)

    def t_core(k):
        return batch_copy(dt_hbm.at[k, 1 - core], t_sum.at[k], tcsend.at[k], tcrecv.at[k], partner)

    def t_peers(k, step):
        to = (cam + step) % cams
        return cam_copy(t_sum.at[k, to], t_peer.at[step - 1, k], tpsend.at[step - 1, k], tprecv.at[step - 1, k], to)

    def t_start(k, carry):
        t_core(k).start()
        return carry

    def t_spread(lo, hi):
        def body(k, carry):
            t_core(k).wait_recv()

            def quarter(q, carry):
                i = k * cams + q

                @pl.when(i + 1 < nz * cams)
                def _():
                    own_load(i + 1).start()

                own_load(i).wait()
                t_sum[k, q] = (t_sum[k, q].astype(f32) + t_own[i % 2].astype(f32)).astype(bf16)
                return carry

            lax.fori_loop(0, cams, quarter, 0)
            for step in range(1, cams):
                t_peers(k, step).start()
            return carry

        lax.fori_loop(lo, hi, body, 0)

    ag_ref[...] = jnp.zeros_like(ag_ref)
    for load in x_loads:
        load.wait()
    loads["z2"].wait()

    def lanes_of(j):
        return pl.ds(pl.multiple_of(j * BLK, BLK), BLK)

    def norm_back(du_ref, z_ref, r_ref, j, gain, row):
        lanes = lanes_of(j)
        s0 = jnp.zeros((n_img, BLK), f32)
        s1 = jnp.zeros((n_img, BLK), f32)
        for p in range(9):
            du = du_ref[p, :, lanes]
            s0 = s0 + du
            s1 = s1 + du * z_ref[p, :, lanes]
        ag_ref[row : row + 1, lanes] = jnp.sum(s1, axis=0, keepdims=True)
        ag_ref[row + 1 : row + 2, lanes] = jnp.sum(s0, axis=0, keepdims=True)
        m0 = group_sum(s0 * gain, ones) * inv_n
        m1 = group_sum(s1 * gain, ones) * inv_n
        rstd = r_ref[:, lanes]
        for p in range(9):
            dv = (du_ref[p, :, lanes] * gain - m0 - z_ref[p, :, lanes] * m1) * rstd
            g_ref[p, :, lanes] = dv.astype(bf16)
            gt_ref[lanes, p * n_img : (p + 1) * n_img] = jnp.transpose(dv).astype(bf16)

    def second(j, carry):
        lanes = lanes_of(j)
        gain, offset = aff_ref[2:3, lanes], aff_ref[3:4, lanes]
        pooled = gp_ref[:, :, :, lanes].reshape(n_img, BLK).astype(f32) * (1.0 / 9.0)
        for p in range(9):
            u = z2_ref[p, :, lanes] * gain + offset + x_ref[p, :, lanes].astype(f32)
            s = sigmoid(u)
            ig_ref[p, :, lanes] = pooled * (s * (1.0 + u * (1.0 - s)))
        norm_back(ig_ref, z2_ref, r2_ref, j, gain, 2)
        return carry

    def first(j, carry):
        lanes = lanes_of(j)
        gain, offset = aff_ref[0:1, lanes], aff_ref[1:2, lanes]
        for p in range(9):
            u = z1_ref[p, :, lanes] * gain + offset
            s = sigmoid(u)
            z2_ref[p, :, lanes] = z2_ref[p, :, lanes] * (s * (1.0 + u * (1.0 - s)))
        norm_back(z2_ref, z1_ref, r1_ref, j, gain, 0)
        return carry

    def width(k):
        return chunk + BLK if k == 5 else chunk

    def core_copy(k):
        cols = pl.ds(0, width(k))
        return batch_copy(
            core_out.at[k % 2, :, :, cols], core_in.at[k % 3, :, :, cols], csend.at[k], crecv.at[k], partner
        )

    def keep(k, d0, lane, v):
        count, wide = v.shape[0] // (2 * rows), v.shape[1]
        parts = v.reshape(count, 2, rows, wide)
        even, odd = parts[:, 0], parts[:, 1]
        dwf[k % 2, d0 : d0 + count, :, lane : lane + wide] = jnp.where(core == 0, even, odd)
        core_out[k % 2, d0 : d0 + count, :, lane : lane + wide] = jnp.where(core == 0, odd, even).astype(bf16)

    def make_chunk(k):
        if k >= 2:
            core_copy(k - 2).wait_send()
        src_ref = a_ref if k < 3 else x_ref
        a = k % 3
        r_lo, r_hi = max(0, 1 - a), min(2, 3 - a)
        for b in range(3):
            c_lo, c_hi = max(0, 1 - b), min(2, 3 - b)
            if b == 1:
                runs = [(3 * r_lo, 3 * (r_hi - r_lo + 1))]
            else:
                runs = [(3 * r + c_lo, c_hi - c_lo + 1) for r in range(r_lo, r_hi + 1)]
            shift = 3 * (a - 1) + b - 1
            for half in range(2):
                acc = None
                for p, m in runs:
                    part = dot(
                        gt_ref[half * 256 : half * 256 + 256, p * n_img : (p + m) * n_img],
                        src_ref[p + shift : p + shift + m].reshape(m * n_img, CH),
                    )
                    acc = part if acc is None else acc + part
                keep(k, half * nz // 2, b * CH, acc)
        if k == 5:
            keep(k, 0, chunk, jnp.transpose(ag_ref[...]))
        core_copy(k).start()

    def term(k, d):
        return dwf[k % 2, d, :, 0 : width(k)] + core_in[k % 3, d, :, 0 : width(k)].astype(f32)

    def line_copy(k, way, s):
        if k == 6:
            return batch_copy(
                t_slots.at[way, s - 1], t_slots.at[way, s], tzsend.at[way, s], tzrecv.at[way, s], me - 2 + 4 * way
            )
        cols = pl.ds(0, width(k))
        return batch_copy(
            slots.at[k % 3, way, s - 1, :, cols], slots.at[k % 3, way, s, :, cols],
            zsend.at[k, way, s], zrecv.at[k, way, s], me - 2 + 4 * way,
        )

    def slot(k, way, s):
        return t_slots.at[way, s] if k == 6 else slots.at[k % 3, way, s, :, pl.ds(0, width(k))]

    def t_term(d):
        total = t_sum[d, cam].astype(f32)
        for step in range(1, cams):
            total = total + t_peer[step - 1, d].astype(f32)
        return total

    def serve(k, s):
        for way in range(2):
            ahead = zi if way else nz - 1 - zi
            d = nz - s + zi if way else s - nz + zi
            ref = slot(k, way, s - 1)

            @pl.when((ahead < nz - 1) & (s > ahead))
            def _():
                own = t_term(d) if k == 6 else term(k, d)

                @pl.when(ahead > 0)
                def _():
                    line_copy(k, way, s - 1).wait_recv()
                    ref[...] = (ref[...].astype(f32) + own).astype(bf16)

                @pl.when(ahead == 0)
                def _():
                    ref[...] = own.astype(bf16)

                line_copy(k, way, s).start()

    def steps(k, part):
        lo, hi = 1 + part * (nz - 1) // 3, 1 + (part + 1) * (nz - 1) // 3
        if hi - lo == 1:
            serve(k, lo)
        elif hi > lo:
            def body(s, carry):
                serve(k, s)
                return carry

            lax.fori_loop(lo, hi, body, 0)

    def service(g):
        k, part = divmod(g, 3)
        if part == 0:
            core_copy(k).wait_recv()
        steps(k, part)

    def collect(k, total, write):
        last = nz - 1

        @pl.when(zi > 0)
        def _():
            line_copy(k, 1, last).wait_recv()

        @pl.when(zi < nz - 1)
        def _():
            line_copy(k, 0, last).wait_recv()

        @pl.when(zi == 0)
        def _():
            write(total + slot(k, 0, last)[...].astype(f32))

        @pl.when(zi == nz - 1)
        def _():
            write(total + slot(k, 1, last)[...].astype(f32))

        @pl.when((zi > 0) & (zi < nz - 1))
        def _():
            write(total + slot(k, 0, last)[...].astype(f32) + slot(k, 1, last)[...].astype(f32))

        def drain(s, carry):
            for way in range(2):
                ahead = zi if way else nz - 1 - zi

                @pl.when((ahead < nz - 1) & (s > ahead))
                def _():
                    line_copy(k, way, s).wait_send()
            return carry

        lax.fori_loop(1, nz, drain, 0)

    def finish(k):
        def write(v):
            genc_ref[:, 1 - k // 3, (k % 3) * chunk : (k % 3 + 1) * chunk] = v[:, 0:chunk]
            if k == 5:
                gaff_ref[...] = jnp.transpose(v[:, chunk:])[0 : gaff_ref.shape[0]]

        collect(k, term(k, zi), write)

    def t_arrived():
        for step in range(1, cams):
            def body(k, carry):
                t_peers(k, step).wait_recv()
                return carry

            lax.fori_loop(0, nz, body, 0)

    def t_final(to, sender):
        return cam_copy(t_all.at[cam], t_all.at[sender], tfsend.at[to], tfrecv.at[sender], to)

    def t_finish():
        def write(v):
            t_all[cam] = v.astype(bf16)

        collect(6, t_term(zi), write)
        for step in range(1, cams):
            t_final((cam + step) % cams, cam).start()

    def t_write():
        for step in range(1, cams):
            other = (cam + step) % cams
            t_final(other, other).wait_recv()

        def cut(q, lo, wide):
            return t_all[q, :, lo : lo + wide].astype(f32)

        for which in range(2):
            gconvs_ref[:, which, :] = cut(which, 0, PART)
            gfilm_ref[:, which, :] = cut(2, which * cond, cond)
        gblk_ref[...] = jnp.transpose(cut(2, 2 * cond, BLK))[0 : gblk_ref.shape[0]]
        gskip_ref[...] = cut(3, 0, CH)
        gdown_ref[...] = cut(3, CH, 3 * CH)

    def input_back(q):
        r, c = divmod(q, 3)
        acc = None
        for a in range(3):
            for b in range(3):
                pr, pc = r - a + 1, c - b + 1
                if 0 <= pr < 3 and 0 <= pc < 3:
                    t = 3 * a + b
                    w = w_ref[:, :, t * CH : (t + 1) * CH].reshape(CH, CH)
                    part = dot(g_ref[3 * pr + pc], w)
                    acc = part if acc is None else acc + part
        return acc

    def back_second(*qs):
        for q in qs:
            if q == 0:
                load_w(1).wait()
            z2_ref[q] = input_back(q)
            if q == 8:
                load_w(0).start()

    def back_first(*qs):
        for q in qs:
            if q == 0:
                load_w(0).wait()
            ig_ref[q] = ig_ref[q] + input_back(q)

    lax.fori_loop(0, 1, second, 0)
    line_wait(cams, nz)
    lax.fori_loop(0, nz, t_start, 0)
    lax.fori_loop(1, CH // BLK, second, 0)
    loads["a"].wait()
    make_chunk(0)
    service(0)
    t_spread(0, nz // 2)
    make_chunk(1)
    service(1)
    t_spread(nz // 2, nz)
    back_second(0, 1, 2)
    service(2)
    back_second(3, 4)
    service(3)
    finish(0)
    make_chunk(2)
    service(4)
    back_second(5, 6)
    service(5)
    back_second(7, 8)
    service(6)
    finish(1)
    loads["z1"].wait()
    lax.fori_loop(0, 2, first, 0)
    service(7)
    lax.fori_loop(2, 4, first, 0)
    service(8)
    make_chunk(3)
    service(9)
    finish(2)
    make_chunk(4)
    service(10)
    back_first(0, 1)
    service(11)
    back_first(2, 3)
    service(12)
    finish(3)
    make_chunk(5)
    service(13)
    back_first(4, 5)
    service(14)
    t_arrived()
    steps(6, 0)
    finish(4)
    back_first(6)
    steps(6, 1)
    back_first(7)
    steps(6, 2)
    back_first(8)
    service(15)
    t_finish()
    service(16)
    service(17)
    t_write()
    finish(5)

    def t_drain(k, carry):
        t_core(k).wait_send()
        for step in range(1, cams):
            t_peers(k, step).wait_send()
        return carry

    lax.fori_loop(0, nz, t_drain, 0)
    for step in range(1, cams):
        t_final((cam + step) % cams, cam).wait_send()
    core_copy(4).wait_send()
    core_copy(5).wait_send()


def call(kernel, outs, in_specs, out_specs, scratch=(), collective_id=None, cost=None):
    extra = {} if collective_id is None else dict(collective_id=collective_id, has_side_effects=True)
    return pl.pallas_call(
        kernel,
        out_shape=[jax.ShapeDtypeStruct(s, d) for s, d in outs],
        in_specs=in_specs,
        out_specs=out_specs,
        scratch_shapes=list(scratch),
        compiler_params=pltpu.CompilerParams(vmem_limit_bytes=VMEM_BYTES, **extra),
        cost_estimate=cost,
    )


def work(microseconds):
    return pl.CostEstimate(
        flops=int(microseconds * 1e9), bytes_accessed=int(microseconds * 3e6), transcendentals=0
    )


V = pl.BlockSpec(memory_space=pltpu.VMEM)
H = pl.BlockSpec(memory_space=pl.ANY)
DMA = pltpu.SemaphoreType.DMA


def time_embed(steps_given, embed_width):
    half_width = embed_width // 2
    frequency = jnp.exp(
        jnp.arange(half_width, dtype=jnp.float32) * (-math.log(10000.0) / (half_width - 1))
    )
    argument = steps_given.astype(jnp.float32)[:, None] * frequency[None, :]
    return jnp.concatenate([jnp.sin(argument), jnp.cos(argument)], axis=1)


def adamw(weight, gradient, moment_one, moment_two, step_rate, weight_decay):
    mean_new = beta_first * moment_one + (1.0 - beta_first) * gradient
    square_new = beta_second * moment_two + (1.0 - beta_second) * gradient * gradient
    mean_hat = mean_new / (1.0 - beta_first**STEP)
    square_hat = square_new / (1.0 - beta_second**STEP)
    weight_new = weight - step_rate * (
        mean_hat / (jnp.sqrt(square_hat) + adam_eps) + weight_decay * weight
    )
    return (weight_new, mean_new, square_new)


def adam_kernel(*refs):
    for i in range(7):
        w_ref, m_ref, v_ref, g_ref = refs[4 * i : 4 * i + 4]
        outs = refs[28 + 3 * i : 31 + 3 * i]

        def update():
            vector = i in (1, 6)
            rate, decay = (rate_vector, 0.0) if vector else (rate_matrix, decay_matrix)
            new = adamw(w_ref[...], g_ref[...], m_ref[...], v_ref[...], rate, decay)
            for ref, value in zip(outs, new):
                ref[...] = value

        if i in (1, 6):
            pl.when(pl.program_id(0) == 0)(update)
        else:
            update()


def adam_call(shown, grads, rows):
    step = min(rows, 8)

    def spec(v):
        if v.shape[0] != rows:
            return pl.BlockSpec(v.shape, lambda r: (0, 0))
        return pl.BlockSpec((step,) + v.shape[1:], lambda r: (r,) + (0,) * (v.ndim - 1))

    ins = []
    for i in range(7):
        ins += [shown[0][i], shown[1][i], shown[2][i], grads[i]]
    outs = [w for w in shown[0] for _ in range(3)]
    return pl.pallas_call(
        adam_kernel,
        grid=(rows // step,),
        out_shape=[jax.ShapeDtypeStruct(v.shape, f32) for v in outs],
        in_specs=[spec(v) for v in ins],
        out_specs=[spec(v) for v in outs],
        compiler_params=pltpu.CompilerParams(vmem_limit_bytes=VMEM_BYTES),
        cost_estimate=work(12),
    )(*ins)


def shards(
    n, images, trajectory, view_mask, timesteps, out_grad,
    encoder_weight, encoder_affine, block_convs, film_weight, skip_weight, down_weight, block_affine,
    first_encoder, first_affine, first_convs, first_film, first_skip, first_down, first_block,
    second_encoder, second_affine, second_convs, second_film, second_skip, second_down, second_block,
):
    ns, nf, ch = trajectory.shape
    cams, obs = images.shape[1], images.shape[3]
    n_img = cams * images.shape[2] * obs
    nz, per = n // 2, ch // n
    cond = film_weight.shape[2]
    wide = 9 * ch
    rows = nf * ns

    def turned(v):
        return jnp.transpose(v.reshape(v.shape[-2:]))

    pairs = jnp.transpose(images[0], (0, 1, 3, 2, 4)).reshape(n_img // obs, 9, obs, ch)
    pos = (9, n_img, ch)
    t_shape = (nz, 2, cams, per, PART)
    wcols = wide + BLK
    z1, r1, act, z2, r2, w_all, enc_aff, x, out_fm, tg_fm, gp, dt = call(
        functools.partial(forward_kernel, n, cams),
        [(pos, f32), ((n_img, ch), f32), (pos, bf16), (pos, f32), ((n_img, ch), f32), ((2, n, per, wcols), bf16),
         ((8, ch), f32), (pos, bf16), ((rows // 2, ch), bf16), ((rows, ch), f32), ((obs, cams, ns, ch), bf16),
         (t_shape, bf16)],
        [V, V, V, V, V, H, V, V, V, V, V, V],
        [H, V, H, H, V, H, V, H, V, V, V, H],
        [pltpu.VMEM((n_img, wide), bf16), pltpu.VMEM((2, n, per, wcols), bf16), pltpu.VMEM(pos, f32),
         pltpu.VMEM((n_img, wide), bf16), pltpu.VMEM(pos, f32), pltpu.VMEM((obs, cams, ns, ch), bf16),
         pltpu.VMEM((cams, obs, ns, ch), bf16), pltpu.VMEM(t_shape, bf16), pltpu.VMEM((2, min(per, 16), 2, wide), f32),
         pltpu.VMEM((BLK, per), f32), pltpu.VMEM((rows // 2, ch), bf16), pltpu.VMEM((rows + 4 * ns, ch), bf16),
         pltpu.VMEM((rows + 4 * ns, ch), bf16), pltpu.VMEM((rows + 4 * ns, ch), bf16), pltpu.VMEM((rows + ns, ch), bf16),
         pltpu.VMEM((BLK, ch), f32), pltpu.VMEM((BLK, ch), f32), pltpu.VMEM((ns, ch), f32),
         pltpu.VMEM((cams, obs, ns, ch), bf16), pltpu.VMEM((obs, cams, ns, ch), bf16),
         pltpu.VMEM((2, nz, 2, per, PART), bf16),
         DMA((2, 2, nz)), DMA((2, nz)), DMA((2, nz)), DMA((2, nz)), DMA((2, ch // BLK)), DMA((11,)),
         DMA((cams,)), DMA((cams,)),
         DMA((2, nz)), DMA((nz,)), DMA((nz, cams)), DMA((nz, cams)), DMA((cams - 1, nz)), DMA((cams - 1, nz)),
         DMA((max(per // 16, 1),)), DMA((9,)), DMA((cams,)), DMA((cams,)), DMA((4,))],
        collective_id=0,
        cost=work(130),
    )(pairs, trajectory, out_grad, view_mask.astype(f32), time_embed(timesteps, TEMB), encoder_weight[0], block_convs,
      film_weight, skip_weight, down_weight, turned(encoder_affine), turned(block_affine))
    block_output = jnp.transpose(out_fm.reshape(nf // 2, ns, ch), (1, 0, 2))
    trajectory_grad = jnp.transpose(tg_fm.reshape(nf, ns, ch), (1, 0, 2))

    chunk = 3 * ch + BLK
    ig, genc, gaff, gconvs, gfilm, gskip, gdown, gblk = call(
        functools.partial(enc_bwd_kernel, n, cams, cond),
        [(pos, f32), ((per, 2, wide), f32), ((4, per), f32), ((per, 2, 5 * ch), f32),
         ((per, 2, cond), f32), ((per, ch), f32), ((per, 3 * ch), f32), ((10, per), f32)],
        [H, H, H, H, V, H, V, V, V, H],
        [V] * 8,
        [pltpu.VMEM(pos, bf16), pltpu.VMEM(pos, bf16), pltpu.VMEM((n, per, wide), bf16), pltpu.VMEM(pos, f32),
         pltpu.VMEM(pos, f32), pltpu.VMEM(pos, bf16), pltpu.VMEM((ch, 9 * n_img), bf16),
         pltpu.VMEM((BLK, ch), f32),
         pltpu.VMEM((2, nz, per, chunk), f32), pltpu.VMEM((2, nz, per, chunk), bf16),
         pltpu.VMEM((3, nz, per, chunk), bf16), pltpu.VMEM((3, 2, nz, per, chunk), bf16),
         pltpu.VMEM((2, per, PART), bf16), pltpu.VMEM((nz, cams, per, PART), bf16),
         pltpu.VMEM((cams - 1, nz, per, PART), bf16), pltpu.VMEM((2, nz, per, PART), bf16),
         pltpu.VMEM((cams, per, PART), bf16),
         DMA((13,)), DMA((6,)), DMA((6,)), DMA((6, 2, nz)), DMA((6, 2, nz)),
         DMA((nz * cams,)), DMA((nz,)), DMA((nz,)), DMA((cams - 1, nz)), DMA((cams - 1, nz)),
         DMA((2, nz)), DMA((2, nz)), DMA((cams,)), DMA((cams,))],
        collective_id=1,
        cost=work(100),
    )(x, act, w_all, z1, r1, z2, r2, enc_aff, gp, dt)
    images_grad = jnp.transpose(ig.reshape((9, obs) + images.shape[1:3] + (ch,)), (2, 3, 1, 0, 4))[None]

    weights = (encoder_weight, encoder_affine, block_convs, film_weight, skip_weight, down_weight, block_affine)
    firsts = (first_encoder, first_affine, first_convs, first_film, first_skip, first_down, first_block)
    seconds = (second_encoder, second_affine, second_convs, second_film, second_skip, second_down, second_block)
    shown = [
        [turned(v) if i in (1, 6) else v.reshape(v.shape[-3:]) if i == 0 else v for i, v in enumerate(group)]
        for group in (weights, firsts, seconds)
    ]
    news = adam_call(shown, (genc, gaff, gconvs, gfilm, gskip, gdown, gblk), per)
    upd = [
        tuple((turned(v) if i in (1, 6) else v).reshape(w.shape) for v in news[3 * i : 3 * i + 3])
        for i, w in enumerate(weights)
    ]
    return (
        (block_output, trajectory_grad, images_grad)
        + tuple(u[0] for u in upd)
        + tuple(u[1] for u in upd)
        + tuple(u[2] for u in upd)
    )


def solution(mesh):
    sample = P(("cam", "batch"))
    params = (P("cam", "batch"), P("cam", "batch")) + (P("batch"),) * 5
    images_spec = P("cam", None, "batch")
    return jax.shard_map(
        functools.partial(shards, mesh.shape["batch"]),
        mesh=mesh,
        in_specs=(images_spec, sample, sample, sample, sample) + params * 3,
        out_specs=(sample, sample, images_spec) + params * 3,
        check_vma=False,
    )
```

```python
import functools
import math

import jax
import jax.numpy as jnp
from jax import lax
from jax.experimental import pallas as pl
from jax.experimental.pallas import tpu as pltpu
from jax.sharding import PartitionSpec as P

TEMB = 128
GROUPS = 8
STEP = 5

norm_eps = 1e-05
beta_first = 0.5
beta_second = 0.5
adam_eps = 1e-08
rate_matrix = 0.02
rate_vector = 0.2
decay_matrix = 0.01

CH = 512
BLK = 128
ENC_GROUP = 16
f32 = jnp.float32
bf16 = jnp.bfloat16
VMEM_BYTES = 61 * 1024 * 1024

NT = (((1,), (1,)), ((), ()))
NN = (((1,), (0,)), ((), ()))
TN = (((0,), (0,)), ((), ()))


def dot(a, b, dims=NN):
    return lax.dot_general(a, b, dims, preferred_element_type=f32)


def group_ones(width, group):
    rows = lax.broadcasted_iota(jnp.int32, (width, width), 0) // group
    cols = lax.broadcasted_iota(jnp.int32, (width, width), 1) // group
    return jnp.where(rows == cols, 1.0, 0.0).astype(bf16)


def group_sum(v, ones):
    high = v.astype(bf16)
    rest = v - high.astype(f32)
    middle = rest.astype(bf16)
    low = (rest - middle.astype(f32)).astype(bf16)
    return dot(high, ones) + dot(middle, ones) + dot(low, ones)


def sigmoid(v):
    return 1.0 / (1.0 + jnp.exp(-v))


def mish_pair(v):
    e = jnp.exp(jnp.minimum(v, 20.0))
    n = e * (e + 2.0)
    inv = 1.0 / (n + 2.0)
    t = n * inv
    return v * t, t + v * (4.0 * e * (1.0 + e)) * inv * inv


def mish_value(v):
    e = jnp.exp(jnp.minimum(v, 20.0))
    n = e * (e + 2.0)
    return v * (n / (n + 2.0))


def span(i):
    return range(max(0, 1 - i), min(2, 3 - i) + 1)


MESH = pl.DeviceIdType.MESH


def batch_copy(src, dst, send_sem, recv_sem, target):
    return pltpu.make_async_remote_copy(
        src_ref=src, dst_ref=dst, send_sem=send_sem, recv_sem=recv_sem,
        device_id={"batch": target}, device_id_type=MESH,
    )


def cam_copy(src, dst, send_sem, recv_sem, target):
    return pltpu.make_async_remote_copy(
        src_ref=src, dst_ref=dst, send_sem=send_sem, recv_sem=recv_sem,
        device_id={"cam": target}, device_id_type=MESH,
    )


def line_barrier(cams, nz):
    line_greet(cams, nz)
    line_wait(cams, nz)


def line_wait(cams, nz):
    zi = lax.axis_index("batch") // 2
    ends = (zi == 0).astype(jnp.int32) + (zi == nz - 1).astype(jnp.int32)
    pl.semaphore_wait(pltpu.get_barrier_semaphore(), cams + 2 - ends)


def line_greet(cams, nz):
    me, cam = lax.axis_index("batch"), lax.axis_index("cam")
    zi, core = me // 2, me % 2
    barrier = pltpu.get_barrier_semaphore()
    pl.semaphore_signal(barrier, inc=1, device_id={"batch": me + 1 - 2 * core}, device_id_type=MESH)
    for step in range(1, cams):
        pl.semaphore_signal(barrier, inc=1, device_id={"cam": (cam + step) % cams}, device_id_type=MESH)

    @pl.when(zi > 0)
    def _():
        pl.semaphore_signal(barrier, inc=1, device_id={"batch": me - 2}, device_id_type=MESH)

    @pl.when(zi < nz - 1)
    def _():
        pl.semaphore_signal(barrier, inc=1, device_id={"batch": me + 2}, device_id_type=MESH)


PART = 5 * CH


def pack_temporal(ref, convs_ref, film_ref, skip_ref, down_ref, ext):
    rows, cond = film_ref.shape[0], film_ref.shape[2]
    for q in range(2):
        ref[q] = convs_ref[:, q, :].astype(bf16)
        ref[2, :, q * cond : (q + 1) * cond] = film_ref[:, q, :].astype(bf16)
    ref[2, :, 2 * cond : 2 * cond + BLK] = ext
    ref[2, :, 2 * cond + BLK :] = jnp.zeros((rows, PART - 2 * cond - BLK), bf16)
    ref[3, :, 0:CH] = skip_ref[...].astype(bf16)
    ref[3, :, CH : 4 * CH] = down_ref[...].astype(bf16)
    ref[3, :, 4 * CH :] = jnp.zeros((rows, PART - 4 * CH), bf16)


def forward_kernel(
    n, cams, img_ref, traj_ref, og_in, mask_ref, emb_ref, enc_hbm, convs_ref, film_ref, skip_ref, down_ref,
    ea_ref, ba_ref,
    z1_out, r1_ref, a_out, z2_out, r2_ref, w_out, aff_ref, x_out, out_ref, tg_ref, gp_ref, dt_out,
    x_ref, w_ref, z1_ref, a_ref, z2_ref, feat_ref, arr_s, t_ref, enc_buf,
    ext_s, og_ref, pad_t, pad_m, pad_h, sum_ref, taff_ref, ag_ref, rstd_ref, dviews_ref, gp_s, dt_buf,
    zsend, zrecv, csend, crecv, wsem, osem, fsend, frecv,
    tzsend, tzrecv, tcsend, tcrecv, tpsend, tprecv, esem, xsem, vsend, vrecv, dsem,
):
    nz = n // 2
    rows = skip_ref.shape[0]
    piece = enc_buf.shape[1]
    spb = BLK // rows
    n_img = x_ref.shape[0]
    me, cam = lax.axis_index("batch"), lax.axis_index("cam")
    zi, core = me // 2, me % 2
    partner = me + 1 - 2 * core
    ones = group_ones(BLK, ENC_GROUP)
    inv_n = 1.0 / (9 * ENC_GROUP)

    def enc_load(i):
        return pltpu.make_async_copy(enc_hbm.at[pl.ds(i * piece, piece)], enc_buf.at[i % 2], esem.at[i])

    enc_load(0).start()
    ext_s[...] = jnp.zeros_like(ext_s)
    ext_s[0:4] = ea_ref[...]
    ext_s[4:14] = ba_ref[...]
    ext = jnp.transpose(ext_s[...]).astype(bf16)
    pack_temporal(t_ref.at[zi, core], convs_ref, film_ref, skip_ref, down_ref, ext)

    line_barrier(cams, nz)

    def tz_copy(k, way):
        ref = t_ref.at[k, core, cam]
        return batch_copy(ref, ref, tzsend.at[way, k], tzrecv.at[k], me - 2 + 4 * way)

    def tc_copy(k, which, q):
        ref = t_ref.at[k, which, q]
        return batch_copy(ref, ref, tcsend.at[k, q], tcrecv.at[k, q], partner)

    def tp_copy(k, step, q):
        ref = t_ref.at[k, core, q]
        return cam_copy(ref, ref, tpsend.at[step - 1, k], tprecv.at[step - 1, k], (cam + step) % cams)

    def t_send(s):
        for k, _, passed, way in moves(s):
            @pl.when(passed)
            def _():
                tz_copy(k, way).start()

    def t_receive(s):
        for k, held, _, way in moves(s):
            @pl.when(held)
            def _():
                tz_copy(k, way).wait_recv()
                for step in range(1, cams):
                    tp_copy(k, step, cam).start()
                tc_copy(k, core, cam).start()

    def t_collect(d):
        for k, held, _, _ in moves(d):
            @pl.when(held & (d > 0))
            def _():
                for step in range(1, cams):
                    q = (cam + cams - step) % cams
                    tp_copy(k, step, q).wait_recv()
                    tc_copy(k, core, q).start()

    def t_complete():
        def body(k, carry):
            for q in range(cams):
                tc_copy(k, 1 - core, q).wait_recv()
            return carry

        lax.fori_loop(0, nz, body, 0)

    ns, nf = traj_ref.shape[0], traj_ref.shape[1]
    frows = ns * nf
    obs = arr_s.shape[1]
    cond = obs * CH + emb_ref.shape[1]
    edge = 2 * ns
    per_pos = frows // n_img
    gones_shape = CH // GROUPS
    ginv = 1.0 / (nf * gones_shape)

    class Part:
        def __init__(self, ref, index, lo, wide):
            self.ref, self.index, self.lo, self.wide = ref, index, lo, wide

        def where(self, key):
            if not isinstance(key, tuple):
                return self.index(slice(self.lo, self.lo + self.wide))
            start, stop, _ = key[1].indices(self.wide)
            return self.index(slice(self.lo + start, self.lo + stop))

        def __getitem__(self, key):
            v = self.ref[self.where(key)]
            return v.reshape(CH, v.shape[-1])

        def __setitem__(self, key, v):
            self.ref[self.where(key)] = v.reshape(nz, 2, rows, v.shape[-1])

    def weight(q, lo, wide):
        return Part(t_ref, lambda cols: (slice(None), slice(None), q, slice(None), cols), lo, wide)

    def grad(buf, lo, wide):
        return Part(dt_buf, lambda cols: (buf, slice(None), slice(None), slice(None), cols), lo, wide)

    wa, wb = weight(0, 0, PART), weight(1, 0, PART)
    f0, f1, wext = weight(2, 0, cond), weight(2, cond, cond), weight(2, 2 * cond, BLK)
    ws, wd = weight(3, 0, CH), weight(3, CH, 3 * CH)

    def dt_save(q, buf):
        return pltpu.make_async_copy(dt_buf.at[buf], dt_out.at[:, :, q], dsem.at[q])

    def blank(buf, lo):
        dt_buf[buf, :, :, :, lo:] = jnp.zeros((nz, 2, rows, PART - lo), bf16)

    def tail(i):
        return taff_ref[4 + i : 5 + i, :]

    def frames(v):
        return v.reshape(nf, ns, CH)

    def keep(i, v):
        z1_ref[per_pos * i : per_pos * (i + 1)] = v.reshape(per_pos, n_img, CH)

    def kept(i):
        return z1_ref[per_pos * i : per_pos * (i + 1)].reshape(nf, ns, CH)

    def fill_edges(pad_ref):
        pad_ref[0:edge, :] = jnp.zeros((edge, CH), bf16)
        pad_ref[edge + frows : edge + frows + edge, :] = jnp.zeros((edge, CH), bf16)

    def fill(pad_ref, v):
        fill_edges(pad_ref)
        pad_ref[edge : edge + frows, :] = v.astype(bf16).reshape(frows, CH)

    def conv5(pad_ref, w):
        return sum(
            dot(pad_ref[t * ns : t * ns + frows, :], w[:, t * CH : (t + 1) * CH], NT) for t in range(5)
        )

    def conv5_back(pad_ref, w):
        return sum(
            dot(pad_ref[(4 - t) * ns : (4 - t) * ns + frows, :], w[:, t * CH : (t + 1) * CH]) for t in range(5)
        )

    def gsum(v):
        return group_sum(v, group_ones(CH, gones_shape)) * ginv

    def norm(v):
        v = frames(v)
        centred = v - gsum(jnp.sum(v, axis=0))[None]
        rstd = lax.rsqrt(gsum(jnp.sum(centred * centred, axis=0)) + norm_eps)
        return centred * rstd[None], rstd

    def norm_back(du, z, rstd, gain):
        s0 = jnp.sum(du, axis=0)
        s1 = jnp.sum(du * z, axis=0)
        dv = (du * gain[None] - gsum(s0 * gain)[None] - z * gsum(s1 * gain)[None]) * rstd[None]
        return dv, jnp.sum(s1, axis=0, keepdims=True), jnp.sum(s0, axis=0, keepdims=True)

    def total(v):
        return jnp.sum(v, axis=(0, 1)).reshape(1, CH)

    def across(v):
        return jnp.transpose(v.reshape(frows, CH)).astype(bf16)

    def temporal_early():
        taff_ref[...] = jnp.transpose(wext[...].astype(f32))
        ag_ref[...] = jnp.zeros_like(ag_ref)
        traj = pad_t[edge : edge + frows, :]
        za, rstd = norm(conv5(pad_t, wa) + tail(4))
        rstd_ref[...] = rstd
        keep(0, za)
        keep(1, dot(traj, ws[...], NT) + tail(8))
        og = og_ref[...]
        dcols = [dot(og, wd[:, t * CH : (t + 1) * CH]).reshape(nf // 2, ns, CH) for t in range(3)]
        before = jnp.concatenate([dcols[0][1:], jnp.zeros((1, ns, CH), f32)], axis=0)
        dsum = jnp.stack([dcols[1], dcols[2] + before], axis=1).reshape(nf, ns, CH)
        keep(2, dsum)
        ag_ref[8:9, :] = total(dsum)
        ag_ref[9:10, :] = jnp.sum(og.astype(f32), axis=0, keepdims=True)
        dskip = dsum.astype(bf16).reshape(frows, CH)
        grad(0, 0, CH)[...] = dot(across(dsum), traj).astype(bf16)
        blank(0, 4 * CH)
        tg_ref[...] = dot(dskip, ws[...])

    def view_copy(to, sender):
        return cam_copy(dviews_ref.at[to], gp_s.at[:, sender], vsend.at[to], vrecv.at[sender], to)

    def temporal_rest():
        mask = mask_ref[...]
        seen = jnp.sum(mask, axis=1, keepdims=True)
        conds, slopes = [], []
        for o in range(obs):
            pooled = sum(mask[:, c : c + 1] * arr_s[c, o].astype(f32) for c in range(cams))
            value, slope = mish_pair(pooled / seen)
            conds.append(value.astype(bf16))
            slopes.append(slope)
        conds.append(mish_value(emb_ref[...]).astype(bf16))
        lanes = [slice(o * CH, (o + 1) * CH) for o in range(obs)] + [slice(obs * CH, cond)]
        scale, shift = [
            sum(dot(v, w[:, cols], NT) for v, cols in zip(conds, lanes)) + tail(i) for i, w in ((6, f0), (7, f1))
        ]
        za = kept(0)
        fill(pad_m, mish_value(za * tail(0)[None] + tail(1)[None]) * scale[None] + shift[None])
        zb, rstd_b = norm(conv5(pad_m, wb) + tail(5))
        act_b, slope = mish_pair(zb * tail(2)[None] + tail(3)[None])
        keep(3, act_b + kept(1))
        dhb, ag_ref[2:3, :], ag_ref[3:4, :] = norm_back(kept(2) * slope, zb, rstd_b, tail(2))
        ag_ref[5:6, :] = total(dhb)
        fill(pad_h, dhb)
        dmid = frames(conv5_back(pad_h, wb))
        za = kept(0)
        act_a, slope = mish_pair(za * tail(0)[None] + tail(1)[None])
        dscale = jnp.sum(dmid * act_a, axis=0)
        dshift = jnp.sum(dmid, axis=0)
        lows = (dscale.astype(bf16), dshift.astype(bf16))
        for o in range(obs):
            dcond = dot(lows[0], f0[:, lanes[o]]) + dot(lows[1], f1[:, lanes[o]])
            dview = dcond * slopes[o] / seen
            for c in range(cams):
                dviews_ref[c, o] = (mask[:, c : c + 1] * dview).astype(bf16)
        for step in range(1, cams):
            view_copy((cam + step) % cams, cam).start()
        gp_s[:, cam] = dviews_ref[cam]

        dha, ag_ref[0:1, :], ag_ref[1:2, :] = norm_back(dmid * scale[None] * slope, za, rstd_ref[...], tail(0))
        ag_ref[4:5, :] = total(dha)
        ag_ref[6:7, :] = jnp.sum(dscale, axis=0, keepdims=True)
        ag_ref[7:8, :] = jnp.sum(dshift, axis=0, keepdims=True)
        dwb = grad(1, 0, PART)
        hb = across(dhb)
        for t in range(5):
            dwb[:, t * CH : (t + 1) * CH] = dot(hb, pad_m[t * ns : t * ns + frows, :]).astype(bf16)
        dt_save(1, 1).start()
        pairs = kept(3).astype(bf16).reshape(nf // 2, 2, ns, CH)
        half = frows // 2
        sum_ref[0:ns, :] = jnp.zeros((ns, CH), bf16)
        sum_ref[ns : ns + half, :] = pairs[:, 1].reshape(half, CH)
        sum_ref[ns + half : ns + 2 * half, :] = pairs[:, 0].reshape(half, CH)
        og = jnp.transpose(og_ref[...].astype(f32)).astype(bf16)
        dwd = grad(0, CH, 3 * CH)
        out = None
        for t, at in enumerate((0, ns + half, ns)):
            cols = sum_ref[at : at + half, :]
            part = dot(cols, wd[:, t * CH : (t + 1) * CH], NT)
            out = part if out is None else out + part
            dwd[:, t * CH : (t + 1) * CH] = dot(og, cols).astype(bf16)
        dt_save(3, 0).start()
        out_ref[...] = (out + tail(9)).astype(bf16)
        fill(pad_h, dha)
        tg_ref[...] = tg_ref[...] + conv5_back(pad_h, wa)
        dt_save(1, 1).wait()
        for base, low in zip((0, cond), lows):
            dw = grad(1, base, cond)
            for v, cols in zip(conds, lanes):
                dw[:, cols] = dot(low, v, TN).astype(bf16)
        grad(1, 2 * cond, BLK)[...] = jnp.transpose(ag_ref[...]).astype(bf16)
        blank(1, 2 * cond + BLK)
        dt_save(2, 1).start()
        dt_save(3, 0).wait()
        dwa = grad(0, 0, PART)
        ha = across(dha)
        for t in range(5):
            dwa[:, t * CH : (t + 1) * CH] = dot(ha, pad_t[t * ns : t * ns + frows, :]).astype(bf16)
        dt_save(0, 0).start()
        for step in range(1, cams):
            other = (cam + step) % cams
            view_copy(other, other).wait_recv()
        gp_ref[...] = gp_s[...]
        dt_save(2, 1).wait()
        dt_save(0, 0).wait()

    def z_copy(conv, k, way):
        ref = w_ref.at[conv, 2 * k + core]
        return batch_copy(ref, ref, zsend.at[conv, way, k], zrecv.at[conv, k], me - 2 + 4 * way)

    def core_copy(conv, k, which):
        ref = w_ref.at[conv, 2 * k + which]
        return batch_copy(ref, ref, csend.at[conv, k], crecv.at[conv, k], partner)

    def moves(s):
        low, high = zi - s, zi + s
        return (
            (high, high < nz, (high < nz) & (zi > 0), 0),
            (low, low >= 0, (low >= 0) & (zi < nz - 1), 1),
        )

    def send(conv, s):
        for k, _, passed, way in moves(s):
            @pl.when(passed)
            def _():
                z_copy(conv, k, way).start()

    def receive(conv, s):
        for k, held, _, way in moves(s):
            @pl.when(held)
            def _():
                z_copy(conv, k, way).wait_recv()
                core_copy(conv, k, core).start()

    t_send(0)
    for q in range(cams):
        tc_copy(zi, core, q).start()
    for conv in range(2):
        w_ref[conv, me, :, 9 * CH :] = ext
    count = rows // piece

    def pack(i, carry):
        @pl.when(i + 1 < count)
        def _():
            enc_load(i + 1).start()

        enc_load(i).wait()
        for conv in range(2):
            w_ref[conv, me, pl.ds(pl.multiple_of(i * piece, piece), piece), 0 : 9 * CH] = (
                enc_buf[i % 2, :, conv, :].astype(bf16)
            )
        return carry

    lax.fori_loop(0, count, pack, 0)

    def x_save(p):
        return pltpu.make_async_copy(x_ref.at[:, p * CH : (p + 1) * CH], x_out.at[p], xsem.at[p])

    fill_edges(pad_t)
    moved = traj_ref[...].astype(f32)
    for f in range(nf):
        pad_t[edge + f * ns : edge + (f + 1) * ns, :] = moved[:, f].astype(bf16)
    moved = og_in[...].astype(f32)
    for f in range(nf // 2):
        og_ref[f * ns : (f + 1) * ns, :] = moved[:, f].astype(bf16)
    half = n_img // 2
    for p in range(9):
        pair = img_ref[:, p].astype(f32)
        for o in range(2):
            x_ref[o * half : (o + 1) * half, p * CH : (p + 1) * CH] = pair[:, o].astype(bf16)
        x_save(p).start()
    for conv in range(2):
        core_copy(conv, zi, core).start()

    def t_step(s, carry):
        @pl.when(s == nz - 1)
        def _():
            send(0, 0)

        t_receive(s)

        @pl.when(s < nz - 1)
        def _():
            t_send(s)
        return carry

    lax.fori_loop(1, nz, t_step, 0)

    def rows_of(conv, j, start, wide):
        block = w_ref[conv, pl.ds(j * spb, spb), :, start : start + wide]
        return block.reshape(BLK, wide)

    def w_save(conv, j):
        part = pl.ds(j * spb, spb)
        return pltpu.make_async_copy(w_ref.at[conv, part], w_out.at[conv, part], wsem.at[conv, j])

    def conv_norm(src_ref, conv, z_ref, r_ref, j):
        lanes = pl.ds(pl.multiple_of(j * BLK, BLK), BLK)
        total = None
        for p in range(9):
            r, c = divmod(p, 3)
            bs = span(c)
            acc = None
            for a in span(r):
                start = (3 * (r + a - 1) + c + bs[0] - 1) * CH
                wide = len(bs) * CH
                part = dot(src_ref[:, start : start + wide], rows_of(conv, j, (3 * a + bs[0]) * CH, wide), NT)
                acc = part if acc is None else acc + part
            z_ref[p, :, lanes] = acc
            total = acc if total is None else total + acc
        mean = group_sum(total, ones) * inv_n
        var = None
        for p in range(9):
            centred = z_ref[p, :, lanes] - mean
            sq = centred * centred
            var = sq if var is None else var + sq
        rstd = lax.rsqrt(group_sum(var, ones) * inv_n + norm_eps)
        r_ref[:, lanes] = rstd
        return lanes, mean, rstd

    def first(j):
        aff_ref[:, lanes_of(j)] = jnp.transpose(rows_of(0, j, 9 * CH, BLK).astype(f32))[0:8]
        lanes, mean, rstd = conv_norm(x_ref, 0, z1_ref, r1_ref, j)
        gain, offset = aff_ref[0:1, lanes], aff_ref[1:2, lanes]
        for p in range(9):
            z = (z1_ref[p, :, lanes] - mean) * rstd
            z1_ref[p, :, lanes] = z
            u = z * gain + offset
            a_ref[:, pl.ds(pl.multiple_of(p * CH + j * BLK, BLK), BLK)] = (u * sigmoid(u)).astype(bf16)

    def second(j):
        lanes, mean, rstd = conv_norm(a_ref, 1, z2_ref, r2_ref, j)
        gain, offset = aff_ref[2:3, lanes], aff_ref[3:4, lanes]
        total = None
        for p in range(9):
            z = (z2_ref[p, :, lanes] - mean) * rstd
            z2_ref[p, :, lanes] = z
            pic = x_ref[:, pl.ds(pl.multiple_of(p * CH + j * BLK, BLK), BLK)].astype(f32)
            u = z * gain + offset + pic
            act = u * sigmoid(u)
            total = act if total is None else total + act
        out = (total * (1.0 / 9.0)).astype(bf16)
        feat_ref[:, :, :, lanes] = out.reshape(feat_ref.shape[:3] + (BLK,))

    def lanes_of(j):
        return pl.ds(pl.multiple_of(j * BLK, BLK), BLK)

    def arrived(conv, k):
        core_copy(conv, k, 1 - core).wait_recv()

    def phase(conv, block):
        streaming = spb == 2

        def step(s, carry):
            if conv == 0:
                @pl.when((s > 0) & (s < nz - 1))
                def _():
                    send(0, s)

                @pl.when(s == nz - 1)
                def _():
                    send(1, 0)
            else:
                @pl.when((s > 0) & (s < nz - 1))
                def _():
                    send(1, s)

            def side(d, carry):
                k = zi + s - 2 * s * d

                @pl.when((k >= 0) & (k < nz) & (s + 1 > d))
                def _():
                    arrived(conv, k)
                    if streaming:
                        w_save(conv, k).start()
                        block(k)
                return carry

            lax.fori_loop(0, 2, side, 0)
            if conv == 1:
                t_collect(2 * s)
                t_collect(2 * s + 1)

                @pl.when(s == nz - 2)
                def _():
                    t_complete()
                    saves[0].wait()
                    temporal_early()

            @pl.when(s < nz - 1)
            def _():
                receive(conv, s + 1)
            return carry

        lax.fori_loop(0, nz, step, 0)
        if not streaming:
            def rest(j, carry):
                w_save(conv, j).start()
                block(j)
                return carry

            lax.fori_loop(0, CH // BLK, rest, 0)

    phase(0, first)
    saves = [pltpu.make_async_copy(z1_ref, z1_out, osem.at[0])]
    saves += [
        pltpu.make_async_copy(a_ref.at[:, p * CH : (p + 1) * CH], a_out.at[p], osem.at[2 + p])
        for p in range(9)
    ]
    for save in saves:
        save.start()
    phase(1, second)
    last = pltpu.make_async_copy(z2_ref, z2_out, osem.at[1])
    last.start()

    def feat_copy(to, sender):
        return cam_copy(feat_ref.at[:, to], arr_s.at[sender], fsend.at[to], frecv.at[sender], to)

    for step in range(1, cams):
        feat_copy((cam + step) % cams, cam).start()
    arr_s[cam] = feat_ref[:, cam]
    for step in range(1, cams):
        other = (cam + step) % cams
        feat_copy(other, other).wait_recv()
    temporal_rest()
    for step in range(1, cams):
        feat_copy((cam + step) % cams, cam).wait_send()

    for conv in range(2):
        def drain(k, carry):
            s = k - zi

            @pl.when((s >= 0) & (s < nz - 1) & (zi > 0))
            def _():
                z_copy(conv, k, 0).wait_send()

            @pl.when((s <= 0) & (s > 1 - nz) & (zi < nz - 1))
            def _():
                z_copy(conv, k, 1).wait_send()

            core_copy(conv, k, core).wait_send()
            return carry

        lax.fori_loop(0, nz, drain, 0)

        def saved(j, carry):
            w_save(conv, j).wait()
            return carry

        lax.fori_loop(0, CH // BLK, saved, 0)
    for save in saves[1:]:
        save.wait()
    last.wait()

    def t_drain(k, carry):
        s = k - zi

        @pl.when((s >= 0) & (s < nz - 1) & (zi > 0))
        def _():
            tz_copy(k, 0).wait_send()

        @pl.when((s <= 0) & (s > 1 - nz) & (zi < nz - 1))
        def _():
            tz_copy(k, 1).wait_send()

        @pl.when(s != 0)
        def _():
            for step in range(1, cams):
                tp_copy(k, step, cam).wait_send()

        for q in range(cams):
            tc_copy(k, core, q).wait_send()
        return carry

    lax.fori_loop(0, nz, t_drain, 0)
    for p in range(9):
        x_save(p).wait()
    for step in range(1, cams):
        view_copy((cam + step) % cams, cam).wait_send()


def enc_bwd_kernel(
    n, cams, cond, x_hbm, a_hbm, w_hbm, z1_hbm, r1_ref, z2_hbm, r2_ref, aff_ref, gp_ref, dt_hbm,
    ig_ref, genc_ref, gaff_ref, gconvs_ref, gfilm_ref, gskip_ref, gdown_ref, gblk_ref,
    x_ref, a_ref, w_ref, z1_ref, z2_ref, g_ref, gt_ref, ag_ref,
    dwf, core_out, core_in, slots, t_own, t_sum, t_peer, t_slots, t_all,
    lsem, csend, crecv, zsend, zrecv,
    tlsem, tcsend, tcrecv, tpsend, tprecv, tzsend, tzrecv, tfsend, tfrecv,
):
    nz = n // 2
    rows = CH // n
    n_img = z1_ref.shape[1]
    me, cam = lax.axis_index("batch"), lax.axis_index("cam")
    zi, core = me // 2, me % 2
    partner = me + 1 - 2 * core
    ones = group_ones(BLK, ENC_GROUP)
    inv_n = 1.0 / (9 * ENC_GROUP)
    chunk = 3 * CH

    def load_w(conv):
        return pltpu.make_async_copy(w_hbm.at[conv, :, :, 0 : 9 * CH], w_ref, lsem.at[3])

    loads = {
        "z2": pltpu.make_async_copy(z2_hbm, z2_ref, lsem.at[0]),
        "z1": pltpu.make_async_copy(z1_hbm, z1_ref, lsem.at[1]),
        "a": pltpu.make_async_copy(a_hbm, a_ref, lsem.at[2]),
    }
    x_loads = [pltpu.make_async_copy(x_hbm, x_ref, lsem.at[4])]
    loads["z2"].start()
    for load in x_loads:
        load.start()
    loads["a"].start()
    load_w(1).start()
    loads["z1"].start()

    def own_load(i):
        return pltpu.make_async_copy(dt_hbm.at[i // cams, core, i % cams], t_own.at[i % 2], tlsem.at[i])

    own_load(0).start()

    line_greet(cams, nz)

    def t_core(k):
        return batch_copy(dt_hbm.at[k, 1 - core], t_sum.at[k], tcsend.at[k], tcrecv.at[k], partner)

    def t_peers(k, step):
        to = (cam + step) % cams
        return cam_copy(t_sum.at[k, to], t_peer.at[step - 1, k], tpsend.at[step - 1, k], tprecv.at[step - 1, k], to)

    def t_start(k, carry):
        t_core(k).start()
        return carry

    def t_spread(lo, hi):
        def body(k, carry):
            t_core(k).wait_recv()

            def quarter(q, carry):
                i = k * cams + q

                @pl.when(i + 1 < nz * cams)
                def _():
                    own_load(i + 1).start()

                own_load(i).wait()
                t_sum[k, q] = (t_sum[k, q].astype(f32) + t_own[i % 2].astype(f32)).astype(bf16)
                return carry

            lax.fori_loop(0, cams, quarter, 0)
            for step in range(1, cams):
                t_peers(k, step).start()
            return carry

        lax.fori_loop(lo, hi, body, 0)

    ag_ref[...] = jnp.zeros_like(ag_ref)
    for load in x_loads:
        load.wait()
    loads["z2"].wait()

    def lanes_of(j):
        return pl.ds(pl.multiple_of(j * BLK, BLK), BLK)

    def norm_back(du_ref, z_ref, r_ref, j, gain, row):
        lanes = lanes_of(j)
        s0 = jnp.zeros((n_img, BLK), f32)
        s1 = jnp.zeros((n_img, BLK), f32)
        for p in range(9):
            du = du_ref[p, :, lanes]
            s0 = s0 + du
            s1 = s1 + du * z_ref[p, :, lanes]
        ag_ref[row : row + 1, lanes] = jnp.sum(s1, axis=0, keepdims=True)
        ag_ref[row + 1 : row + 2, lanes] = jnp.sum(s0, axis=0, keepdims=True)
        m0 = group_sum(s0 * gain, ones) * inv_n
        m1 = group_sum(s1 * gain, ones) * inv_n
        rstd = r_ref[:, lanes]
        for p in range(9):
            dv = (du_ref[p, :, lanes] * gain - m0 - z_ref[p, :, lanes] * m1) * rstd
            g_ref[p, :, lanes] = dv.astype(bf16)
            gt_ref[lanes, p * n_img : (p + 1) * n_img] = jnp.transpose(dv).astype(bf16)

    def second(j, carry):
        lanes = lanes_of(j)
        gain, offset = aff_ref[2:3, lanes], aff_ref[3:4, lanes]
        pooled = gp_ref[:, :, :, lanes].reshape(n_img, BLK).astype(f32) * (1.0 / 9.0)
        for p in range(9):
            u = z2_ref[p, :, lanes] * gain + offset + x_ref[p, :, lanes].astype(f32)
            s = sigmoid(u)
            ig_ref[p, :, lanes] = pooled * (s * (1.0 + u * (1.0 - s)))
        norm_back(ig_ref, z2_ref, r2_ref, j, gain, 2)
        return carry

    def first(j, carry):
        lanes = lanes_of(j)
        gain, offset = aff_ref[0:1, lanes], aff_ref[1:2, lanes]
        for p in range(9):
            u = z1_ref[p, :, lanes] * gain + offset
            s = sigmoid(u)
            z2_ref[p, :, lanes] = z2_ref[p, :, lanes] * (s * (1.0 + u * (1.0 - s)))
        norm_back(z2_ref, z1_ref, r1_ref, j, gain, 0)
        return carry

    def width(k):
        return chunk + BLK if k == 5 else chunk

    def core_copy(k):
        cols = pl.ds(0, width(k))
        return batch_copy(
            core_out.at[k % 2, :, :, cols], core_in.at[k % 3, :, :, cols], csend.at[k], crecv.at[k], partner
        )

    def keep(k, d0, lane, v):
        count, wide = v.shape[0] // (2 * rows), v.shape[1]
        parts = v.reshape(count, 2, rows, wide)
        even, odd = parts[:, 0], parts[:, 1]
        dwf[k % 2, d0 : d0 + count, :, lane : lane + wide] = jnp.where(core == 0, even, odd)
        core_out[k % 2, d0 : d0 + count, :, lane : lane + wide] = jnp.where(core == 0, odd, even).astype(bf16)

    def make_chunk(k):
        if k >= 2:
            core_copy(k - 2).wait_send()
        src_ref = a_ref if k < 3 else x_ref
        a = k % 3
        r_lo, r_hi = max(0, 1 - a), min(2, 3 - a)
        for b in range(3):
            c_lo, c_hi = max(0, 1 - b), min(2, 3 - b)
            if b == 1:
                runs = [(3 * r_lo, 3 * (r_hi - r_lo + 1))]
            else:
                runs = [(3 * r + c_lo, c_hi - c_lo + 1) for r in range(r_lo, r_hi + 1)]
            shift = 3 * (a - 1) + b - 1
            for half in range(2):
                acc = None
                for p, m in runs:
                    part = dot(
                        gt_ref[half * 256 : half * 256 + 256, p * n_img : (p + m) * n_img],
                        src_ref[p + shift : p + shift + m].reshape(m * n_img, CH),
                    )
                    acc = part if acc is None else acc + part
                keep(k, half * nz // 2, b * CH, acc)
        if k == 5:
            keep(k, 0, chunk, jnp.transpose(ag_ref[...]))
        core_copy(k).start()

    def term(k, d):
        return dwf[k % 2, d, :, 0 : width(k)] + core_in[k % 3, d, :, 0 : width(k)].astype(f32)

    def line_copy(k, way, s):
        if k == 6:
            return batch_copy(
                t_slots.at[way, s - 1], t_slots.at[way, s], tzsend.at[way, s], tzrecv.at[way, s], me - 2 + 4 * way
            )
        cols = pl.ds(0, width(k))
        return batch_copy(
            slots.at[k % 3, way, s - 1, :, cols], slots.at[k % 3, way, s, :, cols],
            zsend.at[k, way, s], zrecv.at[k, way, s], me - 2 + 4 * way,
        )

    def slot(k, way, s):
        return t_slots.at[way, s] if k == 6 else slots.at[k % 3, way, s, :, pl.ds(0, width(k))]

    def t_term(d):
        total = t_sum[d, cam].astype(f32)
        for step in range(1, cams):
            total = total + t_peer[step - 1, d].astype(f32)
        return total

    def serve(k, s):
        for way in range(2):
            ahead = zi if way else nz - 1 - zi
            d = nz - s + zi if way else s - nz + zi
            ref = slot(k, way, s - 1)

            @pl.when((ahead < nz - 1) & (s > ahead))
            def _():
                own = t_term(d) if k == 6 else term(k, d)

                @pl.when(ahead > 0)
                def _():
                    line_copy(k, way, s - 1).wait_recv()
                    ref[...] = (ref[...].astype(f32) + own).astype(bf16)

                @pl.when(ahead == 0)
                def _():
                    ref[...] = own.astype(bf16)

                line_copy(k, way, s).start()

    def steps(k, part):
        lo, hi = 1 + part * (nz - 1) // 3, 1 + (part + 1) * (nz - 1) // 3
        if hi - lo == 1:
            serve(k, lo)
        elif hi > lo:
            def body(s, carry):
                serve(k, s)
                return carry

            lax.fori_loop(lo, hi, body, 0)

    def service(g):
        k, part = divmod(g, 3)
        if part == 0:
            core_copy(k).wait_recv()
        steps(k, part)

    def collect(k, total, write):
        last = nz - 1

        @pl.when(zi > 0)
        def _():
            line_copy(k, 1, last).wait_recv()

        @pl.when(zi < nz - 1)
        def _():
            line_copy(k, 0, last).wait_recv()

        @pl.when(zi == 0)
        def _():
            write(total + slot(k, 0, last)[...].astype(f32))

        @pl.when(zi == nz - 1)
        def _():
            write(total + slot(k, 1, last)[...].astype(f32))

        @pl.when((zi > 0) & (zi < nz - 1))
        def _():
            write(total + slot(k, 0, last)[...].astype(f32) + slot(k, 1, last)[...].astype(f32))

        def drain(s, carry):
            for way in range(2):
                ahead = zi if way else nz - 1 - zi

                @pl.when((ahead < nz - 1) & (s > ahead))
                def _():
                    line_copy(k, way, s).wait_send()
            return carry

        lax.fori_loop(1, nz, drain, 0)

    def finish(k):
        def write(v):
            genc_ref[:, 1 - k // 3, (k % 3) * chunk : (k % 3 + 1) * chunk] = v[:, 0:chunk]
            if k == 5:
                gaff_ref[...] = jnp.transpose(v[:, chunk:])[0 : gaff_ref.shape[0]]

        collect(k, term(k, zi), write)

    def t_arrived():
        for step in range(1, cams):
            def body(k, carry):
                t_peers(k, step).wait_recv()
                return carry

            lax.fori_loop(0, nz, body, 0)

    def t_final(to, sender):
        return cam_copy(t_all.at[cam], t_all.at[sender], tfsend.at[to], tfrecv.at[sender], to)

    def t_finish():
        def write(v):
            t_all[cam] = v.astype(bf16)

        collect(6, t_term(zi), write)
        for step in range(1, cams):
            t_final((cam + step) % cams, cam).start()

    def t_write():
        for step in range(1, cams):
            other = (cam + step) % cams
            t_final(other, other).wait_recv()

        def cut(q, lo, wide):
            return t_all[q, :, lo : lo + wide].astype(f32)

        for which in range(2):
            gconvs_ref[:, which, :] = cut(which, 0, PART)
            gfilm_ref[:, which, :] = cut(2, which * cond, cond)
        gblk_ref[...] = jnp.transpose(cut(2, 2 * cond, BLK))[0 : gblk_ref.shape[0]]
        gskip_ref[...] = cut(3, 0, CH)
        gdown_ref[...] = cut(3, CH, 3 * CH)

    def input_back(q):
        r, c = divmod(q, 3)
        acc = None
        for a in range(3):
            for b in range(3):
                pr, pc = r - a + 1, c - b + 1
                if 0 <= pr < 3 and 0 <= pc < 3:
                    t = 3 * a + b
                    w = w_ref[:, :, t * CH : (t + 1) * CH].reshape(CH, CH)
                    part = dot(g_ref[3 * pr + pc], w)
                    acc = part if acc is None else acc + part
        return acc

    def back_second(*qs):
        for q in qs:
            if q == 0:
                load_w(1).wait()
            z2_ref[q] = input_back(q)
            if q == 8:
                load_w(0).start()

    def back_first(*qs):
        for q in qs:
            if q == 0:
                load_w(0).wait()
            ig_ref[q] = ig_ref[q] + input_back(q)

    lax.fori_loop(0, 1, second, 0)
    line_wait(cams, nz)
    lax.fori_loop(0, nz, t_start, 0)
    lax.fori_loop(1, CH // BLK, second, 0)
    loads["a"].wait()
    make_chunk(0)
    service(0)
    t_spread(0, nz // 2)
    make_chunk(1)
    service(1)
    t_spread(nz // 2, nz)
    back_second(0, 1, 2)
    service(2)
    back_second(3, 4)
    service(3)
    finish(0)
    make_chunk(2)
    service(4)
    back_second(5, 6)
    service(5)
    back_second(7, 8)
    service(6)
    finish(1)
    loads["z1"].wait()
    lax.fori_loop(0, 2, first, 0)
    service(7)
    lax.fori_loop(2, 4, first, 0)
    service(8)
    make_chunk(3)
    service(9)
    finish(2)
    make_chunk(4)
    service(10)
    back_first(0, 1)
    service(11)
    back_first(2, 3)
    service(12)
    finish(3)
    make_chunk(5)
    service(13)
    back_first(4, 5)
    service(14)
    t_arrived()
    steps(6, 0)
    finish(4)
    back_first(6)
    steps(6, 1)
    back_first(7)
    steps(6, 2)
    back_first(8)
    service(15)
    t_finish()
    service(16)
    service(17)
    t_write()
    finish(5)

    def t_drain(k, carry):
        t_core(k).wait_send()
        for step in range(1, cams):
            t_peers(k, step).wait_send()
        return carry

    lax.fori_loop(0, nz, t_drain, 0)
    for step in range(1, cams):
        t_final((cam + step) % cams, cam).wait_send()
    core_copy(4).wait_send()
    core_copy(5).wait_send()


def call(kernel, outs, in_specs, out_specs, scratch=(), collective_id=None, cost=None):
    extra = {} if collective_id is None else dict(collective_id=collective_id, has_side_effects=True)
    return pl.pallas_call(
        kernel,
        out_shape=[jax.ShapeDtypeStruct(s, d) for s, d in outs],
        in_specs=in_specs,
        out_specs=out_specs,
        scratch_shapes=list(scratch),
        compiler_params=pltpu.CompilerParams(vmem_limit_bytes=VMEM_BYTES, **extra),
        cost_estimate=cost,
    )


def work(microseconds):
    return pl.CostEstimate(
        flops=int(microseconds * 1e9), bytes_accessed=int(microseconds * 3e6), transcendentals=0
    )


V = pl.BlockSpec(memory_space=pltpu.VMEM)
H = pl.BlockSpec(memory_space=pl.ANY)
DMA = pltpu.SemaphoreType.DMA


def time_embed(steps_given, embed_width):
    half_width = embed_width // 2
    frequency = jnp.exp(
        jnp.arange(half_width, dtype=jnp.float32) * (-math.log(10000.0) / (half_width - 1))
    )
    argument = steps_given.astype(jnp.float32)[:, None] * frequency[None, :]
    return jnp.concatenate([jnp.sin(argument), jnp.cos(argument)], axis=1)


def adamw(weight, gradient, moment_one, moment_two, step_rate, weight_decay):
    mean_new = beta_first * moment_one + (1.0 - beta_first) * gradient
    square_new = beta_second * moment_two + (1.0 - beta_second) * gradient * gradient
    square_hat = square_new * (1.0 / (1.0 - beta_second**STEP))
    root = square_hat * lax.rsqrt(square_hat)
    weight_new = (1.0 - step_rate * weight_decay) * weight - (step_rate / (1.0 - beta_first**STEP)) * (
        mean_new / (root + adam_eps)
    )
    return (weight_new, mean_new, square_new)


def last_kernel(*refs):
    tg_ref, out_ref, ig_ref = refs[28:31]
    tg_new, out_new, ig_new, turn_ref = refs[52:56]
    for p in range(ig_ref.shape[0]):
        for o in range(ig_ref.shape[1]):
            ig_new[:, p, o, :] = ig_ref[p, o]

    @pl.when(pl.program_id(0) == 0)
    def _():
        for f in range(tg_ref.shape[0]):
            tg_new[:, f, :] = tg_ref[f]
        for u in range(out_ref.shape[0]):
            turn_ref[:, u, :] = out_ref[u].astype(f32)
        out_new[...] = turn_ref[...].astype(bf16)

    for i in range(7):
        w_ref, m_ref, v_ref, g_ref = refs[4 * i : 4 * i + 4]
        outs = refs[31 + 3 * i : 34 + 3 * i]

        def update():
            vector = i in (1, 6)
            rate, decay = (rate_vector, 0.0) if vector else (rate_matrix, decay_matrix)
            new = adamw(w_ref[...], g_ref[...], m_ref[...], v_ref[...], rate, decay)
            for ref, value in zip(outs, new):
                ref[...] = value

        if i in (1, 6):
            pl.when(pl.program_id(0) == 0)(update)
        else:
            update()


def last_call(shown, grads, tg, out, ig, rows):
    step = min(rows, 8)
    steps = rows // step

    def whole(shape):
        return pl.BlockSpec(shape, lambda r: (0,) * len(shape))

    def spec(v):
        if v.shape[0] != rows:
            return whole(v.shape)
        return pl.BlockSpec((step,) + v.shape[1:], lambda r: (r,) + (0,) * (v.ndim - 1))

    ins = []
    for i in range(7):
        ins += [shown[0][i], shown[1][i], shown[2][i], grads[i]]
    outs = [w for w in shown[0] for _ in range(3)]
    pos, obs, count, ch = ig.shape
    part = count // steps
    turned = [(v.shape[1], v.shape[0], v.shape[2]) for v in (tg, out)]
    return pl.pallas_call(
        last_kernel,
        grid=(steps,),
        out_shape=[jax.ShapeDtypeStruct(v.shape, f32) for v in outs]
        + [jax.ShapeDtypeStruct(turned[0], f32), jax.ShapeDtypeStruct(turned[1], bf16),
           jax.ShapeDtypeStruct((count, pos, obs, ch), f32)],
        in_specs=[spec(v) for v in ins]
        + [whole(tg.shape), whole(out.shape), pl.BlockSpec((pos, obs, part, ch), lambda r: (0, 0, r, 0))],
        out_specs=[spec(v) for v in outs]
        + [whole(turned[0]), whole(turned[1]), pl.BlockSpec((part, pos, obs, ch), lambda r: (r, 0, 0, 0))],
        scratch_shapes=[pltpu.VMEM(turned[1], f32)],
        compiler_params=pltpu.CompilerParams(vmem_limit_bytes=VMEM_BYTES),
        cost_estimate=work(15),
    )(*ins, tg, out, ig)


def shards(
    n, images, trajectory, view_mask, timesteps, out_grad,
    encoder_weight, encoder_affine, block_convs, film_weight, skip_weight, down_weight, block_affine,
    first_encoder, first_affine, first_convs, first_film, first_skip, first_down, first_block,
    second_encoder, second_affine, second_convs, second_film, second_skip, second_down, second_block,
):
    ns, nf, ch = trajectory.shape
    cams, obs = images.shape[1], images.shape[3]
    n_img = cams * images.shape[2] * obs
    nz, per = n // 2, ch // n
    cond = film_weight.shape[2]
    wide = 9 * ch
    rows = nf * ns

    def turned(v):
        return jnp.transpose(v.reshape(v.shape[-2:]))

    pairs = jnp.transpose(images[0], (0, 1, 3, 2, 4)).reshape(n_img // obs, 9, obs, ch)
    pos = (9, n_img, ch)
    t_shape = (nz, 2, cams, per, PART)
    wcols = wide + BLK
    z1, r1, act, z2, r2, w_all, enc_aff, x, out_fm, tg_fm, gp, dt = call(
        functools.partial(forward_kernel, n, cams),
        [(pos, f32), ((n_img, ch), f32), (pos, bf16), (pos, f32), ((n_img, ch), f32), ((2, n, per, wcols), bf16),
         ((8, ch), f32), (pos, bf16), ((rows // 2, ch), bf16), ((rows, ch), f32), ((obs, cams, ns, ch), bf16),
         (t_shape, bf16)],
        [V, V, V, V, V, H, V, V, V, V, V, V],
        [H, V, H, H, V, H, V, H, V, V, V, H],
        [pltpu.VMEM((n_img, wide), bf16), pltpu.VMEM((2, n, per, wcols), bf16), pltpu.VMEM(pos, f32),
         pltpu.VMEM((n_img, wide), bf16), pltpu.VMEM(pos, f32), pltpu.VMEM((obs, cams, ns, ch), bf16),
         pltpu.VMEM((cams, obs, ns, ch), bf16), pltpu.VMEM(t_shape, bf16), pltpu.VMEM((2, min(per, 16), 2, wide), f32),
         pltpu.VMEM((BLK, per), f32), pltpu.VMEM((rows // 2, ch), bf16), pltpu.VMEM((rows + 4 * ns, ch), bf16),
         pltpu.VMEM((rows + 4 * ns, ch), bf16), pltpu.VMEM((rows + 4 * ns, ch), bf16), pltpu.VMEM((rows + ns, ch), bf16),
         pltpu.VMEM((BLK, ch), f32), pltpu.VMEM((BLK, ch), f32), pltpu.VMEM((ns, ch), f32),
         pltpu.VMEM((cams, obs, ns, ch), bf16), pltpu.VMEM((obs, cams, ns, ch), bf16),
         pltpu.VMEM((2, nz, 2, per, PART), bf16),
         DMA((2, 2, nz)), DMA((2, nz)), DMA((2, nz)), DMA((2, nz)), DMA((2, ch // BLK)), DMA((11,)),
         DMA((cams,)), DMA((cams,)),
         DMA((2, nz)), DMA((nz,)), DMA((nz, cams)), DMA((nz, cams)), DMA((cams - 1, nz)), DMA((cams - 1, nz)),
         DMA((max(per // 16, 1),)), DMA((9,)), DMA((cams,)), DMA((cams,)), DMA((4,))],
        collective_id=0,
        cost=work(130),
    )(pairs, trajectory, out_grad, view_mask.astype(f32), time_embed(timesteps, TEMB), encoder_weight[0], block_convs,
      film_weight, skip_weight, down_weight, turned(encoder_affine), turned(block_affine))
    chunk = 3 * ch + BLK
    ig, genc, gaff, gconvs, gfilm, gskip, gdown, gblk = call(
        functools.partial(enc_bwd_kernel, n, cams, cond),
        [(pos, f32), ((per, 2, wide), f32), ((4, per), f32), ((per, 2, 5 * ch), f32),
         ((per, 2, cond), f32), ((per, ch), f32), ((per, 3 * ch), f32), ((10, per), f32)],
        [H, H, H, H, V, H, V, V, V, H],
        [V] * 8,
        [pltpu.VMEM(pos, bf16), pltpu.VMEM(pos, bf16), pltpu.VMEM((n, per, wide), bf16), pltpu.VMEM(pos, f32),
         pltpu.VMEM(pos, f32), pltpu.VMEM(pos, bf16), pltpu.VMEM((ch, 9 * n_img), bf16),
         pltpu.VMEM((BLK, ch), f32),
         pltpu.VMEM((2, nz, per, chunk), f32), pltpu.VMEM((2, nz, per, chunk), bf16),
         pltpu.VMEM((3, nz, per, chunk), bf16), pltpu.VMEM((3, 2, nz, per, chunk), bf16),
         pltpu.VMEM((2, per, PART), bf16), pltpu.VMEM((nz, cams, per, PART), bf16),
         pltpu.VMEM((cams - 1, nz, per, PART), bf16), pltpu.VMEM((2, nz, per, PART), bf16),
         pltpu.VMEM((cams, per, PART), bf16),
         DMA((13,)), DMA((6,)), DMA((6,)), DMA((6, 2, nz)), DMA((6, 2, nz)),
         DMA((nz * cams,)), DMA((nz,)), DMA((nz,)), DMA((cams - 1, nz)), DMA((cams - 1, nz)),
         DMA((2, nz)), DMA((2, nz)), DMA((cams,)), DMA((cams,))],
        collective_id=1,
        cost=work(100),
    )(x, act, w_all, z1, r1, z2, r2, enc_aff, gp, dt)
    weights = (encoder_weight, encoder_affine, block_convs, film_weight, skip_weight, down_weight, block_affine)
    firsts = (first_encoder, first_affine, first_convs, first_film, first_skip, first_down, first_block)
    seconds = (second_encoder, second_affine, second_convs, second_film, second_skip, second_down, second_block)
    shown = [
        [turned(v) if i in (1, 6) else v.reshape(v.shape[-3:]) if i == 0 else v for i, v in enumerate(group)]
        for group in (weights, firsts, seconds)
    ]
    *news, trajectory_grad, block_output, ig_new = last_call(
        shown, (genc, gaff, gconvs, gfilm, gskip, gdown, gblk),
        tg_fm.reshape(nf, ns, ch), out_fm.reshape(nf // 2, ns, ch), ig.reshape(9, obs, n_img // obs, ch), per,
    )
    images_grad = jnp.transpose(ig_new.reshape(images.shape[1:3] + ig_new.shape[1:]), (0, 1, 3, 2, 4))[None]
    upd = [
        tuple((turned(v) if i in (1, 6) else v).reshape(w.shape) for v in news[3 * i : 3 * i + 3])
        for i, w in enumerate(weights)
    ]
    return (
        (block_output, trajectory_grad, images_grad)
        + tuple(u[0] for u in upd)
        + tuple(u[1] for u in upd)
        + tuple(u[2] for u in upd)
    )


def solution(mesh):
    sample = P(("cam", "batch"))
    params = (P("cam", "batch"), P("cam", "batch")) + (P("batch"),) * 5
    images_spec = P("cam", None, "batch")
    return jax.shard_map(
        functools.partial(shards, mesh.shape["batch"]),
        mesh=mesh,
        in_specs=(images_spec, sample, sample, sample, sample) + params * 3,
        out_specs=(sample, sample, images_spec) + params * 3,
        check_vma=False,
    )
```

```python
import functools
import math

import jax
import jax.numpy as jnp
from jax import lax
from jax.experimental import pallas as pl
from jax.experimental.pallas import tpu as pltpu
from jax.sharding import PartitionSpec as P

TEMB = 128
GROUPS = 8
STEP = 5

norm_eps = 1e-05
beta_first = 0.5
beta_second = 0.5
adam_eps = 1e-08
rate_matrix = 0.02
rate_vector = 0.2
decay_matrix = 0.01

CH = 512
BLK = 128
ENC_GROUP = 16
f32 = jnp.float32
bf16 = jnp.bfloat16
VMEM_BYTES = 61 * 1024 * 1024

NT = (((1,), (1,)), ((), ()))
NN = (((1,), (0,)), ((), ()))
TN = (((0,), (0,)), ((), ()))


def dot(a, b, dims=NN):
    return lax.dot_general(a, b, dims, preferred_element_type=f32)


def group_ones(width, group):
    rows = lax.broadcasted_iota(jnp.int32, (width, width), 0) // group
    cols = lax.broadcasted_iota(jnp.int32, (width, width), 1) // group
    return jnp.where(rows == cols, 1.0, 0.0).astype(bf16)


def group_sum(v, ones):
    high = v.astype(bf16)
    rest = v - high.astype(f32)
    middle = rest.astype(bf16)
    low = (rest - middle.astype(f32)).astype(bf16)
    return dot(high, ones) + dot(middle, ones) + dot(low, ones)


def sigmoid(v):
    return 1.0 / (1.0 + jnp.exp(-v))


def mish_pair(v):
    e = jnp.exp(jnp.minimum(v, 20.0))
    n = e * (e + 2.0)
    inv = 1.0 / (n + 2.0)
    t = n * inv
    return v * t, t + v * (4.0 * e * (1.0 + e)) * inv * inv


def mish_value(v):
    e = jnp.exp(jnp.minimum(v, 20.0))
    n = e * (e + 2.0)
    return v * (n / (n + 2.0))


def span(i):
    return range(max(0, 1 - i), min(2, 3 - i) + 1)


MESH = pl.DeviceIdType.MESH


def batch_copy(src, dst, send_sem, recv_sem, target):
    return pltpu.make_async_remote_copy(
        src_ref=src, dst_ref=dst, send_sem=send_sem, recv_sem=recv_sem,
        device_id={"batch": target}, device_id_type=MESH,
    )


def cam_copy(src, dst, send_sem, recv_sem, target):
    return pltpu.make_async_remote_copy(
        src_ref=src, dst_ref=dst, send_sem=send_sem, recv_sem=recv_sem,
        device_id={"cam": target}, device_id_type=MESH,
    )


def line_barrier(cams, nz):
    line_greet(cams, nz)
    line_wait(cams, nz)


def line_wait(cams, nz):
    zi = lax.axis_index("batch") // 2
    ends = (zi == 0).astype(jnp.int32) + (zi == nz - 1).astype(jnp.int32)
    pl.semaphore_wait(pltpu.get_barrier_semaphore(), cams + 2 - ends)


def line_greet(cams, nz):
    me, cam = lax.axis_index("batch"), lax.axis_index("cam")
    zi, core = me // 2, me % 2
    barrier = pltpu.get_barrier_semaphore()
    pl.semaphore_signal(barrier, inc=1, device_id={"batch": me + 1 - 2 * core}, device_id_type=MESH)
    for step in range(1, cams):
        pl.semaphore_signal(barrier, inc=1, device_id={"cam": (cam + step) % cams}, device_id_type=MESH)

    @pl.when(zi > 0)
    def _():
        pl.semaphore_signal(barrier, inc=1, device_id={"batch": me - 2}, device_id_type=MESH)

    @pl.when(zi < nz - 1)
    def _():
        pl.semaphore_signal(barrier, inc=1, device_id={"batch": me + 2}, device_id_type=MESH)


PART = 5 * CH


def pack_temporal(ref, convs_ref, film_ref, skip_ref, down_ref, ext):
    rows, cond = film_ref.shape[0], film_ref.shape[2]
    for q in range(2):
        ref[q] = convs_ref[:, q, :].astype(bf16)
        ref[2, :, q * cond : (q + 1) * cond] = film_ref[:, q, :].astype(bf16)
    ref[2, :, 2 * cond : 2 * cond + BLK] = ext
    ref[2, :, 2 * cond + BLK :] = jnp.zeros((rows, PART - 2 * cond - BLK), bf16)
    ref[3, :, 0:CH] = skip_ref[...].astype(bf16)
    ref[3, :, CH : 4 * CH] = down_ref[...].astype(bf16)
    ref[3, :, 4 * CH :] = jnp.zeros((rows, PART - 4 * CH), bf16)


def forward_kernel(
    n, cams, img_hbm, traj_ref, og_in, mask_ref, emb_ref, enc_hbm, convs_ref, film_ref, skip_ref, down_ref,
    ea_ref, ba_ref,
    z1_out, r1_ref, a_out, z2_out, r2_ref, w_out, aff_ref, x_out, out_ref, tg_ref, gp_ref, dt_out,
    img_ref, x_ref, w_ref, z1_ref, a_ref, z2_ref, feat_ref, arr_s, t_ref, enc_buf,
    ext_s, og_ref, pad_t, pad_m, pad_h, sum_ref, taff_ref, ag_ref, rstd_ref, dviews_ref, gp_s, dt_buf,
    zsend, zrecv, csend, crecv, wsem, osem, fsend, frecv,
    tzsend, tzrecv, tcsend, tcrecv, tpsend, tprecv, esem, xsem, vsend, vrecv, dsem,
):
    nz = n // 2
    rows = skip_ref.shape[0]
    piece = enc_buf.shape[1]
    spb = BLK // rows
    n_img = x_ref.shape[0]
    me, cam = lax.axis_index("batch"), lax.axis_index("cam")
    zi, core = me // 2, me % 2
    partner = me + 1 - 2 * core
    ones = group_ones(BLK, ENC_GROUP)
    inv_n = 1.0 / (9 * ENC_GROUP)

    def enc_load(i):
        return pltpu.make_async_copy(enc_hbm.at[pl.ds(i * piece, piece)], enc_buf.at[i % 2], esem.at[i])

    enc_load(0).start()
    img_load = pltpu.make_async_copy(img_hbm, img_ref, xsem.at[9])
    img_load.start()
    ext_s[...] = jnp.zeros_like(ext_s)
    ext_s[0:4] = ea_ref[...]
    ext_s[4:14] = ba_ref[...]
    ext = jnp.transpose(ext_s[...]).astype(bf16)
    pack_temporal(t_ref.at[zi, core], convs_ref, film_ref, skip_ref, down_ref, ext)

    line_barrier(cams, nz)

    def tz_copy(k, way):
        ref = t_ref.at[k, core, cam]
        return batch_copy(ref, ref, tzsend.at[way, k], tzrecv.at[k], me - 2 + 4 * way)

    def tc_copy(k, which, q):
        ref = t_ref.at[k, which, q]
        return batch_copy(ref, ref, tcsend.at[k, q], tcrecv.at[k, q], partner)

    def tp_copy(k, step, q):
        ref = t_ref.at[k, core, q]
        return cam_copy(ref, ref, tpsend.at[step - 1, k], tprecv.at[step - 1, k], (cam + step) % cams)

    def t_send(s):
        for k, _, passed, way in moves(s):
            @pl.when(passed)
            def _():
                tz_copy(k, way).start()

    def t_receive(s):
        for k, held, _, way in moves(s):
            @pl.when(held)
            def _():
                tz_copy(k, way).wait_recv()
                for step in range(1, cams):
                    tp_copy(k, step, cam).start()
                tc_copy(k, core, cam).start()

    def t_collect(d):
        for k, held, _, _ in moves(d):
            @pl.when(held & (d > 0))
            def _():
                for step in range(1, cams):
                    q = (cam + cams - step) % cams
                    tp_copy(k, step, q).wait_recv()
                    tc_copy(k, core, q).start()

    def t_complete():
        def body(k, carry):
            for q in range(cams):
                tc_copy(k, 1 - core, q).wait_recv()
            return carry

        lax.fori_loop(0, nz, body, 0)

    ns, nf = traj_ref.shape[0], traj_ref.shape[1]
    frows = ns * nf
    obs = arr_s.shape[1]
    cond = obs * CH + emb_ref.shape[1]
    edge = 2 * ns
    per_pos = frows // n_img
    gones_shape = CH // GROUPS
    ginv = 1.0 / (nf * gones_shape)

    class Part:
        def __init__(self, ref, index, lo, wide):
            self.ref, self.index, self.lo, self.wide = ref, index, lo, wide

        def where(self, key):
            if not isinstance(key, tuple):
                return self.index(slice(self.lo, self.lo + self.wide))
            start, stop, _ = key[1].indices(self.wide)
            return self.index(slice(self.lo + start, self.lo + stop))

        def __getitem__(self, key):
            v = self.ref[self.where(key)]
            return v.reshape(CH, v.shape[-1])

        def __setitem__(self, key, v):
            self.ref[self.where(key)] = v.reshape(nz, 2, rows, v.shape[-1])

    def weight(q, lo, wide):
        return Part(t_ref, lambda cols: (slice(None), slice(None), q, slice(None), cols), lo, wide)

    def grad(buf, lo, wide):
        return Part(dt_buf, lambda cols: (buf, slice(None), slice(None), slice(None), cols), lo, wide)

    wa, wb = weight(0, 0, PART), weight(1, 0, PART)
    f0, f1, wext = weight(2, 0, cond), weight(2, cond, cond), weight(2, 2 * cond, BLK)
    ws, wd = weight(3, 0, CH), weight(3, CH, 3 * CH)

    def dt_save(q, buf):
        return pltpu.make_async_copy(dt_buf.at[buf], dt_out.at[:, :, q], dsem.at[q])

    def blank(buf, lo):
        dt_buf[buf, :, :, :, lo:] = jnp.zeros((nz, 2, rows, PART - lo), bf16)

    def tail(i):
        return taff_ref[4 + i : 5 + i, :]

    def frames(v):
        return v.reshape(nf, ns, CH)

    def keep(i, v):
        z1_ref[per_pos * i : per_pos * (i + 1)] = v.reshape(per_pos, n_img, CH)

    def kept(i):
        return z1_ref[per_pos * i : per_pos * (i + 1)].reshape(nf, ns, CH)

    def fill_edges(pad_ref):
        pad_ref[0:edge, :] = jnp.zeros((edge, CH), bf16)
        pad_ref[edge + frows : edge + frows + edge, :] = jnp.zeros((edge, CH), bf16)

    def fill(pad_ref, v):
        fill_edges(pad_ref)
        pad_ref[edge : edge + frows, :] = v.astype(bf16).reshape(frows, CH)

    def conv5(pad_ref, w):
        return sum(
            dot(pad_ref[t * ns : t * ns + frows, :], w[:, t * CH : (t + 1) * CH], NT) for t in range(5)
        )

    def conv5_back(pad_ref, w):
        return sum(
            dot(pad_ref[(4 - t) * ns : (4 - t) * ns + frows, :], w[:, t * CH : (t + 1) * CH]) for t in range(5)
        )

    def gsum(v):
        return group_sum(v, group_ones(CH, gones_shape)) * ginv

    def norm(v):
        v = frames(v)
        centred = v - gsum(jnp.sum(v, axis=0))[None]
        rstd = lax.rsqrt(gsum(jnp.sum(centred * centred, axis=0)) + norm_eps)
        return centred * rstd[None], rstd

    def norm_back(du, z, rstd, gain):
        s0 = jnp.sum(du, axis=0)
        s1 = jnp.sum(du * z, axis=0)
        dv = (du * gain[None] - gsum(s0 * gain)[None] - z * gsum(s1 * gain)[None]) * rstd[None]
        return dv, jnp.sum(s1, axis=0, keepdims=True), jnp.sum(s0, axis=0, keepdims=True)

    def total(v):
        return jnp.sum(v, axis=(0, 1)).reshape(1, CH)

    def across(v):
        return jnp.transpose(v.reshape(frows, CH)).astype(bf16)

    def temporal_early():
        taff_ref[...] = jnp.transpose(wext[...].astype(f32))
        ag_ref[...] = jnp.zeros_like(ag_ref)
        traj = pad_t[edge : edge + frows, :]
        za, rstd = norm(conv5(pad_t, wa) + tail(4))
        rstd_ref[...] = rstd
        keep(0, za)
        keep(1, dot(traj, ws[...], NT) + tail(8))
        og = og_ref[...]
        dcols = [dot(og, wd[:, t * CH : (t + 1) * CH]).reshape(nf // 2, ns, CH) for t in range(3)]
        before = jnp.concatenate([dcols[0][1:], jnp.zeros((1, ns, CH), f32)], axis=0)
        dsum = jnp.stack([dcols[1], dcols[2] + before], axis=1).reshape(nf, ns, CH)
        keep(2, dsum)
        ag_ref[8:9, :] = total(dsum)
        ag_ref[9:10, :] = jnp.sum(og.astype(f32), axis=0, keepdims=True)
        dskip = dsum.astype(bf16).reshape(frows, CH)
        grad(0, 0, CH)[...] = dot(across(dsum), traj).astype(bf16)
        blank(0, 4 * CH)
        tg_ref[...] = dot(dskip, ws[...])

    def view_copy(to, sender):
        return cam_copy(dviews_ref.at[to], gp_s.at[:, sender], vsend.at[to], vrecv.at[sender], to)

    def temporal_rest():
        mask = mask_ref[...]
        seen = jnp.sum(mask, axis=1, keepdims=True)
        conds, slopes = [], []
        for o in range(obs):
            pooled = sum(mask[:, c : c + 1] * arr_s[c, o].astype(f32) for c in range(cams))
            value, slope = mish_pair(pooled / seen)
            conds.append(value.astype(bf16))
            slopes.append(slope)
        conds.append(mish_value(emb_ref[...]).astype(bf16))
        lanes = [slice(o * CH, (o + 1) * CH) for o in range(obs)] + [slice(obs * CH, cond)]
        scale, shift = [
            sum(dot(v, w[:, cols], NT) for v, cols in zip(conds, lanes)) + tail(i) for i, w in ((6, f0), (7, f1))
        ]
        za = kept(0)
        fill(pad_m, mish_value(za * tail(0)[None] + tail(1)[None]) * scale[None] + shift[None])
        zb, rstd_b = norm(conv5(pad_m, wb) + tail(5))
        act_b, slope = mish_pair(zb * tail(2)[None] + tail(3)[None])
        keep(3, act_b + kept(1))
        dhb, ag_ref[2:3, :], ag_ref[3:4, :] = norm_back(kept(2) * slope, zb, rstd_b, tail(2))
        ag_ref[5:6, :] = total(dhb)
        fill(pad_h, dhb)
        dmid = frames(conv5_back(pad_h, wb))
        za = kept(0)
        act_a, slope = mish_pair(za * tail(0)[None] + tail(1)[None])
        dscale = jnp.sum(dmid * act_a, axis=0)
        dshift = jnp.sum(dmid, axis=0)
        lows = (dscale.astype(bf16), dshift.astype(bf16))
        for o in range(obs):
            dcond = dot(lows[0], f0[:, lanes[o]]) + dot(lows[1], f1[:, lanes[o]])
            dview = dcond * slopes[o] / seen
            for c in range(cams):
                dviews_ref[c, o] = (mask[:, c : c + 1] * dview).astype(bf16)
        for step in range(1, cams):
            view_copy((cam + step) % cams, cam).start()
        gp_s[:, cam] = dviews_ref[cam]

        dha, ag_ref[0:1, :], ag_ref[1:2, :] = norm_back(dmid * scale[None] * slope, za, rstd_ref[...], tail(0))
        ag_ref[4:5, :] = total(dha)
        ag_ref[6:7, :] = jnp.sum(dscale, axis=0, keepdims=True)
        ag_ref[7:8, :] = jnp.sum(dshift, axis=0, keepdims=True)
        dwb = grad(1, 0, PART)
        hb = across(dhb)
        for t in range(5):
            dwb[:, t * CH : (t + 1) * CH] = dot(hb, pad_m[t * ns : t * ns + frows, :]).astype(bf16)
        dt_save(1, 1).start()
        pairs = kept(3).astype(bf16).reshape(nf // 2, 2, ns, CH)
        half = frows // 2
        sum_ref[0:ns, :] = jnp.zeros((ns, CH), bf16)
        sum_ref[ns : ns + half, :] = pairs[:, 1].reshape(half, CH)
        sum_ref[ns + half : ns + 2 * half, :] = pairs[:, 0].reshape(half, CH)
        og = jnp.transpose(og_ref[...].astype(f32)).astype(bf16)
        dwd = grad(0, CH, 3 * CH)
        out = None
        for t, at in enumerate((0, ns + half, ns)):
            cols = sum_ref[at : at + half, :]
            part = dot(cols, wd[:, t * CH : (t + 1) * CH], NT)
            out = part if out is None else out + part
            dwd[:, t * CH : (t + 1) * CH] = dot(og, cols).astype(bf16)
        dt_save(3, 0).start()
        out_ref[...] = (out + tail(9)).astype(bf16)
        fill(pad_h, dha)
        tg_ref[...] = tg_ref[...] + conv5_back(pad_h, wa)
        dt_save(1, 1).wait()
        for base, low in zip((0, cond), lows):
            dw = grad(1, base, cond)
            for v, cols in zip(conds, lanes):
                dw[:, cols] = dot(low, v, TN).astype(bf16)
        grad(1, 2 * cond, BLK)[...] = jnp.transpose(ag_ref[...]).astype(bf16)
        blank(1, 2 * cond + BLK)
        dt_save(2, 1).start()
        dt_save(3, 0).wait()
        dwa = grad(0, 0, PART)
        ha = across(dha)
        for t in range(5):
            dwa[:, t * CH : (t + 1) * CH] = dot(ha, pad_t[t * ns : t * ns + frows, :]).astype(bf16)
        dt_save(0, 0).start()
        for step in range(1, cams):
            other = (cam + step) % cams
            view_copy(other, other).wait_recv()
        gp_ref[...] = gp_s[...]
        dt_save(2, 1).wait()
        dt_save(0, 0).wait()

    def z_copy(conv, k, way):
        ref = w_ref.at[conv, 2 * k + core]
        return batch_copy(ref, ref, zsend.at[conv, way, k], zrecv.at[conv, k], me - 2 + 4 * way)

    def core_copy(conv, k, which):
        ref = w_ref.at[conv, 2 * k + which]
        return batch_copy(ref, ref, csend.at[conv, k], crecv.at[conv, k], partner)

    def moves(s):
        low, high = zi - s, zi + s
        return (
            (high, high < nz, (high < nz) & (zi > 0), 0),
            (low, low >= 0, (low >= 0) & (zi < nz - 1), 1),
        )

    def send(conv, s):
        for k, _, passed, way in moves(s):
            @pl.when(passed)
            def _():
                z_copy(conv, k, way).start()

    def receive(conv, s):
        for k, held, _, way in moves(s):
            @pl.when(held)
            def _():
                z_copy(conv, k, way).wait_recv()
                core_copy(conv, k, core).start()

    t_send(0)
    for q in range(cams):
        tc_copy(zi, core, q).start()
    for conv in range(2):
        w_ref[conv, me, :, 9 * CH :] = ext
    count = rows // piece

    def pack(i, carry):
        @pl.when(i + 1 < count)
        def _():
            enc_load(i + 1).start()

        enc_load(i).wait()
        for conv in range(2):
            w_ref[conv, me, pl.ds(pl.multiple_of(i * piece, piece), piece), 0 : 9 * CH] = (
                enc_buf[i % 2, :, conv, :].astype(bf16)
            )
        return carry

    lax.fori_loop(0, count, pack, 0)

    def x_save(p):
        return pltpu.make_async_copy(x_ref.at[:, p * CH : (p + 1) * CH], x_out.at[p], xsem.at[p])

    fill_edges(pad_t)
    moved = traj_ref[...].astype(f32)
    for f in range(nf):
        pad_t[edge + f * ns : edge + (f + 1) * ns, :] = moved[:, f].astype(bf16)
    moved = og_in[...].astype(f32)
    for f in range(nf // 2):
        og_ref[f * ns : (f + 1) * ns, :] = moved[:, f].astype(bf16)
    half = n_img // 2
    img_load.wait()
    for p in range(9):
        pair = img_ref[:, p].astype(f32)
        for o in range(2):
            x_ref[o * half : (o + 1) * half, p * CH : (p + 1) * CH] = pair[:, o].astype(bf16)
        x_save(p).start()
    for conv in range(2):
        core_copy(conv, zi, core).start()

    def t_step(s, carry):
        @pl.when(s == nz - 1)
        def _():
            send(0, 0)

        t_receive(s)

        @pl.when(s < nz - 1)
        def _():
            t_send(s)
        return carry

    lax.fori_loop(1, nz, t_step, 0)

    def rows_of(conv, j, start, wide):
        block = w_ref[conv, pl.ds(j * spb, spb), :, start : start + wide]
        return block.reshape(BLK, wide)

    def w_save(conv, j):
        part = pl.ds(j * spb, spb)
        return pltpu.make_async_copy(w_ref.at[conv, part], w_out.at[conv, part], wsem.at[conv, j])

    def conv_norm(src_ref, conv, z_ref, r_ref, j):
        lanes = pl.ds(pl.multiple_of(j * BLK, BLK), BLK)
        total = None
        for p in range(9):
            r, c = divmod(p, 3)
            bs = span(c)
            acc = None
            for a in span(r):
                start = (3 * (r + a - 1) + c + bs[0] - 1) * CH
                wide = len(bs) * CH
                part = dot(src_ref[:, start : start + wide], rows_of(conv, j, (3 * a + bs[0]) * CH, wide), NT)
                acc = part if acc is None else acc + part
            z_ref[p, :, lanes] = acc
            total = acc if total is None else total + acc
        mean = group_sum(total, ones) * inv_n
        var = None
        for p in range(9):
            centred = z_ref[p, :, lanes] - mean
            sq = centred * centred
            var = sq if var is None else var + sq
        rstd = lax.rsqrt(group_sum(var, ones) * inv_n + norm_eps)
        r_ref[:, lanes] = rstd
        return lanes, mean, rstd

    def first(j):
        aff_ref[:, lanes_of(j)] = jnp.transpose(rows_of(0, j, 9 * CH, BLK).astype(f32))[0:8]
        lanes, mean, rstd = conv_norm(x_ref, 0, z1_ref, r1_ref, j)
        gain, offset = aff_ref[0:1, lanes], aff_ref[1:2, lanes]
        for p in range(9):
            z = (z1_ref[p, :, lanes] - mean) * rstd
            z1_ref[p, :, lanes] = z
            u = z * gain + offset
            a_ref[:, pl.ds(pl.multiple_of(p * CH + j * BLK, BLK), BLK)] = (u * sigmoid(u)).astype(bf16)

    def second(j):
        lanes, mean, rstd = conv_norm(a_ref, 1, z2_ref, r2_ref, j)
        gain, offset = aff_ref[2:3, lanes], aff_ref[3:4, lanes]
        total = None
        for p in range(9):
            z = (z2_ref[p, :, lanes] - mean) * rstd
            z2_ref[p, :, lanes] = z
            pic = x_ref[:, pl.ds(pl.multiple_of(p * CH + j * BLK, BLK), BLK)].astype(f32)
            u = z * gain + offset + pic
            act = u * sigmoid(u)
            total = act if total is None else total + act
        out = (total * (1.0 / 9.0)).astype(bf16)
        feat_ref[:, :, :, lanes] = out.reshape(feat_ref.shape[:3] + (BLK,))

    def lanes_of(j):
        return pl.ds(pl.multiple_of(j * BLK, BLK), BLK)

    def arrived(conv, k):
        core_copy(conv, k, 1 - core).wait_recv()

    def phase(conv, block):
        streaming = spb == 2

        def step(s, carry):
            if conv == 0:
                @pl.when((s > 0) & (s < nz - 1))
                def _():
                    send(0, s)

                @pl.when(s == nz - 1)
                def _():
                    send(1, 0)
            else:
                @pl.when((s > 0) & (s < nz - 1))
                def _():
                    send(1, s)

            def side(d, carry):
                k = zi + s - 2 * s * d

                @pl.when((k >= 0) & (k < nz) & (s + 1 > d))
                def _():
                    arrived(conv, k)
                    if streaming:
                        w_save(conv, k).start()
                        block(k)
                return carry

            lax.fori_loop(0, 2, side, 0)
            if conv == 1:
                t_collect(2 * s)
                t_collect(2 * s + 1)

                @pl.when(s == nz - 2)
                def _():
                    t_complete()
                    saves[0].wait()
                    temporal_early()

            @pl.when(s < nz - 1)
            def _():
                receive(conv, s + 1)
            return carry

        lax.fori_loop(0, nz, step, 0)
        if not streaming:
            def rest(j, carry):
                w_save(conv, j).start()
                block(j)
                return carry

            lax.fori_loop(0, CH // BLK, rest, 0)

    phase(0, first)
    saves = [pltpu.make_async_copy(z1_ref, z1_out, osem.at[0])]
    saves += [
        pltpu.make_async_copy(a_ref.at[:, p * CH : (p + 1) * CH], a_out.at[p], osem.at[2 + p])
        for p in range(9)
    ]
    for save in saves:
        save.start()
    phase(1, second)
    last = pltpu.make_async_copy(z2_ref, z2_out, osem.at[1])
    last.start()

    def feat_copy(to, sender):
        return cam_copy(feat_ref.at[:, to], arr_s.at[sender], fsend.at[to], frecv.at[sender], to)

    for step in range(1, cams):
        feat_copy((cam + step) % cams, cam).start()
    arr_s[cam] = feat_ref[:, cam]
    for step in range(1, cams):
        other = (cam + step) % cams
        feat_copy(other, other).wait_recv()
    temporal_rest()
    for step in range(1, cams):
        feat_copy((cam + step) % cams, cam).wait_send()

    for conv in range(2):
        def drain(k, carry):
            s = k - zi

            @pl.when((s >= 0) & (s < nz - 1) & (zi > 0))
            def _():
                z_copy(conv, k, 0).wait_send()

            @pl.when((s <= 0) & (s > 1 - nz) & (zi < nz - 1))
            def _():
                z_copy(conv, k, 1).wait_send()

            core_copy(conv, k, core).wait_send()
            return carry

        lax.fori_loop(0, nz, drain, 0)

        def saved(j, carry):
            w_save(conv, j).wait()
            return carry

        lax.fori_loop(0, CH // BLK, saved, 0)
    for save in saves[1:]:
        save.wait()
    last.wait()

    def t_drain(k, carry):
        s = k - zi

        @pl.when((s >= 0) & (s < nz - 1) & (zi > 0))
        def _():
            tz_copy(k, 0).wait_send()

        @pl.when((s <= 0) & (s > 1 - nz) & (zi < nz - 1))
        def _():
            tz_copy(k, 1).wait_send()

        @pl.when(s != 0)
        def _():
            for step in range(1, cams):
                tp_copy(k, step, cam).wait_send()

        for q in range(cams):
            tc_copy(k, core, q).wait_send()
        return carry

    lax.fori_loop(0, nz, t_drain, 0)
    for p in range(9):
        x_save(p).wait()
    for step in range(1, cams):
        view_copy((cam + step) % cams, cam).wait_send()


def enc_bwd_kernel(
    n, cams, cond, x_hbm, a_hbm, w_hbm, z1_hbm, r1_ref, z2_hbm, r2_ref, aff_ref, gp_ref, dt_hbm,
    ig_out, genc_ref, gaff_ref, gconvs_ref, gfilm_ref, gskip_ref, gdown_ref, gblk_ref,
    ig_ref, x_ref, a_ref, w_ref, z1_ref, z2_ref, g_ref, gt_ref, ag_ref,
    dwf, core_out, core_in, slots, t_own, t_sum, t_peer, t_slots, t_all,
    lsem, bsem, isem, csend, crecv, zsend, zrecv,
    tlsem, tcsend, tcrecv, tpsend, tprecv, tzsend, tzrecv, tfsend, tfrecv,
):
    nz = n // 2
    rows = CH // n
    n_img = z1_ref.shape[1]
    me, cam = lax.axis_index("batch"), lax.axis_index("cam")
    zi, core = me // 2, me % 2
    partner = me + 1 - 2 * core
    ones = group_ones(BLK, ENC_GROUP)
    inv_n = 1.0 / (9 * ENC_GROUP)
    chunk = 3 * CH

    def load_w(conv):
        return pltpu.make_async_copy(w_hbm.at[conv, :, :, 0 : 9 * CH], w_ref, lsem.at[3])

    def lanes_of(j):
        return pl.ds(pl.multiple_of(j * BLK, BLK), BLK)

    def block_loads(j):
        cols = lanes_of(j)
        return (
            pltpu.make_async_copy(z2_hbm.at[:, :, cols], z2_ref.at[:, :, cols], bsem.at[0, j]),
            pltpu.make_async_copy(x_hbm.at[:, :, cols], x_ref.at[:, :, cols], bsem.at[1, j]),
        )

    loads = {
        "z1": pltpu.make_async_copy(z1_hbm, z1_ref, lsem.at[1]),
        "a": pltpu.make_async_copy(a_hbm, a_ref, lsem.at[2]),
    }
    for j in range(CH // BLK):
        for load in block_loads(j):
            load.start()

    def own_load(i):
        return pltpu.make_async_copy(dt_hbm.at[i // cams, core, i % cams], t_own.at[i % 2], tlsem.at[i])

    own_load(0).start()

    line_greet(cams, nz)

    def t_core(k):
        return batch_copy(dt_hbm.at[k, 1 - core], t_sum.at[k], tcsend.at[k], tcrecv.at[k], partner)

    def t_peers(k, step):
        to = (cam + step) % cams
        return cam_copy(t_sum.at[k, to], t_peer.at[step - 1, k], tpsend.at[step - 1, k], tprecv.at[step - 1, k], to)

    def t_start(k, carry):
        t_core(k).start()
        return carry

    def t_spread(lo, hi):
        def body(k, carry):
            t_core(k).wait_recv()

            def quarter(q, carry):
                i = k * cams + q

                @pl.when(i + 1 < nz * cams)
                def _():
                    own_load(i + 1).start()

                own_load(i).wait()
                t_sum[k, q] = (t_sum[k, q].astype(f32) + t_own[i % 2].astype(f32)).astype(bf16)
                return carry

            lax.fori_loop(0, cams, quarter, 0)
            for step in range(1, cams):
                t_peers(k, step).start()
            return carry

        lax.fori_loop(lo, hi, body, 0)

    ag_ref[...] = jnp.zeros_like(ag_ref)

    def norm_back(du_ref, z_ref, r_ref, j, gain, row):
        lanes = lanes_of(j)
        s0 = jnp.zeros((n_img, BLK), f32)
        s1 = jnp.zeros((n_img, BLK), f32)
        for p in range(9):
            du = du_ref[p, :, lanes]
            s0 = s0 + du
            s1 = s1 + du * z_ref[p, :, lanes]
        ag_ref[row : row + 1, lanes] = jnp.sum(s1, axis=0, keepdims=True)
        ag_ref[row + 1 : row + 2, lanes] = jnp.sum(s0, axis=0, keepdims=True)
        m0 = group_sum(s0 * gain, ones) * inv_n
        m1 = group_sum(s1 * gain, ones) * inv_n
        rstd = r_ref[:, lanes]
        for p in range(9):
            dv = (du_ref[p, :, lanes] * gain - m0 - z_ref[p, :, lanes] * m1) * rstd
            g_ref[p, :, lanes] = dv.astype(bf16)
            gt_ref[lanes, p * n_img : (p + 1) * n_img] = jnp.transpose(dv).astype(bf16)

    def second(j, carry):
        lanes = lanes_of(j)
        for load in block_loads(j):
            load.wait()
        gain, offset = aff_ref[2:3, lanes], aff_ref[3:4, lanes]
        pooled = gp_ref[:, :, :, lanes].reshape(n_img, BLK).astype(f32) * (1.0 / 9.0)
        for p in range(9):
            u = z2_ref[p, :, lanes] * gain + offset + x_ref[p, :, lanes].astype(f32)
            s = sigmoid(u)
            ig_ref[p, :, lanes] = pooled * (s * (1.0 + u * (1.0 - s)))
        norm_back(ig_ref, z2_ref, r2_ref, j, gain, 2)
        return carry

    def first(j, carry):
        lanes = lanes_of(j)
        gain, offset = aff_ref[0:1, lanes], aff_ref[1:2, lanes]
        for p in range(9):
            u = z1_ref[p, :, lanes] * gain + offset
            s = sigmoid(u)
            z2_ref[p, :, lanes] = z2_ref[p, :, lanes] * (s * (1.0 + u * (1.0 - s)))
        norm_back(z2_ref, z1_ref, r1_ref, j, gain, 0)
        return carry

    def width(k):
        return chunk + BLK if k == 5 else chunk

    def core_copy(k):
        cols = pl.ds(0, width(k))
        return batch_copy(
            core_out.at[k % 2, :, :, cols], core_in.at[k % 3, :, :, cols], csend.at[k], crecv.at[k], partner
        )

    def keep(k, d0, lane, v):
        count, wide = v.shape[0] // (2 * rows), v.shape[1]
        parts = v.reshape(count, 2, rows, wide)
        even, odd = parts[:, 0], parts[:, 1]
        dwf[k % 2, d0 : d0 + count, :, lane : lane + wide] = jnp.where(core == 0, even, odd)
        core_out[k % 2, d0 : d0 + count, :, lane : lane + wide] = jnp.where(core == 0, odd, even).astype(bf16)

    def make_chunk(k):
        if k >= 2:
            core_copy(k - 2).wait_send()
        src_ref = a_ref if k < 3 else x_ref
        a = k % 3
        r_lo, r_hi = max(0, 1 - a), min(2, 3 - a)
        for b in range(3):
            c_lo, c_hi = max(0, 1 - b), min(2, 3 - b)
            if b == 1:
                runs = [(3 * r_lo, 3 * (r_hi - r_lo + 1))]
            else:
                runs = [(3 * r + c_lo, c_hi - c_lo + 1) for r in range(r_lo, r_hi + 1)]
            shift = 3 * (a - 1) + b - 1
            for half in range(2):
                acc = None
                for p, m in runs:
                    part = dot(
                        gt_ref[half * 256 : half * 256 + 256, p * n_img : (p + m) * n_img],
                        src_ref[p + shift : p + shift + m].reshape(m * n_img, CH),
                    )
                    acc = part if acc is None else acc + part
                keep(k, half * nz // 2, b * CH, acc)
        if k == 5:
            keep(k, 0, chunk, jnp.transpose(ag_ref[...]))
        core_copy(k).start()

    def term(k, d):
        return dwf[k % 2, d, :, 0 : width(k)] + core_in[k % 3, d, :, 0 : width(k)].astype(f32)

    def line_copy(k, way, s):
        if k == 6:
            return batch_copy(
                t_slots.at[way, s - 1], t_slots.at[way, s], tzsend.at[way, s], tzrecv.at[way, s], me - 2 + 4 * way
            )
        cols = pl.ds(0, width(k))
        return batch_copy(
            slots.at[k % 3, way, s - 1, :, cols], slots.at[k % 3, way, s, :, cols],
            zsend.at[k, way, s], zrecv.at[k, way, s], me - 2 + 4 * way,
        )

    def slot(k, way, s):
        return t_slots.at[way, s] if k == 6 else slots.at[k % 3, way, s, :, pl.ds(0, width(k))]

    def t_term(d):
        total = t_sum[d, cam].astype(f32)
        for step in range(1, cams):
            total = total + t_peer[step - 1, d].astype(f32)
        return total

    def serve(k, s):
        for way in range(2):
            ahead = zi if way else nz - 1 - zi
            d = nz - s + zi if way else s - nz + zi
            ref = slot(k, way, s - 1)

            @pl.when((ahead < nz - 1) & (s > ahead))
            def _():
                own = t_term(d) if k == 6 else term(k, d)

                @pl.when(ahead > 0)
                def _():
                    line_copy(k, way, s - 1).wait_recv()
                    ref[...] = (ref[...].astype(f32) + own).astype(bf16)

                @pl.when(ahead == 0)
                def _():
                    ref[...] = own.astype(bf16)

                line_copy(k, way, s).start()

    def steps(k, part):
        lo, hi = 1 + part * (nz - 1) // 3, 1 + (part + 1) * (nz - 1) // 3
        if hi - lo == 1:
            serve(k, lo)
        elif hi > lo:
            def body(s, carry):
                serve(k, s)
                return carry

            lax.fori_loop(lo, hi, body, 0)

    def service(g):
        k, part = divmod(g, 3)
        if part == 0:
            core_copy(k).wait_recv()
        steps(k, part)

    def collect(k, total, write):
        last = nz - 1

        @pl.when(zi > 0)
        def _():
            line_copy(k, 1, last).wait_recv()

        @pl.when(zi < nz - 1)
        def _():
            line_copy(k, 0, last).wait_recv()

        @pl.when(zi == 0)
        def _():
            write(total + slot(k, 0, last)[...].astype(f32))

        @pl.when(zi == nz - 1)
        def _():
            write(total + slot(k, 1, last)[...].astype(f32))

        @pl.when((zi > 0) & (zi < nz - 1))
        def _():
            write(total + slot(k, 0, last)[...].astype(f32) + slot(k, 1, last)[...].astype(f32))

        def drain(s, carry):
            for way in range(2):
                ahead = zi if way else nz - 1 - zi

                @pl.when((ahead < nz - 1) & (s > ahead))
                def _():
                    line_copy(k, way, s).wait_send()
            return carry

        lax.fori_loop(1, nz, drain, 0)

    def finish(k):
        def write(v):
            genc_ref[:, 1 - k // 3, (k % 3) * chunk : (k % 3 + 1) * chunk] = v[:, 0:chunk]
            if k == 5:
                gaff_ref[...] = jnp.transpose(v[:, chunk:])[0 : gaff_ref.shape[0]]

        collect(k, term(k, zi), write)

    def t_arrived():
        for step in range(1, cams):
            def body(k, carry):
                t_peers(k, step).wait_recv()
                return carry

            lax.fori_loop(0, nz, body, 0)

    def t_final(to, sender):
        return cam_copy(t_all.at[cam], t_all.at[sender], tfsend.at[to], tfrecv.at[sender], to)

    def t_finish():
        def write(v):
            t_all[cam] = v.astype(bf16)

        collect(6, t_term(zi), write)
        for step in range(1, cams):
            t_final((cam + step) % cams, cam).start()

    def t_write():
        for step in range(1, cams):
            other = (cam + step) % cams
            t_final(other, other).wait_recv()

        def cut(q, lo, wide):
            return t_all[q, :, lo : lo + wide].astype(f32)

        for which in range(2):
            gconvs_ref[:, which, :] = cut(which, 0, PART)
            gfilm_ref[:, which, :] = cut(2, which * cond, cond)
        gblk_ref[...] = jnp.transpose(cut(2, 2 * cond, BLK))[0 : gblk_ref.shape[0]]
        gskip_ref[...] = cut(3, 0, CH)
        gdown_ref[...] = cut(3, CH, 3 * CH)

    def input_back(q):
        r, c = divmod(q, 3)
        acc = None
        for a in range(3):
            for b in range(3):
                pr, pc = r - a + 1, c - b + 1
                if 0 <= pr < 3 and 0 <= pc < 3:
                    t = 3 * a + b
                    w = w_ref[:, :, t * CH : (t + 1) * CH].reshape(CH, CH)
                    part = dot(g_ref[3 * pr + pc], w)
                    acc = part if acc is None else acc + part
        return acc

    def back_second(*qs):
        for q in qs:
            if q == 0:
                load_w(1).wait()
            z2_ref[q] = input_back(q)
            if q == 8:
                load_w(0).start()

    def ig_save(q):
        return pltpu.make_async_copy(ig_ref.at[q], ig_out.at[q], isem.at[q])

    def back_first(*qs):
        for q in qs:
            if q == 0:
                load_w(0).wait()
            ig_ref[q] = ig_ref[q] + input_back(q)
            ig_save(q).start()

    def quarter_of(i):
        return i * nz // 4, (i + 1) * nz // 4

    def t_go(i):
        lax.fori_loop(*quarter_of(i), t_start, 0)

    lax.fori_loop(0, 1, second, 0)
    loads["a"].start()
    line_wait(cams, nz)
    lax.fori_loop(1, CH // BLK, second, 0)
    load_w(1).start()
    loads["a"].wait()
    make_chunk(0)
    service(0)
    t_go(0)
    make_chunk(1)
    service(1)
    t_go(1)
    t_spread(*quarter_of(0))
    loads["z1"].start()
    back_second(0, 1, 2)
    service(2)
    t_go(2)
    t_spread(*quarter_of(1))
    back_second(3, 4)
    service(3)
    finish(0)
    t_go(3)
    t_spread(*quarter_of(2))
    make_chunk(2)
    service(4)
    t_spread(*quarter_of(3))
    back_second(5, 6)
    service(5)
    back_second(7, 8)
    service(6)
    finish(1)
    loads["z1"].wait()
    lax.fori_loop(0, 2, first, 0)
    service(7)
    lax.fori_loop(2, 4, first, 0)
    service(8)
    make_chunk(3)
    service(9)
    finish(2)
    make_chunk(4)
    service(10)
    back_first(0, 1)
    service(11)
    back_first(2, 3)
    service(12)
    finish(3)
    make_chunk(5)
    service(13)
    back_first(4, 5)
    service(14)
    t_arrived()
    steps(6, 0)
    finish(4)
    back_first(6)
    steps(6, 1)
    back_first(7)
    steps(6, 2)
    back_first(8)
    service(15)
    t_finish()
    service(16)
    service(17)
    t_write()
    finish(5)

    for q in range(9):
        ig_save(q).wait()

    def t_drain(k, carry):
        t_core(k).wait_send()
        for step in range(1, cams):
            t_peers(k, step).wait_send()
        return carry

    lax.fori_loop(0, nz, t_drain, 0)
    for step in range(1, cams):
        t_final((cam + step) % cams, cam).wait_send()
    core_copy(4).wait_send()
    core_copy(5).wait_send()


def call(kernel, outs, in_specs, out_specs, scratch=(), collective_id=None, cost=None):
    extra = {} if collective_id is None else dict(collective_id=collective_id, has_side_effects=True)
    return pl.pallas_call(
        kernel,
        out_shape=[jax.ShapeDtypeStruct(s, d) for s, d in outs],
        in_specs=in_specs,
        out_specs=out_specs,
        scratch_shapes=list(scratch),
        compiler_params=pltpu.CompilerParams(vmem_limit_bytes=VMEM_BYTES, **extra),
        cost_estimate=cost,
    )


def work(microseconds):
    return pl.CostEstimate(
        flops=int(microseconds * 1e9), bytes_accessed=int(microseconds * 3e6), transcendentals=0
    )


V = pl.BlockSpec(memory_space=pltpu.VMEM)
H = pl.BlockSpec(memory_space=pl.ANY)
DMA = pltpu.SemaphoreType.DMA


def time_embed(steps_given, embed_width):
    half_width = embed_width // 2
    frequency = jnp.exp(
        jnp.arange(half_width, dtype=jnp.float32) * (-math.log(10000.0) / (half_width - 1))
    )
    argument = steps_given.astype(jnp.float32)[:, None] * frequency[None, :]
    return jnp.concatenate([jnp.sin(argument), jnp.cos(argument)], axis=1)


def adamw(weight, gradient, moment_one, moment_two, step_rate, weight_decay):
    mean_new = beta_first * moment_one + (1.0 - beta_first) * gradient
    square_new = beta_second * moment_two + (1.0 - beta_second) * gradient * gradient
    square_hat = square_new * (1.0 / (1.0 - beta_second**STEP))
    root = square_hat * lax.rsqrt(square_hat)
    weight_new = (1.0 - step_rate * weight_decay) * weight - (step_rate / (1.0 - beta_first**STEP)) * (
        mean_new / (root + adam_eps)
    )
    return (weight_new, mean_new, square_new)


def last_kernel(*refs):
    tg_ref, out_ref, ig_ref = refs[28:31]
    tg_new, out_new, ig_new, turn_ref = refs[52:56]
    for p in range(ig_ref.shape[0]):
        for o in range(ig_ref.shape[1]):
            ig_new[:, p, o, :] = ig_ref[p, o]

    @pl.when(pl.program_id(0) == 0)
    def _():
        for f in range(tg_ref.shape[0]):
            tg_new[:, f, :] = tg_ref[f]
        for u in range(out_ref.shape[0]):
            turn_ref[:, u, :] = out_ref[u].astype(f32)
        out_new[...] = turn_ref[...].astype(bf16)

    for i in range(7):
        w_ref, m_ref, v_ref, g_ref = refs[4 * i : 4 * i + 4]
        outs = refs[31 + 3 * i : 34 + 3 * i]

        def update():
            vector = i in (1, 6)
            rate, decay = (rate_vector, 0.0) if vector else (rate_matrix, decay_matrix)
            new = adamw(w_ref[...], g_ref[...], m_ref[...], v_ref[...], rate, decay)
            for ref, value in zip(outs, new):
                ref[...] = value

        if i in (1, 6):
            pl.when(pl.program_id(0) == 0)(update)
        else:
            update()


def last_call(shown, grads, tg, out, ig, rows):
    step = min(rows, 8)
    steps = rows // step

    def whole(shape):
        return pl.BlockSpec(shape, lambda r: (0,) * len(shape))

    def spec(v):
        if v.shape[0] != rows:
            return whole(v.shape)
        return pl.BlockSpec((step,) + v.shape[1:], lambda r: (r,) + (0,) * (v.ndim - 1))

    ins = []
    for i in range(7):
        ins += [shown[0][i], shown[1][i], shown[2][i], grads[i]]
    outs = [w for w in shown[0] for _ in range(3)]
    pos, obs, count, ch = ig.shape
    part = count // steps
    turned = [(v.shape[1], v.shape[0], v.shape[2]) for v in (tg, out)]
    return pl.pallas_call(
        last_kernel,
        grid=(steps,),
        out_shape=[jax.ShapeDtypeStruct(v.shape, f32) for v in outs]
        + [jax.ShapeDtypeStruct(turned[0], f32), jax.ShapeDtypeStruct(turned[1], bf16),
           jax.ShapeDtypeStruct((count, pos, obs, ch), f32)],
        in_specs=[spec(v) for v in ins]
        + [whole(tg.shape), whole(out.shape), pl.BlockSpec((pos, obs, part, ch), lambda r: (0, 0, r, 0))],
        out_specs=[spec(v) for v in outs]
        + [whole(turned[0]), whole(turned[1]), pl.BlockSpec((part, pos, obs, ch), lambda r: (r, 0, 0, 0))],
        scratch_shapes=[pltpu.VMEM(turned[1], f32)],
        compiler_params=pltpu.CompilerParams(vmem_limit_bytes=VMEM_BYTES),
        cost_estimate=work(15),
    )(*ins, tg, out, ig)


def shards(
    n, images, trajectory, view_mask, timesteps, out_grad,
    encoder_weight, encoder_affine, block_convs, film_weight, skip_weight, down_weight, block_affine,
    first_encoder, first_affine, first_convs, first_film, first_skip, first_down, first_block,
    second_encoder, second_affine, second_convs, second_film, second_skip, second_down, second_block,
):
    ns, nf, ch = trajectory.shape
    cams, obs = images.shape[1], images.shape[3]
    n_img = cams * images.shape[2] * obs
    nz, per = n // 2, ch // n
    cond = film_weight.shape[2]
    wide = 9 * ch
    rows = nf * ns

    def turned(v):
        return jnp.transpose(v.reshape(v.shape[-2:]))

    pairs = jnp.transpose(images[0], (0, 1, 3, 2, 4)).reshape(n_img // obs, 9, obs, ch)
    pos = (9, n_img, ch)
    t_shape = (nz, 2, cams, per, PART)
    wcols = wide + BLK
    z1, r1, act, z2, r2, w_all, enc_aff, x, out_fm, tg_fm, gp, dt = call(
        functools.partial(forward_kernel, n, cams),
        [(pos, f32), ((n_img, ch), f32), (pos, bf16), (pos, f32), ((n_img, ch), f32), ((2, n, per, wcols), bf16),
         ((8, ch), f32), (pos, bf16), ((rows // 2, ch), bf16), ((rows, ch), f32), ((obs, cams, ns, ch), bf16),
         (t_shape, bf16)],
        [H, V, V, V, V, H, V, V, V, V, V, V],
        [H, V, H, H, V, H, V, H, V, V, V, H],
        [pltpu.VMEM((n_img // obs, 9, obs, ch), bf16), pltpu.VMEM((n_img, wide), bf16), pltpu.VMEM((2, n, per, wcols), bf16), pltpu.VMEM(pos, f32),
         pltpu.VMEM((n_img, wide), bf16), pltpu.VMEM(pos, f32), pltpu.VMEM((obs, cams, ns, ch), bf16),
         pltpu.VMEM((cams, obs, ns, ch), bf16), pltpu.VMEM(t_shape, bf16), pltpu.VMEM((2, min(per, 16), 2, wide), f32),
         pltpu.VMEM((BLK, per), f32), pltpu.VMEM((rows // 2, ch), bf16), pltpu.VMEM((rows + 4 * ns, ch), bf16),
         pltpu.VMEM((rows + 4 * ns, ch), bf16), pltpu.VMEM((rows + 4 * ns, ch), bf16), pltpu.VMEM((rows + ns, ch), bf16),
         pltpu.VMEM((BLK, ch), f32), pltpu.VMEM((BLK, ch), f32), pltpu.VMEM((ns, ch), f32),
         pltpu.VMEM((cams, obs, ns, ch), bf16), pltpu.VMEM((obs, cams, ns, ch), bf16),
         pltpu.VMEM((2, nz, 2, per, PART), bf16),
         DMA((2, 2, nz)), DMA((2, nz)), DMA((2, nz)), DMA((2, nz)), DMA((2, ch // BLK)), DMA((11,)),
         DMA((cams,)), DMA((cams,)),
         DMA((2, nz)), DMA((nz,)), DMA((nz, cams)), DMA((nz, cams)), DMA((cams - 1, nz)), DMA((cams - 1, nz)),
         DMA((max(per // 16, 1),)), DMA((10,)), DMA((cams,)), DMA((cams,)), DMA((4,))],
        collective_id=0,
        cost=work(130),
    )(pairs, trajectory, out_grad, view_mask.astype(f32), time_embed(timesteps, TEMB), encoder_weight[0], block_convs,
      film_weight, skip_weight, down_weight, turned(encoder_affine), turned(block_affine))
    chunk = 3 * ch + BLK
    ig, genc, gaff, gconvs, gfilm, gskip, gdown, gblk = call(
        functools.partial(enc_bwd_kernel, n, cams, cond),
        [(pos, f32), ((per, 2, wide), f32), ((4, per), f32), ((per, 2, 5 * ch), f32),
         ((per, 2, cond), f32), ((per, ch), f32), ((per, 3 * ch), f32), ((10, per), f32)],
        [H, H, H, H, V, H, V, V, V, H],
        [H] + [V] * 7,
        [pltpu.VMEM(pos, f32), pltpu.VMEM(pos, bf16), pltpu.VMEM(pos, bf16), pltpu.VMEM((n, per, wide), bf16), pltpu.VMEM(pos, f32),
         pltpu.VMEM(pos, f32), pltpu.VMEM(pos, bf16), pltpu.VMEM((ch, 9 * n_img), bf16),
         pltpu.VMEM((BLK, ch), f32),
         pltpu.VMEM((2, nz, per, chunk), f32), pltpu.VMEM((2, nz, per, chunk), bf16),
         pltpu.VMEM((3, nz, per, chunk), bf16), pltpu.VMEM((3, 2, nz, per, chunk), bf16),
         pltpu.VMEM((2, per, PART), bf16), pltpu.VMEM((nz, cams, per, PART), bf16),
         pltpu.VMEM((cams - 1, nz, per, PART), bf16), pltpu.VMEM((2, nz, per, PART), bf16),
         pltpu.VMEM((cams, per, PART), bf16),
         DMA((4,)), DMA((2, ch // BLK)), DMA((9,)), DMA((6,)), DMA((6,)), DMA((6, 2, nz)), DMA((6, 2, nz)),
         DMA((nz * cams,)), DMA((nz,)), DMA((nz,)), DMA((cams - 1, nz)), DMA((cams - 1, nz)),
         DMA((2, nz)), DMA((2, nz)), DMA((cams,)), DMA((cams,))],
        collective_id=1,
        cost=work(100),
    )(x, act, w_all, z1, r1, z2, r2, enc_aff, gp, dt)
    weights = (encoder_weight, encoder_affine, block_convs, film_weight, skip_weight, down_weight, block_affine)
    firsts = (first_encoder, first_affine, first_convs, first_film, first_skip, first_down, first_block)
    seconds = (second_encoder, second_affine, second_convs, second_film, second_skip, second_down, second_block)
    shown = [
        [turned(v) if i in (1, 6) else v.reshape(v.shape[-3:]) if i == 0 else v for i, v in enumerate(group)]
        for group in (weights, firsts, seconds)
    ]
    *news, trajectory_grad, block_output, ig_new = last_call(
        shown, (genc, gaff, gconvs, gfilm, gskip, gdown, gblk),
        tg_fm.reshape(nf, ns, ch), out_fm.reshape(nf // 2, ns, ch), ig.reshape(9, obs, n_img // obs, ch), per,
    )
    images_grad = jnp.transpose(ig_new.reshape(images.shape[1:3] + ig_new.shape[1:]), (0, 1, 3, 2, 4))[None]
    upd = [
        tuple((turned(v) if i in (1, 6) else v).reshape(w.shape) for v in news[3 * i : 3 * i + 3])
        for i, w in enumerate(weights)
    ]
    return (
        (block_output, trajectory_grad, images_grad)
        + tuple(u[0] for u in upd)
        + tuple(u[1] for u in upd)
        + tuple(u[2] for u in upd)
    )


def solution(mesh):
    sample = P(("cam", "batch"))
    params = (P("cam", "batch"), P("cam", "batch")) + (P("batch"),) * 5
    images_spec = P("cam", None, "batch")
    return jax.shard_map(
        functools.partial(shards, mesh.shape["batch"]),
        mesh=mesh,
        in_specs=(images_spec, sample, sample, sample, sample) + params * 3,
        out_specs=(sample, sample, images_spec) + params * 3,
        check_vma=False,
    )
```

```python
import functools
import math

import jax
import jax.numpy as jnp
from jax import lax
from jax.experimental import pallas as pl
from jax.experimental.pallas import tpu as pltpu
from jax.sharding import PartitionSpec as P

TEMB = 128
GROUPS = 8
STEP = 5

norm_eps = 1e-05
beta_first = 0.5
beta_second = 0.5
adam_eps = 1e-08
rate_matrix = 0.02
rate_vector = 0.2
decay_matrix = 0.01

CH = 512
BLK = 128
ENC_GROUP = 16
f32 = jnp.float32
bf16 = jnp.bfloat16
VMEM_BYTES = 61 * 1024 * 1024

NT = (((1,), (1,)), ((), ()))
NN = (((1,), (0,)), ((), ()))
TN = (((0,), (0,)), ((), ()))


def dot(a, b, dims=NN):
    return lax.dot_general(a, b, dims, preferred_element_type=f32)


def group_ones(width, group):
    rows = lax.broadcasted_iota(jnp.int32, (width, width), 0) // group
    cols = lax.broadcasted_iota(jnp.int32, (width, width), 1) // group
    return jnp.where(rows == cols, 1.0, 0.0).astype(bf16)


def group_sum(v, ones):
    high = v.astype(bf16)
    rest = v - high.astype(f32)
    middle = rest.astype(bf16)
    low = (rest - middle.astype(f32)).astype(bf16)
    return dot(high, ones) + dot(middle, ones) + dot(low, ones)


def sigmoid(v):
    return 1.0 / (1.0 + jnp.exp(-v))


def mish_pair(v):
    e = jnp.exp(jnp.minimum(v, 20.0))
    n = e * (e + 2.0)
    inv = 1.0 / (n + 2.0)
    t = n * inv
    return v * t, t + v * (4.0 * e * (1.0 + e)) * inv * inv


def mish_value(v):
    e = jnp.exp(jnp.minimum(v, 20.0))
    n = e * (e + 2.0)
    return v * (n / (n + 2.0))


def span(i):
    return range(max(0, 1 - i), min(2, 3 - i) + 1)


MESH = pl.DeviceIdType.MESH


def batch_copy(src, dst, send_sem, recv_sem, target):
    return pltpu.make_async_remote_copy(
        src_ref=src, dst_ref=dst, send_sem=send_sem, recv_sem=recv_sem,
        device_id={"batch": target}, device_id_type=MESH,
    )


def cam_copy(src, dst, send_sem, recv_sem, target):
    return pltpu.make_async_remote_copy(
        src_ref=src, dst_ref=dst, send_sem=send_sem, recv_sem=recv_sem,
        device_id={"cam": target}, device_id_type=MESH,
    )


def line_wait(cams, nz):
    zi = lax.axis_index("batch") // 2
    ends = (zi == 0).astype(jnp.int32) + (zi == nz - 1).astype(jnp.int32)
    pl.semaphore_wait(pltpu.get_barrier_semaphore(), cams + 2 - ends)


def line_greet(cams, nz):
    me, cam = lax.axis_index("batch"), lax.axis_index("cam")
    zi, core = me // 2, me % 2
    barrier = pltpu.get_barrier_semaphore()
    pl.semaphore_signal(barrier, inc=1, device_id={"batch": me + 1 - 2 * core}, device_id_type=MESH)
    for step in range(1, cams):
        pl.semaphore_signal(barrier, inc=1, device_id={"cam": (cam + step) % cams}, device_id_type=MESH)

    @pl.when(zi > 0)
    def _():
        pl.semaphore_signal(barrier, inc=1, device_id={"batch": me - 2}, device_id_type=MESH)

    @pl.when(zi < nz - 1)
    def _():
        pl.semaphore_signal(barrier, inc=1, device_id={"batch": me + 2}, device_id_type=MESH)


PART = 5 * CH


def pack_part(q, ref, convs_ref, film_ref, skip_ref, down_ref, ext):
    rows, cond = film_ref.shape[0], film_ref.shape[2]
    if q < 2:
        ref[q] = convs_ref[:, q, :].astype(bf16)
    elif q == 2:
        for which in range(2):
            ref[2, :, which * cond : (which + 1) * cond] = film_ref[:, which, :].astype(bf16)
        ref[2, :, 2 * cond : 2 * cond + BLK] = ext
        ref[2, :, 2 * cond + BLK :] = jnp.zeros((rows, PART - 2 * cond - BLK), bf16)
    else:
        ref[3, :, 0:CH] = skip_ref[...].astype(bf16)
        ref[3, :, CH : 4 * CH] = down_ref[...].astype(bf16)
        ref[3, :, 4 * CH :] = jnp.zeros((rows, PART - 4 * CH), bf16)


def forward_kernel(
    n, cams, img_hbm, traj_ref, og_in, mask_in, emb_ref, enc_hbm, convs_ref, film_ref, skip_ref, down_ref,
    ea_ref, ba_ref,
    z1_out, r1_ref, a_out, z2_out, r2_ref, w_out, aff_ref, x_out, slope_out, out_ref, tg_ref, gp_ref, dt_out,
    img_ref, x_ref, w_ref, z1_ref, a_ref, z2_ref, feat_ref, arr_s, t_ref, enc_buf,
    mask_s, ext_s, og_ref, pad_t, pad_m, pad_h, sum_ref, taff_ref, ag_ref, rstd_ref, dviews_ref, gp_s, dt_buf,
    zsend, zrecv, csend, crecv, wsem, osem, fsend, frecv,
    tzsend, tzrecv, tcsend, tcrecv, tpsend, tprecv, esem, xsem, vsend, vrecv, dsem,
):
    nz = n // 2
    rows = skip_ref.shape[0]
    piece = enc_buf.shape[1]
    spb = BLK // rows
    n_img = x_ref.shape[0]
    me, cam = lax.axis_index("batch"), lax.axis_index("cam")
    zi, core = me // 2, me % 2
    partner = me + 1 - 2 * core
    ones = group_ones(BLK, ENC_GROUP)
    inv_n = 1.0 / (9 * ENC_GROUP)

    def enc_load(i):
        return pltpu.make_async_copy(enc_hbm.at[pl.ds(i * piece, piece)], enc_buf.at[i % 2], esem.at[i])

    enc_load(0).start()
    img_load = pltpu.make_async_copy(img_hbm, img_ref, xsem.at[9])
    img_load.start()
    ext_s[...] = jnp.zeros_like(ext_s)
    ext_s[0:4] = ea_ref[...]
    ext_s[4:14] = ba_ref[...]
    ext = jnp.transpose(ext_s[...]).astype(bf16)
    line_greet(cams, nz)

    def pack_own(q):
        pack_part(q, t_ref.at[zi, core], convs_ref, film_ref, skip_ref, down_ref, ext)

    for q in range(cams):
        pl.when(cam == q)(functools.partial(pack_own, q))
    line_wait(cams, nz)

    def tz_copy(k, way):
        ref = t_ref.at[k, core, cam]
        return batch_copy(ref, ref, tzsend.at[way, k], tzrecv.at[k], me - 2 + 4 * way)

    def tc_copy(k, which, q):
        ref = t_ref.at[k, which, q]
        return batch_copy(ref, ref, tcsend.at[k, q], tcrecv.at[k, q], partner)

    def tp_copy(k, step, q):
        ref = t_ref.at[k, core, q]
        return cam_copy(ref, ref, tpsend.at[step - 1, k], tprecv.at[step - 1, k], (cam + step) % cams)

    def t_send(s):
        for k, _, passed, way in moves(s):
            @pl.when(passed)
            def _():
                tz_copy(k, way).start()

    def t_receive(s):
        for k, held, _, way in moves(s):
            @pl.when(held)
            def _():
                tz_copy(k, way).wait_recv()
                for step in range(1, cams):
                    tp_copy(k, step, cam).start()
                tc_copy(k, core, cam).start()

    def t_collect(d):
        for k, held, _, _ in moves(d):
            @pl.when(held & (d > 0))
            def _():
                for step in range(1, cams):
                    q = (cam + cams - step) % cams
                    tp_copy(k, step, q).wait_recv()
                    tc_copy(k, core, q).start()

    def t_complete():
        def body(k, carry):
            for q in range(cams):
                tc_copy(k, 1 - core, q).wait_recv()
            return carry

        lax.fori_loop(0, nz, body, 0)

    ns, nf = traj_ref.shape[0], traj_ref.shape[1]
    frows = ns * nf
    obs = arr_s.shape[1]
    cond = obs * CH + emb_ref.shape[1]
    edge = 2 * ns
    per_pos = frows // n_img
    gones_shape = CH // GROUPS
    ginv = 1.0 / (nf * gones_shape)

    class Part:
        def __init__(self, ref, index, lo, wide):
            self.ref, self.index, self.lo, self.wide = ref, index, lo, wide

        def where(self, key):
            if not isinstance(key, tuple):
                return self.index(slice(self.lo, self.lo + self.wide))
            start, stop, _ = key[1].indices(self.wide)
            return self.index(slice(self.lo + start, self.lo + stop))

        def __getitem__(self, key):
            v = self.ref[self.where(key)]
            return v.reshape(CH, v.shape[-1])

        def __setitem__(self, key, v):
            self.ref[self.where(key)] = v.reshape(nz, 2, rows, v.shape[-1])

    def weight(q, lo, wide):
        return Part(t_ref, lambda cols: (slice(None), slice(None), q, slice(None), cols), lo, wide)

    def grad(buf, lo, wide):
        return Part(dt_buf, lambda cols: (buf, slice(None), slice(None), slice(None), cols), lo, wide)

    wa, wb = weight(0, 0, PART), weight(1, 0, PART)
    f0, f1, wext = weight(2, 0, cond), weight(2, cond, cond), weight(2, 2 * cond, BLK)
    ws, wd = weight(3, 0, CH), weight(3, CH, 3 * CH)

    def dt_save(q, buf):
        return pltpu.make_async_copy(dt_buf.at[buf], dt_out.at[:, :, q], dsem.at[q])

    def blank(buf, lo):
        dt_buf[buf, :, :, :, lo:] = jnp.zeros((nz, 2, rows, PART - lo), bf16)

    def tail(i):
        return taff_ref[4 + i : 5 + i, :]

    def frames(v):
        return v.reshape(nf, ns, CH)

    def keep(i, v):
        z1_ref[per_pos * i : per_pos * (i + 1)] = v.reshape(per_pos, n_img, CH)

    def kept(i):
        return z1_ref[per_pos * i : per_pos * (i + 1)].reshape(nf, ns, CH)

    def fill_edges(pad_ref):
        pad_ref[0:edge, :] = jnp.zeros((edge, CH), bf16)
        pad_ref[edge + frows : edge + frows + edge, :] = jnp.zeros((edge, CH), bf16)

    def fill(pad_ref, v):
        fill_edges(pad_ref)
        pad_ref[edge : edge + frows, :] = v.astype(bf16).reshape(frows, CH)

    def conv5(pad_ref, w):
        return sum(
            dot(pad_ref[t * ns : t * ns + frows, :], w[:, t * CH : (t + 1) * CH], NT) for t in range(5)
        )

    def conv5_back(pad_ref, w):
        return sum(
            dot(pad_ref[(4 - t) * ns : (4 - t) * ns + frows, :], w[:, t * CH : (t + 1) * CH]) for t in range(5)
        )

    def gsum(v):
        return group_sum(v, group_ones(CH, gones_shape)) * ginv

    def norm(v):
        v = frames(v)
        centred = v - gsum(jnp.sum(v, axis=0))[None]
        rstd = lax.rsqrt(gsum(jnp.sum(centred * centred, axis=0)) + norm_eps)
        return centred * rstd[None], rstd

    def norm_back(du, z, rstd, gain):
        s0 = jnp.sum(du, axis=0)
        s1 = jnp.sum(du * z, axis=0)
        dv = (du * gain[None] - gsum(s0 * gain)[None] - z * gsum(s1 * gain)[None]) * rstd[None]
        return dv, jnp.sum(s1, axis=0, keepdims=True), jnp.sum(s0, axis=0, keepdims=True)

    def total(v):
        return jnp.sum(v, axis=(0, 1)).reshape(1, CH)

    def across(v):
        return jnp.transpose(v.reshape(frows, CH)).astype(bf16)

    def temporal_early():
        taff_ref[...] = jnp.transpose(wext[...].astype(f32))
        ag_ref[...] = jnp.zeros_like(ag_ref)
        traj = pad_t[edge : edge + frows, :]
        za, rstd = norm(conv5(pad_t, wa) + tail(4))
        rstd_ref[...] = rstd
        keep(0, za)
        keep(1, dot(traj, ws[...], NT) + tail(8))
        og = og_ref[...]
        dcols = [dot(og, wd[:, t * CH : (t + 1) * CH]).reshape(nf // 2, ns, CH) for t in range(3)]
        before = jnp.concatenate([dcols[0][1:], jnp.zeros((1, ns, CH), f32)], axis=0)
        dsum = jnp.stack([dcols[1], dcols[2] + before], axis=1).reshape(nf, ns, CH)
        keep(2, dsum)
        ag_ref[8:9, :] = total(dsum)
        ag_ref[9:10, :] = jnp.sum(og.astype(f32), axis=0, keepdims=True)
        dskip = dsum.astype(bf16).reshape(frows, CH)
        grad(0, 0, CH)[...] = dot(across(dsum), traj).astype(bf16)
        blank(0, 4 * CH)
        tg_ref[...] = dot(dskip, ws[...])

    def view_copy(to, sender):
        return cam_copy(dviews_ref.at[to], gp_s.at[:, sender], vsend.at[to], vrecv.at[sender], to)

    def temporal_rest():
        mask_s[...] = jnp.zeros_like(mask_s)
        mask_s[0:cams, 0:ns] = mask_in[...].astype(f32)
        mask = jnp.transpose(mask_s[...])[0:ns, 0:cams]
        seen = jnp.sum(mask, axis=1, keepdims=True)
        conds, slopes = [], []
        for o in range(obs):
            pooled = sum(mask[:, c : c + 1] * arr_s[c, o].astype(f32) for c in range(cams))
            value, slope = mish_pair(pooled / seen)
            conds.append(value.astype(bf16))
            slopes.append(slope)
        conds.append(mish_value(emb_ref[...]).astype(bf16))
        lanes = [slice(o * CH, (o + 1) * CH) for o in range(obs)] + [slice(obs * CH, cond)]
        scale, shift = [
            sum(dot(v, w[:, cols], NT) for v, cols in zip(conds, lanes)) + tail(i) for i, w in ((6, f0), (7, f1))
        ]
        za = kept(0)
        fill(pad_m, mish_value(za * tail(0)[None] + tail(1)[None]) * scale[None] + shift[None])
        zb, rstd_b = norm(conv5(pad_m, wb) + tail(5))
        act_b, slope = mish_pair(zb * tail(2)[None] + tail(3)[None])
        keep(3, act_b + kept(1))
        dhb, ag_ref[2:3, :], ag_ref[3:4, :] = norm_back(kept(2) * slope, zb, rstd_b, tail(2))
        ag_ref[5:6, :] = total(dhb)
        fill(pad_h, dhb)
        dmid = frames(conv5_back(pad_h, wb))
        za = kept(0)
        act_a, slope = mish_pair(za * tail(0)[None] + tail(1)[None])
        dscale = jnp.sum(dmid * act_a, axis=0)
        dshift = jnp.sum(dmid, axis=0)
        lows = (dscale.astype(bf16), dshift.astype(bf16))
        for o in range(obs):
            dcond = dot(lows[0], f0[:, lanes[o]]) + dot(lows[1], f1[:, lanes[o]])
            dview = dcond * slopes[o] / seen
            for c in range(cams):
                dviews_ref[c, o] = (mask[:, c : c + 1] * dview).astype(bf16)
        for step in range(1, cams):
            view_copy((cam + step) % cams, cam).start()
        gp_s[:, cam] = dviews_ref[cam]

        dha, ag_ref[0:1, :], ag_ref[1:2, :] = norm_back(dmid * scale[None] * slope, za, rstd_ref[...], tail(0))
        ag_ref[4:5, :] = total(dha)
        ag_ref[6:7, :] = jnp.sum(dscale, axis=0, keepdims=True)
        ag_ref[7:8, :] = jnp.sum(dshift, axis=0, keepdims=True)
        dwb = grad(1, 0, PART)
        hb = across(dhb)
        for t in range(5):
            dwb[:, t * CH : (t + 1) * CH] = dot(hb, pad_m[t * ns : t * ns + frows, :]).astype(bf16)
        dt_save(1, 1).start()
        pairs = kept(3).astype(bf16).reshape(nf // 2, 2, ns, CH)
        half = frows // 2
        sum_ref[0:ns, :] = jnp.zeros((ns, CH), bf16)
        sum_ref[ns : ns + half, :] = pairs[:, 1].reshape(half, CH)
        sum_ref[ns + half : ns + 2 * half, :] = pairs[:, 0].reshape(half, CH)
        og = jnp.transpose(og_ref[...].astype(f32)).astype(bf16)
        dwd = grad(0, CH, 3 * CH)
        out = None
        for t, at in enumerate((0, ns + half, ns)):
            cols = sum_ref[at : at + half, :]
            part = dot(cols, wd[:, t * CH : (t + 1) * CH], NT)
            out = part if out is None else out + part
            dwd[:, t * CH : (t + 1) * CH] = dot(og, cols).astype(bf16)
        dt_save(3, 0).start()
        out_ref[...] = (out + tail(9)).astype(bf16)
        fill(pad_h, dha)
        tg_ref[...] = tg_ref[...] + conv5_back(pad_h, wa)
        dt_save(1, 1).wait()
        for base, low in zip((0, cond), lows):
            dw = grad(1, base, cond)
            for v, cols in zip(conds, lanes):
                dw[:, cols] = dot(low, v, TN).astype(bf16)
        grad(1, 2 * cond, BLK)[...] = jnp.transpose(ag_ref[...]).astype(bf16)
        blank(1, 2 * cond + BLK)
        dt_save(2, 1).start()
        dt_save(3, 0).wait()
        dwa = grad(0, 0, PART)
        ha = across(dha)
        for t in range(5):
            dwa[:, t * CH : (t + 1) * CH] = dot(ha, pad_t[t * ns : t * ns + frows, :]).astype(bf16)
        dt_save(0, 0).start()
        for step in range(1, cams):
            other = (cam + step) % cams
            view_copy(other, other).wait_recv()
        gp_ref[...] = gp_s[...]
        dt_save(2, 1).wait()
        dt_save(0, 0).wait()

    def z_copy(conv, k, way):
        ref = w_ref.at[conv, 2 * k + core]
        return batch_copy(ref, ref, zsend.at[conv, way, k], zrecv.at[conv, k], me - 2 + 4 * way)

    def core_copy(conv, k, which):
        ref = w_ref.at[conv, 2 * k + which]
        return batch_copy(ref, ref, csend.at[conv, k], crecv.at[conv, k], partner)

    def moves(s):
        low, high = zi - s, zi + s
        return (
            (high, high < nz, (high < nz) & (zi > 0), 0),
            (low, low >= 0, (low >= 0) & (zi < nz - 1), 1),
        )

    def send(conv, s):
        for k, _, passed, way in moves(s):
            @pl.when(passed)
            def _():
                z_copy(conv, k, way).start()

    def receive(conv, s):
        for k, held, _, way in moves(s):
            @pl.when(held)
            def _():
                z_copy(conv, k, way).wait_recv()
                core_copy(conv, k, core).start()

    t_send(0)
    for q in range(cams):
        pl.when(cam != q)(functools.partial(pack_own, q))
    for q in range(cams):
        tc_copy(zi, core, q).start()
    for conv in range(2):
        w_ref[conv, me, :, 9 * CH :] = ext
    count = rows // piece

    def pack(i, carry):
        @pl.when(i + 1 < count)
        def _():
            enc_load(i + 1).start()

        enc_load(i).wait()
        for conv in range(2):
            w_ref[conv, me, pl.ds(pl.multiple_of(i * piece, piece), piece), 0 : 9 * CH] = (
                enc_buf[i % 2, :, conv, :].astype(bf16)
            )
        return carry

    lax.fori_loop(0, count, pack, 0)

    def x_save(p):
        return pltpu.make_async_copy(x_ref.at[:, p * CH : (p + 1) * CH], x_out.at[p], xsem.at[p])

    fill_edges(pad_t)
    moved = traj_ref[...].astype(f32)
    for f in range(nf):
        pad_t[edge + f * ns : edge + (f + 1) * ns, :] = moved[:, f].astype(bf16)
    moved = og_in[...].astype(f32)
    for f in range(nf // 2):
        og_ref[f * ns : (f + 1) * ns, :] = moved[:, f].astype(bf16)
    half = n_img // 2
    img_load.wait()
    for p in range(9):
        pair = img_ref[:, p].astype(f32)
        for o in range(2):
            x_ref[o * half : (o + 1) * half, p * CH : (p + 1) * CH] = pair[:, o].astype(bf16)
        x_save(p).start()
    for conv in range(2):
        core_copy(conv, zi, core).start()

    def t_step(s, carry):
        @pl.when(s == nz - 1)
        def _():
            send(0, 0)

        t_receive(s)

        @pl.when(s < nz - 1)
        def _():
            t_send(s)
        return carry

    lax.fori_loop(1, nz, t_step, 0)

    def rows_of(conv, j, start, wide):
        block = w_ref[conv, pl.ds(j * spb, spb), :, start : start + wide]
        return block.reshape(BLK, wide)

    def w_save(conv, j):
        part = pl.ds(j * spb, spb)
        return pltpu.make_async_copy(w_ref.at[conv, part], w_out.at[conv, part], wsem.at[conv, j])

    def conv_norm(src_ref, conv, z_ref, r_ref, j):
        lanes = pl.ds(pl.multiple_of(j * BLK, BLK), BLK)
        total = None
        for p in range(9):
            r, c = divmod(p, 3)
            bs = span(c)
            acc = None
            for a in span(r):
                start = (3 * (r + a - 1) + c + bs[0] - 1) * CH
                wide = len(bs) * CH
                part = dot(src_ref[:, start : start + wide], rows_of(conv, j, (3 * a + bs[0]) * CH, wide), NT)
                acc = part if acc is None else acc + part
            z_ref[p, :, lanes] = acc
            total = acc if total is None else total + acc
        mean = group_sum(total, ones) * inv_n
        var = None
        for p in range(9):
            centred = z_ref[p, :, lanes] - mean
            sq = centred * centred
            var = sq if var is None else var + sq
        rstd = lax.rsqrt(group_sum(var, ones) * inv_n + norm_eps)
        r_ref[:, lanes] = rstd
        return lanes, mean, rstd

    def first(j):
        aff_ref[:, lanes_of(j)] = jnp.transpose(rows_of(0, j, 9 * CH, BLK).astype(f32))[0:8]
        lanes, mean, rstd = conv_norm(x_ref, 0, z1_ref, r1_ref, j)
        gain, offset = aff_ref[0:1, lanes], aff_ref[1:2, lanes]
        for p in range(9):
            z = (z1_ref[p, :, lanes] - mean) * rstd
            z1_ref[p, :, lanes] = z
            u = z * gain + offset
            a_ref[:, pl.ds(pl.multiple_of(p * CH + j * BLK, BLK), BLK)] = (u * sigmoid(u)).astype(bf16)

    def second(j):
        lanes, mean, rstd = conv_norm(a_ref, 1, z2_ref, r2_ref, j)
        gain, offset = aff_ref[2:3, lanes], aff_ref[3:4, lanes]
        total = None
        for p in range(9):
            z = (z2_ref[p, :, lanes] - mean) * rstd
            z2_ref[p, :, lanes] = z
            cols = pl.ds(pl.multiple_of(p * CH + j * BLK, BLK), BLK)
            u = z * gain + offset + x_ref[:, cols].astype(f32)
            s = sigmoid(u)
            act = u * s
            x_ref[:, cols] = (s + act * (1.0 - s)).astype(bf16)
            total = act if total is None else total + act
        out = (total * (1.0 / 9.0)).astype(bf16)
        feat_ref[:, :, :, lanes] = out.reshape(feat_ref.shape[:3] + (BLK,))

    def lanes_of(j):
        return pl.ds(pl.multiple_of(j * BLK, BLK), BLK)

    def arrived(conv, k):
        core_copy(conv, k, 1 - core).wait_recv()

    def phase(conv, block):
        streaming = spb == 2

        def step(s, carry):
            if conv == 0:
                @pl.when((s > 0) & (s < nz - 1))
                def _():
                    send(0, s)

                @pl.when(s == nz - 1)
                def _():
                    send(1, 0)
            else:
                @pl.when((s > 0) & (s < nz - 1))
                def _():
                    send(1, s)

            def side(d, carry):
                k = zi + s - 2 * s * d

                @pl.when((k >= 0) & (k < nz) & (s + 1 > d))
                def _():
                    arrived(conv, k)
                    if streaming:
                        w_save(conv, k).start()
                        block(k)
                return carry

            lax.fori_loop(0, 2, side, 0)
            if conv == 1:
                t_collect(2 * s)
                t_collect(2 * s + 1)

                @pl.when(s == nz - 2)
                def _():
                    t_complete()
                    saves[0].wait()
                    temporal_early()

            @pl.when(s < nz - 1)
            def _():
                receive(conv, s + 1)
            return carry

        lax.fori_loop(0, nz, step, 0)
        if not streaming:
            def rest(j, carry):
                w_save(conv, j).start()
                block(j)
                return carry

            lax.fori_loop(0, CH // BLK, rest, 0)

    phase(0, first)
    saves = [pltpu.make_async_copy(z1_ref, z1_out, osem.at[0])]
    saves += [
        pltpu.make_async_copy(a_ref.at[:, p * CH : (p + 1) * CH], a_out.at[p], osem.at[2 + p])
        for p in range(9)
    ]
    for save in saves:
        save.start()
    for p in range(9):
        x_save(p).wait()
    phase(1, second)
    last = pltpu.make_async_copy(z2_ref, z2_out, osem.at[1])
    last.start()

    def slope_save(p):
        return pltpu.make_async_copy(x_ref.at[:, p * CH : (p + 1) * CH], slope_out.at[p], xsem.at[p])

    for p in range(9):
        slope_save(p).start()

    def feat_copy(to, sender):
        return cam_copy(feat_ref.at[:, to], arr_s.at[sender], fsend.at[to], frecv.at[sender], to)

    for step in range(1, cams):
        feat_copy((cam + step) % cams, cam).start()
    arr_s[cam] = feat_ref[:, cam]
    for step in range(1, cams):
        other = (cam + step) % cams
        feat_copy(other, other).wait_recv()
    temporal_rest()
    for step in range(1, cams):
        feat_copy((cam + step) % cams, cam).wait_send()

    for conv in range(2):
        def drain(k, carry):
            s = k - zi

            @pl.when((s >= 0) & (s < nz - 1) & (zi > 0))
            def _():
                z_copy(conv, k, 0).wait_send()

            @pl.when((s <= 0) & (s > 1 - nz) & (zi < nz - 1))
            def _():
                z_copy(conv, k, 1).wait_send()

            core_copy(conv, k, core).wait_send()
            return carry

        lax.fori_loop(0, nz, drain, 0)

        def saved(j, carry):
            w_save(conv, j).wait()
            return carry

        lax.fori_loop(0, CH // BLK, saved, 0)
    for save in saves[1:]:
        save.wait()
    last.wait()

    def t_drain(k, carry):
        s = k - zi

        @pl.when((s >= 0) & (s < nz - 1) & (zi > 0))
        def _():
            tz_copy(k, 0).wait_send()

        @pl.when((s <= 0) & (s > 1 - nz) & (zi < nz - 1))
        def _():
            tz_copy(k, 1).wait_send()

        @pl.when(s != 0)
        def _():
            for step in range(1, cams):
                tp_copy(k, step, cam).wait_send()

        for q in range(cams):
            tc_copy(k, core, q).wait_send()
        return carry

    lax.fori_loop(0, nz, t_drain, 0)
    for p in range(9):
        slope_save(p).wait()
    for step in range(1, cams):
        view_copy((cam + step) % cams, cam).wait_send()


def enc_bwd_kernel(
    n, cams, cond, x_hbm, slope_hbm, a_hbm, w_hbm, z1_hbm, r1_ref, z2_hbm, r2_ref, aff_ref, gp_ref, dt_hbm,
    ig_out, genc_ref, gaff_ref, gconvs_ref, gfilm_ref, gskip_ref, gdown_ref, gblk_ref,
    ig_ref, x_ref, a_ref, w_ref, z1_ref, z2_ref, g_ref, gt_ref, ag_ref,
    dwf, core_out, core_in, slots, t_own, t_sum, t_peer, t_slots, t_all,
    lsem, bsem, isem, csend, crecv, zsend, zrecv,
    tlsem, tcsend, tcrecv, tpsend, tprecv, tzsend, tzrecv, tfsend, tfrecv,
):
    nz = n // 2
    rows = CH // n
    n_img = z1_ref.shape[1]
    me, cam = lax.axis_index("batch"), lax.axis_index("cam")
    zi, core = me // 2, me % 2
    partner = me + 1 - 2 * core
    ones = group_ones(BLK, ENC_GROUP)
    inv_n = 1.0 / (9 * ENC_GROUP)
    chunk = 3 * CH

    def load_w(conv):
        return pltpu.make_async_copy(w_hbm.at[conv, :, :, 0 : 9 * CH], w_ref, lsem.at[3])

    def lanes_of(j):
        return pl.ds(pl.multiple_of(j * BLK, BLK), BLK)

    def block_loads(j):
        cols = lanes_of(j)
        return (
            pltpu.make_async_copy(z2_hbm.at[:, :, cols], z2_ref.at[:, :, cols], bsem.at[0, j]),
            pltpu.make_async_copy(slope_hbm.at[:, :, cols], g_ref.at[:, :, cols], bsem.at[1, j]),
        )

    loads = {
        "z1": pltpu.make_async_copy(z1_hbm, z1_ref, lsem.at[1]),
        "a": pltpu.make_async_copy(a_hbm, a_ref, lsem.at[2]),
        "x": pltpu.make_async_copy(x_hbm, x_ref, lsem.at[0]),
    }
    for j in range(CH // BLK):
        for load in block_loads(j):
            load.start()

    def own_load(i):
        return pltpu.make_async_copy(dt_hbm.at[i // cams, core, i % cams], t_own.at[i % 2], tlsem.at[i])

    own_load(0).start()

    line_greet(cams, nz)

    def t_core(k):
        return batch_copy(dt_hbm.at[k, 1 - core], t_sum.at[k], tcsend.at[k], tcrecv.at[k], partner)

    def t_peers(k, step):
        to = (cam + step) % cams
        return cam_copy(t_sum.at[k, to], t_peer.at[step - 1, k], tpsend.at[step - 1, k], tprecv.at[step - 1, k], to)

    def t_start(k, carry):
        t_core(k).start()
        return carry

    def t_spread(lo, hi):
        def body(k, carry):
            t_core(k).wait_recv()

            def quarter(q, carry):
                i = k * cams + q

                @pl.when(i + 1 < nz * cams)
                def _():
                    own_load(i + 1).start()

                own_load(i).wait()
                t_sum[k, q] = (t_sum[k, q].astype(f32) + t_own[i % 2].astype(f32)).astype(bf16)
                return carry

            lax.fori_loop(0, cams, quarter, 0)
            for step in range(1, cams):
                t_peers(k, step).start()
            return carry

        lax.fori_loop(lo, hi, body, 0)

    ag_ref[...] = jnp.zeros_like(ag_ref)

    def norm_back(du_ref, z_ref, r_ref, j, gain, row):
        lanes = lanes_of(j)
        s0 = jnp.zeros((n_img, BLK), f32)
        s1 = jnp.zeros((n_img, BLK), f32)
        for p in range(9):
            du = du_ref[p, :, lanes]
            s0 = s0 + du
            s1 = s1 + du * z_ref[p, :, lanes]
        ag_ref[row : row + 1, lanes] = jnp.sum(s1, axis=0, keepdims=True)
        ag_ref[row + 1 : row + 2, lanes] = jnp.sum(s0, axis=0, keepdims=True)
        m0 = group_sum(s0 * gain, ones) * inv_n
        m1 = group_sum(s1 * gain, ones) * inv_n
        rstd = r_ref[:, lanes]
        for p in range(9):
            dv = (du_ref[p, :, lanes] * gain - m0 - z_ref[p, :, lanes] * m1) * rstd
            g_ref[p, :, lanes] = dv.astype(bf16)
            gt_ref[lanes, p * n_img : (p + 1) * n_img] = jnp.transpose(dv).astype(bf16)

    def second(j, carry):
        lanes = lanes_of(j)
        for load in block_loads(j):
            load.wait()
        pooled = gp_ref[:, :, :, lanes].reshape(n_img, BLK).astype(f32) * (1.0 / 9.0)
        for p in range(9):
            ig_ref[p, :, lanes] = pooled * g_ref[p, :, lanes].astype(f32)
        norm_back(ig_ref, z2_ref, r2_ref, j, aff_ref[2:3, lanes], 2)
        return carry

    def first(j, carry):
        lanes = lanes_of(j)
        gain, offset = aff_ref[0:1, lanes], aff_ref[1:2, lanes]
        for p in range(9):
            u = z1_ref[p, :, lanes] * gain + offset
            s = sigmoid(u)
            z2_ref[p, :, lanes] = z2_ref[p, :, lanes] * (s * (1.0 + u * (1.0 - s)))
        norm_back(z2_ref, z1_ref, r1_ref, j, gain, 0)
        return carry

    def width(k):
        return chunk + BLK if k == 5 else chunk

    def core_copy(k):
        cols = pl.ds(0, width(k))
        return batch_copy(
            core_out.at[k % 2, :, :, cols], core_in.at[k % 3, :, :, cols], csend.at[k], crecv.at[k], partner
        )

    def keep(k, d0, lane, v):
        count, wide = v.shape[0] // (2 * rows), v.shape[1]
        parts = v.reshape(count, 2, rows, wide)
        even, odd = parts[:, 0], parts[:, 1]
        dwf[k % 2, d0 : d0 + count, :, lane : lane + wide] = jnp.where(core == 0, even, odd)
        core_out[k % 2, d0 : d0 + count, :, lane : lane + wide] = jnp.where(core == 0, odd, even).astype(bf16)

    def make_chunk(k):
        if k >= 2:
            core_copy(k - 2).wait_send()
        src_ref = a_ref if k < 3 else x_ref
        a = k % 3
        r_lo, r_hi = max(0, 1 - a), min(2, 3 - a)
        for b in range(3):
            c_lo, c_hi = max(0, 1 - b), min(2, 3 - b)
            if b == 1:
                runs = [(3 * r_lo, 3 * (r_hi - r_lo + 1))]
            else:
                runs = [(3 * r + c_lo, c_hi - c_lo + 1) for r in range(r_lo, r_hi + 1)]
            shift = 3 * (a - 1) + b - 1
            for half in range(2):
                acc = None
                for p, m in runs:
                    part = dot(
                        gt_ref[half * 256 : half * 256 + 256, p * n_img : (p + m) * n_img],
                        src_ref[p + shift : p + shift + m].reshape(m * n_img, CH),
                    )
                    acc = part if acc is None else acc + part
                keep(k, half * nz // 2, b * CH, acc)
        if k == 5:
            keep(k, 0, chunk, jnp.transpose(ag_ref[...]))
        core_copy(k).start()

    def term(k, d):
        return dwf[k % 2, d, :, 0 : width(k)] + core_in[k % 3, d, :, 0 : width(k)].astype(f32)

    def line_copy(k, way, s):
        if k == 6:
            return batch_copy(
                t_slots.at[way, s - 1], t_slots.at[way, s], tzsend.at[way, s], tzrecv.at[way, s], me - 2 + 4 * way
            )
        cols = pl.ds(0, width(k))
        return batch_copy(
            slots.at[k % 3, way, s - 1, :, cols], slots.at[k % 3, way, s, :, cols],
            zsend.at[k, way, s], zrecv.at[k, way, s], me - 2 + 4 * way,
        )

    def slot(k, way, s):
        return t_slots.at[way, s] if k == 6 else slots.at[k % 3, way, s, :, pl.ds(0, width(k))]

    def t_term(d):
        total = t_sum[d, cam].astype(f32)
        for step in range(1, cams):
            total = total + t_peer[step - 1, d].astype(f32)
        return total

    def serve(k, s):
        for way in range(2):
            ahead = zi if way else nz - 1 - zi
            d = nz - s + zi if way else s - nz + zi
            ref = slot(k, way, s - 1)

            @pl.when((ahead < nz - 1) & (s > ahead))
            def _():
                own = t_term(d) if k == 6 else term(k, d)

                @pl.when(ahead > 0)
                def _():
                    line_copy(k, way, s - 1).wait_recv()
                    ref[...] = (ref[...].astype(f32) + own).astype(bf16)

                @pl.when(ahead == 0)
                def _():
                    ref[...] = own.astype(bf16)

                line_copy(k, way, s).start()

    def steps(k, part):
        lo, hi = 1 + part * (nz - 1) // 3, 1 + (part + 1) * (nz - 1) // 3
        if hi - lo == 1:
            serve(k, lo)
        elif hi > lo:
            def body(s, carry):
                serve(k, s)
                return carry

            lax.fori_loop(lo, hi, body, 0)

    def service(g):
        k, part = divmod(g, 3)
        if part == 0:
            core_copy(k).wait_recv()
        steps(k, part)

    def collect(k, total, write):
        last = nz - 1

        @pl.when(zi > 0)
        def _():
            line_copy(k, 1, last).wait_recv()

        @pl.when(zi < nz - 1)
        def _():
            line_copy(k, 0, last).wait_recv()

        @pl.when(zi == 0)
        def _():
            write(total + slot(k, 0, last)[...].astype(f32))

        @pl.when(zi == nz - 1)
        def _():
            write(total + slot(k, 1, last)[...].astype(f32))

        @pl.when((zi > 0) & (zi < nz - 1))
        def _():
            write(total + slot(k, 0, last)[...].astype(f32) + slot(k, 1, last)[...].astype(f32))

        def drain(s, carry):
            for way in range(2):
                ahead = zi if way else nz - 1 - zi

                @pl.when((ahead < nz - 1) & (s > ahead))
                def _():
                    line_copy(k, way, s).wait_send()
            return carry

        lax.fori_loop(1, nz, drain, 0)

    def finish(k):
        def write(v):
            genc_ref[:, 1 - k // 3, (k % 3) * chunk : (k % 3 + 1) * chunk] = v[:, 0:chunk]
            if k == 5:
                gaff_ref[...] = jnp.transpose(v[:, chunk:])[0 : gaff_ref.shape[0]]

        collect(k, term(k, zi), write)

    def t_arrived():
        for step in range(1, cams):
            def body(k, carry):
                t_peers(k, step).wait_recv()
                return carry

            lax.fori_loop(0, nz, body, 0)

    def t_final(to, sender):
        return cam_copy(t_all.at[cam], t_all.at[sender], tfsend.at[to], tfrecv.at[sender], to)

    def t_finish():
        def write(v):
            t_all[cam] = v.astype(bf16)

        collect(6, t_term(zi), write)
        for step in range(1, cams):
            t_final((cam + step) % cams, cam).start()

    def t_write():
        for step in range(1, cams):
            other = (cam + step) % cams
            t_final(other, other).wait_recv()

        def cut(q, lo, wide):
            return t_all[q, :, lo : lo + wide].astype(f32)

        for which in range(2):
            gconvs_ref[:, which, :] = cut(which, 0, PART)
            gfilm_ref[:, which, :] = cut(2, which * cond, cond)
        gblk_ref[...] = jnp.transpose(cut(2, 2 * cond, BLK))[0 : gblk_ref.shape[0]]
        gskip_ref[...] = cut(3, 0, CH)
        gdown_ref[...] = cut(3, CH, 3 * CH)

    def input_back(q):
        r, c = divmod(q, 3)
        acc = None
        for a in range(3):
            for b in range(3):
                pr, pc = r - a + 1, c - b + 1
                if 0 <= pr < 3 and 0 <= pc < 3:
                    t = 3 * a + b
                    w = w_ref[:, :, t * CH : (t + 1) * CH].reshape(CH, CH)
                    part = dot(g_ref[3 * pr + pc], w)
                    acc = part if acc is None else acc + part
        return acc

    def back_second(*qs):
        for q in qs:
            if q == 0:
                load_w(1).wait()
            z2_ref[q] = input_back(q)
            if q == 8:
                load_w(0).start()

    def ig_save(q):
        return pltpu.make_async_copy(a_ref.at[q], ig_out.at[q], isem.at[q])

    def back_first(*qs):
        for q in qs:
            if q == 0:
                load_w(0).wait()
            a_ref[q] = (ig_ref[q] + input_back(q)).astype(bf16)
            ig_save(q).start()

    def quarter_of(i):
        return i * nz // 4, (i + 1) * nz // 4

    def t_go(i):
        lax.fori_loop(*quarter_of(i), t_start, 0)

    lax.fori_loop(0, 1, second, 0)
    loads["a"].start()
    line_wait(cams, nz)
    lax.fori_loop(1, CH // BLK, second, 0)
    load_w(1).start()
    loads["a"].wait()
    make_chunk(0)
    service(0)
    t_go(0)
    make_chunk(1)
    service(1)
    t_go(1)
    t_spread(*quarter_of(0))
    loads["z1"].start()
    loads["x"].start()
    back_second(0, 1, 2)
    service(2)
    t_go(2)
    t_spread(*quarter_of(1))
    back_second(3, 4)
    service(3)
    finish(0)
    t_go(3)
    t_spread(*quarter_of(2))
    make_chunk(2)
    service(4)
    t_spread(*quarter_of(3))
    back_second(5, 6)
    service(5)
    back_second(7, 8)
    service(6)
    finish(1)
    loads["z1"].wait()
    loads["x"].wait()
    lax.fori_loop(0, 2, first, 0)
    service(7)
    lax.fori_loop(2, 4, first, 0)
    service(8)
    make_chunk(3)
    service(9)
    finish(2)
    make_chunk(4)
    service(10)
    back_first(0, 1)
    service(11)
    back_first(2, 3)
    service(12)
    finish(3)
    make_chunk(5)
    service(13)
    back_first(4, 5)
    service(14)
    t_arrived()
    steps(6, 0)
    finish(4)
    back_first(6)
    steps(6, 1)
    back_first(7)
    steps(6, 2)
    back_first(8)
    service(15)
    t_finish()
    service(16)
    service(17)
    t_write()
    finish(5)

    for q in range(9):
        ig_save(q).wait()

    def t_drain(k, carry):
        t_core(k).wait_send()
        for step in range(1, cams):
            t_peers(k, step).wait_send()
        return carry

    lax.fori_loop(0, nz, t_drain, 0)
    for step in range(1, cams):
        t_final((cam + step) % cams, cam).wait_send()
    core_copy(4).wait_send()
    core_copy(5).wait_send()


def call(kernel, outs, in_specs, out_specs, scratch=(), collective_id=None, cost=None):
    extra = {} if collective_id is None else dict(collective_id=collective_id, has_side_effects=True)
    return pl.pallas_call(
        kernel,
        out_shape=[jax.ShapeDtypeStruct(s, d) for s, d in outs],
        in_specs=in_specs,
        out_specs=out_specs,
        scratch_shapes=list(scratch),
        compiler_params=pltpu.CompilerParams(vmem_limit_bytes=VMEM_BYTES, **extra),
        cost_estimate=cost,
    )


def work(microseconds):
    return pl.CostEstimate(
        flops=int(microseconds * 1e9), bytes_accessed=int(microseconds * 3e6), transcendentals=0
    )


V = pl.BlockSpec(memory_space=pltpu.VMEM)
H = pl.BlockSpec(memory_space=pl.ANY)
DMA = pltpu.SemaphoreType.DMA


def time_embed(steps_given, embed_width):
    half_width = embed_width // 2
    frequency = jnp.exp(
        jnp.arange(half_width, dtype=jnp.float32) * (-math.log(10000.0) / (half_width - 1))
    )
    argument = steps_given.astype(jnp.float32)[:, None] * frequency[None, :]
    return jnp.concatenate([jnp.sin(argument), jnp.cos(argument)], axis=1)


def adamw(weight, gradient, moment_one, moment_two, step_rate, weight_decay):
    mean_new = beta_first * moment_one + (1.0 - beta_first) * gradient
    square_new = beta_second * moment_two + (1.0 - beta_second) * gradient * gradient
    square_hat = square_new * (1.0 / (1.0 - beta_second**STEP))
    root = square_hat * lax.rsqrt(square_hat)
    weight_new = (1.0 - step_rate * weight_decay) * weight - (step_rate / (1.0 - beta_first**STEP)) * (
        mean_new / (root + adam_eps)
    )
    return (weight_new, mean_new, square_new)


def last_kernel(*refs):
    tg_ref, out_ref, ig_ref = refs[28:31]
    tg_new, out_new, ig_new, turn_ref = refs[52:56]
    for p in range(ig_ref.shape[0]):
        for o in range(ig_ref.shape[1]):
            ig_new[:, p, o, :] = ig_ref[p, o].astype(f32)

    @pl.when(pl.program_id(0) == 0)
    def _():
        for f in range(tg_ref.shape[0]):
            tg_new[:, f, :] = tg_ref[f]
        for u in range(out_ref.shape[0]):
            turn_ref[:, u, :] = out_ref[u].astype(f32)
        out_new[...] = turn_ref[...].astype(bf16)

    for i in range(7):
        w_ref, m_ref, v_ref, g_ref = refs[4 * i : 4 * i + 4]
        outs = refs[31 + 3 * i : 34 + 3 * i]

        def update():
            vector = i in (1, 6)
            rate, decay = (rate_vector, 0.0) if vector else (rate_matrix, decay_matrix)
            new = adamw(w_ref[...], g_ref[...], m_ref[...], v_ref[...], rate, decay)
            for ref, value in zip(outs, new):
                ref[...] = value

        if i in (1, 6):
            pl.when(pl.program_id(0) == 0)(update)
        else:
            update()


def last_call(shown, grads, tg, out, ig, rows):
    step = min(rows, 8)
    steps = rows // step

    def whole(shape):
        return pl.BlockSpec(shape, lambda r: (0,) * len(shape))

    def spec(v):
        if v.shape[0] != rows:
            return whole(v.shape)
        return pl.BlockSpec((step,) + v.shape[1:], lambda r: (r,) + (0,) * (v.ndim - 1))

    ins = []
    for i in range(7):
        ins += [shown[0][i], shown[1][i], shown[2][i], grads[i]]
    outs = [w for w in shown[0] for _ in range(3)]
    pos, obs, count, ch = ig.shape
    part = count // steps
    turned = [(v.shape[1], v.shape[0], v.shape[2]) for v in (tg, out)]
    return pl.pallas_call(
        last_kernel,
        grid=(steps,),
        out_shape=[jax.ShapeDtypeStruct(v.shape, f32) for v in outs]
        + [jax.ShapeDtypeStruct(turned[0], f32), jax.ShapeDtypeStruct(turned[1], bf16),
           jax.ShapeDtypeStruct((count, pos, obs, ch), f32)],
        in_specs=[spec(v) for v in ins]
        + [whole(tg.shape), whole(out.shape), pl.BlockSpec((pos, obs, part, ch), lambda r: (0, 0, r, 0))],
        out_specs=[spec(v) for v in outs]
        + [whole(turned[0]), whole(turned[1]), pl.BlockSpec((part, pos, obs, ch), lambda r: (r, 0, 0, 0))],
        scratch_shapes=[pltpu.VMEM(turned[1], f32)],
        compiler_params=pltpu.CompilerParams(vmem_limit_bytes=VMEM_BYTES),
        cost_estimate=work(15),
    )(*ins, tg, out, ig)


def shards(
    n, images, trajectory, view_mask, timesteps, out_grad,
    encoder_weight, encoder_affine, block_convs, film_weight, skip_weight, down_weight, block_affine,
    first_encoder, first_affine, first_convs, first_film, first_skip, first_down, first_block,
    second_encoder, second_affine, second_convs, second_film, second_skip, second_down, second_block,
):
    ns, nf, ch = trajectory.shape
    cams, obs = images.shape[1], images.shape[3]
    n_img = cams * images.shape[2] * obs
    nz, per = n // 2, ch // n
    cond = film_weight.shape[2]
    wide = 9 * ch
    rows = nf * ns

    def turned(v):
        return jnp.transpose(v.reshape(v.shape[-2:]))

    pairs = jnp.transpose(images[0], (0, 1, 3, 2, 4)).reshape(n_img // obs, 9, obs, ch)
    pos = (9, n_img, ch)
    t_shape = (nz, 2, cams, per, PART)
    wcols = wide + BLK
    z1, r1, act, z2, r2, w_all, enc_aff, x, slope, out_fm, tg_fm, gp, dt = call(
        functools.partial(forward_kernel, n, cams),
        [(pos, f32), ((n_img, ch), f32), (pos, bf16), (pos, f32), ((n_img, ch), f32), ((2, n, per, wcols), bf16),
         ((8, ch), f32), (pos, bf16), (pos, bf16), ((rows // 2, ch), bf16), ((rows, ch), f32), ((obs, cams, ns, ch), bf16),
         (t_shape, bf16)],
        [H, V, V, V, V, H, V, V, V, V, V, V],
        [H, V, H, H, V, H, V, H, H, V, V, V, H],
        [pltpu.VMEM((n_img // obs, 9, obs, ch), bf16), pltpu.VMEM((n_img, wide), bf16), pltpu.VMEM((2, n, per, wcols), bf16), pltpu.VMEM(pos, f32),
         pltpu.VMEM((n_img, wide), bf16), pltpu.VMEM(pos, f32), pltpu.VMEM((obs, cams, ns, ch), bf16),
         pltpu.VMEM((cams, obs, ns, ch), bf16), pltpu.VMEM(t_shape, bf16), pltpu.VMEM((2, min(per, 16), 2, wide), f32),
         pltpu.VMEM((BLK, BLK), f32), pltpu.VMEM((BLK, per), f32), pltpu.VMEM((rows // 2, ch), bf16), pltpu.VMEM((rows + 4 * ns, ch), bf16),
         pltpu.VMEM((rows + 4 * ns, ch), bf16), pltpu.VMEM((rows + 4 * ns, ch), bf16), pltpu.VMEM((rows + ns, ch), bf16),
         pltpu.VMEM((BLK, ch), f32), pltpu.VMEM((BLK, ch), f32), pltpu.VMEM((ns, ch), f32),
         pltpu.VMEM((cams, obs, ns, ch), bf16), pltpu.VMEM((obs, cams, ns, ch), bf16),
         pltpu.VMEM((2, nz, 2, per, PART), bf16),
         DMA((2, 2, nz)), DMA((2, nz)), DMA((2, nz)), DMA((2, nz)), DMA((2, ch // BLK)), DMA((11,)),
         DMA((cams,)), DMA((cams,)),
         DMA((2, nz)), DMA((nz,)), DMA((nz, cams)), DMA((nz, cams)), DMA((cams - 1, nz)), DMA((cams - 1, nz)),
         DMA((max(per // 16, 1),)), DMA((10,)), DMA((cams,)), DMA((cams,)), DMA((4,))],
        collective_id=0,
        cost=work(130),
    )(pairs, trajectory, out_grad, jnp.transpose(view_mask), time_embed(timesteps, TEMB), encoder_weight[0], block_convs,
      film_weight, skip_weight, down_weight, turned(encoder_affine), turned(block_affine))
    chunk = 3 * ch + BLK
    ig, genc, gaff, gconvs, gfilm, gskip, gdown, gblk = call(
        functools.partial(enc_bwd_kernel, n, cams, cond),
        [(pos, bf16), ((per, 2, wide), f32), ((4, per), f32), ((per, 2, 5 * ch), f32),
         ((per, 2, cond), f32), ((per, ch), f32), ((per, 3 * ch), f32), ((10, per), f32)],
        [H, H, H, H, H, V, H, V, V, V, H],
        [H] + [V] * 7,
        [pltpu.VMEM(pos, f32), pltpu.VMEM(pos, bf16), pltpu.VMEM(pos, bf16), pltpu.VMEM((n, per, wide), bf16), pltpu.VMEM(pos, f32),
         pltpu.VMEM(pos, f32), pltpu.VMEM(pos, bf16), pltpu.VMEM((ch, 9 * n_img), bf16),
         pltpu.VMEM((BLK, ch), f32),
         pltpu.VMEM((2, nz, per, chunk), f32), pltpu.VMEM((2, nz, per, chunk), bf16),
         pltpu.VMEM((3, nz, per, chunk), bf16), pltpu.VMEM((3, 2, nz, per, chunk), bf16),
         pltpu.VMEM((2, per, PART), bf16), pltpu.VMEM((nz, cams, per, PART), bf16),
         pltpu.VMEM((cams - 1, nz, per, PART), bf16), pltpu.VMEM((2, nz, per, PART), bf16),
         pltpu.VMEM((cams, per, PART), bf16),
         DMA((4,)), DMA((2, ch // BLK)), DMA((9,)), DMA((6,)), DMA((6,)), DMA((6, 2, nz)), DMA((6, 2, nz)),
         DMA((nz * cams,)), DMA((nz,)), DMA((nz,)), DMA((cams - 1, nz)), DMA((cams - 1, nz)),
         DMA((2, nz)), DMA((2, nz)), DMA((cams,)), DMA((cams,))],
        collective_id=1,
        cost=work(100),
    )(x, slope, act, w_all, z1, r1, z2, r2, enc_aff, gp, dt)
    weights = (encoder_weight, encoder_affine, block_convs, film_weight, skip_weight, down_weight, block_affine)
    firsts = (first_encoder, first_affine, first_convs, first_film, first_skip, first_down, first_block)
    seconds = (second_encoder, second_affine, second_convs, second_film, second_skip, second_down, second_block)
    shown = [
        [turned(v) if i in (1, 6) else v.reshape(v.shape[-3:]) if i == 0 else v for i, v in enumerate(group)]
        for group in (weights, firsts, seconds)
    ]
    *news, trajectory_grad, block_output, ig_new = last_call(
        shown, (genc, gaff, gconvs, gfilm, gskip, gdown, gblk),
        tg_fm.reshape(nf, ns, ch), out_fm.reshape(nf // 2, ns, ch), ig.reshape(9, obs, n_img // obs, ch), per,
    )
    images_grad = jnp.transpose(ig_new.reshape(images.shape[1:3] + ig_new.shape[1:]), (0, 1, 3, 2, 4))[None]
    upd = [
        tuple((turned(v) if i in (1, 6) else v).reshape(w.shape) for v in news[3 * i : 3 * i + 3])
        for i, w in enumerate(weights)
    ]
    return (
        (block_output, trajectory_grad, images_grad)
        + tuple(u[0] for u in upd)
        + tuple(u[1] for u in upd)
        + tuple(u[2] for u in upd)
    )


def solution(mesh):
    sample = P(("cam", "batch"))
    params = (P("cam", "batch"), P("cam", "batch")) + (P("batch"),) * 5
    images_spec = P("cam", None, "batch")
    return jax.shard_map(
        functools.partial(shards, mesh.shape["batch"]),
        mesh=mesh,
        in_specs=(images_spec, sample, sample, sample, sample) + params * 3,
        out_specs=(sample, sample, images_spec) + params * 3,
        check_vma=False,
    )
```

```python
import functools
import math

import jax
import jax.numpy as jnp
from jax import lax
from jax.experimental import pallas as pl
from jax.experimental.pallas import tpu as pltpu
from jax.sharding import PartitionSpec as P

TEMB = 128
GROUPS = 8
STEP = 5

norm_eps = 1e-05
beta_first = 0.5
beta_second = 0.5
adam_eps = 1e-08
rate_matrix = 0.02
rate_vector = 0.2
decay_matrix = 0.01

CH = 512
BLK = 128
ENC_GROUP = 16
f32 = jnp.float32
bf16 = jnp.bfloat16
VMEM_BYTES = 61 * 1024 * 1024

NT = (((1,), (1,)), ((), ()))
NN = (((1,), (0,)), ((), ()))
TN = (((0,), (0,)), ((), ()))


def dot(a, b, dims=NN):
    return lax.dot_general(a, b, dims, preferred_element_type=f32)


def group_ones(width, group):
    rows = lax.broadcasted_iota(jnp.int32, (width, width), 0) // group
    cols = lax.broadcasted_iota(jnp.int32, (width, width), 1) // group
    return jnp.where(rows == cols, 1.0, 0.0).astype(bf16)


def group_sum(v, ones):
    high = v.astype(bf16)
    rest = v - high.astype(f32)
    middle = rest.astype(bf16)
    low = (rest - middle.astype(f32)).astype(bf16)
    return dot(high, ones) + dot(middle, ones) + dot(low, ones)


def sigmoid(v):
    return 1.0 / (1.0 + jnp.exp(-v))


def mish_pair(v):
    e = jnp.exp(jnp.minimum(v, 20.0))
    n = e * (e + 2.0)
    inv = 1.0 / (n + 2.0)
    t = n * inv
    return v * t, t + v * (4.0 * e * (1.0 + e)) * inv * inv


def mish_value(v):
    e = jnp.exp(jnp.minimum(v, 20.0))
    n = e * (e + 2.0)
    return v * (n / (n + 2.0))


def span(i):
    return range(max(0, 1 - i), min(2, 3 - i) + 1)


MESH = pl.DeviceIdType.MESH


def batch_copy(src, dst, send_sem, recv_sem, target):
    return pltpu.make_async_remote_copy(
        src_ref=src, dst_ref=dst, send_sem=send_sem, recv_sem=recv_sem,
        device_id={"batch": target}, device_id_type=MESH,
    )


def cam_copy(src, dst, send_sem, recv_sem, target):
    return pltpu.make_async_remote_copy(
        src_ref=src, dst_ref=dst, send_sem=send_sem, recv_sem=recv_sem,
        device_id={"cam": target}, device_id_type=MESH,
    )


def line_wait(cams, nz):
    zi = lax.axis_index("batch") // 2
    ends = (zi == 0).astype(jnp.int32) + (zi == nz - 1).astype(jnp.int32)
    pl.semaphore_wait(pltpu.get_barrier_semaphore(), cams + 2 - ends)


def line_greet(cams, nz):
    me, cam = lax.axis_index("batch"), lax.axis_index("cam")
    zi, core = me // 2, me % 2
    barrier = pltpu.get_barrier_semaphore()
    pl.semaphore_signal(barrier, inc=1, device_id={"batch": me + 1 - 2 * core}, device_id_type=MESH)
    for step in range(1, cams):
        pl.semaphore_signal(barrier, inc=1, device_id={"cam": (cam + step) % cams}, device_id_type=MESH)

    @pl.when(zi > 0)
    def _():
        pl.semaphore_signal(barrier, inc=1, device_id={"batch": me - 2}, device_id_type=MESH)

    @pl.when(zi < nz - 1)
    def _():
        pl.semaphore_signal(barrier, inc=1, device_id={"batch": me + 2}, device_id_type=MESH)


PART = 5 * CH


def pack_part(q, ref, convs_ref, film_ref, skip_ref, down_ref, ext):
    rows, cond = film_ref.shape[0], film_ref.shape[2]
    if q < 2:
        ref[q] = convs_ref[:, q, :].astype(bf16)
    elif q == 2:
        for which in range(2):
            ref[2, :, which * cond : (which + 1) * cond] = film_ref[:, which, :].astype(bf16)
        ref[2, :, 2 * cond : 2 * cond + BLK] = ext
        ref[2, :, 2 * cond + BLK :] = jnp.zeros((rows, PART - 2 * cond - BLK), bf16)
    else:
        ref[3, :, 0:CH] = skip_ref[...].astype(bf16)
        ref[3, :, CH : 4 * CH] = down_ref[...].astype(bf16)
        ref[3, :, 4 * CH :] = jnp.zeros((rows, PART - 4 * CH), bf16)


def forward_kernel(
    n, cams, img_hbm, traj_ref, og_in, mask_in, emb_ref, enc_hbm, convs_ref, film_ref, skip_ref, down_ref,
    ea_ref, ba_ref,
    z1_out, r1_ref, a_out, z2_out, r2_ref, w_out, aff_ref, x_out, slope_out, out_ref, tg_ref, gp_ref, dt_out,
    img_ref, x_ref, w_ref, z1_ref, a_ref, z2_ref, feat_ref, arr_s, t_ref, enc_buf,
    mask_s, ext_s, og_ref, pad_t, pad_m, pad_h, sum_ref, taff_ref, ag_ref, rstd_ref, dviews_ref, gp_s, dt_buf,
    zsend, zrecv, csend, crecv, wsem, osem, fsend, frecv,
    tzsend, tzrecv, tcsend, tcrecv, tpsend, tprecv, esem, xsem, vsend, vrecv, dsem,
):
    nz = n // 2
    rows = skip_ref.shape[0]
    piece = enc_buf.shape[1]
    spb = BLK // rows
    n_img = x_ref.shape[0]
    me, cam = lax.axis_index("batch"), lax.axis_index("cam")
    zi, core = me // 2, me % 2
    partner = me + 1 - 2 * core
    ones = group_ones(BLK, ENC_GROUP)
    inv_n = 1.0 / (9 * ENC_GROUP)

    def enc_load(i):
        return pltpu.make_async_copy(enc_hbm.at[pl.ds(i * piece, piece)], enc_buf.at[i % 2], esem.at[i])

    enc_load(0).start()
    img_load = pltpu.make_async_copy(img_hbm, img_ref, xsem.at[9])
    img_load.start()
    ext_s[...] = jnp.zeros_like(ext_s)
    ext_s[0:4] = ea_ref[...]
    ext_s[4:14] = ba_ref[...]
    ext = jnp.transpose(ext_s[...]).astype(bf16)
    line_greet(cams, nz)

    def pack_own(q):
        pack_part(q, t_ref.at[zi, core], convs_ref, film_ref, skip_ref, down_ref, ext)

    for q in range(cams):
        pl.when(cam == q)(functools.partial(pack_own, q))
    line_wait(cams, nz)

    def tz_copy(k, way):
        ref = t_ref.at[k, core, cam]
        return batch_copy(ref, ref, tzsend.at[way, k], tzrecv.at[k], me - 2 + 4 * way)

    def tc_copy(k, which, q):
        ref = t_ref.at[k, which, q]
        return batch_copy(ref, ref, tcsend.at[k, q], tcrecv.at[k, q], partner)

    def tp_copy(k, step, q):
        ref = t_ref.at[k, core, q]
        return cam_copy(ref, ref, tpsend.at[step - 1, k], tprecv.at[step - 1, k], (cam + step) % cams)

    def t_send(s):
        for k, _, passed, way in moves(s):
            @pl.when(passed)
            def _():
                tz_copy(k, way).start()

    def t_receive(s):
        for k, held, _, way in moves(s):
            @pl.when(held)
            def _():
                tz_copy(k, way).wait_recv()
                for step in range(1, cams):
                    tp_copy(k, step, cam).start()
                tc_copy(k, core, cam).start()

    def t_collect(d):
        for k, held, _, _ in moves(d):
            @pl.when(held & (d > 0))
            def _():
                for step in range(1, cams):
                    q = (cam + cams - step) % cams
                    tp_copy(k, step, q).wait_recv()
                    tc_copy(k, core, q).start()

    def t_complete():
        def body(k, carry):
            for q in range(cams):
                tc_copy(k, 1 - core, q).wait_recv()
            return carry

        lax.fori_loop(0, nz, body, 0)

    ns, nf = traj_ref.shape[0], traj_ref.shape[1]
    frows = ns * nf
    obs = arr_s.shape[1]
    cond = obs * CH + emb_ref.shape[1]
    edge = 2 * ns
    per_pos = frows // n_img
    gones_shape = CH // GROUPS
    ginv = 1.0 / (nf * gones_shape)

    class Part:
        def __init__(self, ref, index, lo, wide):
            self.ref, self.index, self.lo, self.wide = ref, index, lo, wide

        def where(self, key):
            if not isinstance(key, tuple):
                return self.index(slice(self.lo, self.lo + self.wide))
            start, stop, _ = key[1].indices(self.wide)
            return self.index(slice(self.lo + start, self.lo + stop))

        def __getitem__(self, key):
            v = self.ref[self.where(key)]
            return v.reshape(CH, v.shape[-1])

        def __setitem__(self, key, v):
            self.ref[self.where(key)] = v.reshape(nz, 2, rows, v.shape[-1])

    def weight(q, lo, wide):
        return Part(t_ref, lambda cols: (slice(None), slice(None), q, slice(None), cols), lo, wide)

    def grad(buf, lo, wide):
        return Part(dt_buf, lambda cols: (buf, slice(None), slice(None), slice(None), cols), lo, wide)

    wa, wb = weight(0, 0, PART), weight(1, 0, PART)
    f0, f1, wext = weight(2, 0, cond), weight(2, cond, cond), weight(2, 2 * cond, BLK)
    ws, wd = weight(3, 0, CH), weight(3, CH, 3 * CH)

    def dt_save(q, buf):
        return pltpu.make_async_copy(dt_buf.at[buf], dt_out.at[:, :, q], dsem.at[q])

    def blank(buf, lo):
        dt_buf[buf, :, :, :, lo:] = jnp.zeros((nz, 2, rows, PART - lo), bf16)

    def tail(i):
        return taff_ref[4 + i : 5 + i, :]

    def frames(v):
        return v.reshape(nf, ns, CH)

    def keep(i, v):
        z1_ref[per_pos * i : per_pos * (i + 1)] = v.reshape(per_pos, n_img, CH)

    def kept(i):
        return z1_ref[per_pos * i : per_pos * (i + 1)].reshape(nf, ns, CH)

    def fill_edges(pad_ref):
        pad_ref[0:edge, :] = jnp.zeros((edge, CH), bf16)
        pad_ref[edge + frows : edge + frows + edge, :] = jnp.zeros((edge, CH), bf16)

    def fill(pad_ref, v):
        fill_edges(pad_ref)
        pad_ref[edge : edge + frows, :] = v.astype(bf16).reshape(frows, CH)

    def conv5(pad_ref, w):
        return sum(
            dot(pad_ref[t * ns : t * ns + frows, :], w[:, t * CH : (t + 1) * CH], NT) for t in range(5)
        )

    def conv5_back(pad_ref, w):
        return sum(
            dot(pad_ref[(4 - t) * ns : (4 - t) * ns + frows, :], w[:, t * CH : (t + 1) * CH]) for t in range(5)
        )

    def gsum(v):
        return group_sum(v, group_ones(CH, gones_shape)) * ginv

    def norm(v):
        v = frames(v)
        centred = v - gsum(jnp.sum(v, axis=0))[None]
        rstd = lax.rsqrt(gsum(jnp.sum(centred * centred, axis=0)) + norm_eps)
        return centred * rstd[None], rstd

    def norm_back(du, z, rstd, gain):
        s0 = jnp.sum(du, axis=0)
        s1 = jnp.sum(du * z, axis=0)
        dv = (du * gain[None] - gsum(s0 * gain)[None] - z * gsum(s1 * gain)[None]) * rstd[None]
        return dv, jnp.sum(s1, axis=0, keepdims=True), jnp.sum(s0, axis=0, keepdims=True)

    def total(v):
        return jnp.sum(v, axis=(0, 1)).reshape(1, CH)

    def across(v):
        return jnp.transpose(v.reshape(frows, CH)).astype(bf16)

    def temporal_early():
        taff_ref[...] = jnp.transpose(wext[...].astype(f32))
        ag_ref[...] = jnp.zeros_like(ag_ref)
        traj = pad_t[edge : edge + frows, :]
        za, rstd = norm(conv5(pad_t, wa) + tail(4))
        rstd_ref[...] = rstd
        keep(0, za)
        keep(1, dot(traj, ws[...], NT) + tail(8))
        og = og_ref[...]
        dcols = [dot(og, wd[:, t * CH : (t + 1) * CH]).reshape(nf // 2, ns, CH) for t in range(3)]
        before = jnp.concatenate([dcols[0][1:], jnp.zeros((1, ns, CH), f32)], axis=0)
        dsum = jnp.stack([dcols[1], dcols[2] + before], axis=1).reshape(nf, ns, CH)
        keep(2, dsum)
        ag_ref[8:9, :] = total(dsum)
        ag_ref[9:10, :] = jnp.sum(og.astype(f32), axis=0, keepdims=True)
        dskip = dsum.astype(bf16).reshape(frows, CH)
        grad(0, 0, CH)[...] = dot(across(dsum), traj).astype(bf16)
        blank(0, 4 * CH)
        tg_ref[...] = dot(dskip, ws[...])

    def view_copy(to, sender):
        return cam_copy(dviews_ref.at[to], gp_s.at[:, sender], vsend.at[to], vrecv.at[sender], to)

    def temporal_rest():
        mask_s[...] = jnp.zeros_like(mask_s)
        mask_s[0:cams, 0:ns] = mask_in[...].astype(f32)
        mask = jnp.transpose(mask_s[...])[0:ns, 0:cams]
        seen = jnp.sum(mask, axis=1, keepdims=True)
        conds, slopes = [], []
        for o in range(obs):
            pooled = sum(mask[:, c : c + 1] * arr_s[c, o].astype(f32) for c in range(cams))
            value, slope = mish_pair(pooled / seen)
            conds.append(value.astype(bf16))
            slopes.append(slope)
        conds.append(mish_value(emb_ref[...]).astype(bf16))
        lanes = [slice(o * CH, (o + 1) * CH) for o in range(obs)] + [slice(obs * CH, cond)]
        scale, shift = [
            sum(dot(v, w[:, cols], NT) for v, cols in zip(conds, lanes)) + tail(i) for i, w in ((6, f0), (7, f1))
        ]
        za = kept(0)
        fill(pad_m, mish_value(za * tail(0)[None] + tail(1)[None]) * scale[None] + shift[None])
        zb, rstd_b = norm(conv5(pad_m, wb) + tail(5))
        act_b, slope = mish_pair(zb * tail(2)[None] + tail(3)[None])
        keep(3, act_b + kept(1))
        dhb, ag_ref[2:3, :], ag_ref[3:4, :] = norm_back(kept(2) * slope, zb, rstd_b, tail(2))
        ag_ref[5:6, :] = total(dhb)
        fill(pad_h, dhb)
        dmid = frames(conv5_back(pad_h, wb))
        za = kept(0)
        act_a, slope = mish_pair(za * tail(0)[None] + tail(1)[None])
        dscale = jnp.sum(dmid * act_a, axis=0)
        dshift = jnp.sum(dmid, axis=0)
        lows = (dscale.astype(bf16), dshift.astype(bf16))
        for o in range(obs):
            dcond = dot(lows[0], f0[:, lanes[o]]) + dot(lows[1], f1[:, lanes[o]])
            dview = dcond * slopes[o] / seen
            for c in range(cams):
                dviews_ref[c, o] = (mask[:, c : c + 1] * dview).astype(bf16)
        for step in range(1, cams):
            view_copy((cam + step) % cams, cam).start()
        gp_s[:, cam] = dviews_ref[cam]

        dha, ag_ref[0:1, :], ag_ref[1:2, :] = norm_back(dmid * scale[None] * slope, za, rstd_ref[...], tail(0))
        ag_ref[4:5, :] = total(dha)
        ag_ref[6:7, :] = jnp.sum(dscale, axis=0, keepdims=True)
        ag_ref[7:8, :] = jnp.sum(dshift, axis=0, keepdims=True)
        dwb = grad(1, 0, PART)
        hb = across(dhb)
        for t in range(5):
            dwb[:, t * CH : (t + 1) * CH] = dot(hb, pad_m[t * ns : t * ns + frows, :]).astype(bf16)
        dt_save(1, 1).start()
        pairs = kept(3).astype(bf16).reshape(nf // 2, 2, ns, CH)
        half = frows // 2
        sum_ref[0:ns, :] = jnp.zeros((ns, CH), bf16)
        sum_ref[ns : ns + half, :] = pairs[:, 1].reshape(half, CH)
        sum_ref[ns + half : ns + 2 * half, :] = pairs[:, 0].reshape(half, CH)
        og = jnp.transpose(og_ref[...].astype(f32)).astype(bf16)
        dwd = grad(0, CH, 3 * CH)
        out = None
        for t, at in enumerate((0, ns + half, ns)):
            cols = sum_ref[at : at + half, :]
            part = dot(cols, wd[:, t * CH : (t + 1) * CH], NT)
            out = part if out is None else out + part
            dwd[:, t * CH : (t + 1) * CH] = dot(og, cols).astype(bf16)
        dt_save(3, 0).start()
        out_ref[...] = (out + tail(9)).astype(bf16)
        fill(pad_h, dha)
        tg_ref[...] = tg_ref[...] + conv5_back(pad_h, wa)
        dt_save(1, 1).wait()
        for base, low in zip((0, cond), lows):
            dw = grad(1, base, cond)
            for v, cols in zip(conds, lanes):
                dw[:, cols] = dot(low, v, TN).astype(bf16)
        grad(1, 2 * cond, BLK)[...] = jnp.transpose(ag_ref[...]).astype(bf16)
        blank(1, 2 * cond + BLK)
        dt_save(2, 1).start()
        dt_save(3, 0).wait()
        dwa = grad(0, 0, PART)
        ha = across(dha)
        for t in range(5):
            dwa[:, t * CH : (t + 1) * CH] = dot(ha, pad_t[t * ns : t * ns + frows, :]).astype(bf16)
        dt_save(0, 0).start()
        for step in range(1, cams):
            other = (cam + step) % cams
            view_copy(other, other).wait_recv()
        gp_ref[...] = gp_s[...]
        dt_save(2, 1).wait()
        dt_save(0, 0).wait()

    def z_copy(conv, k, way):
        ref = w_ref.at[conv, 2 * k + core]
        return batch_copy(ref, ref, zsend.at[conv, way, k], zrecv.at[conv, k], me - 2 + 4 * way)

    def core_copy(conv, k, which):
        ref = w_ref.at[conv, 2 * k + which]
        return batch_copy(ref, ref, csend.at[conv, k], crecv.at[conv, k], partner)

    def moves(s):
        low, high = zi - s, zi + s
        return (
            (high, high < nz, (high < nz) & (zi > 0), 0),
            (low, low >= 0, (low >= 0) & (zi < nz - 1), 1),
        )

    def send(conv, s):
        for k, _, passed, way in moves(s):
            @pl.when(passed)
            def _():
                z_copy(conv, k, way).start()

    def receive(conv, s):
        for k, held, _, way in moves(s):
            @pl.when(held)
            def _():
                z_copy(conv, k, way).wait_recv()
                core_copy(conv, k, core).start()

    t_send(0)
    for q in range(cams):
        pl.when(cam != q)(functools.partial(pack_own, q))
    for q in range(cams):
        tc_copy(zi, core, q).start()
    for conv in range(2):
        w_ref[conv, me, :, 9 * CH :] = ext
    count = rows // piece

    def pack(i, carry):
        @pl.when(i + 1 < count)
        def _():
            enc_load(i + 1).start()

        enc_load(i).wait()
        for conv in range(2):
            w_ref[conv, me, pl.ds(pl.multiple_of(i * piece, piece), piece), 0 : 9 * CH] = (
                enc_buf[i % 2, :, conv, :].astype(bf16)
            )
        return carry

    lax.fori_loop(0, count, pack, 0)

    for conv in range(2):
        core_copy(conv, zi, core).start()

    def t_step(s, carry):
        @pl.when(s == nz - 1)
        def _():
            send(0, 0)

        t_receive(s)

        @pl.when(s < nz - 1)
        def _():
            t_send(s)
        return carry

    lax.fori_loop(1, nz, t_step, 0)

    def x_save(p):
        return pltpu.make_async_copy(x_ref.at[:, p * CH : (p + 1) * CH], x_out.at[p], xsem.at[p])

    fill_edges(pad_t)
    moved = traj_ref[...].astype(f32)
    for f in range(nf):
        pad_t[edge + f * ns : edge + (f + 1) * ns, :] = moved[:, f].astype(bf16)
    moved = og_in[...].astype(f32)
    for f in range(nf // 2):
        og_ref[f * ns : (f + 1) * ns, :] = moved[:, f].astype(bf16)
    half = n_img // 2
    img_load.wait()
    for p in range(9):
        pair = img_ref[:, p].astype(f32)
        for o in range(2):
            x_ref[o * half : (o + 1) * half, p * CH : (p + 1) * CH] = pair[:, o].astype(bf16)
        x_save(p).start()

    def rows_of(conv, j, start, wide):
        block = w_ref[conv, pl.ds(j * spb, spb), :, start : start + wide]
        return block.reshape(BLK, wide)

    def w_save(conv, j):
        part = pl.ds(j * spb, spb)
        return pltpu.make_async_copy(w_ref.at[conv, part], w_out.at[conv, part], wsem.at[conv, j])

    def conv_norm(src_ref, conv, z_ref, r_ref, j):
        lanes = pl.ds(pl.multiple_of(j * BLK, BLK), BLK)
        total = None
        for p in range(9):
            r, c = divmod(p, 3)
            bs = span(c)
            acc = None
            for a in span(r):
                start = (3 * (r + a - 1) + c + bs[0] - 1) * CH
                wide = len(bs) * CH
                part = dot(src_ref[:, start : start + wide], rows_of(conv, j, (3 * a + bs[0]) * CH, wide), NT)
                acc = part if acc is None else acc + part
            z_ref[p, :, lanes] = acc
            total = acc if total is None else total + acc
        mean = group_sum(total, ones) * inv_n
        var = None
        for p in range(9):
            centred = z_ref[p, :, lanes] - mean
            sq = centred * centred
            var = sq if var is None else var + sq
        rstd = lax.rsqrt(group_sum(var, ones) * inv_n + norm_eps)
        r_ref[:, lanes] = rstd
        return lanes, mean, rstd

    def first(j):
        aff_ref[:, lanes_of(j)] = jnp.transpose(rows_of(0, j, 9 * CH, BLK).astype(f32))[0:8]
        lanes, mean, rstd = conv_norm(x_ref, 0, z1_ref, r1_ref, j)
        gain, offset = aff_ref[0:1, lanes], aff_ref[1:2, lanes]
        for p in range(9):
            z = (z1_ref[p, :, lanes] - mean) * rstd
            z1_ref[p, :, lanes] = z
            u = z * gain + offset
            a_ref[:, pl.ds(pl.multiple_of(p * CH + j * BLK, BLK), BLK)] = (u * sigmoid(u)).astype(bf16)

    def second(j):
        lanes, mean, rstd = conv_norm(a_ref, 1, z2_ref, r2_ref, j)
        gain, offset = aff_ref[2:3, lanes], aff_ref[3:4, lanes]
        total = None
        for p in range(9):
            z = (z2_ref[p, :, lanes] - mean) * rstd
            z2_ref[p, :, lanes] = z
            cols = pl.ds(pl.multiple_of(p * CH + j * BLK, BLK), BLK)
            u = z * gain + offset + x_ref[:, cols].astype(f32)
            s = sigmoid(u)
            act = u * s
            x_ref[:, cols] = (s + act * (1.0 - s)).astype(bf16)
            total = act if total is None else total + act
        out = (total * (1.0 / 9.0)).astype(bf16)
        feat_ref[:, :, :, lanes] = out.reshape(feat_ref.shape[:3] + (BLK,))

    def lanes_of(j):
        return pl.ds(pl.multiple_of(j * BLK, BLK), BLK)

    def arrived(conv, k):
        core_copy(conv, k, 1 - core).wait_recv()

    def phase(conv, block):
        streaming = spb == 2

        def step(s, carry):
            if conv == 0:
                @pl.when((s > 0) & (s < nz - 1))
                def _():
                    send(0, s)

                @pl.when(s == nz - 1)
                def _():
                    send(1, 0)
            else:
                @pl.when((s > 0) & (s < nz - 1))
                def _():
                    send(1, s)

            def side(d, carry):
                k = zi + s - 2 * s * d

                @pl.when((k >= 0) & (k < nz) & (s + 1 > d))
                def _():
                    arrived(conv, k)
                    if streaming:
                        w_save(conv, k).start()
                        block(k)
                return carry

            lax.fori_loop(0, 2, side, 0)
            if conv == 1:
                t_collect(2 * s)
                t_collect(2 * s + 1)

                @pl.when(s == nz - 2)
                def _():
                    t_complete()
                    saves[0].wait()
                    temporal_early()

            @pl.when(s < nz - 1)
            def _():
                receive(conv, s + 1)
            return carry

        lax.fori_loop(0, nz, step, 0)
        if not streaming:
            def rest(j, carry):
                w_save(conv, j).start()
                block(j)
                return carry

            lax.fori_loop(0, CH // BLK, rest, 0)

    phase(0, first)
    saves = [pltpu.make_async_copy(z1_ref, z1_out, osem.at[0])]
    saves += [
        pltpu.make_async_copy(a_ref.at[:, p * CH : (p + 1) * CH], a_out.at[p], osem.at[2 + p])
        for p in range(9)
    ]
    for save in saves:
        save.start()
    for p in range(9):
        x_save(p).wait()
    phase(1, second)
    last = pltpu.make_async_copy(z2_ref, z2_out, osem.at[1])
    last.start()

    def slope_save(p):
        return pltpu.make_async_copy(x_ref.at[:, p * CH : (p + 1) * CH], slope_out.at[p], xsem.at[p])

    for p in range(9):
        slope_save(p).start()

    def feat_copy(to, sender):
        return cam_copy(feat_ref.at[:, to], arr_s.at[sender], fsend.at[to], frecv.at[sender], to)

    for step in range(1, cams):
        feat_copy((cam + step) % cams, cam).start()
    arr_s[cam] = feat_ref[:, cam]
    for step in range(1, cams):
        other = (cam + step) % cams
        feat_copy(other, other).wait_recv()
    temporal_rest()
    for step in range(1, cams):
        feat_copy((cam + step) % cams, cam).wait_send()

    for conv in range(2):
        def drain(k, carry):
            s = k - zi

            @pl.when((s >= 0) & (s < nz - 1) & (zi > 0))
            def _():
                z_copy(conv, k, 0).wait_send()

            @pl.when((s <= 0) & (s > 1 - nz) & (zi < nz - 1))
            def _():
                z_copy(conv, k, 1).wait_send()

            core_copy(conv, k, core).wait_send()
            return carry

        lax.fori_loop(0, nz, drain, 0)

        def saved(j, carry):
            w_save(conv, j).wait()
            return carry

        lax.fori_loop(0, CH // BLK, saved, 0)
    for save in saves[1:]:
        save.wait()
    last.wait()

    def t_drain(k, carry):
        s = k - zi

        @pl.when((s >= 0) & (s < nz - 1) & (zi > 0))
        def _():
            tz_copy(k, 0).wait_send()

        @pl.when((s <= 0) & (s > 1 - nz) & (zi < nz - 1))
        def _():
            tz_copy(k, 1).wait_send()

        @pl.when(s != 0)
        def _():
            for step in range(1, cams):
                tp_copy(k, step, cam).wait_send()

        for q in range(cams):
            tc_copy(k, core, q).wait_send()
        return carry

    lax.fori_loop(0, nz, t_drain, 0)
    for p in range(9):
        slope_save(p).wait()
    for step in range(1, cams):
        view_copy((cam + step) % cams, cam).wait_send()


def enc_bwd_kernel(
    n, cams, cond, x_hbm, slope_hbm, a_hbm, w_hbm, z1_hbm, r1_ref, z2_hbm, r2_ref, aff_ref, gp_ref, dt_hbm,
    ig_out, genc_ref, gaff_ref, gconvs_ref, gfilm_ref, gskip_ref, gdown_ref, gblk_ref,
    ig_ref, x_ref, a_ref, w_ref, z1_ref, z2_ref, g_ref, gt_ref, ag_ref,
    dwf, core_out, core_in, slots, t_own, t_sum, t_peer, t_slots, t_all,
    lsem, bsem, isem, csend, crecv, zsend, zrecv,
    tlsem, tcsend, tcrecv, tpsend, tprecv, tzsend, tzrecv, tfsend, tfrecv,
):
    nz = n // 2
    rows = CH // n
    n_img = z1_ref.shape[1]
    me, cam = lax.axis_index("batch"), lax.axis_index("cam")
    zi, core = me // 2, me % 2
    partner = me + 1 - 2 * core
    ones = group_ones(BLK, ENC_GROUP)
    inv_n = 1.0 / (9 * ENC_GROUP)
    chunk = 3 * CH

    def load_w(conv):
        return pltpu.make_async_copy(w_hbm.at[conv, :, :, 0 : 9 * CH], w_ref, lsem.at[3])

    def lanes_of(j):
        return pl.ds(pl.multiple_of(j * BLK, BLK), BLK)

    def block_loads(j):
        cols = lanes_of(j)
        return (
            pltpu.make_async_copy(z2_hbm.at[:, :, cols], z2_ref.at[:, :, cols], bsem.at[0, j]),
            pltpu.make_async_copy(slope_hbm.at[:, :, cols], g_ref.at[:, :, cols], bsem.at[1, j]),
        )

    loads = {
        "z1": pltpu.make_async_copy(z1_hbm, z1_ref, lsem.at[1]),
        "a": pltpu.make_async_copy(a_hbm, a_ref, lsem.at[2]),
        "x": pltpu.make_async_copy(x_hbm, x_ref, lsem.at[0]),
    }
    for j in range(CH // BLK):
        for load in block_loads(j):
            load.start()

    def own_load(i):
        return pltpu.make_async_copy(dt_hbm.at[i // cams, core, i % cams], t_own.at[i % 2], tlsem.at[i])

    own_load(0).start()

    line_greet(cams, nz)

    def t_core(k):
        return batch_copy(dt_hbm.at[k, 1 - core], t_sum.at[k], tcsend.at[k], tcrecv.at[k], partner)

    def t_peers(k, step):
        to = (cam + step) % cams
        return cam_copy(t_sum.at[k, to], t_peer.at[step - 1, k], tpsend.at[step - 1, k], tprecv.at[step - 1, k], to)

    def t_start(k, carry):
        t_core(k).start()
        return carry

    def t_spread(lo, hi):
        def body(k, carry):
            t_core(k).wait_recv()

            def quarter(q, carry):
                i = k * cams + q

                @pl.when(i + 1 < nz * cams)
                def _():
                    own_load(i + 1).start()

                own_load(i).wait()
                t_sum[k, q] = (t_sum[k, q].astype(f32) + t_own[i % 2].astype(f32)).astype(bf16)
                return carry

            lax.fori_loop(0, cams, quarter, 0)
            for step in range(1, cams):
                t_peers(k, step).start()
            return carry

        lax.fori_loop(lo, hi, body, 0)

    ag_ref[...] = jnp.zeros_like(ag_ref)

    def norm_back(du_ref, z_ref, r_ref, j, gain, row):
        lanes = lanes_of(j)
        s0 = jnp.zeros((n_img, BLK), f32)
        s1 = jnp.zeros((n_img, BLK), f32)
        for p in range(9):
            du = du_ref[p, :, lanes]
            s0 = s0 + du
            s1 = s1 + du * z_ref[p, :, lanes]
        ag_ref[row : row + 1, lanes] = jnp.sum(s1, axis=0, keepdims=True)
        ag_ref[row + 1 : row + 2, lanes] = jnp.sum(s0, axis=0, keepdims=True)
        m0 = group_sum(s0 * gain, ones) * inv_n
        m1 = group_sum(s1 * gain, ones) * inv_n
        rstd = r_ref[:, lanes]
        for p in range(9):
            dv = (du_ref[p, :, lanes] * gain - m0 - z_ref[p, :, lanes] * m1) * rstd
            g_ref[p, :, lanes] = dv.astype(bf16)
            gt_ref[lanes, p * n_img : (p + 1) * n_img] = jnp.transpose(dv).astype(bf16)

    def second(j, carry):
        lanes = lanes_of(j)
        for load in block_loads(j):
            load.wait()
        pooled = gp_ref[:, :, :, lanes].reshape(n_img, BLK).astype(f32) * (1.0 / 9.0)
        for p in range(9):
            ig_ref[p, :, lanes] = pooled * g_ref[p, :, lanes].astype(f32)
        norm_back(ig_ref, z2_ref, r2_ref, j, aff_ref[2:3, lanes], 2)
        return carry

    def first(j, carry):
        lanes = lanes_of(j)
        gain, offset = aff_ref[0:1, lanes], aff_ref[1:2, lanes]
        for p in range(9):
            u = z1_ref[p, :, lanes] * gain + offset
            s = sigmoid(u)
            z2_ref[p, :, lanes] = z2_ref[p, :, lanes] * (s * (1.0 + u * (1.0 - s)))
        norm_back(z2_ref, z1_ref, r1_ref, j, gain, 0)
        return carry

    def width(k):
        return chunk + BLK if k == 5 else chunk

    def core_copy(k):
        cols = pl.ds(0, width(k))
        return batch_copy(
            core_out.at[k % 2, :, :, cols], core_in.at[k % 3, :, :, cols], csend.at[k], crecv.at[k], partner
        )

    def keep(k, d0, lane, v):
        count, wide = v.shape[0] // (2 * rows), v.shape[1]
        parts = v.reshape(count, 2, rows, wide)
        even, odd = parts[:, 0], parts[:, 1]
        dwf[k % 2, d0 : d0 + count, :, lane : lane + wide] = jnp.where(core == 0, even, odd)
        core_out[k % 2, d0 : d0 + count, :, lane : lane + wide] = jnp.where(core == 0, odd, even).astype(bf16)

    def make_chunk(k):
        if k >= 2:
            core_copy(k - 2).wait_send()
        src_ref = a_ref if k < 3 else x_ref
        a = k % 3
        r_lo, r_hi = max(0, 1 - a), min(2, 3 - a)
        for b in range(3):
            c_lo, c_hi = max(0, 1 - b), min(2, 3 - b)
            if b == 1:
                runs = [(3 * r_lo, 3 * (r_hi - r_lo + 1))]
            else:
                runs = [(3 * r + c_lo, c_hi - c_lo + 1) for r in range(r_lo, r_hi + 1)]
            shift = 3 * (a - 1) + b - 1
            for half in range(2):
                acc = None
                for p, m in runs:
                    part = dot(
                        gt_ref[half * 256 : half * 256 + 256, p * n_img : (p + m) * n_img],
                        src_ref[p + shift : p + shift + m].reshape(m * n_img, CH),
                    )
                    acc = part if acc is None else acc + part
                keep(k, half * nz // 2, b * CH, acc)
        if k == 5:
            keep(k, 0, chunk, jnp.transpose(ag_ref[...]))
        core_copy(k).start()

    def term(k, d):
        return dwf[k % 2, d, :, 0 : width(k)] + core_in[k % 3, d, :, 0 : width(k)].astype(f32)

    def line_copy(k, way, s):
        if k == 6:
            return batch_copy(
                t_slots.at[way, s - 1], t_slots.at[way, s], tzsend.at[way, s], tzrecv.at[way, s], me - 2 + 4 * way
            )
        cols = pl.ds(0, width(k))
        return batch_copy(
            slots.at[k % 3, way, s - 1, :, cols], slots.at[k % 3, way, s, :, cols],
            zsend.at[k, way, s], zrecv.at[k, way, s], me - 2 + 4 * way,
        )

    def slot(k, way, s):
        return t_slots.at[way, s] if k == 6 else slots.at[k % 3, way, s, :, pl.ds(0, width(k))]

    def t_term(d):
        total = t_sum[d, cam].astype(f32)
        for step in range(1, cams):
            total = total + t_peer[step - 1, d].astype(f32)
        return total

    def serve(k, s):
        for way in range(2):
            ahead = zi if way else nz - 1 - zi
            d = nz - s + zi if way else s - nz + zi
            ref = slot(k, way, s - 1)

            @pl.when((ahead < nz - 1) & (s > ahead))
            def _():
                own = t_term(d) if k == 6 else term(k, d)

                @pl.when(ahead > 0)
                def _():
                    line_copy(k, way, s - 1).wait_recv()
                    ref[...] = (ref[...].astype(f32) + own).astype(bf16)

                @pl.when(ahead == 0)
                def _():
                    ref[...] = own.astype(bf16)

                line_copy(k, way, s).start()

    def steps(k, part):
        lo, hi = 1 + part * (nz - 1) // 3, 1 + (part + 1) * (nz - 1) // 3
        if hi - lo == 1:
            serve(k, lo)
        elif hi > lo:
            def body(s, carry):
                serve(k, s)
                return carry

            lax.fori_loop(lo, hi, body, 0)

    def service(g):
        k, part = divmod(g, 3)
        if part == 0:
            core_copy(k).wait_recv()
        steps(k, part)

    def collect(k, total, write):
        last = nz - 1

        @pl.when(zi > 0)
        def _():
            line_copy(k, 1, last).wait_recv()

        @pl.when(zi < nz - 1)
        def _():
            line_copy(k, 0, last).wait_recv()

        @pl.when(zi == 0)
        def _():
            write(total + slot(k, 0, last)[...].astype(f32))

        @pl.when(zi == nz - 1)
        def _():
            write(total + slot(k, 1, last)[...].astype(f32))

        @pl.when((zi > 0) & (zi < nz - 1))
        def _():
            write(total + slot(k, 0, last)[...].astype(f32) + slot(k, 1, last)[...].astype(f32))

        def drain(s, carry):
            for way in range(2):
                ahead = zi if way else nz - 1 - zi

                @pl.when((ahead < nz - 1) & (s > ahead))
                def _():
                    line_copy(k, way, s).wait_send()
            return carry

        lax.fori_loop(1, nz, drain, 0)

    def finish(k):
        def write(v):
            genc_ref[:, 1 - k // 3, (k % 3) * chunk : (k % 3 + 1) * chunk] = v[:, 0:chunk]
            if k == 5:
                gaff_ref[...] = jnp.transpose(v[:, chunk:])[0 : gaff_ref.shape[0]]

        collect(k, term(k, zi), write)

    def t_arrived():
        for step in range(1, cams):
            def body(k, carry):
                t_peers(k, step).wait_recv()
                return carry

            lax.fori_loop(0, nz, body, 0)

    def t_final(to, sender):
        return cam_copy(t_all.at[cam], t_all.at[sender], tfsend.at[to], tfrecv.at[sender], to)

    def t_finish():
        def write(v):
            t_all[cam] = v.astype(bf16)

        collect(6, t_term(zi), write)
        for step in range(1, cams):
            t_final((cam + step) % cams, cam).start()

    def t_write():
        for step in range(1, cams):
            other = (cam + step) % cams
            t_final(other, other).wait_recv()

        def cut(q, lo, wide):
            return t_all[q, :, lo : lo + wide].astype(f32)

        for which in range(2):
            gconvs_ref[:, which, :] = cut(which, 0, PART)
            gfilm_ref[:, which, :] = cut(2, which * cond, cond)
        gblk_ref[...] = jnp.transpose(cut(2, 2 * cond, BLK))[0 : gblk_ref.shape[0]]
        gskip_ref[...] = cut(3, 0, CH)
        gdown_ref[...] = cut(3, CH, 3 * CH)

    def input_back(q):
        r, c = divmod(q, 3)
        acc = None
        for a in range(3):
            for b in range(3):
                pr, pc = r - a + 1, c - b + 1
                if 0 <= pr < 3 and 0 <= pc < 3:
                    t = 3 * a + b
                    w = w_ref[:, :, t * CH : (t + 1) * CH].reshape(CH, CH)
                    part = dot(g_ref[3 * pr + pc], w)
                    acc = part if acc is None else acc + part
        return acc

    def back_second(*qs):
        for q in qs:
            if q == 0:
                load_w(1).wait()
            z2_ref[q] = input_back(q)
            if q == 8:
                load_w(0).start()

    def ig_save(q):
        return pltpu.make_async_copy(a_ref.at[q], ig_out.at[q], isem.at[q])

    def back_first(*qs):
        for q in qs:
            if q == 0:
                load_w(0).wait()
            a_ref[q] = (ig_ref[q] + input_back(q)).astype(bf16)
            ig_save(q).start()

    def quarter_of(i):
        return i * nz // 4, (i + 1) * nz // 4

    def t_go(i):
        lax.fori_loop(*quarter_of(i), t_start, 0)

    lax.fori_loop(0, 1, second, 0)
    loads["a"].start()
    line_wait(cams, nz)
    lax.fori_loop(1, CH // BLK, second, 0)
    load_w(1).start()
    loads["a"].wait()
    make_chunk(0)
    back_second(0)
    service(0)
    t_go(0)
    make_chunk(1)
    service(1)
    t_go(1)
    t_spread(*quarter_of(0))
    loads["z1"].start()
    loads["x"].start()
    back_second(1, 2)
    service(2)
    t_go(2)
    t_spread(*quarter_of(1))
    back_second(3, 4)
    service(3)
    finish(0)
    t_go(3)
    t_spread(*quarter_of(2))
    make_chunk(2)
    service(4)
    t_spread(*quarter_of(3))
    back_second(5, 6)
    service(5)
    back_second(7, 8)
    service(6)
    finish(1)
    loads["z1"].wait()
    loads["x"].wait()
    lax.fori_loop(0, 2, first, 0)
    service(7)
    lax.fori_loop(2, 4, first, 0)
    service(8)
    make_chunk(3)
    service(9)
    finish(2)
    make_chunk(4)
    service(10)
    back_first(0, 1)
    service(11)
    back_first(2, 3)
    service(12)
    finish(3)
    make_chunk(5)
    service(13)
    back_first(4, 5)
    service(14)
    t_arrived()
    steps(6, 0)
    finish(4)
    back_first(6)
    steps(6, 1)
    back_first(7)
    steps(6, 2)
    back_first(8)
    service(15)
    t_finish()
    service(16)
    service(17)
    t_write()
    finish(5)

    for q in range(9):
        ig_save(q).wait()

    def t_drain(k, carry):
        t_core(k).wait_send()
        for step in range(1, cams):
            t_peers(k, step).wait_send()
        return carry

    lax.fori_loop(0, nz, t_drain, 0)
    for step in range(1, cams):
        t_final((cam + step) % cams, cam).wait_send()
    core_copy(4).wait_send()
    core_copy(5).wait_send()


def call(kernel, outs, in_specs, out_specs, scratch=(), collective_id=None, cost=None):
    extra = {} if collective_id is None else dict(collective_id=collective_id, has_side_effects=True)
    return pl.pallas_call(
        kernel,
        out_shape=[jax.ShapeDtypeStruct(s, d) for s, d in outs],
        in_specs=in_specs,
        out_specs=out_specs,
        scratch_shapes=list(scratch),
        compiler_params=pltpu.CompilerParams(vmem_limit_bytes=VMEM_BYTES, **extra),
        cost_estimate=cost,
    )


def work(microseconds):
    return pl.CostEstimate(
        flops=int(microseconds * 1e9), bytes_accessed=int(microseconds * 3e6), transcendentals=0
    )


V = pl.BlockSpec(memory_space=pltpu.VMEM)
H = pl.BlockSpec(memory_space=pl.ANY)
DMA = pltpu.SemaphoreType.DMA


def time_embed(steps_given, embed_width):
    half_width = embed_width // 2
    frequency = jnp.exp(
        jnp.arange(half_width, dtype=jnp.float32) * (-math.log(10000.0) / (half_width - 1))
    )
    argument = steps_given.astype(jnp.float32)[:, None] * frequency[None, :]
    return jnp.concatenate([jnp.sin(argument), jnp.cos(argument)], axis=1)


def adamw(weight, gradient, moment_one, moment_two, step_rate, weight_decay):
    mean_new = beta_first * moment_one + (1.0 - beta_first) * gradient
    square_new = beta_second * moment_two + (1.0 - beta_second) * gradient * gradient
    square_hat = square_new * (1.0 / (1.0 - beta_second**STEP))
    root = square_hat * lax.rsqrt(square_hat)
    weight_new = (1.0 - step_rate * weight_decay) * weight - (step_rate / (1.0 - beta_first**STEP)) * (
        mean_new / (root + adam_eps)
    )
    return (weight_new, mean_new, square_new)


def last_kernel(*refs):
    tg_ref, out_ref, ig_ref = refs[28:31]
    tg_new, out_new, ig_new, turn_ref = refs[52:56]
    for p in range(ig_ref.shape[0]):
        for o in range(ig_ref.shape[1]):
            ig_new[:, p, o, :] = ig_ref[p, o].astype(f32)

    @pl.when(pl.program_id(0) == 0)
    def _():
        for f in range(tg_ref.shape[0]):
            tg_new[:, f, :] = tg_ref[f]
        for u in range(out_ref.shape[0]):
            turn_ref[:, u, :] = out_ref[u].astype(f32)
        out_new[...] = turn_ref[...].astype(bf16)

    for i in range(7):
        w_ref, m_ref, v_ref, g_ref = refs[4 * i : 4 * i + 4]
        outs = refs[31 + 3 * i : 34 + 3 * i]

        def update():
            vector = i in (1, 6)
            rate, decay = (rate_vector, 0.0) if vector else (rate_matrix, decay_matrix)
            new = adamw(w_ref[...], g_ref[...], m_ref[...], v_ref[...], rate, decay)
            for ref, value in zip(outs, new):
                ref[...] = value

        if i in (1, 6):
            pl.when(pl.program_id(0) == 0)(update)
        else:
            update()


def last_call(shown, grads, tg, out, ig, rows):
    step = min(rows, 8)
    steps = rows // step

    def whole(shape):
        return pl.BlockSpec(shape, lambda r: (0,) * len(shape))

    def spec(v):
        if v.shape[0] != rows:
            return whole(v.shape)
        return pl.BlockSpec((step,) + v.shape[1:], lambda r: (r,) + (0,) * (v.ndim - 1))

    ins = []
    for i in range(7):
        ins += [shown[0][i], shown[1][i], shown[2][i], grads[i]]
    outs = [w for w in shown[0] for _ in range(3)]
    pos, obs, count, ch = ig.shape
    part = count // steps
    turned = [(v.shape[1], v.shape[0], v.shape[2]) for v in (tg, out)]
    return pl.pallas_call(
        last_kernel,
        grid=(steps,),
        out_shape=[jax.ShapeDtypeStruct(v.shape, f32) for v in outs]
        + [jax.ShapeDtypeStruct(turned[0], f32), jax.ShapeDtypeStruct(turned[1], bf16),
           jax.ShapeDtypeStruct((count, pos, obs, ch), f32)],
        in_specs=[spec(v) for v in ins]
        + [whole(tg.shape), whole(out.shape), pl.BlockSpec((pos, obs, part, ch), lambda r: (0, 0, r, 0))],
        out_specs=[spec(v) for v in outs]
        + [whole(turned[0]), whole(turned[1]), pl.BlockSpec((part, pos, obs, ch), lambda r: (r, 0, 0, 0))],
        scratch_shapes=[pltpu.VMEM(turned[1], f32)],
        compiler_params=pltpu.CompilerParams(vmem_limit_bytes=VMEM_BYTES),
        cost_estimate=work(15),
    )(*ins, tg, out, ig)


def shards(
    n, images, trajectory, view_mask, timesteps, out_grad,
    encoder_weight, encoder_affine, block_convs, film_weight, skip_weight, down_weight, block_affine,
    first_encoder, first_affine, first_convs, first_film, first_skip, first_down, first_block,
    second_encoder, second_affine, second_convs, second_film, second_skip, second_down, second_block,
):
    ns, nf, ch = trajectory.shape
    cams, obs = images.shape[1], images.shape[3]
    n_img = cams * images.shape[2] * obs
    nz, per = n // 2, ch // n
    cond = film_weight.shape[2]
    wide = 9 * ch
    rows = nf * ns

    def turned(v):
        return jnp.transpose(v.reshape(v.shape[-2:]))

    pairs = jnp.transpose(images[0], (0, 1, 3, 2, 4)).reshape(n_img // obs, 9, obs, ch)
    pos = (9, n_img, ch)
    t_shape = (nz, 2, cams, per, PART)
    wcols = wide + BLK
    z1, r1, act, z2, r2, w_all, enc_aff, x, slope, out_fm, tg_fm, gp, dt = call(
        functools.partial(forward_kernel, n, cams),
        [(pos, f32), ((n_img, ch), f32), (pos, bf16), (pos, f32), ((n_img, ch), f32), ((2, n, per, wcols), bf16),
         ((8, ch), f32), (pos, bf16), (pos, bf16), ((rows // 2, ch), bf16), ((rows, ch), f32), ((obs, cams, ns, ch), bf16),
         (t_shape, bf16)],
        [H, V, V, V, V, H, V, V, V, V, V, V],
        [H, V, H, H, V, H, V, H, H, V, V, V, H],
        [pltpu.VMEM((n_img // obs, 9, obs, ch), bf16), pltpu.VMEM((n_img, wide), bf16), pltpu.VMEM((2, n, per, wcols), bf16), pltpu.VMEM(pos, f32),
         pltpu.VMEM((n_img, wide), bf16), pltpu.VMEM(pos, f32), pltpu.VMEM((obs, cams, ns, ch), bf16),
         pltpu.VMEM((cams, obs, ns, ch), bf16), pltpu.VMEM(t_shape, bf16), pltpu.VMEM((2, min(per, 16), 2, wide), f32),
         pltpu.VMEM((BLK, BLK), f32), pltpu.VMEM((BLK, per), f32), pltpu.VMEM((rows // 2, ch), bf16), pltpu.VMEM((rows + 4 * ns, ch), bf16),
         pltpu.VMEM((rows + 4 * ns, ch), bf16), pltpu.VMEM((rows + 4 * ns, ch), bf16), pltpu.VMEM((rows + ns, ch), bf16),
         pltpu.VMEM((BLK, ch), f32), pltpu.VMEM((BLK, ch), f32), pltpu.VMEM((ns, ch), f32),
         pltpu.VMEM((cams, obs, ns, ch), bf16), pltpu.VMEM((obs, cams, ns, ch), bf16),
         pltpu.VMEM((2, nz, 2, per, PART), bf16),
         DMA((2, 2, nz)), DMA((2, nz)), DMA((2, nz)), DMA((2, nz)), DMA((2, ch // BLK)), DMA((11,)),
         DMA((cams,)), DMA((cams,)),
         DMA((2, nz)), DMA((nz,)), DMA((nz, cams)), DMA((nz, cams)), DMA((cams - 1, nz)), DMA((cams - 1, nz)),
         DMA((max(per // 16, 1),)), DMA((10,)), DMA((cams,)), DMA((cams,)), DMA((4,))],
        collective_id=0,
        cost=work(130),
    )(pairs, trajectory, out_grad, jnp.transpose(view_mask), time_embed(timesteps, TEMB), encoder_weight[0], block_convs,
      film_weight, skip_weight, down_weight, turned(encoder_affine), turned(block_affine))
    chunk = 3 * ch + BLK
    ig, genc, gaff, gconvs, gfilm, gskip, gdown, gblk = call(
        functools.partial(enc_bwd_kernel, n, cams, cond),
        [(pos, bf16), ((per, 2, wide), f32), ((4, per), f32), ((per, 2, 5 * ch), f32),
         ((per, 2, cond), f32), ((per, ch), f32), ((per, 3 * ch), f32), ((10, per), f32)],
        [H, H, H, H, H, V, H, V, V, V, H],
        [H] + [V] * 7,
        [pltpu.VMEM(pos, f32), pltpu.VMEM(pos, bf16), pltpu.VMEM(pos, bf16), pltpu.VMEM((n, per, wide), bf16), pltpu.VMEM(pos, f32),
         pltpu.VMEM(pos, f32), pltpu.VMEM(pos, bf16), pltpu.VMEM((ch, 9 * n_img), bf16),
         pltpu.VMEM((BLK, ch), f32),
         pltpu.VMEM((2, nz, per, chunk), f32), pltpu.VMEM((2, nz, per, chunk), bf16),
         pltpu.VMEM((3, nz, per, chunk), bf16), pltpu.VMEM((3, 2, nz, per, chunk), bf16),
         pltpu.VMEM((2, per, PART), bf16), pltpu.VMEM((nz, cams, per, PART), bf16),
         pltpu.VMEM((cams - 1, nz, per, PART), bf16), pltpu.VMEM((2, nz, per, PART), bf16),
         pltpu.VMEM((cams, per, PART), bf16),
         DMA((4,)), DMA((2, ch // BLK)), DMA((9,)), DMA((6,)), DMA((6,)), DMA((6, 2, nz)), DMA((6, 2, nz)),
         DMA((nz * cams,)), DMA((nz,)), DMA((nz,)), DMA((cams - 1, nz)), DMA((cams - 1, nz)),
         DMA((2, nz)), DMA((2, nz)), DMA((cams,)), DMA((cams,))],
        collective_id=1,
        cost=work(100),
    )(x, slope, act, w_all, z1, r1, z2, r2, enc_aff, gp, dt)
    weights = (encoder_weight, encoder_affine, block_convs, film_weight, skip_weight, down_weight, block_affine)
    firsts = (first_encoder, first_affine, first_convs, first_film, first_skip, first_down, first_block)
    seconds = (second_encoder, second_affine, second_convs, second_film, second_skip, second_down, second_block)
    shown = [
        [turned(v) if i in (1, 6) else v.reshape(v.shape[-3:]) if i == 0 else v for i, v in enumerate(group)]
        for group in (weights, firsts, seconds)
    ]
    *news, trajectory_grad, block_output, ig_new = last_call(
        shown, (genc, gaff, gconvs, gfilm, gskip, gdown, gblk),
        tg_fm.reshape(nf, ns, ch), out_fm.reshape(nf // 2, ns, ch), ig.reshape(9, obs, n_img // obs, ch), per,
    )
    images_grad = jnp.transpose(ig_new.reshape(images.shape[1:3] + ig_new.shape[1:]), (0, 1, 3, 2, 4))[None]
    upd = [
        tuple((turned(v) if i in (1, 6) else v).reshape(w.shape) for v in news[3 * i : 3 * i + 3])
        for i, w in enumerate(weights)
    ]
    return (
        (block_output, trajectory_grad, images_grad)
        + tuple(u[0] for u in upd)
        + tuple(u[1] for u in upd)
        + tuple(u[2] for u in upd)
    )


def solution(mesh):
    sample = P(("cam", "batch"))
    params = (P("cam", "batch"), P("cam", "batch")) + (P("batch"),) * 5
    images_spec = P("cam", None, "batch")
    return jax.shard_map(
        functools.partial(shards, mesh.shape["batch"]),
        mesh=mesh,
        in_specs=(images_spec, sample, sample, sample, sample) + params * 3,
        out_specs=(sample, sample, images_spec) + params * 3,
        check_vma=False,
    )
```

```python
import functools
import math

import jax
import jax.numpy as jnp
from jax import lax
from jax.experimental import pallas as pl
from jax.experimental.pallas import tpu as pltpu
from jax.sharding import PartitionSpec as P

TEMB = 128
GROUPS = 8
STEP = 5

norm_eps = 1e-05
beta_first = 0.5
beta_second = 0.5
adam_eps = 1e-08
rate_matrix = 0.02
rate_vector = 0.2
decay_matrix = 0.01

CH = 512
BLK = 128
ENC_GROUP = 16
f32 = jnp.float32
bf16 = jnp.bfloat16
VMEM_BYTES = 61 * 1024 * 1024

NT = (((1,), (1,)), ((), ()))
NN = (((1,), (0,)), ((), ()))
TN = (((0,), (0,)), ((), ()))


def dot(a, b, dims=NN):
    return lax.dot_general(a, b, dims, preferred_element_type=f32)


def group_ones(width, group):
    rows = lax.broadcasted_iota(jnp.int32, (width, width), 0) // group
    cols = lax.broadcasted_iota(jnp.int32, (width, width), 1) // group
    return jnp.where(rows == cols, 1.0, 0.0).astype(bf16)


def group_sum(v, ones):
    high = v.astype(bf16)
    rest = v - high.astype(f32)
    middle = rest.astype(bf16)
    low = (rest - middle.astype(f32)).astype(bf16)
    return dot(high, ones) + dot(middle, ones) + dot(low, ones)


def sigmoid(v):
    return 1.0 / (1.0 + jnp.exp(-v))


def mish_pair(v):
    e = jnp.exp(jnp.minimum(v, 20.0))
    n = e * (e + 2.0)
    inv = 1.0 / (n + 2.0)
    t = n * inv
    return v * t, t + v * (4.0 * e * (1.0 + e)) * inv * inv


def mish_value(v):
    e = jnp.exp(jnp.minimum(v, 20.0))
    n = e * (e + 2.0)
    return v * (n / (n + 2.0))


def span(i):
    return range(max(0, 1 - i), min(2, 3 - i) + 1)


MESH = pl.DeviceIdType.MESH


def batch_copy(src, dst, send_sem, recv_sem, target):
    return pltpu.make_async_remote_copy(
        src_ref=src, dst_ref=dst, send_sem=send_sem, recv_sem=recv_sem,
        device_id={"batch": target}, device_id_type=MESH,
    )


def cam_copy(src, dst, send_sem, recv_sem, target):
    return pltpu.make_async_remote_copy(
        src_ref=src, dst_ref=dst, send_sem=send_sem, recv_sem=recv_sem,
        device_id={"cam": target}, device_id_type=MESH,
    )


def line_wait(cams, nz):
    zi = lax.axis_index("batch") // 2
    ends = (zi == 0).astype(jnp.int32) + (zi == nz - 1).astype(jnp.int32)
    pl.semaphore_wait(pltpu.get_barrier_semaphore(), cams + 2 - ends)


def line_greet(cams, nz):
    me, cam = lax.axis_index("batch"), lax.axis_index("cam")
    zi, core = me // 2, me % 2
    barrier = pltpu.get_barrier_semaphore()
    pl.semaphore_signal(barrier, inc=1, device_id={"batch": me + 1 - 2 * core}, device_id_type=MESH)
    for step in range(1, cams):
        pl.semaphore_signal(barrier, inc=1, device_id={"cam": (cam + step) % cams}, device_id_type=MESH)

    @pl.when(zi > 0)
    def _():
        pl.semaphore_signal(barrier, inc=1, device_id={"batch": me - 2}, device_id_type=MESH)

    @pl.when(zi < nz - 1)
    def _():
        pl.semaphore_signal(barrier, inc=1, device_id={"batch": me + 2}, device_id_type=MESH)


PART = 5 * CH


def pack_part(q, ref, convs_ref, film_ref, skip_ref, down_ref, ext):
    rows, cond = film_ref.shape[0], film_ref.shape[2]
    if q < 2:
        ref[q] = convs_ref[:, q, :].astype(bf16)
    elif q == 2:
        for which in range(2):
            ref[2, :, which * cond : (which + 1) * cond] = film_ref[:, which, :].astype(bf16)
        ref[2, :, 2 * cond : 2 * cond + BLK] = ext
        ref[2, :, 2 * cond + BLK :] = jnp.zeros((rows, PART - 2 * cond - BLK), bf16)
    else:
        ref[3, :, 0:CH] = skip_ref[...].astype(bf16)
        ref[3, :, CH : 4 * CH] = down_ref[...].astype(bf16)
        ref[3, :, 4 * CH :] = jnp.zeros((rows, PART - 4 * CH), bf16)


def forward_kernel(
    n, cams, img_hbm, traj_ref, og_in, mask_in, emb_ref, enc_hbm, convs_ref, film_ref, skip_ref, down_ref,
    ea_ref, ba_ref,
    z1_out, r1_ref, a_out, z2_out, r2_ref, w_out, aff_ref, x_out, slope_out, out_ref, tg_ref, gp_ref, dt_out,
    img_ref, x_ref, w_ref, z1_ref, a_ref, z2_ref, feat_ref, arr_s, t_ref, enc_buf,
    mask_s, ext_s, og_ref, pad_t, pad_m, pad_h, sum_ref, taff_ref, ag_ref, rstd_ref, dviews_ref, gp_s, dt_buf,
    zsend, zrecv, csend, crecv, wsem, osem, fsend, frecv,
    tzsend, tzrecv, tcsend, tcrecv, tpsend, tprecv, esem, xsem, vsend, vrecv, dsem,
):
    nz = n // 2
    rows = skip_ref.shape[0]
    piece = enc_buf.shape[1]
    spb = BLK // rows
    n_img = x_ref.shape[0]
    me, cam = lax.axis_index("batch"), lax.axis_index("cam")
    zi, core = me // 2, me % 2
    partner = me + 1 - 2 * core
    ones = group_ones(BLK, ENC_GROUP)
    inv_n = 1.0 / (9 * ENC_GROUP)

    def enc_load(i):
        return pltpu.make_async_copy(enc_hbm.at[pl.ds(i * piece, piece)], enc_buf.at[i % 2], esem.at[i])

    enc_load(0).start()
    img_load = pltpu.make_async_copy(img_hbm, img_ref, xsem.at[9])
    img_load.start()
    ext_s[...] = jnp.zeros_like(ext_s)
    ext_s[0:4] = ea_ref[...]
    ext_s[4:14] = ba_ref[...]
    ext = jnp.transpose(ext_s[...]).astype(bf16)
    line_greet(cams, nz)

    def pack_own(q):
        pack_part(q, t_ref.at[zi, core], convs_ref, film_ref, skip_ref, down_ref, ext)

    for q in range(cams):
        pl.when(cam == q)(functools.partial(pack_own, q))
    line_wait(cams, nz)

    def tz_copy(k, way):
        ref = t_ref.at[k, core, cam]
        return batch_copy(ref, ref, tzsend.at[way, k], tzrecv.at[k], me - 2 + 4 * way)

    def tc_copy(k, which, q):
        ref = t_ref.at[k, which, q]
        return batch_copy(ref, ref, tcsend.at[k, q], tcrecv.at[k, q], partner)

    def tp_copy(k, step, q):
        ref = t_ref.at[k, core, q]
        return cam_copy(ref, ref, tpsend.at[step - 1, k], tprecv.at[step - 1, k], (cam + step) % cams)

    def t_send(s):
        for k, _, passed, way in moves(s):
            @pl.when(passed)
            def _():
                tz_copy(k, way).start()

    def t_receive(s):
        for k, held, _, way in moves(s):
            @pl.when(held)
            def _():
                tz_copy(k, way).wait_recv()
                for step in range(1, cams):
                    tp_copy(k, step, cam).start()
                tc_copy(k, core, cam).start()

    def t_collect(d):
        for k, held, _, _ in moves(d):
            @pl.when(held & (d > 0))
            def _():
                for step in range(1, cams):
                    q = (cam + cams - step) % cams
                    tp_copy(k, step, q).wait_recv()
                    tc_copy(k, core, q).start()

    def t_complete():
        def body(k, carry):
            for q in range(cams):
                tc_copy(k, 1 - core, q).wait_recv()
            return carry

        lax.fori_loop(0, nz, body, 0)

    ns, nf = traj_ref.shape[0], traj_ref.shape[1]
    frows = ns * nf
    obs = arr_s.shape[1]
    cond = obs * CH + emb_ref.shape[1]
    edge = 2 * ns
    per_pos = frows // n_img
    gones_shape = CH // GROUPS
    ginv = 1.0 / (nf * gones_shape)

    class Part:
        def __init__(self, ref, index, lo, wide):
            self.ref, self.index, self.lo, self.wide = ref, index, lo, wide

        def where(self, key):
            if not isinstance(key, tuple):
                return self.index(slice(self.lo, self.lo + self.wide))
            start, stop, _ = key[1].indices(self.wide)
            return self.index(slice(self.lo + start, self.lo + stop))

        def __getitem__(self, key):
            v = self.ref[self.where(key)]
            return v.reshape(CH, v.shape[-1])

        def __setitem__(self, key, v):
            self.ref[self.where(key)] = v.reshape(nz, 2, rows, v.shape[-1])

    def weight(q, lo, wide):
        return Part(t_ref, lambda cols: (slice(None), slice(None), q, slice(None), cols), lo, wide)

    def grad(buf, lo, wide):
        return Part(dt_buf, lambda cols: (buf, slice(None), slice(None), slice(None), cols), lo, wide)

    wa, wb = weight(0, 0, PART), weight(1, 0, PART)
    f0, f1, wext = weight(2, 0, cond), weight(2, cond, cond), weight(2, 2 * cond, BLK)
    ws, wd = weight(3, 0, CH), weight(3, CH, 3 * CH)

    def dt_save(q, buf):
        return pltpu.make_async_copy(dt_buf.at[buf], dt_out.at[:, :, q], dsem.at[q])

    def blank(buf, lo):
        dt_buf[buf, :, :, :, lo:] = jnp.zeros((nz, 2, rows, PART - lo), bf16)

    def tail(i):
        return taff_ref[4 + i : 5 + i, :]

    def frames(v):
        return v.reshape(nf, ns, CH)

    def keep(i, v):
        z1_ref[per_pos * i : per_pos * (i + 1)] = v.reshape(per_pos, n_img, CH)

    def kept(i):
        return z1_ref[per_pos * i : per_pos * (i + 1)].reshape(nf, ns, CH)

    def fill_edges(pad_ref):
        pad_ref[0:edge, :] = jnp.zeros((edge, CH), bf16)
        pad_ref[edge + frows : edge + frows + edge, :] = jnp.zeros((edge, CH), bf16)

    def fill(pad_ref, v):
        fill_edges(pad_ref)
        pad_ref[edge : edge + frows, :] = v.astype(bf16).reshape(frows, CH)

    def conv5(pad_ref, w):
        return sum(
            dot(pad_ref[t * ns : t * ns + frows, :], w[:, t * CH : (t + 1) * CH], NT) for t in range(5)
        )

    def conv5_back(pad_ref, w):
        return sum(
            dot(pad_ref[(4 - t) * ns : (4 - t) * ns + frows, :], w[:, t * CH : (t + 1) * CH]) for t in range(5)
        )

    def gsum(v):
        return group_sum(v, group_ones(CH, gones_shape)) * ginv

    def norm(v):
        v = frames(v)
        centred = v - gsum(jnp.sum(v, axis=0))[None]
        rstd = lax.rsqrt(gsum(jnp.sum(centred * centred, axis=0)) + norm_eps)
        return centred * rstd[None], rstd

    def norm_back(du, z, rstd, gain):
        s0 = jnp.sum(du, axis=0)
        s1 = jnp.sum(du * z, axis=0)
        dv = (du * gain[None] - gsum(s0 * gain)[None] - z * gsum(s1 * gain)[None]) * rstd[None]
        return dv, jnp.sum(s1, axis=0, keepdims=True), jnp.sum(s0, axis=0, keepdims=True)

    def total(v):
        return jnp.sum(v, axis=(0, 1)).reshape(1, CH)

    def across(v):
        return jnp.transpose(v.reshape(frows, CH)).astype(bf16)

    def temporal_early():
        taff_ref[...] = jnp.transpose(wext[...].astype(f32))
        ag_ref[...] = jnp.zeros_like(ag_ref)
        traj = pad_t[edge : edge + frows, :]
        za, rstd = norm(conv5(pad_t, wa) + tail(4))
        rstd_ref[...] = rstd
        keep(0, za)
        keep(1, dot(traj, ws[...], NT) + tail(8))
        og = og_ref[...]
        dcols = [dot(og, wd[:, t * CH : (t + 1) * CH]).reshape(nf // 2, ns, CH) for t in range(3)]
        before = jnp.concatenate([dcols[0][1:], jnp.zeros((1, ns, CH), f32)], axis=0)
        dsum = jnp.stack([dcols[1], dcols[2] + before], axis=1).reshape(nf, ns, CH)
        keep(2, dsum)
        ag_ref[8:9, :] = total(dsum)
        ag_ref[9:10, :] = jnp.sum(og.astype(f32), axis=0, keepdims=True)
        dskip = dsum.astype(bf16).reshape(frows, CH)
        grad(0, 0, CH)[...] = dot(across(dsum), traj).astype(bf16)
        blank(0, 4 * CH)
        tg_ref[...] = dot(dskip, ws[...])

    def view_copy(to, sender):
        return cam_copy(dviews_ref.at[to], gp_s.at[:, sender], vsend.at[to], vrecv.at[sender], to)

    def temporal_rest():
        mask_s[...] = jnp.zeros_like(mask_s)
        mask_s[0:cams, 0:ns] = mask_in[...].astype(f32)
        mask = jnp.transpose(mask_s[...])[0:ns, 0:cams]
        seen = jnp.sum(mask, axis=1, keepdims=True)
        conds, slopes = [], []
        for o in range(obs):
            pooled = sum(mask[:, c : c + 1] * arr_s[c, o].astype(f32) for c in range(cams))
            value, slope = mish_pair(pooled / seen)
            conds.append(value.astype(bf16))
            slopes.append(slope)
        conds.append(mish_value(emb_ref[...]).astype(bf16))
        lanes = [slice(o * CH, (o + 1) * CH) for o in range(obs)] + [slice(obs * CH, cond)]
        scale, shift = [
            sum(dot(v, w[:, cols], NT) for v, cols in zip(conds, lanes)) + tail(i) for i, w in ((6, f0), (7, f1))
        ]
        za = kept(0)
        fill(pad_m, mish_value(za * tail(0)[None] + tail(1)[None]) * scale[None] + shift[None])
        zb, rstd_b = norm(conv5(pad_m, wb) + tail(5))
        act_b, slope = mish_pair(zb * tail(2)[None] + tail(3)[None])
        keep(3, act_b + kept(1))
        dhb, ag_ref[2:3, :], ag_ref[3:4, :] = norm_back(kept(2) * slope, zb, rstd_b, tail(2))
        ag_ref[5:6, :] = total(dhb)
        fill(pad_h, dhb)
        dmid = frames(conv5_back(pad_h, wb))
        za = kept(0)
        act_a, slope = mish_pair(za * tail(0)[None] + tail(1)[None])
        dscale = jnp.sum(dmid * act_a, axis=0)
        dshift = jnp.sum(dmid, axis=0)
        lows = (dscale.astype(bf16), dshift.astype(bf16))
        for o in range(obs):
            dcond = dot(lows[0], f0[:, lanes[o]]) + dot(lows[1], f1[:, lanes[o]])
            dview = dcond * slopes[o] / seen
            for c in range(cams):
                dviews_ref[c, o] = (mask[:, c : c + 1] * dview).astype(bf16)
        for step in range(1, cams):
            view_copy((cam + step) % cams, cam).start()
        gp_s[:, cam] = dviews_ref[cam]

        dha, ag_ref[0:1, :], ag_ref[1:2, :] = norm_back(dmid * scale[None] * slope, za, rstd_ref[...], tail(0))
        ag_ref[4:5, :] = total(dha)
        ag_ref[6:7, :] = jnp.sum(dscale, axis=0, keepdims=True)
        ag_ref[7:8, :] = jnp.sum(dshift, axis=0, keepdims=True)
        dwb = grad(1, 0, PART)
        hb = across(dhb)
        for t in range(5):
            dwb[:, t * CH : (t + 1) * CH] = dot(hb, pad_m[t * ns : t * ns + frows, :]).astype(bf16)
        dt_save(1, 1).start()
        pairs = kept(3).astype(bf16).reshape(nf // 2, 2, ns, CH)
        half = frows // 2
        sum_ref[0:ns, :] = jnp.zeros((ns, CH), bf16)
        sum_ref[ns : ns + half, :] = pairs[:, 1].reshape(half, CH)
        sum_ref[ns + half : ns + 2 * half, :] = pairs[:, 0].reshape(half, CH)
        og = jnp.transpose(og_ref[...].astype(f32)).astype(bf16)
        dwd = grad(0, CH, 3 * CH)
        out = None
        for t, at in enumerate((0, ns + half, ns)):
            cols = sum_ref[at : at + half, :]
            part = dot(cols, wd[:, t * CH : (t + 1) * CH], NT)
            out = part if out is None else out + part
            dwd[:, t * CH : (t + 1) * CH] = dot(og, cols).astype(bf16)
        dt_save(3, 0).start()
        out_ref[...] = (out + tail(9)).astype(bf16)
        dt_save(1, 1).wait()
        for base, low in zip((0, cond), lows):
            dw = grad(1, base, cond)
            for v, cols in zip(conds, lanes):
                dw[:, cols] = dot(low, v, TN).astype(bf16)
        grad(1, 2 * cond, BLK)[...] = jnp.transpose(ag_ref[...]).astype(bf16)
        blank(1, 2 * cond + BLK)
        dt_save(2, 1).start()
        dt_save(3, 0).wait()
        dwa = grad(0, 0, PART)
        ha = across(dha)
        for t in range(5):
            dwa[:, t * CH : (t + 1) * CH] = dot(ha, pad_t[t * ns : t * ns + frows, :]).astype(bf16)
        dt_save(0, 0).start()
        fill(pad_h, dha)
        tg_ref[...] = tg_ref[...] + conv5_back(pad_h, wa)
        for step in range(1, cams):
            other = (cam + step) % cams
            view_copy(other, other).wait_recv()
        gp_ref[...] = gp_s[...]
        dt_save(2, 1).wait()
        dt_save(0, 0).wait()

    def z_copy(conv, k, way):
        ref = w_ref.at[conv, 2 * k + core]
        return batch_copy(ref, ref, zsend.at[conv, way, k], zrecv.at[conv, k], me - 2 + 4 * way)

    def core_copy(conv, k, which):
        ref = w_ref.at[conv, 2 * k + which]
        return batch_copy(ref, ref, csend.at[conv, k], crecv.at[conv, k], partner)

    def moves(s):
        low, high = zi - s, zi + s
        return (
            (high, high < nz, (high < nz) & (zi > 0), 0),
            (low, low >= 0, (low >= 0) & (zi < nz - 1), 1),
        )

    def send(conv, s):
        for k, _, passed, way in moves(s):
            @pl.when(passed)
            def _():
                z_copy(conv, k, way).start()

    def receive(conv, s):
        for k, held, _, way in moves(s):
            @pl.when(held)
            def _():
                z_copy(conv, k, way).wait_recv()
                core_copy(conv, k, core).start()

    t_send(0)
    for q in range(cams):
        pl.when(cam != q)(functools.partial(pack_own, q))
    for q in range(cams):
        tc_copy(zi, core, q).start()
    for conv in range(2):
        w_ref[conv, me, :, 9 * CH :] = ext
    count = rows // piece

    def pack(i, carry):
        @pl.when(i + 1 < count)
        def _():
            enc_load(i + 1).start()

        enc_load(i).wait()
        for conv in range(2):
            w_ref[conv, me, pl.ds(pl.multiple_of(i * piece, piece), piece), 0 : 9 * CH] = (
                enc_buf[i % 2, :, conv, :].astype(bf16)
            )
        return carry

    lax.fori_loop(0, count, pack, 0)

    for conv in range(2):
        core_copy(conv, zi, core).start()

    def t_step(s, carry):
        @pl.when(s == nz - 1)
        def _():
            send(0, 0)

        t_receive(s)

        @pl.when(s < nz - 1)
        def _():
            t_send(s)
        return carry

    lax.fori_loop(1, nz, t_step, 0)

    def x_save(p):
        return pltpu.make_async_copy(x_ref.at[:, p * CH : (p + 1) * CH], x_out.at[p], xsem.at[p])

    fill_edges(pad_t)
    moved = traj_ref[...].astype(f32)
    for f in range(nf):
        pad_t[edge + f * ns : edge + (f + 1) * ns, :] = moved[:, f].astype(bf16)
    moved = og_in[...].astype(f32)
    for f in range(nf // 2):
        og_ref[f * ns : (f + 1) * ns, :] = moved[:, f].astype(bf16)
    half = n_img // 2
    img_load.wait()
    for p in range(9):
        pair = img_ref[:, p].astype(f32)
        for o in range(2):
            x_ref[o * half : (o + 1) * half, p * CH : (p + 1) * CH] = pair[:, o].astype(bf16)
        x_save(p).start()

    def rows_of(conv, j, start, wide):
        block = w_ref[conv, pl.ds(j * spb, spb), :, start : start + wide]
        return block.reshape(BLK, wide)

    def w_save(conv, j):
        part = pl.ds(j * spb, spb)
        return pltpu.make_async_copy(w_ref.at[conv, part], w_out.at[conv, part], wsem.at[conv, j])

    def conv_norm(src_ref, conv, z_ref, r_ref, j):
        lanes = pl.ds(pl.multiple_of(j * BLK, BLK), BLK)
        total = None
        for p in range(9):
            r, c = divmod(p, 3)
            bs = span(c)
            acc = None
            for a in span(r):
                start = (3 * (r + a - 1) + c + bs[0] - 1) * CH
                wide = len(bs) * CH
                part = dot(src_ref[:, start : start + wide], rows_of(conv, j, (3 * a + bs[0]) * CH, wide), NT)
                acc = part if acc is None else acc + part
            z_ref[p, :, lanes] = acc
            total = acc if total is None else total + acc
        mean = group_sum(total, ones) * inv_n
        var = None
        for p in range(9):
            centred = z_ref[p, :, lanes] - mean
            sq = centred * centred
            var = sq if var is None else var + sq
        rstd = lax.rsqrt(group_sum(var, ones) * inv_n + norm_eps)
        r_ref[:, lanes] = rstd
        return lanes, mean, rstd

    def first(j):
        aff_ref[:, lanes_of(j)] = jnp.transpose(rows_of(0, j, 9 * CH, BLK).astype(f32))[0:8]
        lanes, mean, rstd = conv_norm(x_ref, 0, z1_ref, r1_ref, j)
        gain, offset = aff_ref[0:1, lanes], aff_ref[1:2, lanes]
        for p in range(9):
            z = (z1_ref[p, :, lanes] - mean) * rstd
            z1_ref[p, :, lanes] = z
            u = z * gain + offset
            a_ref[:, pl.ds(pl.multiple_of(p * CH + j * BLK, BLK), BLK)] = (u * sigmoid(u)).astype(bf16)

    def second(j):
        lanes, mean, rstd = conv_norm(a_ref, 1, z2_ref, r2_ref, j)
        gain, offset = aff_ref[2:3, lanes], aff_ref[3:4, lanes]
        total = None
        for p in range(9):
            z = (z2_ref[p, :, lanes] - mean) * rstd
            z2_ref[p, :, lanes] = z
            cols = pl.ds(pl.multiple_of(p * CH + j * BLK, BLK), BLK)
            u = z * gain + offset + x_ref[:, cols].astype(f32)
            s = sigmoid(u)
            act = u * s
            x_ref[:, cols] = (s + act * (1.0 - s)).astype(bf16)
            total = act if total is None else total + act
        out = (total * (1.0 / 9.0)).astype(bf16)
        feat_ref[:, :, :, lanes] = out.reshape(feat_ref.shape[:3] + (BLK,))

    def lanes_of(j):
        return pl.ds(pl.multiple_of(j * BLK, BLK), BLK)

    def arrived(conv, k):
        core_copy(conv, k, 1 - core).wait_recv()

    def phase(conv, block):
        streaming = spb == 2

        def step(s, carry):
            if conv == 0:
                @pl.when((s > 0) & (s < nz - 1))
                def _():
                    send(0, s)

                @pl.when(s == nz - 1)
                def _():
                    send(1, 0)
            else:
                @pl.when((s > 0) & (s < nz - 1))
                def _():
                    send(1, s)

            def side(d, carry):
                k = zi + s - 2 * s * d

                @pl.when((k >= 0) & (k < nz) & (s + 1 > d))
                def _():
                    arrived(conv, k)
                    if streaming:
                        w_save(conv, k).start()
                        block(k)
                return carry

            lax.fori_loop(0, 2, side, 0)
            if conv == 1:
                t_collect(2 * s)
                t_collect(2 * s + 1)

                @pl.when(s == nz - 2)
                def _():
                    t_complete()
                    saves[0].wait()
                    temporal_early()

            @pl.when(s < nz - 1)
            def _():
                receive(conv, s + 1)
            return carry

        lax.fori_loop(0, nz, step, 0)
        if not streaming:
            def rest(j, carry):
                w_save(conv, j).start()
                block(j)
                return carry

            lax.fori_loop(0, CH // BLK, rest, 0)

    phase(0, first)
    saves = [pltpu.make_async_copy(z1_ref, z1_out, osem.at[0])]
    saves += [
        pltpu.make_async_copy(a_ref.at[:, p * CH : (p + 1) * CH], a_out.at[p], osem.at[2 + p])
        for p in range(9)
    ]
    for save in saves:
        save.start()
    for p in range(9):
        x_save(p).wait()
    phase(1, second)
    last = pltpu.make_async_copy(z2_ref, z2_out, osem.at[1])
    last.start()

    def slope_save(p):
        return pltpu.make_async_copy(x_ref.at[:, p * CH : (p + 1) * CH], slope_out.at[p], xsem.at[p])

    for p in range(9):
        slope_save(p).start()

    def feat_copy(to, sender):
        return cam_copy(feat_ref.at[:, to], arr_s.at[sender], fsend.at[to], frecv.at[sender], to)

    for step in range(1, cams):
        feat_copy((cam + step) % cams, cam).start()
    arr_s[cam] = feat_ref[:, cam]
    for step in range(1, cams):
        other = (cam + step) % cams
        feat_copy(other, other).wait_recv()
    temporal_rest()
    for step in range(1, cams):
        feat_copy((cam + step) % cams, cam).wait_send()

    for conv in range(2):
        def drain(k, carry):
            s = k - zi

            @pl.when((s >= 0) & (s < nz - 1) & (zi > 0))
            def _():
                z_copy(conv, k, 0).wait_send()

            @pl.when((s <= 0) & (s > 1 - nz) & (zi < nz - 1))
            def _():
                z_copy(conv, k, 1).wait_send()

            core_copy(conv, k, core).wait_send()
            return carry

        lax.fori_loop(0, nz, drain, 0)

        def saved(j, carry):
            w_save(conv, j).wait()
            return carry

        lax.fori_loop(0, CH // BLK, saved, 0)
    for save in saves[1:]:
        save.wait()
    last.wait()

    def t_drain(k, carry):
        s = k - zi

        @pl.when((s >= 0) & (s < nz - 1) & (zi > 0))
        def _():
            tz_copy(k, 0).wait_send()

        @pl.when((s <= 0) & (s > 1 - nz) & (zi < nz - 1))
        def _():
            tz_copy(k, 1).wait_send()

        @pl.when(s != 0)
        def _():
            for step in range(1, cams):
                tp_copy(k, step, cam).wait_send()

        for q in range(cams):
            tc_copy(k, core, q).wait_send()
        return carry

    lax.fori_loop(0, nz, t_drain, 0)
    for p in range(9):
        slope_save(p).wait()
    for step in range(1, cams):
        view_copy((cam + step) % cams, cam).wait_send()


def enc_bwd_kernel(
    n, cams, cond, x_hbm, slope_hbm, a_hbm, w_hbm, z1_hbm, r1_ref, z2_hbm, r2_ref, aff_ref, gp_ref, dt_hbm,
    ig_out, genc_ref, gaff_ref, gconvs_ref, gfilm_ref, gskip_ref, gdown_ref, gblk_ref,
    ig_ref, x_ref, a_ref, w_ref, z1_ref, z2_ref, g_ref, gt_ref, ag_ref,
    dwf, core_out, core_in, slots, t_own, t_sum, t_peer, t_slots, t_all,
    lsem, bsem, isem, csend, crecv, zsend, zrecv,
    tlsem, tcsend, tcrecv, tpsend, tprecv, tzsend, tzrecv, tfsend, tfrecv,
):
    nz = n // 2
    rows = CH // n
    n_img = z1_ref.shape[1]
    me, cam = lax.axis_index("batch"), lax.axis_index("cam")
    zi, core = me // 2, me % 2
    partner = me + 1 - 2 * core
    ones = group_ones(BLK, ENC_GROUP)
    inv_n = 1.0 / (9 * ENC_GROUP)
    chunk = 3 * CH

    def load_w(conv):
        return pltpu.make_async_copy(w_hbm.at[conv, :, :, 0 : 9 * CH], w_ref, lsem.at[3])

    def lanes_of(j):
        return pl.ds(pl.multiple_of(j * BLK, BLK), BLK)

    def block_loads(j):
        cols = lanes_of(j)
        return (
            pltpu.make_async_copy(z2_hbm.at[:, :, cols], z2_ref.at[:, :, cols], bsem.at[0, j]),
            pltpu.make_async_copy(slope_hbm.at[:, :, cols], g_ref.at[:, :, cols], bsem.at[1, j]),
        )

    loads = {
        "z1": pltpu.make_async_copy(z1_hbm, z1_ref, lsem.at[1]),
        "a": pltpu.make_async_copy(a_hbm, a_ref, lsem.at[2]),
        "x": pltpu.make_async_copy(x_hbm, x_ref, lsem.at[0]),
    }
    for j in range(CH // BLK):
        for load in block_loads(j):
            load.start()

    def own_load(i):
        return pltpu.make_async_copy(dt_hbm.at[i // cams, core, i % cams], t_own.at[i % 2], tlsem.at[i])

    own_load(0).start()

    line_greet(cams, nz)

    def t_core(k):
        return batch_copy(dt_hbm.at[k, 1 - core], t_sum.at[k], tcsend.at[k], tcrecv.at[k], partner)

    def t_peers(k, step):
        to = (cam + step) % cams
        return cam_copy(t_sum.at[k, to], t_peer.at[step - 1, k], tpsend.at[step - 1, k], tprecv.at[step - 1, k], to)

    def t_start(k, carry):
        t_core(k).start()
        return carry

    def t_spread(lo, hi):
        def body(k, carry):
            t_core(k).wait_recv()

            def quarter(q, carry):
                i = k * cams + q

                @pl.when(i + 1 < nz * cams)
                def _():
                    own_load(i + 1).start()

                own_load(i).wait()
                t_sum[k, q] = (t_sum[k, q].astype(f32) + t_own[i % 2].astype(f32)).astype(bf16)
                return carry

            lax.fori_loop(0, cams, quarter, 0)
            for step in range(1, cams):
                t_peers(k, step).start()
            return carry

        lax.fori_loop(lo, hi, body, 0)

    ag_ref[...] = jnp.zeros_like(ag_ref)

    def norm_back(du_ref, z_ref, r_ref, j, gain, row):
        lanes = lanes_of(j)
        s0 = jnp.zeros((n_img, BLK), f32)
        s1 = jnp.zeros((n_img, BLK), f32)
        for p in range(9):
            du = du_ref[p, :, lanes]
            s0 = s0 + du
            s1 = s1 + du * z_ref[p, :, lanes]
        ag_ref[row : row + 1, lanes] = jnp.sum(s1, axis=0, keepdims=True)
        ag_ref[row + 1 : row + 2, lanes] = jnp.sum(s0, axis=0, keepdims=True)
        m0 = group_sum(s0 * gain, ones) * inv_n
        m1 = group_sum(s1 * gain, ones) * inv_n
        rstd = r_ref[:, lanes]
        for p in range(9):
            dv = (du_ref[p, :, lanes] * gain - m0 - z_ref[p, :, lanes] * m1) * rstd
            g_ref[p, :, lanes] = dv.astype(bf16)
            gt_ref[lanes, p * n_img : (p + 1) * n_img] = jnp.transpose(dv).astype(bf16)

    def second(j, carry):
        lanes = lanes_of(j)
        for load in block_loads(j):
            load.wait()
        pooled = gp_ref[:, :, :, lanes].reshape(n_img, BLK).astype(f32) * (1.0 / 9.0)
        for p in range(9):
            ig_ref[p, :, lanes] = pooled * g_ref[p, :, lanes].astype(f32)
        norm_back(ig_ref, z2_ref, r2_ref, j, aff_ref[2:3, lanes], 2)
        return carry

    def first(j, carry):
        lanes = lanes_of(j)
        gain, offset = aff_ref[0:1, lanes], aff_ref[1:2, lanes]
        for p in range(9):
            u = z1_ref[p, :, lanes] * gain + offset
            s = sigmoid(u)
            z2_ref[p, :, lanes] = z2_ref[p, :, lanes] * (s * (1.0 + u * (1.0 - s)))
        norm_back(z2_ref, z1_ref, r1_ref, j, gain, 0)
        return carry

    def width(k):
        return chunk + BLK if k == 5 else chunk

    def core_copy(k):
        cols = pl.ds(0, width(k))
        return batch_copy(
            core_out.at[k % 2, :, :, cols], core_in.at[k % 3, :, :, cols], csend.at[k], crecv.at[k], partner
        )

    def keep(k, d0, lane, v):
        count, wide = v.shape[0] // (2 * rows), v.shape[1]
        parts = v.reshape(count, 2, rows, wide)
        even, odd = parts[:, 0], parts[:, 1]
        dwf[k % 2, d0 : d0 + count, :, lane : lane + wide] = jnp.where(core == 0, even, odd)
        core_out[k % 2, d0 : d0 + count, :, lane : lane + wide] = jnp.where(core == 0, odd, even).astype(bf16)

    def make_chunk(k):
        if k >= 2:
            core_copy(k - 2).wait_send()
        src_ref = a_ref if k < 3 else x_ref
        a = k % 3
        r_lo, r_hi = max(0, 1 - a), min(2, 3 - a)
        for b in range(3):
            c_lo, c_hi = max(0, 1 - b), min(2, 3 - b)
            if b == 1:
                runs = [(3 * r_lo, 3 * (r_hi - r_lo + 1))]
            else:
                runs = [(3 * r + c_lo, c_hi - c_lo + 1) for r in range(r_lo, r_hi + 1)]
            shift = 3 * (a - 1) + b - 1
            for half in range(2):
                acc = None
                for p, m in runs:
                    part = dot(
                        gt_ref[half * 256 : half * 256 + 256, p * n_img : (p + m) * n_img],
                        src_ref[p + shift : p + shift + m].reshape(m * n_img, CH),
                    )
                    acc = part if acc is None else acc + part
                keep(k, half * nz // 2, b * CH, acc)
        if k == 5:
            keep(k, 0, chunk, jnp.transpose(ag_ref[...]))
        core_copy(k).start()

    def term(k, d):
        return dwf[k % 2, d, :, 0 : width(k)] + core_in[k % 3, d, :, 0 : width(k)].astype(f32)

    def line_copy(k, way, s):
        if k == 6:
            return batch_copy(
                t_slots.at[way, s - 1], t_slots.at[way, s], tzsend.at[way, s], tzrecv.at[way, s], me - 2 + 4 * way
            )
        cols = pl.ds(0, width(k))
        return batch_copy(
            slots.at[k % 3, way, s - 1, :, cols], slots.at[k % 3, way, s, :, cols],
            zsend.at[k, way, s], zrecv.at[k, way, s], me - 2 + 4 * way,
        )

    def slot(k, way, s):
        return t_slots.at[way, s] if k == 6 else slots.at[k % 3, way, s, :, pl.ds(0, width(k))]

    def t_term(d):
        total = t_sum[d, cam].astype(f32)
        for step in range(1, cams):
            total = total + t_peer[step - 1, d].astype(f32)
        return total

    def serve(k, s):
        for way in range(2):
            ahead = zi if way else nz - 1 - zi
            d = nz - s + zi if way else s - nz + zi
            ref = slot(k, way, s - 1)

            @pl.when((ahead < nz - 1) & (s > ahead))
            def _():
                own = t_term(d) if k == 6 else term(k, d)

                @pl.when(ahead > 0)
                def _():
                    line_copy(k, way, s - 1).wait_recv()
                    ref[...] = (ref[...].astype(f32) + own).astype(bf16)

                @pl.when(ahead == 0)
                def _():
                    ref[...] = own.astype(bf16)

                line_copy(k, way, s).start()

    def steps(k, part):
        lo, hi = 1 + part * (nz - 1) // 3, 1 + (part + 1) * (nz - 1) // 3
        if hi - lo == 1:
            serve(k, lo)
        elif hi > lo:
            def body(s, carry):
                serve(k, s)
                return carry

            lax.fori_loop(lo, hi, body, 0)

    def service(g):
        k, part = divmod(g, 3)
        if part == 0:
            core_copy(k).wait_recv()
        steps(k, part)

    def collect(k, total, write):
        last = nz - 1

        @pl.when(zi > 0)
        def _():
            line_copy(k, 1, last).wait_recv()

        @pl.when(zi < nz - 1)
        def _():
            line_copy(k, 0, last).wait_recv()

        @pl.when(zi == 0)
        def _():
            write(total + slot(k, 0, last)[...].astype(f32))

        @pl.when(zi == nz - 1)
        def _():
            write(total + slot(k, 1, last)[...].astype(f32))

        @pl.when((zi > 0) & (zi < nz - 1))
        def _():
            write(total + slot(k, 0, last)[...].astype(f32) + slot(k, 1, last)[...].astype(f32))

        def drain(s, carry):
            for way in range(2):
                ahead = zi if way else nz - 1 - zi

                @pl.when((ahead < nz - 1) & (s > ahead))
                def _():
                    line_copy(k, way, s).wait_send()
            return carry

        lax.fori_loop(1, nz, drain, 0)

    def finish(k):
        def write(v):
            genc_ref[:, 1 - k // 3, (k % 3) * chunk : (k % 3 + 1) * chunk] = v[:, 0:chunk]
            if k == 5:
                gaff_ref[...] = jnp.transpose(v[:, chunk:])[0 : gaff_ref.shape[0]]

        collect(k, term(k, zi), write)

    def t_arrived():
        for step in range(1, cams):
            def body(k, carry):
                t_peers(k, step).wait_recv()
                return carry

            lax.fori_loop(0, nz, body, 0)

    def t_final(to, sender):
        return cam_copy(t_all.at[cam], t_all.at[sender], tfsend.at[to], tfrecv.at[sender], to)

    def t_finish():
        def write(v):
            t_all[cam] = v.astype(bf16)

        collect(6, t_term(zi), write)
        for step in range(1, cams):
            t_final((cam + step) % cams, cam).start()

    def t_write():
        for step in range(1, cams):
            other = (cam + step) % cams
            t_final(other, other).wait_recv()

        def cut(q, lo, wide):
            return t_all[q, :, lo : lo + wide].astype(f32)

        for which in range(2):
            gconvs_ref[:, which, :] = cut(which, 0, PART)
            gfilm_ref[:, which, :] = cut(2, which * cond, cond)
        gblk_ref[...] = jnp.transpose(cut(2, 2 * cond, BLK))[0 : gblk_ref.shape[0]]
        gskip_ref[...] = cut(3, 0, CH)
        gdown_ref[...] = cut(3, CH, 3 * CH)

    def input_back(q):
        r, c = divmod(q, 3)
        acc = None
        for a in range(3):
            for b in range(3):
                pr, pc = r - a + 1, c - b + 1
                if 0 <= pr < 3 and 0 <= pc < 3:
                    t = 3 * a + b
                    w = w_ref[:, :, t * CH : (t + 1) * CH].reshape(CH, CH)
                    part = dot(g_ref[3 * pr + pc], w)
                    acc = part if acc is None else acc + part
        return acc

    def back_second(*qs):
        for q in qs:
            if q == 0:
                load_w(1).wait()
            z2_ref[q] = input_back(q)
            if q == 8:
                load_w(0).start()

    def ig_save(q):
        return pltpu.make_async_copy(a_ref.at[q], ig_out.at[q], isem.at[q])

    def back_first(*qs):
        for q in qs:
            if q == 0:
                load_w(0).wait()
            a_ref[q] = (ig_ref[q] + input_back(q)).astype(bf16)
            ig_save(q).start()

    def quarter_of(i):
        return i * nz // 4, (i + 1) * nz // 4

    def t_go(i):
        lax.fori_loop(*quarter_of(i), t_start, 0)

    lax.fori_loop(0, 1, second, 0)
    loads["a"].start()
    line_wait(cams, nz)
    lax.fori_loop(1, CH // BLK, second, 0)
    load_w(1).start()
    loads["a"].wait()
    make_chunk(0)
    back_second(0)
    service(0)
    t_go(0)
    make_chunk(1)
    service(1)
    t_go(1)
    t_spread(*quarter_of(0))
    loads["z1"].start()
    loads["x"].start()
    back_second(1, 2)
    service(2)
    t_go(2)
    t_spread(*quarter_of(1))
    back_second(3, 4)
    service(3)
    finish(0)
    t_go(3)
    t_spread(*quarter_of(2))
    make_chunk(2)
    service(4)
    t_spread(*quarter_of(3))
    back_second(5, 6)
    service(5)
    back_second(7, 8)
    service(6)
    finish(1)
    loads["z1"].wait()
    loads["x"].wait()
    lax.fori_loop(0, 2, first, 0)
    service(7)
    lax.fori_loop(2, 4, first, 0)
    service(8)
    make_chunk(3)
    service(9)
    finish(2)
    make_chunk(4)
    service(10)
    back_first(0, 1)
    service(11)
    back_first(2, 3)
    service(12)
    finish(3)
    make_chunk(5)
    service(13)
    back_first(4, 5)
    service(14)
    t_arrived()
    steps(6, 0)
    finish(4)
    back_first(6)
    steps(6, 1)
    back_first(7)
    steps(6, 2)
    back_first(8)
    service(15)
    t_finish()
    service(16)
    service(17)
    t_write()
    finish(5)

    for q in range(9):
        ig_save(q).wait()

    def t_drain(k, carry):
        t_core(k).wait_send()
        for step in range(1, cams):
            t_peers(k, step).wait_send()
        return carry

    lax.fori_loop(0, nz, t_drain, 0)
    for step in range(1, cams):
        t_final((cam + step) % cams, cam).wait_send()
    core_copy(4).wait_send()
    core_copy(5).wait_send()


def call(kernel, outs, in_specs, out_specs, scratch=(), collective_id=None, cost=None):
    extra = {} if collective_id is None else dict(collective_id=collective_id, has_side_effects=True)
    return pl.pallas_call(
        kernel,
        out_shape=[jax.ShapeDtypeStruct(s, d) for s, d in outs],
        in_specs=in_specs,
        out_specs=out_specs,
        scratch_shapes=list(scratch),
        compiler_params=pltpu.CompilerParams(vmem_limit_bytes=VMEM_BYTES, **extra),
        cost_estimate=cost,
    )


def work(microseconds):
    return pl.CostEstimate(
        flops=int(microseconds * 1e9), bytes_accessed=int(microseconds * 3e6), transcendentals=0
    )


V = pl.BlockSpec(memory_space=pltpu.VMEM)
H = pl.BlockSpec(memory_space=pl.ANY)
DMA = pltpu.SemaphoreType.DMA


def time_embed(steps_given, embed_width):
    half_width = embed_width // 2
    frequency = jnp.exp(
        jnp.arange(half_width, dtype=jnp.float32) * (-math.log(10000.0) / (half_width - 1))
    )
    argument = steps_given.astype(jnp.float32)[:, None] * frequency[None, :]
    return jnp.concatenate([jnp.sin(argument), jnp.cos(argument)], axis=1)


def adamw(weight, gradient, moment_one, moment_two, step_rate, weight_decay):
    mean_new = beta_first * moment_one + (1.0 - beta_first) * gradient
    square_new = beta_second * moment_two + (1.0 - beta_second) * gradient * gradient
    square_hat = square_new * (1.0 / (1.0 - beta_second**STEP))
    root = square_hat * lax.rsqrt(square_hat)
    weight_new = (1.0 - step_rate * weight_decay) * weight - (step_rate / (1.0 - beta_first**STEP)) * (
        mean_new / (root + adam_eps)
    )
    return (weight_new, mean_new, square_new)


def last_kernel(*refs):
    tg_ref, out_ref, ig_ref = refs[28:31]
    tg_new, out_new, ig_new, turn_ref = refs[52:56]
    for p in range(ig_ref.shape[0]):
        for o in range(ig_ref.shape[1]):
            ig_new[:, p, o, :] = ig_ref[p, o].astype(f32)

    @pl.when(pl.program_id(0) == 0)
    def _():
        for f in range(tg_ref.shape[0]):
            tg_new[:, f, :] = tg_ref[f]
        for u in range(out_ref.shape[0]):
            turn_ref[:, u, :] = out_ref[u].astype(f32)
        out_new[...] = turn_ref[...].astype(bf16)

    for i in range(7):
        w_ref, m_ref, v_ref, g_ref = refs[4 * i : 4 * i + 4]
        outs = refs[31 + 3 * i : 34 + 3 * i]

        def update():
            vector = i in (1, 6)
            rate, decay = (rate_vector, 0.0) if vector else (rate_matrix, decay_matrix)
            new = adamw(w_ref[...], g_ref[...], m_ref[...], v_ref[...], rate, decay)
            for ref, value in zip(outs, new):
                ref[...] = value

        if i in (1, 6):
            pl.when(pl.program_id(0) == 0)(update)
        else:
            update()


def last_call(shown, grads, tg, out, ig, rows):
    step = min(rows, 8)
    steps = rows // step

    def whole(shape):
        return pl.BlockSpec(shape, lambda r: (0,) * len(shape))

    def spec(v):
        if v.shape[0] != rows:
            return whole(v.shape)
        return pl.BlockSpec((step,) + v.shape[1:], lambda r: (r,) + (0,) * (v.ndim - 1))

    ins = []
    for i in range(7):
        ins += [shown[0][i], shown[1][i], shown[2][i], grads[i]]
    outs = [w for w in shown[0] for _ in range(3)]
    pos, obs, count, ch = ig.shape
    part = count // steps
    turned = [(v.shape[1], v.shape[0], v.shape[2]) for v in (tg, out)]
    return pl.pallas_call(
        last_kernel,
        grid=(steps,),
        out_shape=[jax.ShapeDtypeStruct(v.shape, f32) for v in outs]
        + [jax.ShapeDtypeStruct(turned[0], f32), jax.ShapeDtypeStruct(turned[1], bf16),
           jax.ShapeDtypeStruct((count, pos, obs, ch), f32)],
        in_specs=[spec(v) for v in ins]
        + [whole(tg.shape), whole(out.shape), pl.BlockSpec((pos, obs, part, ch), lambda r: (0, 0, r, 0))],
        out_specs=[spec(v) for v in outs]
        + [whole(turned[0]), whole(turned[1]), pl.BlockSpec((part, pos, obs, ch), lambda r: (r, 0, 0, 0))],
        scratch_shapes=[pltpu.VMEM(turned[1], f32)],
        compiler_params=pltpu.CompilerParams(vmem_limit_bytes=VMEM_BYTES),
        cost_estimate=work(15),
    )(*ins, tg, out, ig)


def shards(
    n, images, trajectory, view_mask, timesteps, out_grad,
    encoder_weight, encoder_affine, block_convs, film_weight, skip_weight, down_weight, block_affine,
    first_encoder, first_affine, first_convs, first_film, first_skip, first_down, first_block,
    second_encoder, second_affine, second_convs, second_film, second_skip, second_down, second_block,
):
    ns, nf, ch = trajectory.shape
    cams, obs = images.shape[1], images.shape[3]
    n_img = cams * images.shape[2] * obs
    nz, per = n // 2, ch // n
    cond = film_weight.shape[2]
    wide = 9 * ch
    rows = nf * ns

    def turned(v):
        return jnp.transpose(v.reshape(v.shape[-2:]))

    pairs = jnp.transpose(images[0], (0, 1, 3, 2, 4)).reshape(n_img // obs, 9, obs, ch)
    pos = (9, n_img, ch)
    t_shape = (nz, 2, cams, per, PART)
    wcols = wide + BLK
    z1, r1, act, z2, r2, w_all, enc_aff, x, slope, out_fm, tg_fm, gp, dt = call(
        functools.partial(forward_kernel, n, cams),
        [(pos, f32), ((n_img, ch), f32), (pos, bf16), (pos, f32), ((n_img, ch), f32), ((2, n, per, wcols), bf16),
         ((8, ch), f32), (pos, bf16), (pos, bf16), ((rows // 2, ch), bf16), ((rows, ch), f32), ((obs, cams, ns, ch), bf16),
         (t_shape, bf16)],
        [H, V, V, V, V, H, V, V, V, V, V, V],
        [H, V, H, H, V, H, V, H, H, V, V, V, H],
        [pltpu.VMEM((n_img // obs, 9, obs, ch), bf16), pltpu.VMEM((n_img, wide), bf16), pltpu.VMEM((2, n, per, wcols), bf16), pltpu.VMEM(pos, f32),
         pltpu.VMEM((n_img, wide), bf16), pltpu.VMEM(pos, f32), pltpu.VMEM((obs, cams, ns, ch), bf16),
         pltpu.VMEM((cams, obs, ns, ch), bf16), pltpu.VMEM(t_shape, bf16), pltpu.VMEM((2, min(per, 16), 2, wide), f32),
         pltpu.VMEM((BLK, BLK), f32), pltpu.VMEM((BLK, per), f32), pltpu.VMEM((rows // 2, ch), bf16), pltpu.VMEM((rows + 4 * ns, ch), bf16),
         pltpu.VMEM((rows + 4 * ns, ch), bf16), pltpu.VMEM((rows + 4 * ns, ch), bf16), pltpu.VMEM((rows + ns, ch), bf16),
         pltpu.VMEM((BLK, ch), f32), pltpu.VMEM((BLK, ch), f32), pltpu.VMEM((ns, ch), f32),
         pltpu.VMEM((cams, obs, ns, ch), bf16), pltpu.VMEM((obs, cams, ns, ch), bf16),
         pltpu.VMEM((2, nz, 2, per, PART), bf16),
         DMA((2, 2, nz)), DMA((2, nz)), DMA((2, nz)), DMA((2, nz)), DMA((2, ch // BLK)), DMA((11,)),
         DMA((cams,)), DMA((cams,)),
         DMA((2, nz)), DMA((nz,)), DMA((nz, cams)), DMA((nz, cams)), DMA((cams - 1, nz)), DMA((cams - 1, nz)),
         DMA((max(per // 16, 1),)), DMA((10,)), DMA((cams,)), DMA((cams,)), DMA((4,))],
        collective_id=0,
        cost=work(130),
    )(pairs, trajectory, out_grad, jnp.transpose(view_mask), time_embed(timesteps, TEMB), encoder_weight[0], block_convs,
      film_weight, skip_weight, down_weight, turned(encoder_affine), turned(block_affine))
    chunk = 3 * ch + BLK
    ig, genc, gaff, gconvs, gfilm, gskip, gdown, gblk = call(
        functools.partial(enc_bwd_kernel, n, cams, cond),
        [(pos, bf16), ((per, 2, wide), f32), ((4, per), f32), ((per, 2, 5 * ch), f32),
         ((per, 2, cond), f32), ((per, ch), f32), ((per, 3 * ch), f32), ((10, per), f32)],
        [H, H, H, H, H, V, H, V, V, V, H],
        [H] + [V] * 7,
        [pltpu.VMEM(pos, f32), pltpu.VMEM(pos, bf16), pltpu.VMEM(pos, bf16), pltpu.VMEM((n, per, wide), bf16), pltpu.VMEM(pos, f32),
         pltpu.VMEM(pos, f32), pltpu.VMEM(pos, bf16), pltpu.VMEM((ch, 9 * n_img), bf16),
         pltpu.VMEM((BLK, ch), f32),
         pltpu.VMEM((2, nz, per, chunk), f32), pltpu.VMEM((2, nz, per, chunk), bf16),
         pltpu.VMEM((3, nz, per, chunk), bf16), pltpu.VMEM((3, 2, nz, per, chunk), bf16),
         pltpu.VMEM((2, per, PART), bf16), pltpu.VMEM((nz, cams, per, PART), bf16),
         pltpu.VMEM((cams - 1, nz, per, PART), bf16), pltpu.VMEM((2, nz, per, PART), bf16),
         pltpu.VMEM((cams, per, PART), bf16),
         DMA((4,)), DMA((2, ch // BLK)), DMA((9,)), DMA((6,)), DMA((6,)), DMA((6, 2, nz)), DMA((6, 2, nz)),
         DMA((nz * cams,)), DMA((nz,)), DMA((nz,)), DMA((cams - 1, nz)), DMA((cams - 1, nz)),
         DMA((2, nz)), DMA((2, nz)), DMA((cams,)), DMA((cams,))],
        collective_id=1,
        cost=work(100),
    )(x, slope, act, w_all, z1, r1, z2, r2, enc_aff, gp, dt)
    weights = (encoder_weight, encoder_affine, block_convs, film_weight, skip_weight, down_weight, block_affine)
    firsts = (first_encoder, first_affine, first_convs, first_film, first_skip, first_down, first_block)
    seconds = (second_encoder, second_affine, second_convs, second_film, second_skip, second_down, second_block)
    shown = [
        [turned(v) if i in (1, 6) else v.reshape(v.shape[-3:]) if i == 0 else v for i, v in enumerate(group)]
        for group in (weights, firsts, seconds)
    ]
    *news, trajectory_grad, block_output, ig_new = last_call(
        shown, (genc, gaff, gconvs, gfilm, gskip, gdown, gblk),
        tg_fm.reshape(nf, ns, ch), out_fm.reshape(nf // 2, ns, ch), ig.reshape(9, obs, n_img // obs, ch), per,
    )
    images_grad = jnp.transpose(ig_new.reshape(images.shape[1:3] + ig_new.shape[1:]), (0, 1, 3, 2, 4))[None]
    upd = [
        tuple((turned(v) if i in (1, 6) else v).reshape(w.shape) for v in news[3 * i : 3 * i + 3])
        for i, w in enumerate(weights)
    ]
    return (
        (block_output, trajectory_grad, images_grad)
        + tuple(u[0] for u in upd)
        + tuple(u[1] for u in upd)
        + tuple(u[2] for u in upd)
    )


def solution(mesh):
    sample = P(("cam", "batch"))
    params = (P("cam", "batch"), P("cam", "batch")) + (P("batch"),) * 5
    images_spec = P("cam", None, "batch")
    return jax.shard_map(
        functools.partial(shards, mesh.shape["batch"]),
        mesh=mesh,
        in_specs=(images_spec, sample, sample, sample, sample) + params * 3,
        out_specs=(sample, sample, images_spec) + params * 3,
        check_vma=False,
    )
```
